32 devices in a mesh: dp: 2 (over core), seq: 4 (over z), fsdp: 4 (over y, x).
Axes of the slice: x: 2, y: 2, z: 4, core: 2. Of those that a mesh axis runs over, the one named last changes fastest.
Arguments:
- hidden_in: bfloat16 [16, 512, 1024], P(('dp', 'fsdp'), 'seq'), may hold values from -6 to 6
- lengths: int32 [16], P(('dp', 'fsdp')), may hold values from 1 to 512, as said below
- norm_gain: float32 [1024], P('fsdp'), may hold values from 0.5 to 1.5
- in_weight: bfloat16 [1024, 4096], P('fsdp'), may hold values from -0.1875 to 0.1875
- conv_weight: float32 [4, 2048], P(None, 'fsdp'), may hold values from -2.5 to 2.5
- conv_bias: float32 [2048], P('fsdp'), may hold values from -0.5 to 0.5
- xproj_weight: bfloat16 [2048, 96], P('fsdp'), may hold values from -0.125 to 0.125
- dt_weight: bfloat16 [64, 2048], P(None, 'fsdp'), may hold values from -0.75 to 0.75
- dt_bias: float32 [2048], P('fsdp'), may hold values from -4.5 to -2
- a_log: float32 [16, 2048], P(None, 'fsdp'), may hold values from -4 to 2.5
- skip_gain: float32 [2048], P('fsdp'), may hold values from 0.5 to 1.5
- out_weight: bfloat16 [2048, 1024], P('fsdp'), may hold values from -0.125 to 0.125
- out_grad: bfloat16 [16, 512, 1024], P(('dp', 'fsdp'), 'seq'), may hold values from -6 to 6
Outputs:
- hidden_out: bfloat16 [16, 512, 1024], P(('dp', 'fsdp'), 'seq')
- input_grad: bfloat16 [16, 512, 1024], P(('dp', 'fsdp'), 'seq')
- grad_norm_gain: float32 [1024], P('fsdp')
- grad_in_weight: float32 [1024, 4096], P('fsdp')
- grad_conv_weight: float32 [4, 2048], P(None, 'fsdp')
- grad_conv_bias: float32 [2048], P('fsdp')
- grad_xproj_weight: float32 [2048, 96], P('fsdp')
- grad_dt_weight: float32 [64, 2048], P(None, 'fsdp')
- grad_dt_bias: float32 [2048], P('fsdp')
- grad_a_log: float32 [16, 2048], P(None, 'fsdp')
- grad_skip_gain: float32 [2048], P('fsdp')
- grad_out_weight: float32 [2048, 1024], P('fsdp')
The draws below stay inside these ranges and needn't reach their ends.
Inputs may be any that keep to these rules, and one draw needn't show every extreme that they name: `lengths`: in each aligned run of 2 contexts (those of one group of the seq axis) one context has all 512 tokens valid; padding lies after a context's valid tokens.
All inputs are finite; a program needn't handle non-finite values.
Results may differ from the reference program's by a relative error of at most 0.012.
Values may be sent and summed in bfloat16 or wider, within the bound.
A program may use at most 256 MiB of HBM per device.

```python
import math
import jax
import jax.numpy as jnp
from jax import lax

D = 1024
E = 2048
N = 16
R = 64
CONV = 4
SEQS = 2
LENGTH = 512
CONTEXTS = 16


def draw_lengths(key, part):
    key = jax.random.fold_in(key, 11)
    pick_key, length_key = jax.random.split(key)
    groups = CONTEXTS // SEQS
    short = jax.random.randint(length_key, (groups, SEQS), 1, LENGTH + 1)
    which = jax.random.randint(pick_key, (groups, 1), 0, SEQS)
    whole = jnp.arange(SEQS)[None, :] == which
    return jnp.where(whole, LENGTH, short).reshape(CONTEXTS).astype(jnp.int32)


def block_scale(key, extent, cuts, smallest, largest):
    def one(dim, parts):
        draws = jax.random.uniform(jax.random.fold_in(jax.random.fold_in(key, 6), dim), (parts,), jnp.float32, smallest / len(cuts), largest / len(cuts))
        return jnp.repeat(jnp.exp(draws), extent[dim] // parts).reshape((-1,) + (1,) * (len(extent) - dim - 1))

    factor_of = one(*cuts[0])
    for cut in cuts[1:]:
        factor_of = factor_of * one(*cut)
    return factor_of


def bell_draw(rng, shape, spread, limit, cuts=(), dtype=jnp.bfloat16):
    values = jax.random.normal(rng, shape, jnp.float32) * spread
    if len(cuts) > 0:
        values = block_scale(rng, shape, cuts, -0.22, 0.18) * values
    return jnp.clip(values, min=-limit, max=limit).astype(dtype)


def setup_inputs(seed: int = 0) -> dict:
    splits = jax.random.split(jax.random.key(seed), 14)
    hidden_in = bell_draw(splits[0], (CONTEXTS, LENGTH, D), 1.0, 6.0, ((0, 8), (1, 4)))
    lengths = draw_lengths(jax.random.fold_in(splits[13], 71), 0)
    norm_gain = jnp.clip(1.0 + 0.1 * jax.random.normal(splits[2], (D,), jnp.float32), 0.5, 1.5)
    in_weight = bell_draw(splits[3], (D, 2 * E), D ** -0.5, 0.1875, ((0, 4),))
    conv_weight = bell_draw(splits[4], (CONV, E), 0.5, 2.5, ((1, 4),), jnp.float32)
    conv_bias = jnp.clip(jax.random.uniform(splits[5], (E,), jnp.float32, -0.5, 0.5) * block_scale(splits[5], (E,), ((0, 4),), -0.4, 0.0), -0.5, 0.5)
    xproj_weight = bell_draw(splits[6], (E, R + 2 * N), E ** -0.5, 0.125, ((0, 4),))
    dt_weight = bell_draw(splits[7], (R, E), R ** -0.5, 0.75, ((1, 4),))
    dt_bias = jnp.clip(-4.5 + 2.5 * jax.random.uniform(splits[8], (E,), jnp.float32) ** block_scale(splits[8], (E,), ((0, 4),), -0.2, 0.2), -4.5, -2.0)
    a_log = jnp.clip(-4.0 + 6.5 * jax.random.uniform(splits[9], (N, E), jnp.float32) ** block_scale(splits[9], (N, E), ((1, 4),), -0.2, 0.2), -4.0, 2.5)
    skip_gain = jnp.clip(0.5 + 1.0 * jax.random.uniform(splits[10], (E,), jnp.float32) ** block_scale(splits[10], (E,), ((0, 4),), -0.2, 0.2), 0.5, 1.5)
    out_weight = bell_draw(splits[11], (E, D), E ** -0.5, 0.125, ((0, 4),))
    out_grad = bell_draw(splits[12], (CONTEXTS, LENGTH, D), 1.0, 6.0, ((0, 8), (1, 4)))
    return {"hidden_in": hidden_in, "lengths": lengths, "norm_gain": norm_gain, "in_weight": in_weight, "conv_weight": conv_weight, "conv_bias": conv_bias, "xproj_weight": xproj_weight, "dt_weight": dt_weight, "dt_bias": dt_bias, "a_log": a_log, "skip_gain": skip_gain, "out_weight": out_weight, "out_grad": out_grad}


@jax.custom_vjp
def low(v):
    return lax.optimization_barrier(v.astype(jnp.bfloat16)).astype(jnp.float32)

@jax.custom_vjp
def low_back(v):
    return v

def low_keep(v):
    return (low(v), None)

def low_pass(kept, grad):
    return (grad,)

def back_keep(v):
    return (v, None)

def back_low(kept, grad):
    return (low(grad),)
low.defvjp(low_keep, low_pass)
low_back.defvjp(back_keep, back_low)
EPS = 1e-05
HIGH = lax.Precision.HIGHEST

def matmul(left, right):
    return jnp.dot(left, right, precision=HIGH, preferred_element_type=jnp.float32)

def selective(delta, drive, bmat, cmat, rates):
    block = math.gcd(LENGTH, 64)

    def one_block(carry, inputs):
        state, decay = carry

        def one_token(h, item):
            d, v, b, c = item
            h = jnp.exp(d[None, :] * decay) * h + v[None, :] * b[:, None]
            return (h, lax.optimization_barrier(jnp.sum(c[:, None] * h, 0)))
        state, outputs = lax.scan(one_token, state, inputs)
        return ((state, decay), outputs)
    shaped = tuple((v.reshape(LENGTH // block, block, v.shape[-1]) for v in (delta, drive, bmat, cmat)))
    start = (jnp.zeros((N, E), jnp.float32), rates)
    _, outputs = lax.scan(jax.checkpoint(one_block), start, shaped)
    return outputs.reshape(LENGTH, E)

def mixer_forward(params, x, length):
    gain, w_in, conv_w, conv_b, w_proj, w_step, step_bias, log_rate, skip, w_out = params
    inverse = lax.rsqrt(lax.optimization_barrier(jnp.mean(x * x, -1, keepdims=True)) + EPS)
    normed = low(x * inverse * gain)
    mixed = low(low_back(matmul(normed, w_in)))
    stream, gate_in = (mixed[:, :E], mixed[:, E:])
    padded = jnp.concatenate([jnp.zeros((CONV - 1, E), jnp.float32), stream], 0)
    conv_out = conv_b + sum((conv_w[k] * padded[k:k + LENGTH] for k in range(CONV)))
    u_val = low(jax.nn.silu(conv_out))
    proj = low_back(matmul(u_val, w_proj))
    step_low = low(proj[:, :R])
    bmat = proj[:, R:R + N]
    cmat = proj[:, R + N:]
    delta = jax.nn.softplus(low_back(matmul(step_low, w_step)) + step_bias)
    rates = -jnp.exp(log_rate)
    y_val = selective(delta, delta * u_val, bmat, cmat, rates) + skip * u_val
    gated = low(y_val * jax.nn.silu(gate_in))
    branch = matmul(gated, w_out)
    mask = (jnp.arange(LENGTH) < length).astype(jnp.float32)[:, None]
    return x + mask * branch

def reference(hidden_in, lengths, norm_gain, in_weight, conv_weight, conv_bias, xproj_weight, dt_weight, dt_bias, a_log, skip_gain, out_weight, out_grad):
    params = tuple((v.astype(jnp.float32) for v in (norm_gain, in_weight, conv_weight, conv_bias, xproj_weight, dt_weight, dt_bias, a_log, skip_gain, out_weight)))

    def per_context(totals, item):
        x, length, cotangent = item

        def forward(inputs, weights):
            return mixer_forward(weights, inputs, length)
        result, pullback = jax.vjp(forward, x.astype(jnp.float32), params)
        x_grad, weight_grads = pullback(cotangent.astype(jnp.float32))
        totals = jax.tree.map(jnp.add, totals, weight_grads)
        return (totals, (result.astype(jnp.bfloat16), x_grad.astype(jnp.bfloat16)))
    zero = jax.tree.map(jnp.zeros_like, params)
    grads, (outputs, input_grads) = lax.scan(per_context, zero, (hidden_in, lengths, out_grad))
    return (outputs, input_grads, grads[0], grads[1], grads[2], grads[3], grads[4], grads[5], grads[6], grads[7], grads[8], grads[9])
```

```python
import functools
import math

import jax
import jax.numpy as jnp
import numpy as np
from jax import lax
from jax.experimental import pallas as pl
from jax.experimental.pallas import tpu as pltpu
from jax.sharding import PartitionSpec as P

EPS = 1e-05
LOG2E = math.log2(math.e)
LANES = 128
GROUP = 16
F32 = jnp.float32
BF16 = jnp.bfloat16
MESH = pl.DeviceIdType.MESH
HR = 128
CHUNK = 512
SLACK = 1


def passed_along(value, axis, by):
    size = lax.axis_size(axis)
    pairs = [(i, i + by) for i in range(size) if 0 <= i + by < size]
    return lax.ppermute(value, axis, pairs)


def silu_grad(v):
    s = jax.nn.sigmoid(v)
    return s * (1.0 + v * (1.0 - s))


def ends_kernel(d_ref, v_ref, dy_ref, b_ref, c_ref, a_ref, h_ref, p_ref):
    state, width = a_ref.shape
    groups = d_ref.shape[1]
    cuts = [slice(j, j + LANES) for j in range(0, width, LANES)]
    rates = [a_ref[:, s] for s in cuts]

    def step(i, carry):
        h, run, p = (list(v) for v in carry)
        for k in range(GROUP):
            b = b_ref[0, i * GROUP + k]
            c = c_ref[0, i * GROUP + k]
            for j, s in enumerate(cuts):
                row = lambda ref: jnp.broadcast_to(ref[0, i, k : k + 1, s], (state, LANES))
                factor = jnp.exp2(row(d_ref) * rates[j])
                h[j] = factor * h[j] + row(v_ref) * b
                run[j] = run[j] * factor
                p[j] = p[j] + run[j] * (c * row(dy_ref))
        return tuple(h), tuple(run), tuple(p)

    zero = tuple(jnp.zeros((state, LANES), F32) for _ in cuts)
    one = tuple(jnp.ones((state, LANES), F32) for _ in cuts)
    h, _, p = lax.fori_loop(0, groups, step, (zero, one, zero))
    for j, s in enumerate(cuts):
        h_ref[0, :, s] = h[j]
        p_ref[0, :, s] = p[j]


def sweep_kernel(
    d_ref, v_ref, dy_ref, b_ref, c_ref, a_ref, h0_ref, p0_ref, cbd_ref, bbd_ref, one_ref,
    y_ref, dg_ref, dp_ref, cacc_ref, bacc_ref, racc_ref, h_s, a_s, g_s, w_s,
):
    state, width = a_ref.shape
    groups = d_ref.shape[1]
    cuts = [slice(j, j + LANES) for j in range(0, width, LANES)]
    rates = [a_ref[:, s] for s in cuts]
    across = (((1,), (1,)), ((), ()))

    @pl.when(pl.program_id(1) == 0)
    def _():
        cacc_ref[...] = jnp.zeros_like(cacc_ref)
        bacc_ref[...] = jnp.zeros_like(bacc_ref)

    h_s[0] = h0_ref[0]

    def forward(i, h):
        h = list(h)
        for k in range(GROUP):
            t = i * GROUP + k
            b = b_ref[0, t]
            for j, s in enumerate(cuts):
                row = lambda ref: jnp.broadcast_to(ref[0, i, k : k + 1, s], (state, LANES))
                factor = jnp.exp2(row(d_ref) * rates[j])
                h[j] = factor * h[j] + row(v_ref) * b
                h_s[t + 1, :, s] = h[j]
                a_s[t, :, s] = factor
        held = h_s[pl.ds(i * GROUP + 1, GROUP)].reshape(GROUP * state, width).astype(BF16)
        y_ref[0, i] = jnp.dot(cbd_ref[0, i], held, preferred_element_type=F32)
        cacc_ref[0, i] += lax.dot_general(
            dy_ref[0, i].astype(BF16), held, across, preferred_element_type=F32
        )
        return tuple(h)

    lax.fori_loop(0, groups, forward, tuple(h0_ref[0, :, s] for s in cuts))

    def backward(turn, carry):
        i = groups - 1 - turn
        p, total = (list(v) for v in carry)
        for k in reversed(range(GROUP)):
            t = i * GROUP + k
            c = c_ref[0, t]
            for j, s in enumerate(cuts):
                row = lambda ref: jnp.broadcast_to(ref[0, i, k : k + 1, s], (state, LANES))
                g = c * row(dy_ref) + p[j]
                p[j] = a_s[t, :, s] * g
                w = p[j] * h_s[t, :, s]
                total[j] = total[j] + w * row(d_ref)
                g_s[k, :, s] = g.astype(BF16)
                w_s[k, :, s] = (w * rates[j]).astype(BF16)
        g_all = g_s[...].reshape(GROUP * state, width)
        dg_ref[0, i] = jnp.dot(bbd_ref[0, i], g_all, preferred_element_type=F32)
        dp_ref[0, i] = jnp.dot(
            one_ref[...], w_s[...].reshape(GROUP * state, width), preferred_element_type=F32
        )
        bacc_ref[0, i] += lax.dot_general(
            v_ref[0, i].astype(BF16), g_all, across, preferred_element_type=F32
        )
        return tuple(p), tuple(total)

    zero = tuple(jnp.zeros((state, LANES), F32) for _ in cuts)
    start = tuple(p0_ref[0, :, s] for s in cuts)
    _, total = lax.fori_loop(0, groups, backward, (start, zero))
    for j, s in enumerate(cuts):
        racc_ref[0, :, s] = total[j]


def gather_kernel(plan, *refs):
    n = 5
    srcs, dsts = refs[:n], refs[n:2*n]
    send, recv, local = refs[2*n:]
    d, f = lax.axis_index("dp"), lax.axis_index("fsdp")
    fx, fy, fd = f ^ 1, f ^ 2, f ^ 3
    sib = {"dp": 1 - d}
    tox, toy = {"fsdp": fx}, {"fsdp": fy}
    barrier = pltpu.get_barrier_semaphore()
    for who in (tox, toy, sib):
        pl.semaphore_signal(barrier, inc=1, device_id=who, device_id_type=MESH)
    pl.semaphore_wait(barrier, 3)

    def window(p, owner, half, q):
        k, dim, cols = plan[p]
        rows = srcs[k].shape[0]
        part = rows // 4
        at = (half * 2 + q) * part
        c = cols or (0, srcs[k].shape[1])
        if dim == 0:
            return dsts[k].at[pl.ds(pl.multiple_of(owner * rows + at, part), part), c[0]:c[1]]
        w = c[1] - c[0]
        return dsts[k].at[pl.ds(pl.multiple_of(at, part), part), pl.ds(pl.multiple_of(owner * w, w), w)]

    def own(p, half, q):
        k, dim, cols = plan[p]
        part = srcs[k].shape[0] // 4
        c = cols or (0, srcs[k].shape[1])
        return srcs[k].at[pl.ds(pl.multiple_of((half * 2 + q) * part, part), part), c[0]:c[1]]

    def copy(src, dst, p, kind, who):
        return pltpu.make_async_remote_copy(src_ref=src, dst_ref=dst, send_sem=send.at[p, kind], recv_sem=recv.at[p, kind], device_id=who, device_id_type=MESH)

    locals_ = []
    started = []
    for p in range(len(plan)):
        for q in (0, 1):
            a = copy(own(p, d, q), window(p, f, d, q), p, q, tox); a.start()
            b = copy(own(p, d, 1 - q), window(p, f, d, 1 - q), p, 3 - q, toy); b.start()
            started += [a, b]
    for p in range(len(plan)):
        for half in (0, 1):
            for q in (0, 1):
                c = pltpu.make_async_copy(own(p, half, q), window(p, f, half, q), local.at[p, half * 2 + q]); c.start(); locals_.append(c)
    def arrived(p, kind, owner, half, q):
        w = window(p, owner, half, q)
        copy(w, w, p, kind, sib).wait_recv()
        return w
    for p in range(len(plan)):
        for kind, owner, q in ((0, fx, 0), (3, fy, 1), (1, fx, 1), (2, fy, 0)):
            w = arrived(p, kind, owner, d, q)
            if kind == 0:
                c = copy(w, w, p, 4, toy); c.start(); started.append(c)
            if kind == 3:
                c = copy(w, w, p, 5, tox); c.start(); started.append(c)
            c = copy(w, w, p, 6 + kind, sib); c.start(); started.append(c)
    for p in range(len(plan)):
        for kind, q in ((4, 0), (5, 1)):
            w = arrived(p, kind, fd, d, q)
            c = copy(w, w, p, 6 + kind, sib); c.start(); started.append(c)
    for p in range(len(plan)):
        for kind, owner, q in ((0, fx, 0), (3, fy, 1), (1, fx, 1), (2, fy, 0), (4, fd, 0), (5, fd, 1)):
            arrived(p, 6 + kind, owner, 1 - d, q)
    for c in started: c.wait_send()
    for c in locals_: c.wait()

def gather(in_w, out_w, xp, dt, small):
    ops = (in_w, out_w, xp, dt, small)
    dims = (0, 0, 0, 1, 1)
    half = in_w.shape[1] // 2
    plan = ((0, 0, (0, half)), (2, 0, None), (3, 1, None), (4, 1, None), (0, 0, (half, 2 * half)), (1, 0, None))
    def full(v, dim):
        s = list(v.shape); s[dim] *= 4
        return jax.ShapeDtypeStruct(tuple(s), v.dtype)
    m = len(plan)
    return pl.pallas_call(functools.partial(gather_kernel, plan),
        in_specs=[pl.BlockSpec(memory_space=pltpu.VMEM)] * 5,
        out_specs=[pl.BlockSpec(memory_space=pl.ANY)] * 5,
        out_shape=[full(v, dm) for v, dm in zip(ops, dims)],
        scratch_shapes=[pltpu.SemaphoreType.DMA((m, 12)), pltpu.SemaphoreType.DMA((m, 12)), pltpu.SemaphoreType.DMA((m, 4))],
        compiler_params=pltpu.CompilerParams(collective_id=0, has_side_effects=True, vmem_limit_bytes=40<<20), name="gather")(*ops)


def reduce_kernel(span, made, sets, lhs, rhs, pre, out, g, ra, rx, ry, mine, zlo, zhi, zout, send, recv):
    d, s, f = (lax.axis_index(a) for a in ("dp", "seq", "fsdp"))
    fx, fy, fd = f ^ 1, f ^ 2, f ^ 3
    chunks = out.shape[0]
    q = HR // 2
    root = (span - 1) // 2
    tox, toy, sib = {"fsdp": fx}, {"fsdp": fy}, {"dp": 1 - d}
    up, down = {"seq": jnp.minimum(s + 1, span - 1)}, {"seq": jnp.maximum(s - 1, 0)}
    barrier = pltpu.get_barrier_semaphore()
    for who in (tox, toy, sib):
        pl.semaphore_signal(barrier, inc=1, device_id=who, device_id_type=MESH)
    @pl.when(s > 0)
    def _(): pl.semaphore_signal(barrier, inc=1, device_id=down, device_id_type=MESH)
    @pl.when(s < span - 1)
    def _(): pl.semaphore_signal(barrier, inc=1, device_id=up, device_id_type=MESH)
    ends = (s == 0) | (s == span - 1)
    pl.semaphore_wait(barrier, jnp.where(ends, 4, 5) if span > 1 else 3)

    def copy(kind, c, src, dst, who):
        return pltpu.make_async_remote_copy(src_ref=src, dst_ref=dst, send_sem=send.at[kind, c], recv_sem=recv.at[kind, c], device_id=who, device_id_type=MESH)
    lo, hi = slice(0, q), slice(q, HR)
    A = lambda c: copy(0, c, g.at[c, :, 1 - d], ra.at[c], sib)
    X = lambda c: (copy(1, c, ra.at[c, fd, lo], rx.at[c, 0], tox), copy(2, c, ra.at[c, fx, lo], rx.at[c, 1], tox))
    XV = lambda c: copy(3, c, ra.at[c, fx, hi], rx.at[c, 2], tox)
    Y = lambda c: (copy(4, c, ra.at[c, fd, hi], ry.at[c, 0], toy), copy(5, c, ra.at[c, fy, hi], ry.at[c, 2], toy))
    YV = lambda c: copy(6, c, ra.at[c, fy, lo], ry.at[c, 1], toy)
    ZU = lambda c: copy(7, c, zout.at[c], zlo.at[c], up)
    ZD = lambda c: copy(8, c, zout.at[c], zhi.at[c], down)
    TU = lambda c: copy(9, c, out.at[c, d], out.at[c, d], up)
    TD = lambda c: copy(10, c, out.at[c, d], out.at[c, d], down)
    D = lambda c: copy(11, c, out.at[c, d], out.at[c, d], sib)
    below, above = s < root, s > root
    spot = jnp.where(below, s, jnp.where(above, span - 1 - s, 0))
    far = jnp.abs(s - root)
    most = max(root, span - 1 - root)

    def stage(c, body):
        @pl.when((c >= 0) & (c < chunks))
        def _(): body(c)

    def produce(c):
        @pl.when(c < made)
        def _():
            for j in range(4):
                for h in range(2):
                    g[c, j, h] = pre[c, j, h]
        @pl.when(c >= made)
        def _():
            k = 0
            for first in sets[1:]:
                k = k + (c >= first).astype(jnp.int32)
            right = rhs[c - made]
            for j in range(4):
                t = jnp.dot(lhs[k, pl.ds(j * 2 * HR, 2 * HR)], right, preferred_element_type=F32).astype(BF16)
                g[c, j, 0] = t[:HR]
                g[c, j, 1] = t[HR:]
        A(c).start()

    def first_sum(c):
        A(c).wait_recv()
        for j in range(4):
            ra[c, j] = (ra[c, j].astype(F32) + g[c, j, d].astype(F32)).astype(BF16)
        for t in X(c) + Y(c):
            t.start()

    def second_sum(c):
        X(c)[0].wait_recv()
        ra[c, fy, lo] = (ra[c, fy, lo].astype(F32) + rx[c, 0].astype(F32)).astype(BF16)
        YV(c).start()
        Y(c)[0].wait_recv()
        ra[c, fx, hi] = (ra[c, fx, hi].astype(F32) + ry[c, 0].astype(F32)).astype(BF16)
        XV(c).start()

    def third_sum(c):
        X(c)[1].wait_recv(); Y(c)[1].wait_recv(); XV(c).wait_recv(); YV(c).wait_recv()
        for k, rows in enumerate((lo, hi)):
            mine[c, rows] = ra[c, f, rows].astype(F32) + rx[c, 1 + k].astype(F32) + ry[c, 1 + k].astype(F32)

    def inward(c):
        @pl.when(below & (s > 0))
        def _():
            ZU(c).wait_recv()
            zout[c] = (mine[c] + zlo[c].astype(F32)).astype(BF16)
        @pl.when(above & (s < span - 1))
        def _():
            ZD(c).wait_recv()
            zout[c] = (mine[c] + zhi[c].astype(F32)).astype(BF16)
        @pl.when((s != root) & ((s == 0) | (s == span - 1)))
        def _():
            zout[c] = mine[c].astype(BF16)
        pl.when(below)(lambda: ZU(c).start())
        pl.when(above)(lambda: ZD(c).start())

    def at_root(c):
        total = mine[c]
        if root > 0:
            ZU(c).wait_recv()
            total = total + zlo[c].astype(F32)
        if span - 1 > root:
            ZD(c).wait_recv()
            total = total + zhi[c].astype(F32)
        out[c, d] = total.astype(BF16)
        if root > 0: TD(c).start()
        if span - 1 > root: TU(c).start()
        D(c).start()

    def outward(c):
        @pl.when(above)
        def _():
            TU(c).wait_recv()
            pl.when(s < span - 1)(lambda: TU(c).start())
        @pl.when(below)
        def _():
            TD(c).wait_recv()
            pl.when(s > 0)(lambda: TD(c).start())
        D(c).start()

    base = 1 + 2 * SLACK + 1
    def step(i, carry):
        stage(i, produce)
        stage(i - 1, first_sum)
        stage(i - 1 - SLACK, second_sum)
        stage(i - 1 - 2 * SLACK, third_sum)
        pl.when(s != root)(lambda: stage(i - base - SLACK * spot, inward))
        pl.when(s == root)(lambda: stage(i - base - SLACK * most, at_root))
        pl.when(s != root)(lambda: stage(i - base - SLACK * most - SLACK * far, outward))
        return carry
    lax.fori_loop(0, chunks + base + 2 * SLACK * most + 1, step, 0)

    def finish(c, carry):
        D(c).wait_recv()
        A(c).wait_send()
        for t in X(c) + Y(c) + (XV(c), YV(c)): t.wait_send()
        pl.when(below)(lambda: ZU(c).wait_send())
        pl.when(above)(lambda: ZD(c).wait_send())
        if root > 0: pl.when((s <= root) & (s > 0))(lambda: TD(c).wait_send())
        if span - 1 > root: pl.when((s >= root) & (s < span - 1))(lambda: TU(c).wait_send())
        D(c).wait_send()
        return carry
    lax.fori_loop(0, chunks, finish, 0)

def reduce_grads(lhs, rhs, pre, sets):
    made, nb, cw = pre.shape[0], rhs.shape[0], rhs.shape[2]
    n = made + nb
    span = lax.axis_size("seq")
    v = pltpu.VMEM
    return pl.pallas_call(functools.partial(reduce_kernel, span, made, sets),
        in_specs=[pl.BlockSpec(memory_space=v)] * 3, out_specs=pl.BlockSpec(memory_space=v),
        out_shape=jax.ShapeDtypeStruct((n, 2, HR, cw), BF16),
        scratch_shapes=[v((n, 4, 2, HR, cw), BF16), v((n, 4, HR, cw), BF16), v((n, 3, HR // 2, cw), BF16), v((n, 3, HR // 2, cw), BF16), v((n, HR, cw), F32), v((n, HR, cw), BF16), v((n, HR, cw), BF16), v((n, HR, cw), BF16),
            pltpu.SemaphoreType.DMA((12, n)), pltpu.SemaphoreType.DMA((12, n))],
        compiler_params=pltpu.CompilerParams(collective_id=1, has_side_effects=True, vmem_limit_bytes=60 << 20), name="reduce")(lhs, rhs, pre)


def block_diagonal(v):
    seqs, ctx, state = v.shape
    eye = jnp.eye(GROUP, dtype=F32)[None, None, :, :, None]
    spread = v.reshape(seqs, ctx // GROUP, GROUP, 1, state) * eye
    return spread.reshape(seqs, ctx // GROUP, GROUP, GROUP * state).astype(BF16)


def diagonal_blocks(v):
    seqs, groups, _, wide = v.shape
    state = wide // GROUP
    eye = jnp.eye(GROUP, dtype=F32)[None, None, :, :, None]
    picked = jnp.sum(v.reshape(seqs, groups, GROUP, GROUP, state) * eye, 3)
    return picked.reshape(seqs * groups * GROUP, state)


def local_specs(seqs, ctx, inner, state, width):
    groups = ctx // GROUP
    tok = pl.BlockSpec((1, groups, GROUP, width), lambda c, j: (c, 0, 0, j))
    wide = pl.BlockSpec((1, ctx, state, LANES), lambda c, j: (c, 0, 0, 0))
    rate = pl.BlockSpec((state, width), lambda c, j: (0, j))
    end = pl.BlockSpec((1, state, width), lambda c, j: (c, 0, j))
    diag = pl.BlockSpec((1, groups, GROUP, GROUP * state), lambda c, j: (c, 0, 0, 0))
    return tok, wide, rate, end, diag


def local_ends(delta, drive, dy, b_wide, c_wide, rates):
    seqs, groups, _, inner = delta.shape
    state = rates.shape[0]
    width = 512
    tok, wide, rate, end, _ = local_specs(seqs, groups * GROUP, inner, state, width)
    return pl.pallas_call(
        ends_kernel,
        grid=(seqs, inner // width),
        in_specs=[tok, tok, tok, wide, wide, rate],
        out_specs=[end, end],
        out_shape=[jax.ShapeDtypeStruct((seqs, state, inner), F32)] * 2,
        compiler_params=pltpu.CompilerParams(vmem_limit_bytes=56 << 20),
        name="ends",
    )(delta, drive, dy, b_wide, c_wide, rates)


def sweep(delta, drive, dy, b_in, c_in, b_wide, c_wide, rates, start, final):
    seqs, groups, _, inner = delta.shape
    ctx = groups * GROUP
    state = rates.shape[0]
    width = 512
    tok, wide, rate, end, diag = local_specs(seqs, ctx, inner, state, width)
    ones = block_diagonal(jnp.ones((1, GROUP, state), F32))[0, 0]
    token_shape = jax.ShapeDtypeStruct(delta.shape, F32)
    diag_shape = jax.ShapeDtypeStruct((seqs, groups, GROUP, GROUP * state), F32)
    return pl.pallas_call(
        sweep_kernel,
        grid=(seqs, inner // width),
        in_specs=[tok, tok, tok, wide, wide, rate, end, end, diag, diag]
        + [pl.BlockSpec(ones.shape, lambda c, j: (0, 0))],
        out_specs=[tok, tok, tok, diag, diag, end],
        out_shape=[token_shape] * 3
        + [diag_shape] * 2
        + [jax.ShapeDtypeStruct((seqs, state, inner), F32)],
        scratch_shapes=[
            pltpu.VMEM((ctx + 1, state, width), F32),
            pltpu.VMEM((ctx, state, width), F32),
            pltpu.VMEM((GROUP, state, width), BF16),
            pltpu.VMEM((GROUP, state, width), BF16),
        ],
        compiler_params=pltpu.CompilerParams(vmem_limit_bytes=56 << 20),
        name="sweep",
    )(
        delta, drive, dy, b_wide, c_wide, rates, start, final,
        block_diagonal(c_in), block_diagonal(b_in), ones,
    )


def body(
    hidden_in, lengths, norm_gain, in_weight, conv_weight, conv_bias, xproj_weight,
    dt_weight, dt_bias, a_log, skip_gain, out_weight, out_grad,
):
    seqs, ctx, width = hidden_in.shape
    taps, share = conv_weight.shape
    state = a_log.shape[0]
    rank = dt_weight.shape[0]
    reach = taps - 1
    rows = ctx * seqs
    groups = ctx // GROUP
    small = jnp.concatenate(
        [conv_weight, a_log, conv_bias[None], dt_bias[None], skip_gain[None]]
        + [jnp.pad(norm_gain, (0, share - norm_gain.shape[0]))[None]],
        0,
    )
    used = small.shape[0]
    small = jnp.pad(small, ((0, -used % 32), (0, 0)))
    in_matrix, out_matrix, proj_matrix, step_matrix, small = gather(
        in_weight, out_weight, xproj_weight, dt_weight, small
    )
    gain = small[used - 1].reshape(-1, share)[:, : norm_gain.shape[0]].reshape(-1)
    conv_taps, log_rate = small[:taps], small[taps : taps + state]
    conv_shift, step_bias, skip = (small[taps + state + i] for i in range(3))
    inner = proj_matrix.shape[0]
    dot = lambda a, b: jnp.dot(a, b, preferred_element_type=F32)

    x_tok = hidden_in.astype(F32)
    position = lax.axis_index("seq") * ctx + jnp.arange(ctx, dtype=jnp.int32)
    mask = (position[None, :] < lengths[:, None]).astype(F32)[:, :, None]

    def normalised(x):
        inverse = lax.rsqrt(jnp.mean(x * x, -1, keepdims=True) + EPS)
        return inverse, (x * inverse * gain).astype(BF16)

    inverse, normed = normalised(x_tok)
    normed = normed.reshape(rows, width)
    mixed = dot(normed, in_matrix).astype(BF16)
    stream = mixed[:, :inner].reshape(seqs, ctx, inner)
    gate_in = mixed[:, inner:].astype(F32).reshape(seqs, ctx, inner)
    before = passed_along(stream[:, ctx - reach :], "seq", 1)
    extended = jnp.concatenate([before, stream], 1).astype(F32)
    conv_out = conv_shift + sum(conv_taps[k] * extended[:, k : k + ctx] for k in range(taps))
    u_low = jax.nn.silu(conv_out).astype(BF16)
    u_rows = u_low.reshape(rows, inner)
    proj = dot(u_rows, proj_matrix)
    step_low = proj[:, :rank].astype(BF16)
    b_in = proj[:, rank : rank + state].reshape(seqs, ctx, state)
    c_in = proj[:, rank + state :].reshape(seqs, ctx, state)
    raw = dot(step_low, step_matrix).reshape(seqs, ctx, inner) + step_bias
    delta = jax.nn.softplus(raw)
    rates = -jnp.exp(log_rate)
    rates2 = rates * LOG2E
    u_float = u_low.astype(F32)
    drive = delta * u_float

    cotangent = out_grad.astype(F32)
    branch_grad = (cotangent * mask).astype(BF16).reshape(rows, width)
    gated_grad = lax.dot_general(
        branch_grad, out_matrix, (((1,), (1,)), ((), ())), preferred_element_type=F32
    ).reshape(seqs, ctx, inner)
    gate_act = jax.nn.silu(gate_in)
    y_grad = gated_grad * gate_act

    grouped = lambda v: v.reshape(seqs, groups, GROUP, inner)
    b_wide = jnp.broadcast_to(b_in[..., None], (seqs, ctx, state, LANES))
    c_wide = jnp.broadcast_to(c_in[..., None], (seqs, ctx, state, LANES))
    scan_args = (grouped(delta), grouped(drive), grouped(y_grad))
    local_end, local_back = local_ends(*scan_args, b_wide, c_wide, rates2)

    blocks = lax.axis_size("seq")
    me = lax.axis_index("seq")
    ends = lax.all_gather(jnp.stack([local_end, local_back]).astype(BF16), "seq")
    sums = lax.all_gather(jnp.sum(delta, 1), "seq")
    start = jnp.zeros((seqs, state, inner), F32)
    final = jnp.zeros((seqs, state, inner), F32)
    for k in range(blocks):
        decay = jnp.exp2(sums[k][:, None, :] * rates2)
        start = jnp.where(k < me, decay * start + ends[k, 0].astype(F32), start)
        r = blocks - 1 - k
        decay = jnp.exp2(sums[r][:, None, :] * rates2)
        final = jnp.where(r > me, decay * final + ends[r, 1].astype(F32), final)

    y, drive_grad, delta_part, c_acc, b_acc, rate_grad = sweep(
        *scan_args, b_in, c_in, b_wide, c_wide, rates2, start, final
    )
    ungrouped = lambda v: v.reshape(seqs, ctx, inner)
    y_val = ungrouped(y) + skip * u_float
    drive_grad = ungrouped(drive_grad)
    c_grad, b_grad = diagonal_blocks(c_acc), diagonal_blocks(b_acc)
    log_grad = jnp.sum(rate_grad, 0) * rates

    gated = (y_val * gate_act).astype(BF16).reshape(rows, inner)
    branch = dot(gated, out_matrix).reshape(seqs, ctx, width)
    hidden_out = (x_tok + mask * branch).astype(BF16)
    contract = lambda a, b: lax.dot_general(
        a, b, (((0,), (0,)), ((), ())), preferred_element_type=F32
    )
    out_w_grad = contract(gated, branch_grad)
    z_grad = gated_grad * y_val * silu_grad(gate_in)
    skip_grad = jnp.sum(y_grad * u_float, (0, 1))
    delta_grad = drive_grad * u_float + ungrouped(delta_part) * (1.0 / LOG2E)
    u_grad = y_grad * skip + drive_grad * delta
    raw_grad = delta_grad * jax.nn.sigmoid(raw)
    bias_grad = jnp.sum(raw_grad, (0, 1))
    raw_low = raw_grad.astype(BF16).reshape(rows, inner)
    step_w_grad = contract(step_low, raw_low)
    step_grad = lax.dot_general(
        raw_low, step_matrix, (((1,), (1,)), ((), ())), preferred_element_type=F32
    )
    proj_grad = jnp.concatenate([step_grad, b_grad, c_grad], 1).astype(BF16)
    proj_w_grad = contract(proj_grad, u_rows)
    u_grad = u_grad + lax.dot_general(
        proj_grad, proj_matrix, (((1,), (1,)), ((), ())), preferred_element_type=F32
    ).reshape(seqs, ctx, inner)
    conv_grad = u_grad * silu_grad(conv_out)
    shift_grad = jnp.sum(conv_grad, (0, 1))
    taps_grad = jnp.stack(
        [jnp.sum(conv_grad * extended[:, k : k + ctx], (0, 1)) for k in range(taps)], 0
    )
    after = passed_along(conv_grad[:, :reach], "seq", -1)
    later = jnp.concatenate([conv_grad, after], 1)
    stream_grad = sum(conv_taps[k] * later[:, reach - k : reach - k + ctx] for k in range(taps))
    mixed_grad = jnp.concatenate(
        [stream_grad.reshape(rows, inner), z_grad.reshape(rows, inner)], 1
    ).astype(BF16)
    in_w_grad = contract(normed, mixed_grad)
    normed_grad = lax.dot_general(
        mixed_grad, in_matrix, (((1,), (1,)), ((), ())), preferred_element_type=F32
    ).reshape(seqs, ctx, width)
    gain_grad = jnp.sum(normed_grad * x_tok * inverse, (0, 1))
    scaled = normed_grad * gain
    x_grad = (
        inverse * scaled
        - x_tok * inverse * inverse * inverse * jnp.mean(scaled * x_tok, -1, keepdims=True)
        + cotangent
    )
    input_grad = x_grad.astype(BF16)

    shards = lax.axis_size("fsdp")
    gain_rows = jnp.pad(gain_grad.reshape(shards, -1), ((0, 0), (0, share - width // shards)))
    rest = jnp.concatenate(
        [taps_grad, log_grad, shift_grad[None], bias_grad[None], skip_grad[None]]
        + [gain_rows.reshape(1, inner), step_w_grad, proj_w_grad],
        0,
    )
    rest = jnp.pad(rest, ((0, 2 * HR - rest.shape[0]), (0, 0))).astype(BF16)
    pre = rest.reshape(2, HR, shards, share // CHUNK, CHUNK).transpose(3, 2, 0, 1, 4)
    tall = gated.T.reshape(shards, 2, 2, HR, rows).transpose(2, 0, 1, 3, 4)
    lhs = jnp.concatenate([tall.reshape(2, -1, rows), normed.T[None]], 0)
    right = branch_grad.reshape(rows, -1, CHUNK).transpose(1, 0, 2)
    mixed_right = mixed_grad.reshape(rows, -1, CHUNK).transpose(1, 0, 2)
    made, part = pre.shape[0], right.shape[0]
    sums = reduce_grads(
        lhs, jnp.concatenate([right, right, mixed_right], 0), pre, (made, made + part, made + 2 * part)
    ).astype(F32)
    rest = sums[:made].transpose(1, 2, 0, 3).reshape(2 * HR, share)
    out_w = sums[made : made + 2 * part].reshape(2, part, 2, HR, CHUNK).transpose(2, 0, 3, 1, 4)
    out_w = out_w.reshape(-1, width)
    in_w = sums[made + 2 * part :].transpose(1, 2, 0, 3).reshape(2 * HR, 2 * inner)
    at = taps + state
    return (
        hidden_out, input_grad, rest[at + 3, : width // shards], in_w, rest[:taps], rest[at],
        rest[at + 4 + rank : at + 4 + rank + proj_matrix.shape[1]].T, rest[at + 4 : at + 4 + rank],
        rest[at + 1], rest[taps:at], rest[at + 2], out_w,
    )


def solution(mesh):
    tokens = P(("dp", "fsdp"), "seq", None)
    return jax.shard_map(
        body,
        mesh=mesh,
        in_specs=(
            tokens, P(("dp", "fsdp")), P("fsdp"), P("fsdp", None), P(None, "fsdp"), P("fsdp"),
            P("fsdp", None), P(None, "fsdp"), P("fsdp"), P(None, "fsdp"), P("fsdp"),
            P("fsdp", None), tokens,
        ),
        out_specs=(
            tokens, tokens, P("fsdp"), P("fsdp", None), P(None, "fsdp"), P("fsdp"),
            P("fsdp", None), P(None, "fsdp"), P("fsdp"), P(None, "fsdp"), P("fsdp"),
            P("fsdp", None),
        ),
        check_vma=False,
    )
```

```python
import functools
import math

import jax
import jax.numpy as jnp
import numpy as np
from jax import lax
from jax.experimental import pallas as pl
from jax.experimental.pallas import tpu as pltpu
from jax.sharding import PartitionSpec as P

EPS = 1e-05
LOG2E = math.log2(math.e)
LANES = 128
GROUP = 16
F32 = jnp.float32
BF16 = jnp.bfloat16
MESH = pl.DeviceIdType.MESH
HR = 128
CHUNK = 512
SLACK = 1
TAPS = 4


def passed_along(value, axis, by):
    size = lax.axis_size(axis)
    pairs = [(i, i + by) for i in range(size) if 0 <= i + by < size]
    return lax.ppermute(value, axis, pairs)


def silu_grad(v):
    s = jax.nn.sigmoid(v)
    return s * (1.0 + v * (1.0 - s))


def ends_kernel(d_ref, v_ref, dy_ref, b_ref, c_ref, a_ref, h_ref, p_ref):
    state, width = a_ref.shape
    groups = d_ref.shape[1]
    cuts = [slice(j, j + LANES) for j in range(0, width, LANES)]
    rates = [a_ref[:, s] for s in cuts]

    def step(i, carry):
        h, run, p = (list(v) for v in carry)
        for k in range(GROUP):
            b = b_ref[0, i * GROUP + k]
            c = c_ref[0, i * GROUP + k]
            for j, s in enumerate(cuts):
                row = lambda ref: jnp.broadcast_to(ref[0, i, k : k + 1, s], (state, LANES))
                factor = jnp.exp2(row(d_ref) * rates[j])
                h[j] = factor * h[j] + row(v_ref) * b
                run[j] = run[j] * factor
                p[j] = p[j] + run[j] * (c * row(dy_ref))
        return tuple(h), tuple(run), tuple(p)

    zero = tuple(jnp.zeros((state, LANES), F32) for _ in cuts)
    one = tuple(jnp.ones((state, LANES), F32) for _ in cuts)
    h, _, p = lax.fori_loop(0, groups, step, (zero, one, zero))
    for j, s in enumerate(cuts):
        h_ref[0, :, s] = h[j]
        p_ref[0, :, s] = p[j]


def silu_parts(v):
    s = jax.nn.sigmoid(v)
    return v * s, s * (1.0 + v * (1.0 - s))


def sweep_kernel(
    d_ref, u_ref, dy_ref, gg_ref, z_ref, raw_ref, b_ref, c_ref, small_ref, h0_ref, p0_ref,
    cbd_ref, bbd_ref, one_ref,
    gated_ref, zg_ref, ug_ref, rl_ref, cacc_ref, bacc_ref, racc_ref, sums_ref,
    v_s, y_s, h_s, a_s, g_s, w_s,
):
    groups, width = d_ref.shape[1], d_ref.shape[3]
    state = b_ref.shape[2]
    cuts = [slice(j, j + LANES) for j in range(0, width, LANES)]
    all_rates = -jnp.exp(small_ref[TAPS : TAPS + state]) * LOG2E
    rates = [all_rates[:, s] for s in cuts]
    skip = small_ref[TAPS + state + 2 : TAPS + state + 3]
    across = (((1,), (1,)), ((), ()))

    @pl.when(pl.program_id(1) == 0)
    def _():
        cacc_ref[...] = jnp.zeros_like(cacc_ref)
        bacc_ref[...] = jnp.zeros_like(bacc_ref)

    h_s[0] = h0_ref[0]

    def forward(i, h):
        h = list(h)
        u = u_ref[0, i].astype(F32)
        v_s[i] = d_ref[0, i] * u
        for k in range(GROUP):
            t = i * GROUP + k
            b = b_ref[0, t]
            for j, s in enumerate(cuts):
                factor = jnp.exp2(jnp.broadcast_to(d_ref[0, i, k : k + 1, s], (state, LANES)) * rates[j])
                h[j] = factor * h[j] + jnp.broadcast_to(v_s[i, k : k + 1, s], (state, LANES)) * b
                h_s[t + 1, :, s] = h[j]
                a_s[t, :, s] = factor
        held = h_s[pl.ds(i * GROUP + 1, GROUP)].reshape(GROUP * state, width).astype(BF16)
        y = jnp.dot(cbd_ref[0, i], held, preferred_element_type=F32) + skip * u
        cacc_ref[0, i] += lax.dot_general(
            dy_ref[0, i].astype(BF16), held, across, preferred_element_type=F32
        )
        gate, slope = silu_parts(z_ref[0, i].astype(F32))
        gated_ref[0, i] = (y * gate).astype(BF16)
        zg_ref[0, 0, i] = (gg_ref[0, i] * y * slope).astype(BF16)
        return tuple(h)

    lax.fori_loop(0, groups, forward, tuple(h0_ref[0, :, s] for s in cuts))

    def backward(turn, carry):
        i = groups - 1 - turn
        p, total, sums = (list(v) for v in carry)
        for k in reversed(range(GROUP)):
            t = i * GROUP + k
            c = c_ref[0, t]
            for j, s in enumerate(cuts):
                row = lambda ref: jnp.broadcast_to(ref[0, i, k : k + 1, s], (state, LANES))
                g = c * row(dy_ref) + p[j]
                p[j] = a_s[t, :, s] * g
                w = p[j] * h_s[t, :, s]
                total[j] = total[j] + w * row(d_ref)
                g_s[k, :, s] = g.astype(BF16)
                w_s[k, :, s] = (w * rates[j]).astype(BF16)
        g_all = g_s[...].reshape(GROUP * state, width)
        drive_grad = jnp.dot(bbd_ref[0, i], g_all, preferred_element_type=F32)
        delta_part = jnp.dot(
            one_ref[...], w_s[...].reshape(GROUP * state, width), preferred_element_type=F32
        )
        bacc_ref[0, i] += lax.dot_general(
            v_s[i].astype(BF16), g_all, across, preferred_element_type=F32
        )
        u, dy, delta = u_ref[0, i].astype(F32), dy_ref[0, i], d_ref[0, i]
        raw_grad = (drive_grad * u + delta_part * (1.0 / LOG2E)) * jax.nn.sigmoid(raw_ref[0, i])
        rl_ref[0, i] = raw_grad.astype(BF16)
        ug_ref[0, i] = dy * skip + drive_grad * delta
        sums[0] = sums[0] + (dy * u)[:8] + (dy * u)[8:]
        sums[1] = sums[1] + raw_grad[:8] + raw_grad[8:]
        return tuple(p), tuple(total), tuple(sums)

    zero = tuple(jnp.zeros((state, LANES), F32) for _ in cuts)
    start = tuple(p0_ref[0, :, s] for s in cuts)
    none = jnp.zeros((8, width), F32)
    _, total, sums = lax.fori_loop(0, groups, backward, (start, zero, (none, none)))
    for j, s in enumerate(cuts):
        racc_ref[0, :, s] = total[j]
    sums_ref[0, 0] = sums[0]
    sums_ref[0, 1] = sums[1]


def gather_kernel(plan, *refs):
    n = 5
    srcs, dsts = refs[:n], refs[n:2*n]
    send, recv, local = refs[2*n:]
    d, f = lax.axis_index("dp"), lax.axis_index("fsdp")
    fx, fy, fd = f ^ 1, f ^ 2, f ^ 3
    sib = {"dp": 1 - d}
    tox, toy = {"fsdp": fx}, {"fsdp": fy}
    barrier = pltpu.get_barrier_semaphore()
    for who in (tox, toy, sib):
        pl.semaphore_signal(barrier, inc=1, device_id=who, device_id_type=MESH)
    pl.semaphore_wait(barrier, 3)

    def window(p, owner, half, q):
        k, dim, cols = plan[p]
        rows = srcs[k].shape[0]
        part = rows // 4
        at = (half * 2 + q) * part
        c = cols or (0, srcs[k].shape[1])
        if dim == 0:
            return dsts[k].at[pl.ds(pl.multiple_of(owner * rows + at, part), part), c[0]:c[1]]
        w = c[1] - c[0]
        return dsts[k].at[pl.ds(pl.multiple_of(at, part), part), pl.ds(pl.multiple_of(owner * w, w), w)]

    def own(p, half, q):
        k, dim, cols = plan[p]
        part = srcs[k].shape[0] // 4
        c = cols or (0, srcs[k].shape[1])
        return srcs[k].at[pl.ds(pl.multiple_of((half * 2 + q) * part, part), part), c[0]:c[1]]

    def copy(src, dst, p, kind, who):
        return pltpu.make_async_remote_copy(src_ref=src, dst_ref=dst, send_sem=send.at[p, kind], recv_sem=recv.at[p, kind], device_id=who, device_id_type=MESH)

    locals_ = []
    started = []
    for p in range(len(plan)):
        for q in (0, 1):
            a = copy(own(p, d, q), window(p, f, d, q), p, q, tox); a.start()
            b = copy(own(p, d, 1 - q), window(p, f, d, 1 - q), p, 3 - q, toy); b.start()
            started += [a, b]
    for p in range(len(plan)):
        for half in (0, 1):
            for q in (0, 1):
                c = pltpu.make_async_copy(own(p, half, q), window(p, f, half, q), local.at[p, half * 2 + q]); c.start(); locals_.append(c)
    def arrived(p, kind, owner, half, q):
        w = window(p, owner, half, q)
        copy(w, w, p, kind, sib).wait_recv()
        return w
    for p in range(len(plan)):
        for kind, owner, q in ((0, fx, 0), (3, fy, 1), (1, fx, 1), (2, fy, 0)):
            w = arrived(p, kind, owner, d, q)
            if kind == 0:
                c = copy(w, w, p, 4, toy); c.start(); started.append(c)
            if kind == 3:
                c = copy(w, w, p, 5, tox); c.start(); started.append(c)
            c = copy(w, w, p, 6 + kind, sib); c.start(); started.append(c)
    for p in range(len(plan)):
        for kind, q in ((4, 0), (5, 1)):
            w = arrived(p, kind, fd, d, q)
            c = copy(w, w, p, 6 + kind, sib); c.start(); started.append(c)
    for p in range(len(plan)):
        for kind, owner, q in ((0, fx, 0), (3, fy, 1), (1, fx, 1), (2, fy, 0), (4, fd, 0), (5, fd, 1)):
            arrived(p, 6 + kind, owner, 1 - d, q)
    for c in started: c.wait_send()
    for c in locals_: c.wait()

def gather(in_w, out_w, xp, dt, small):
    ops = (in_w, out_w, xp, dt, small)
    dims = (0, 0, 0, 1, 1)
    half = in_w.shape[1] // 2
    plan = ((0, 0, (0, half)), (2, 0, None), (3, 1, None), (4, 1, None), (0, 0, (half, 2 * half)), (1, 0, None))
    def full(v, dim):
        s = list(v.shape); s[dim] *= 4
        return jax.ShapeDtypeStruct(tuple(s), v.dtype)
    m = len(plan)
    return pl.pallas_call(functools.partial(gather_kernel, plan),
        in_specs=[pl.BlockSpec(memory_space=pltpu.VMEM)] * 5,
        out_specs=[pl.BlockSpec(memory_space=pl.ANY)] * 5,
        out_shape=[full(v, dm) for v, dm in zip(ops, dims)],
        scratch_shapes=[pltpu.SemaphoreType.DMA((m, 12)), pltpu.SemaphoreType.DMA((m, 12)), pltpu.SemaphoreType.DMA((m, 4))],
        compiler_params=pltpu.CompilerParams(collective_id=0, has_side_effects=True, vmem_limit_bytes=40<<20), name="gather")(*ops)


def back_kernel(
    span, state, rank,
    gated, zg, ug, rl, u, conv, lead, step_low, cacc, bacc, normed, x, og, bg, mask,
    in_w, out_w, xp, dt, small, racc, sums,
    hidden_out, input_grad, out_sum, in_sum, rest_sum,
    pg, mixed, cg, ng, rest, g, ra, rx, ry, zlo, zhi, tot, send, recv, halo, local,
):
    d, s, f = (lax.axis_index(a) for a in ("dp", "seq", "fsdp"))
    fx, fy, fd = f ^ 1, f ^ 2, f ^ 3
    chunks = tot.shape[0]
    rows, width = x.shape
    inner = gated.shape[1]
    seqs = cg.shape[0]
    ctx = rows // seqs
    parts = inner // CHUNK
    out_chunks = 2 * width // CHUNK
    in_chunks = 2 * parts
    last = out_chunks + in_chunks
    slots = g.shape[0]
    q = HR // 2
    root = (span - 1) // 2
    tox, toy, sib = {"fsdp": fx}, {"fsdp": fy}, {"dp": 1 - d}
    up, down = {"seq": jnp.minimum(s + 1, span - 1)}, {"seq": jnp.maximum(s - 1, 0)}
    contract = (((0,), (0,)), ((), ()))
    across = (((1,), (1,)), ((), ()))
    dot = lambda a, b, dims=(((1,), (0,)), ((), ())): lax.dot_general(
        a, b, dims, preferred_element_type=F32
    )

    cg[:, ctx:] = jnp.zeros((seqs, cg.shape[1] - ctx, inner), F32)
    barrier = pltpu.get_barrier_semaphore()
    for who in (tox, toy, sib):
        pl.semaphore_signal(barrier, inc=1, device_id=who, device_id_type=MESH)

    @pl.when(s > 0)
    def _():
        pl.semaphore_signal(barrier, inc=1, device_id=down, device_id_type=MESH)

    @pl.when(s < span - 1)
    def _():
        pl.semaphore_signal(barrier, inc=1, device_id=up, device_id_type=MESH)

    ends = (s == 0) | (s == span - 1)
    pl.semaphore_wait(barrier, jnp.where(ends, 4, 5) if span > 1 else 3)

    def copy(kind, c, src, dst, who):
        return pltpu.make_async_remote_copy(
            src_ref=src, dst_ref=dst, send_sem=send.at[kind, c], recv_sem=recv.at[kind, c],
            device_id=who, device_id_type=MESH,
        )

    lo, hi = slice(0, q), slice(q, HR)
    A = lambda c: copy(0, c, g.at[lax.rem(c, slots), :, 1 - d], ra.at[c], sib)
    X0 = lambda c: copy(1, c, ra.at[c, fd, lo], rx.at[c, 0], tox)
    X1 = lambda c: copy(2, c, ra.at[c, fx, lo], rx.at[c, 1], tox)
    X2 = lambda c: copy(3, c, ra.at[c, fx, hi], rx.at[c, 2], tox)
    Y0 = lambda c: copy(4, c, ra.at[c, fd, hi], ry.at[c, 0], toy)
    Y2 = lambda c: copy(5, c, ra.at[c, fy, hi], ry.at[c, 2], toy)
    Y1 = lambda c: copy(6, c, ra.at[c, fy, lo], ry.at[c, 1], toy)
    ZU = lambda c: copy(7, c, ra.at[c, f], zlo.at[c], up)
    ZD = lambda c: copy(8, c, ra.at[c, f], zhi.at[c], down)
    TU = lambda c: copy(9, c, tot.at[c, d], tot.at[c, d], up)
    TD = lambda c: copy(10, c, tot.at[c, d], tot.at[c, d], down)
    D = lambda c: copy(11, c, tot.at[c, d], tot.at[c, d], sib)
    below, above = s < root, s > root
    spot = jnp.where(below, s, jnp.where(above, span - 1 - s, 0))
    far = jnp.abs(s - root)
    most = max(root, span - 1 - root)

    def stage(c, run):
        @pl.when((c >= 0) & (c < chunks))
        def _():
            run(c)

    def produce(c):
        slot = lax.rem(c, slots)

        @pl.when(c >= slots)
        def _():
            A(c - slots).wait_send()

        @pl.when(c < out_chunks)
        def _():
            r = c // (width // CHUNK)
            col = lax.rem(c, width // CHUNK) * CHUNK
            right = bg[:, pl.ds(pl.multiple_of(col, CHUNK), CHUNK)]
            for j in range(4):
                for h in range(2):
                    at = j * (inner // 4) + h * (inner // 8) + r * HR
                    left = gated[:, pl.ds(pl.multiple_of(at, HR), HR)]
                    g[slot, j, h] = dot(left, right, contract).astype(BF16)

        @pl.when((c >= out_chunks) & (c < last))
        def _():
            right = mixed[c - out_chunks]
            for j in range(4):
                t = dot(normed[:, j * 2 * HR : (j + 1) * 2 * HR], right, contract).astype(BF16)
                g[slot, j, 0] = t[:HR]
                g[slot, j, 1] = t[HR:]

        @pl.when(c == last)
        def _():
            for j in range(4):
                for h in range(2):
                    cols = slice(j * CHUNK, (j + 1) * CHUNK)
                    g[slot, j, h] = rest[h * HR : (h + 1) * HR, cols].astype(BF16)

        A(c).start()

    def first_sum(c):
        A(c).wait_recv()
        for j in range(4):
            own = g[lax.rem(c, slots), j, d]
            ra[c, j] = (ra[c, j].astype(F32) + own.astype(F32)).astype(BF16)
        X0(c).start()
        Y0(c).start()
        X1(c).start()
        Y2(c).start()

    def second_sum(c):
        X0(c).wait_recv()
        ra[c, fy, lo] = (ra[c, fy, lo].astype(F32) + rx[c, 0].astype(F32)).astype(BF16)
        Y1(c).start()
        Y0(c).wait_recv()
        ra[c, fx, hi] = (ra[c, fx, hi].astype(F32) + ry[c, 0].astype(F32)).astype(BF16)
        X2(c).start()

    def third_sum(c):
        X1(c).wait_recv()
        Y2(c).wait_recv()
        X2(c).wait_recv()
        Y1(c).wait_recv()
        for k, part in enumerate((lo, hi)):
            total = ra[c, f, part].astype(F32) + rx[c, 1 + k].astype(F32) + ry[c, 1 + k].astype(F32)
            ra[c, f, part] = total.astype(BF16)

    def inward(c):
        @pl.when(below & (s > 0))
        def _():
            ZU(c).wait_recv()
            ra[c, f] = (ra[c, f].astype(F32) + zlo[c].astype(F32)).astype(BF16)

        @pl.when(above & (s < span - 1))
        def _():
            ZD(c).wait_recv()
            ra[c, f] = (ra[c, f].astype(F32) + zhi[c].astype(F32)).astype(BF16)

        pl.when(below)(lambda: ZU(c).start())
        pl.when(above)(lambda: ZD(c).start())

    def at_root(c):
        total = ra[c, f].astype(F32)
        if root > 0:
            ZU(c).wait_recv()
            total = total + zlo[c].astype(F32)
        if span - 1 > root:
            ZD(c).wait_recv()
            total = total + zhi[c].astype(F32)
        tot[c, d] = total.astype(BF16)
        if root > 0:
            TD(c).start()
        if span - 1 > root:
            TU(c).start()
        D(c).start()

    def outward(c):
        @pl.when(above)
        def _():
            TU(c).wait_recv()
            pl.when(s < span - 1)(lambda: TU(c).start())

        @pl.when(below)
        def _():
            TD(c).wait_recv()
            pl.when(s > 0)(lambda: TD(c).start())

        D(c).start()

    tile = 2 * LANES

    def columns(t, size=tile):
        return pl.ds(pl.multiple_of(t * size, size), size)

    def proj_work():
        step_grad = dot(rl[...], dt[...], across)
        r = lax.broadcasted_iota(jnp.int32, (rows, GROUP * state), 0)
        k = lax.broadcasted_iota(jnp.int32, (rows, GROUP * state), 1)
        own = lax.rem(r, GROUP) == k // state
        pick = lambda v: jnp.where(own, v[...], 0.0).astype(BF16)
        at = lax.rem(lax.broadcasted_iota(jnp.int32, (GROUP * state, LANES), 0), state)
        col = lax.broadcasted_iota(jnp.int32, (GROUP * state, LANES), 1)
        fold = lambda first: (col == at + first).astype(F32).astype(BF16)
        grads = jnp.concatenate([step_grad, jnp.zeros((rows, LANES - rank), F32)], 1)
        grads = grads + dot(pick(bacc), fold(rank)) + dot(pick(cacc), fold(rank + state))
        pg[...] = grads.astype(BF16)
        rest[...] = jnp.zeros(rest.shape, F32)
        first = TAPS + state + 4
        used = rank + 2 * state

        def weights(t, carry):
            cols = columns(t)
            rest[first : first + rank, cols] = dot(step_low[...], rl[:, cols], contract)
            rest[first + rank : first + rank + used, cols] = dot(pg[...], u[:, cols], contract)[:used]
            logs = racc[0, :, cols]
            kept = sums[0, :, :, cols]
            for c in range(1, seqs):
                logs = logs + racc[c, :, cols]
                kept = kept + sums[c, :, :, cols]
            rest[TAPS : TAPS + state, cols] = -logs * jnp.exp(small[TAPS : TAPS + state, cols])
            at = TAPS + state
            rest[at + 1 : at + 2, cols] = jnp.sum(kept[1], 0, keepdims=True)
            rest[at + 2 : at + 3, cols] = jnp.sum(kept[0], 0, keepdims=True)
            return carry

        lax.fori_loop(0, inner // tile, weights, 0)

    def conv_work(first, count):
        def one(t, carry):
            cols = columns(t)
            shift = jnp.zeros((1, tile), F32)
            taps = [jnp.zeros((1, tile), F32) for _ in range(TAPS)]
            for c in range(seqs):
                tok = slice(c * ctx, (c + 1) * ctx)
                weight = xp[columns(t)]
                back = dot(pg[tok, : weight.shape[1]], weight, across)
                _, slope = silu_parts(conv[tok, cols])
                grad = (ug[tok, cols] + back) * slope
                cg[c, :ctx, cols] = grad
                before = lead[c, :, cols].astype(F32)
                shift = shift + jnp.sum(grad, 0, keepdims=True)
                for k in range(TAPS):
                    at = GROUP - TAPS + 1 + k
                    taps[k] = taps[k] + jnp.sum(grad * before[at : at + ctx], 0, keepdims=True)
            for k in range(TAPS):
                rest[k : k + 1, cols] = taps[k]
            rest[TAPS + state : TAPS + state + 1, cols] = shift
            return carry

        lax.fori_loop(first, first + count, one, 0)

    edge = cg.shape[1] - ctx
    H = lambda: pltpu.make_async_remote_copy(
        src_ref=cg.at[:, :edge], dst_ref=cg.at[:, ctx:], send_sem=halo.at[0],
        recv_sem=halo.at[1], device_id=down, device_id_type=MESH,
    )

    def halo_send():
        pl.when(s > 0)(lambda: H().start())

    def stream_work():
        pl.when(s < span - 1)(lambda: H().wait_recv())

        def one(t, carry):
            cols = columns(t)
            for c in range(seqs):
                total = 0.0
                for k in range(TAPS):
                    at = TAPS - 1 - k
                    total = total + small[k : k + 1, cols] * cg[c, at : at + ctx, cols]
                half = pl.ds(pl.multiple_of(lax.rem(t, 2) * tile, tile), tile)
                mixed[parts + t // 2, c * ctx : (c + 1) * ctx, half] = total.astype(BF16)
            return carry

        lax.fori_loop(0, inner // tile, one, 0)
        pl.when(s > 0)(lambda: H().wait_send())

    def hidden_work():
        def one(t, carry):
            cols = columns(t)
            branch = dot(gated[...], out_w[:, cols])
            keep = mask[...]
            keep = jnp.concatenate([keep] * (tile // LANES), 1)
            hidden_out[:, cols] = (x[:, cols].astype(F32) + keep * branch).astype(BF16)
            return carry

        lax.fori_loop(0, width // tile, one, 0)

    def norm_work(first, count):
        def one(k, carry):
            cols = columns(lax.rem(k + parts, 2 * parts), CHUNK)
            ng[...] += dot(mixed[k], in_w[:, cols], across)
            return carry

        if first == 0:
            ng[...] = jnp.zeros(ng.shape, F32)
        lax.fori_loop(first, first + count, one, 0)

    def input_work():
        share = width // 4
        at = TAPS + state + 3
        gain = jnp.concatenate(
            [small[at : at + 1, j * CHUNK : j * CHUNK + share] for j in range(4)], 1
        )

        def one(r, total):
            tok = pl.ds(pl.multiple_of(r * GROUP, GROUP), GROUP)
            xs = x[tok].astype(F32)
            inverse = lax.rsqrt(jnp.mean(xs * xs, -1, keepdims=True) + EPS)
            grad = ng[tok]
            scaled = grad * gain
            slope = jnp.mean(scaled * xs, -1, keepdims=True)
            out = inverse * scaled - xs * (inverse * inverse * inverse * slope)
            input_grad[tok] = (out + og[tok].astype(F32)).astype(BF16)
            return total + grad * (xs * inverse)

        total = lax.fori_loop(0, rows // GROUP, one, jnp.zeros((GROUP, width), F32))
        total = jnp.sum(total, 0, keepdims=True)
        for j in range(4):
            rest[at : at + 1, j * CHUNK : j * CHUNK + share] = total[:, j * share : (j + 1) * share]

    mixed[:parts] = zg[...]
    tiles = inner // tile
    work = {
        0: proj_work,
        1: lambda: conv_work(0, tiles // 2),
        2: lambda: conv_work(tiles // 2, tiles // 2),
        3: halo_send,
        4: hidden_work,
        5: stream_work,
        last - 4: lambda: norm_work(0, parts),
        last - 3: lambda: norm_work(parts, parts),
        last - 2: input_work,
    }
    base = 1 + 2 * SLACK + 1

    def step(i, carry):
        stage(i, produce)
        stage(i - 1, first_sum)
        stage(i - 1 - SLACK, second_sum)
        stage(i - 1 - 2 * SLACK, third_sum)
        pl.when(s != root)(lambda: stage(i - base - SLACK * spot, inward))
        pl.when(s == root)(lambda: stage(i - base - SLACK * most, at_root))
        pl.when(s != root)(lambda: stage(i - base - SLACK * most - SLACK * far, outward))
        for at, run in work.items():
            pl.when(i == at)(run)
        return carry

    lax.fori_loop(0, chunks + base + 2 * SLACK * most + 1, step, 0)

    def finish(c, carry):
        pl.when(c >= chunks - slots)(lambda: A(c).wait_send())
        for t in (X0, X1, X2, Y0, Y1, Y2):
            t(c).wait_send()
        pl.when(below)(lambda: ZU(c).wait_send())
        pl.when(above)(lambda: ZD(c).wait_send())
        if root > 0:
            pl.when((s <= root) & (s > 0))(lambda: TD(c).wait_send())
        if span - 1 > root:
            pl.when((s >= root) & (s < span - 1))(lambda: TU(c).wait_send())
        D(c).wait_send()
        D(c).wait_recv()
        return carry

    lax.fori_loop(0, chunks, finish, 0)
    copies = []
    for c in range(chunks):
        for h in range(2):
            if c < out_chunks:
                r, col = c // (width // CHUNK), c % (width // CHUNK)
                first = h * (inner // 8) + r * HR
                to = out_sum.at[first : first + HR, col * CHUNK : (col + 1) * CHUNK]
            elif c < last:
                col = (c - out_chunks + parts) % (2 * parts)
                to = in_sum.at[h * HR : (h + 1) * HR, col * CHUNK : (col + 1) * CHUNK]
            else:
                to = rest_sum.at[h * HR : (h + 1) * HR]
            copies.append(pltpu.make_async_copy(tot.at[c, h], to, local.at[c, h]))
    for one in copies:
        one.start()
    for one in copies:
        one.wait()


def back(*args):
    gated, zg, _, _, _, _, _, step_low, cacc, _, _, x = args[:12]
    in_w, out_w = args[15:17]
    rows, inner = gated.shape
    width = x.shape[1]
    state = cacc.shape[1] // GROUP
    rank = step_low.shape[1]
    seqs = args[20].shape[0]
    span = lax.axis_size("seq")
    out_chunks, in_chunks = 2 * width // CHUNK, 2 * inner // CHUNK
    n = out_chunks + in_chunks + 1
    vmem, dma = pltpu.VMEM, pltpu.SemaphoreType.DMA
    any_space = pl.BlockSpec(memory_space=pl.ANY)
    whole = pl.BlockSpec(memory_space=vmem)
    shape = jax.ShapeDtypeStruct
    return pl.pallas_call(
        functools.partial(back_kernel, span, state, rank),
        in_specs=[whole] * len(args),
        out_specs=[whole, whole, any_space, any_space, any_space],
        out_shape=[
            shape((rows, width), BF16),
            shape((rows, width), BF16),
            shape((inner // 4, width), BF16),
            shape((width // 4, 2 * inner), BF16),
            shape((2 * HR, CHUNK), BF16),
        ],
        scratch_shapes=[
            vmem((rows, LANES), BF16),
            vmem((in_chunks, rows, CHUNK), BF16),
            vmem((seqs, rows // seqs + 8, inner), F32),
            vmem((rows, width), F32),
            vmem((2 * HR, inner), F32),
            vmem((4, 4, 2, HR, CHUNK), BF16),
            vmem((n, 4, HR, CHUNK), BF16),
            vmem((n, 3, HR // 2, CHUNK), BF16),
            vmem((n, 3, HR // 2, CHUNK), BF16),
            vmem((n, HR, CHUNK), BF16),
            vmem((n, HR, CHUNK), BF16),
            vmem((n, 2, HR, CHUNK), BF16),
            dma((12, n)),
            dma((12, n)),
            dma((2,)),
            dma((n, 2)),
        ],
        compiler_params=pltpu.CompilerParams(
            collective_id=1, has_side_effects=True, vmem_limit_bytes=63 << 20
        ),
        name="back",
    )(*args)


def block_diagonal(v):
    seqs, ctx, state = v.shape
    eye = jnp.eye(GROUP, dtype=F32)[None, None, :, :, None]
    spread = v.reshape(seqs, ctx // GROUP, GROUP, 1, state) * eye
    return spread.reshape(seqs, ctx // GROUP, GROUP, GROUP * state).astype(BF16)


def local_specs(seqs, ctx, inner, state, width):
    groups = ctx // GROUP
    tok = pl.BlockSpec((1, groups, GROUP, width), lambda c, j: (c, 0, 0, j))
    wide = pl.BlockSpec((1, ctx, state, LANES), lambda c, j: (c, 0, 0, 0))
    rate = pl.BlockSpec((state, width), lambda c, j: (0, j))
    end = pl.BlockSpec((1, state, width), lambda c, j: (c, 0, j))
    diag = pl.BlockSpec((1, groups, GROUP, GROUP * state), lambda c, j: (c, 0, 0, 0))
    return tok, wide, rate, end, diag


def local_ends(delta, drive, dy, b_wide, c_wide, rates):
    seqs, groups, _, inner = delta.shape
    state = rates.shape[0]
    width = 512
    tok, wide, rate, end, _ = local_specs(seqs, groups * GROUP, inner, state, width)
    return pl.pallas_call(
        ends_kernel,
        grid=(seqs, inner // width),
        in_specs=[tok, tok, tok, wide, wide, rate],
        out_specs=[end, end],
        out_shape=[jax.ShapeDtypeStruct((seqs, state, inner), F32)] * 2,
        compiler_params=pltpu.CompilerParams(vmem_limit_bytes=56 << 20),
        name="ends",
    )(delta, drive, dy, b_wide, c_wide, rates)


def sweep(delta, u, dy, gated_grad, gate_in, raw, b_in, c_in, b_wide, c_wide, small, start, final):
    seqs, groups, _, inner = delta.shape
    ctx = groups * GROUP
    state = b_in.shape[2]
    width = CHUNK
    tok, wide, _, end, diag = local_specs(seqs, ctx, inner, state, width)
    ones = block_diagonal(jnp.ones((1, GROUP, state), F32))[0, 0]
    token = lambda t: jax.ShapeDtypeStruct(delta.shape, t)
    diag_shape = jax.ShapeDtypeStruct((seqs, groups, GROUP, GROUP * state), F32)
    chunked = pl.BlockSpec((1, 1, groups, GROUP, width), lambda c, j: (j, c, 0, 0, 0))
    chunked_shape = jax.ShapeDtypeStruct((inner // width, seqs, groups, GROUP, width), BF16)
    vmem = pltpu.VMEM
    return pl.pallas_call(
        sweep_kernel,
        grid=(seqs, inner // width),
        in_specs=[tok] * 6
        + [wide, wide, pl.BlockSpec((small.shape[0], width), lambda c, j: (0, j)), end, end]
        + [diag, diag, pl.BlockSpec(ones.shape, lambda c, j: (0, 0))],
        out_specs=[tok, chunked, tok, tok, diag, diag, end]
        + [pl.BlockSpec((1, 2, 8, width), lambda c, j: (c, 0, 0, j))],
        out_shape=[token(BF16), chunked_shape, token(F32), token(BF16)]
        + [diag_shape] * 2
        + [jax.ShapeDtypeStruct((seqs, state, inner), F32)]
        + [jax.ShapeDtypeStruct((seqs, 2, 8, inner), F32)],
        scratch_shapes=[
            vmem((groups, GROUP, width), F32),
            vmem((groups, GROUP, width), F32),
            vmem((ctx + 1, state, width), F32),
            vmem((ctx, state, width), F32),
            vmem((GROUP, state, width), BF16),
            vmem((GROUP, state, width), BF16),
        ],
        compiler_params=pltpu.CompilerParams(vmem_limit_bytes=56 << 20),
        name="sweep",
    )(
        delta, u, dy, gated_grad, gate_in, raw, b_wide, c_wide, small, start, final,
        block_diagonal(c_in), block_diagonal(b_in), ones,
    )


def body(
    hidden_in, lengths, norm_gain, in_weight, conv_weight, conv_bias, xproj_weight,
    dt_weight, dt_bias, a_log, skip_gain, out_weight, out_grad,
):
    seqs, ctx, width = hidden_in.shape
    taps, share = conv_weight.shape
    state = a_log.shape[0]
    rank = dt_weight.shape[0]
    reach = taps - 1
    rows = ctx * seqs
    groups = ctx // GROUP
    small = jnp.concatenate(
        [conv_weight, a_log, conv_bias[None], dt_bias[None], skip_gain[None]]
        + [jnp.pad(norm_gain, (0, share - norm_gain.shape[0]))[None]],
        0,
    )
    used = small.shape[0]
    small = jnp.pad(small, ((0, -used % 32), (0, 0)))
    in_matrix, out_matrix, proj_matrix, step_matrix, small = gather(
        in_weight, out_weight, xproj_weight, dt_weight, small
    )
    gain = small[used - 1].reshape(-1, share)[:, : norm_gain.shape[0]].reshape(-1)
    conv_taps, log_rate = small[:taps], small[taps : taps + state]
    conv_shift, step_bias, skip = (small[taps + state + i] for i in range(3))
    inner = proj_matrix.shape[0]
    dot = lambda a, b: jnp.dot(a, b, preferred_element_type=F32)

    x_tok = hidden_in.astype(F32)
    position = lax.axis_index("seq") * ctx + jnp.arange(ctx, dtype=jnp.int32)
    mask = (position[None, :] < lengths[:, None]).astype(F32)[:, :, None]

    def normalised(x):
        inverse = lax.rsqrt(jnp.mean(x * x, -1, keepdims=True) + EPS)
        return inverse, (x * inverse * gain).astype(BF16)

    inverse, normed = normalised(x_tok)
    normed = normed.reshape(rows, width)
    mixed = dot(normed, in_matrix).astype(BF16)
    stream = mixed[:, :inner].reshape(seqs, ctx, inner)
    gate_in = mixed[:, inner:].astype(F32).reshape(seqs, ctx, inner)
    before = passed_along(stream[:, ctx - reach :], "seq", 1)
    extended = jnp.concatenate([before, stream], 1).astype(F32)
    conv_out = conv_shift + sum(conv_taps[k] * extended[:, k : k + ctx] for k in range(taps))
    u_low = jax.nn.silu(conv_out).astype(BF16)
    u_rows = u_low.reshape(rows, inner)
    proj = dot(u_rows, proj_matrix)
    step_low = proj[:, :rank].astype(BF16)
    b_in = proj[:, rank : rank + state].reshape(seqs, ctx, state)
    c_in = proj[:, rank + state :].reshape(seqs, ctx, state)
    raw = dot(step_low, step_matrix).reshape(seqs, ctx, inner) + step_bias
    delta = jax.nn.softplus(raw)
    rates = -jnp.exp(log_rate)
    rates2 = rates * LOG2E
    u_float = u_low.astype(F32)
    drive = delta * u_float

    cotangent = out_grad.astype(F32)
    branch_grad = (cotangent * mask).astype(BF16).reshape(rows, width)
    gated_grad = lax.dot_general(
        branch_grad, out_matrix, (((1,), (1,)), ((), ())), preferred_element_type=F32
    ).reshape(seqs, ctx, inner)
    gate_act = jax.nn.silu(gate_in)
    y_grad = gated_grad * gate_act

    grouped = lambda v: v.reshape(seqs, groups, GROUP, inner)
    b_wide = jnp.broadcast_to(b_in[..., None], (seqs, ctx, state, LANES))
    c_wide = jnp.broadcast_to(c_in[..., None], (seqs, ctx, state, LANES))
    scan_args = (grouped(delta), grouped(drive), grouped(y_grad))
    local_end, local_back = local_ends(*scan_args, b_wide, c_wide, rates2)

    blocks = lax.axis_size("seq")
    me = lax.axis_index("seq")
    ends = lax.all_gather(jnp.stack([local_end, local_back]).astype(BF16), "seq")
    sums = lax.all_gather(jnp.sum(delta, 1), "seq")
    start = jnp.zeros((seqs, state, inner), F32)
    final = jnp.zeros((seqs, state, inner), F32)
    for k in range(blocks):
        decay = jnp.exp2(sums[k][:, None, :] * rates2)
        start = jnp.where(k < me, decay * start + ends[k, 0].astype(F32), start)
        r = blocks - 1 - k
        decay = jnp.exp2(sums[r][:, None, :] * rates2)
        final = jnp.where(r > me, decay * final + ends[r, 1].astype(F32), final)

    gated, z_grad, u_grad, raw_low, c_acc, b_acc, rate_grad, sums = sweep(
        grouped(delta), grouped(u_low), grouped(y_grad), grouped(gated_grad),
        grouped(mixed[:, inner:]), grouped(raw), b_in, c_in, b_wide, c_wide, small, start, final,
    )
    flat = lambda v: v.reshape(rows, -1)
    lead = jnp.concatenate([jnp.zeros((seqs, GROUP - reach, inner), BF16), before, stream], 1)
    hidden_out, input_grad, out_sum, in_sum, rest = back(
        flat(gated), z_grad.reshape(-1, rows, CHUNK), flat(u_grad), flat(raw_low), u_rows,
        flat(conv_out), lead, step_low, flat(c_acc), flat(b_acc), normed, flat(hidden_in),
        flat(out_grad), branch_grad, jnp.broadcast_to(mask, (seqs, ctx, LANES)).reshape(rows, LANES),
        in_matrix, out_matrix, proj_matrix, step_matrix, small, rate_grad, sums,
    )
    rest = rest.astype(F32)
    shards = lax.axis_size("fsdp")
    at = taps + state
    return (
        hidden_out.reshape(seqs, ctx, width), input_grad.reshape(seqs, ctx, width),
        rest[at + 3, : width // shards], in_sum.astype(F32), rest[:taps], rest[at],
        rest[at + 4 + rank : at + 4 + rank + proj_matrix.shape[1]].T, rest[at + 4 : at + 4 + rank],
        rest[at + 1], rest[taps:at], rest[at + 2], out_sum.astype(F32),
    )


def solution(mesh):
    tokens = P(("dp", "fsdp"), "seq", None)
    return jax.shard_map(
        body,
        mesh=mesh,
        in_specs=(
            tokens, P(("dp", "fsdp")), P("fsdp"), P("fsdp", None), P(None, "fsdp"), P("fsdp"),
            P("fsdp", None), P(None, "fsdp"), P("fsdp"), P(None, "fsdp"), P("fsdp"),
            P("fsdp", None), tokens,
        ),
        out_specs=(
            tokens, tokens, P("fsdp"), P("fsdp", None), P(None, "fsdp"), P("fsdp"),
            P("fsdp", None), P(None, "fsdp"), P("fsdp"), P(None, "fsdp"), P("fsdp"),
            P("fsdp", None),
        ),
        check_vma=False,
    )
```

```python
import functools
import math

import jax
import jax.numpy as jnp
import numpy as np
from jax import lax
from jax.experimental import pallas as pl
from jax.experimental.pallas import tpu as pltpu
from jax.sharding import PartitionSpec as P

EPS = 1e-05
LOG2E = math.log2(math.e)
LANES = 128
GROUP = 16
F32 = jnp.float32
BF16 = jnp.bfloat16
MESH = pl.DeviceIdType.MESH
HR = 128
CHUNK = 512
SLACK = 1
TAPS = 4


def silu_parts(v):
    s = jax.nn.sigmoid(v)
    return v * s, s * (1.0 + v * (1.0 - s))


def sweep_kernel(
    d_ref, u_ref, dy_ref, gg_ref, z_ref, raw_ref, b_ref, c_ref, small_ref, h0_ref, p0_ref,
    cbd_ref, bbd_ref, one_ref,
    gated_ref, zg_ref, ug_ref, rl_ref, cacc_ref, bacc_ref, racc_ref, sums_ref,
    v_s, y_s, h_s, a_s, g_s, w_s,
):
    groups, width = d_ref.shape[1], d_ref.shape[3]
    state = b_ref.shape[2]
    cuts = [slice(j, j + LANES) for j in range(0, width, LANES)]
    all_rates = -jnp.exp(small_ref[TAPS : TAPS + state]) * LOG2E
    rates = [all_rates[:, s] for s in cuts]
    skip = small_ref[TAPS + state + 2 : TAPS + state + 3]
    across = (((1,), (1,)), ((), ()))

    @pl.when(pl.program_id(1) == 0)
    def _():
        cacc_ref[...] = jnp.zeros_like(cacc_ref)
        bacc_ref[...] = jnp.zeros_like(bacc_ref)

    h_s[0] = h0_ref[0]

    def forward(i, h):
        h = list(h)
        u = u_ref[0, i].astype(F32)
        v_s[i] = d_ref[0, i] * u
        for k in range(GROUP):
            t = i * GROUP + k
            b = b_ref[0, t]
            for j, s in enumerate(cuts):
                factor = jnp.exp2(jnp.broadcast_to(d_ref[0, i, k : k + 1, s], (state, LANES)) * rates[j])
                h[j] = factor * h[j] + jnp.broadcast_to(v_s[i, k : k + 1, s], (state, LANES)) * b
                h_s[t + 1, :, s] = h[j]
                a_s[t, :, s] = factor
        held = h_s[pl.ds(i * GROUP + 1, GROUP)].reshape(GROUP * state, width).astype(BF16)
        y = jnp.dot(cbd_ref[0, i], held, preferred_element_type=F32) + skip * u
        cacc_ref[0, i] += lax.dot_general(
            dy_ref[0, i].astype(BF16), held, across, preferred_element_type=F32
        )
        gate, slope = silu_parts(z_ref[0, i].astype(F32))
        gated_ref[0, i] = (y * gate).astype(BF16)
        zg_ref[0, 0, i] = (gg_ref[0, i] * y * slope).astype(BF16)
        return tuple(h)

    lax.fori_loop(0, groups, forward, tuple(h0_ref[0, :, s] for s in cuts))

    def backward(turn, carry):
        i = groups - 1 - turn
        p, total, sums = (list(v) for v in carry)
        for k in reversed(range(GROUP)):
            t = i * GROUP + k
            c = c_ref[0, t]
            for j, s in enumerate(cuts):
                row = lambda ref: jnp.broadcast_to(ref[0, i, k : k + 1, s], (state, LANES))
                g = c * row(dy_ref) + p[j]
                p[j] = a_s[t, :, s] * g
                w = p[j] * h_s[t, :, s]
                total[j] = total[j] + w * row(d_ref)
                g_s[k, :, s] = g.astype(BF16)
                w_s[k, :, s] = (w * rates[j]).astype(BF16)
        g_all = g_s[...].reshape(GROUP * state, width)
        drive_grad = jnp.dot(bbd_ref[0, i], g_all, preferred_element_type=F32)
        delta_part = jnp.dot(
            one_ref[...], w_s[...].reshape(GROUP * state, width), preferred_element_type=F32
        )
        bacc_ref[0, i] += lax.dot_general(
            v_s[i].astype(BF16), g_all, across, preferred_element_type=F32
        )
        u, dy, delta = u_ref[0, i].astype(F32), dy_ref[0, i], d_ref[0, i]
        raw_grad = (drive_grad * u + delta_part * (1.0 / LOG2E)) * jax.nn.sigmoid(raw_ref[0, i])
        rl_ref[0, i] = raw_grad.astype(BF16)
        ug_ref[0, i] = dy * skip + drive_grad * delta
        sums[0] = sums[0] + (dy * u)[:8] + (dy * u)[8:]
        sums[1] = sums[1] + raw_grad[:8] + raw_grad[8:]
        return tuple(p), tuple(total), tuple(sums)

    zero = tuple(jnp.zeros((state, LANES), F32) for _ in cuts)
    start = tuple(p0_ref[0, :, s] for s in cuts)
    none = jnp.zeros((8, width), F32)
    _, total, sums = lax.fori_loop(0, groups, backward, (start, zero, (none, none)))
    for j, s in enumerate(cuts):
        racc_ref[0, :, s] = total[j]
    sums_ref[0, 0] = sums[0]
    sums_ref[0, 1] = sums[1]


def front_kernel(
    span,
    x, og, lengths, taps_own, log_own, cbias_own, dbias_own, skip_own, gain_own,
    in_own, out_own, xp_own, dt_own,
    normed_out, bg, mask, lead, conv, u, gate, raw, delta, bw, cw, bbd, cbd, gg, dy, step_low,
    start, final, in_full, out_full, xp_full, dt_full, small_full,
    in_w, out_w, xp, dt, small, small_own, hx, acc, zacc, normed, v, proj, ends, sums,
    ends_in, sums_in,
    send, recv, halo, relay_send, relay_recv, sums_send, sums_recv, local, keep,
):
    d, s, f = (lax.axis_index(a) for a in ("dp", "seq", "fsdp"))
    fx, fy, fd = f ^ 1, f ^ 2, f ^ 3
    tox, toy, sib = {"fsdp": fx}, {"fsdp": fy}, {"dp": 1 - d}
    rows, width = x.shape
    inner = u.shape[1]
    seqs = bw.shape[0]
    ctx = rows // seqs
    state, rank = log_own.shape[0], dt_own.shape[0]
    groups = ctx // GROUP
    share = inner // 4
    at_state, at_bias = TAPS, TAPS + state
    across = (((1,), (1,)), ((), ()))
    dot = lambda a, b, dims=(((1,), (0,)), ((), ())): lax.dot_general(
        a, b, dims, preferred_element_type=F32
    )

    for c in range(seqs):
        hx[c] = jnp.zeros((GROUP, width), BF16)
    barrier = pltpu.get_barrier_semaphore()
    for who in (tox, toy, sib):
        pl.semaphore_signal(barrier, inc=1, device_id=who, device_id_type=MESH)

    def greet(o, carry):
        who = {"seq": lax.rem(s + o, span)}
        pl.semaphore_signal(barrier, inc=1, device_id=who, device_id_type=MESH)
        return carry

    lax.fori_loop(1, span, greet, 0)
    small_own[...] = jnp.zeros(small_own.shape, F32)
    small_own[:TAPS] = taps_own[...]
    small_own[at_state:at_bias] = log_own[...]
    small_own[at_bias : at_bias + 1] = cbias_own[...]
    small_own[at_bias + 1 : at_bias + 2] = dbias_own[...]
    small_own[at_bias + 2 : at_bias + 3] = skip_own[...]
    small_own[at_bias + 3 : at_bias + 4, : width // 4] = gain_own[...]
    pl.semaphore_wait(barrier, 2 + span)

    SMALL, STREAM, PROJ, STEP, GATE, OUT = range(6)
    plan = (
        (small_own, small, 1, None),
        (in_own, in_w, 0, (0, inner)),
        (xp_own, xp, 0, None),
        (dt_own, dt, 1, None),
        (in_own, in_w, 0, (inner, 2 * inner)),
        (out_own, out_w, 0, None),
    )

    def window(p, owner, half, q):
        src, dst, dim, cols = plan[p]
        high, wide = src.shape
        part = high // 4
        at = (half * 2 + q) * part
        lo, hi = cols or (0, wide)
        if dim == 0:
            return dst.at[pl.ds(pl.multiple_of(owner * high + at, part), part), lo:hi]
        col = pl.ds(pl.multiple_of(owner * wide, wide), wide)
        return dst.at[pl.ds(pl.multiple_of(at, part), part), col]

    def own(p, half, q):
        src, _, _, cols = plan[p]
        high, wide = src.shape
        part = high // 4
        lo, hi = cols or (0, wide)
        return src.at[pl.ds(pl.multiple_of((half * 2 + q) * part, part), part), lo:hi]

    def copy(src, dst, p, kind, who):
        return pltpu.make_async_remote_copy(
            src_ref=src, dst_ref=dst, send_sem=send.at[p, kind], recv_sem=recv.at[p, kind],
            device_id=who, device_id_type=MESH,
        )

    started = []

    def go(one):
        one.start()
        started.append(one)

    def start_own(p):
        for q in (0, 1):
            go(copy(own(p, d, q), window(p, f, d, q), p, q, tox))
            go(copy(own(p, d, 1 - q), window(p, f, d, 1 - q), p, 3 - q, toy))

    def place_own(p):
        for half in (0, 1):
            for q in (0, 1):
                pltpu.make_async_copy(
                    own(p, half, q), window(p, f, half, q), local.at[p, half * 2 + q]
                ).start()

    def own_ready(p):
        for half in (0, 1):
            for q in (0, 1):
                pltpu.make_async_copy(
                    own(p, half, q), window(p, f, half, q), local.at[p, half * 2 + q]
                ).wait()

    def arrived(p, kind, owner, half, q):
        w = window(p, owner, half, q)
        copy(w, w, p, kind, sib).wait_recv()
        return w

    near = ((0, fx, 0), (3, fy, 1), (1, fx, 1), (2, fy, 0))
    diagonal = ((4, fd, 0), (5, fd, 1))

    def serve_near(p):
        for kind, owner, q in near:
            w = arrived(p, kind, owner, d, q)
            if kind == 0:
                go(copy(w, w, p, 4, toy))
            if kind == 3:
                go(copy(w, w, p, 5, tox))
            go(copy(w, w, p, 6 + kind, sib))

    def serve_far(p):
        for kind, owner, q in diagonal:
            w = arrived(p, kind, owner, d, q)
            go(copy(w, w, p, 6 + kind, sib))

    def near_ready(p):
        for kind, owner, q in near:
            arrived(p, 6 + kind, owner, 1 - d, q)

    def far_ready(p):
        for kind, owner, q in diagonal:
            arrived(p, 6 + kind, owner, 1 - d, q)

    for p in (SMALL, STREAM, PROJ, STEP):
        start_own(p)
    for p in range(6):
        place_own(p)
    def edges(c):
        return pltpu.make_async_remote_copy(
            src_ref=x.at[(c + 1) * ctx - GROUP : (c + 1) * ctx], dst_ref=hx.at[c],
            send_sem=halo.at[0, c], recv_sem=halo.at[1, c],
            device_id={"seq": jnp.minimum(s + 1, span - 1)}, device_id_type=MESH,
        )

    @pl.when(s < span - 1)
    def _():
        for c in range(seqs):
            edges(c).start()

    for c in range(seqs):
        t = s * ctx + lax.broadcasted_iota(jnp.int32, (ctx, LANES), 0)
        mask[c * ctx : (c + 1) * ctx] = (t < lengths[c]).astype(F32)

    def mask_step(r, carry):
        tok = pl.ds(pl.multiple_of(r * GROUP, GROUP), GROUP)
        held = jnp.concatenate([mask[tok]] * (width // LANES), 1)
        bg[tok] = (og[tok].astype(F32) * held).astype(BF16)
        return carry

    lax.fori_loop(0, rows // GROUP, mask_step, 0)

    serve_near(SMALL)
    serve_far(SMALL)
    near_ready(SMALL)
    far_ready(SMALL)
    own_ready(SMALL)

    @pl.when(s > 0)
    def _():
        for c in range(seqs):
            edges(c).wait_recv()

    gain_at = at_bias + 3
    gain = jnp.concatenate(
        [small[gain_at : gain_at + 1, j * share : j * share + width // 4] for j in range(4)], 1
    )

    def normalised(v):
        v = v.astype(F32)
        inverse = lax.rsqrt(jnp.mean(v * v, -1, keepdims=True) + EPS)
        return (v * inverse * gain).astype(BF16)

    def norm_step(r, carry):
        tok = pl.ds(pl.multiple_of(r * GROUP, GROUP), GROUP)
        normed[tok] = normalised(x[tok])
        normed_out[tok] = normed[tok]
        return carry

    lax.fori_loop(0, rows // GROUP, norm_step, 0)
    for c in range(seqs):
        normed[rows + c * GROUP : rows + (c + 1) * GROUP] = normalised(hx[c])

    def project(total, high, first, owner, fresh):
        shard = pl.ds(pl.multiple_of(owner * (width // 4), width // 4), width // 4)
        left = normed[:high, shard]

        def one(t, carry):
            cols = pl.ds(pl.multiple_of(t * CHUNK, CHUNK), CHUNK)
            right = in_w[shard, pl.ds(pl.multiple_of(first + t * CHUNK, CHUNK), CHUNK)]
            part = dot(left, right)
            total[:, cols] = part if fresh else total[:, cols] + part
            return carry

        lax.fori_loop(0, inner // CHUNK, one, 0)

    tall = rows + seqs * GROUP
    own_ready(STREAM)
    project(acc, tall, 0, f, True)
    serve_near(STREAM)
    start_own(GATE)
    start_own(OUT)
    near_ready(STREAM)
    project(acc, tall, 0, fx, False)
    project(acc, tall, 0, fy, False)
    serve_far(STREAM)
    for p in (PROJ, STEP):
        serve_near(p)
        serve_far(p)
    far_ready(STREAM)
    project(acc, tall, 0, fd, False)

    tile = 2 * LANES

    def columns(t, size=tile):
        return pl.ds(pl.multiple_of(t * size, size), size)

    def conv_step(t, carry):
        cols = columns(t)
        for c in range(seqs):
            before = acc[rows + c * GROUP : rows + (c + 1) * GROUP, cols].astype(BF16)
            stream = acc[c * ctx : (c + 1) * ctx, cols].astype(BF16)
            lead[c, :GROUP, cols] = before
            lead[c, GROUP:, cols] = stream
            held = jnp.concatenate([before, stream], 0).astype(F32)
            total = small[at_bias : at_bias + 1, cols]
            for k in range(TAPS):
                at = GROUP - TAPS + 1 + k
                total = total + small[k : k + 1, cols] * held[at : at + ctx]
            conv[c * ctx : (c + 1) * ctx, cols] = total
            u[c * ctx : (c + 1) * ctx, cols] = (total * jax.nn.sigmoid(total)).astype(BF16)
        return carry

    lax.fori_loop(0, inner // tile, conv_step, 0)
    for p in (PROJ, STEP):
        near_ready(p)
        far_ready(p)
        own_ready(p)
    proj[...] = dot(u[...], xp[...])
    step_low[...] = proj[:, :rank].astype(BF16)

    def wide_step(i, carry):
        tok = pl.ds(pl.multiple_of(i * GROUP, GROUP), GROUP)
        held = proj[tok]
        for ref, first in ((bw, rank), (cw, rank + state)):
            value = held[:, first : first + state]
            c, at = i // groups, lax.rem(i, groups)
            ref[c, pl.ds(pl.multiple_of(at * GROUP, GROUP), GROUP)] = jnp.broadcast_to(
                value[:, :, None], (GROUP, state, LANES)
            )
        return carry

    lax.fori_loop(0, rows // GROUP, wide_step, 0)
    r = lax.broadcasted_iota(jnp.int32, (rows, GROUP * state), 0)
    k = lax.broadcasted_iota(jnp.int32, (rows, GROUP * state), 1)
    mine = lax.rem(r, GROUP) == k // state
    at = lax.broadcasted_iota(jnp.int32, (proj.shape[1], GROUP * state), 0)
    col = lax.rem(lax.broadcasted_iota(jnp.int32, (proj.shape[1], GROUP * state), 1), state)
    for ref, first in ((bbd, rank), (cbd, rank + state)):
        spread = (at == col + first).astype(F32).astype(BF16)
        ref[...] = jnp.where(mine, dot(proj[...].astype(BF16), spread), 0.0).astype(BF16)

    def delta_step(t, carry):
        cols = columns(t)
        for c in range(seqs):
            tok = slice(c * ctx, (c + 1) * ctx)
            value = dot(step_low[tok], dt[:, cols]) + small[at_bias + 1 : at_bias + 2, cols]
            raw[tok, cols] = value
            value = jnp.maximum(value, 0.0) + jnp.log1p(jnp.exp(-jnp.abs(value)))
            for i in range(groups):
                delta[c * groups + i, :, cols] = value[i * GROUP : (i + 1) * GROUP]
            sums[c : c + 1, cols] = jnp.sum(value, 0, keepdims=True)
            value = value * u[tok, cols].astype(F32)
            for i in range(groups):
                v[c * groups + i, :, cols] = value[i * GROUP : (i + 1) * GROUP]
        return carry

    sums[...] = jnp.zeros(sums.shape, F32)
    lax.fori_loop(0, inner // tile, delta_step, 0)

    def sums_copy(j):
        return pltpu.make_async_remote_copy(
            src_ref=sums, dst_ref=sums_in.at[s], send_sem=sums_send.at[j],
            recv_sem=sums_recv.at[s], device_id={"seq": j}, device_id_type=MESH,
        )

    def sums_start(o, carry):
        sums_copy(lax.rem(s + o, span)).start()
        return carry

    lax.fori_loop(1, span, sums_start, 0)

    def ends_copy(j, way, c):
        return pltpu.make_async_remote_copy(
            src_ref=ends.at[way, c], dst_ref=ends_in.at[s, c], send_sem=relay_send.at[j, c],
            recv_sem=relay_recv.at[s, c], device_id={"seq": j}, device_id_type=MESH,
        )

    def ends_start(first, count, way, c):
        def one(j, carry):
            ends_copy(j, way, c).start()
            return carry

        lax.fori_loop(first, count, one, 0)

    def forward_ends(c):
        for j in range(0, inner, CHUNK):
            cuts = [slice(j + i, j + i + LANES) for i in range(0, CHUNK, LANES)]
            rates = [-jnp.exp(small[at_state:at_bias, cut]) * LOG2E for cut in cuts]

            def one(i, h):
                h = list(h)
                for k in range(GROUP):
                    b = bw[c, i * GROUP + k]
                    for n, cut in enumerate(cuts):
                        step = delta[c * groups + i, k : k + 1, cut]
                        factor = jnp.exp2(jnp.broadcast_to(step, (state, LANES)) * rates[n])
                        row = jnp.broadcast_to(v[c * groups + i, k : k + 1, cut], (state, LANES))
                        h[n] = factor * h[n] + row * b
                return tuple(h)

            zero = tuple(jnp.zeros((state, LANES), F32) for _ in cuts)
            h = lax.fori_loop(0, groups, one, zero)
            for n, cut in enumerate(cuts):
                ends[0, c, :, cut] = h[n].astype(BF16)

    def backward_ends(c):
        for j in range(0, inner, CHUNK):
            cuts = [slice(j + i, j + i + LANES) for i in range(0, CHUNK, LANES)]
            rates = [-jnp.exp(small[at_state:at_bias, cut]) * LOG2E for cut in cuts]

            def one(i, carry):
                run, p = (list(value) for value in carry)
                for k in range(GROUP):
                    read = cw[c, i * GROUP + k]
                    for n, cut in enumerate(cuts):
                        step = delta[c * groups + i, k : k + 1, cut]
                        factor = jnp.exp2(jnp.broadcast_to(step, (state, LANES)) * rates[n])
                        row = dy[c * groups + i, k : k + 1, cut]
                        run[n] = run[n] * factor
                        p[n] = p[n] + run[n] * (read * jnp.broadcast_to(row, (state, LANES)))
                return tuple(run), tuple(p)

            one_s = tuple(jnp.ones((state, LANES), F32) for _ in cuts)
            zero = tuple(jnp.zeros((state, LANES), F32) for _ in cuts)
            _, p = lax.fori_loop(0, groups, one, (one_s, zero))
            for n, cut in enumerate(cuts):
                ends[1, c, :, cut] = p[n].astype(BF16)

    forward_ends(0)
    ends_start(s + 1, span, 0, 0)
    serve_near(GATE)
    own_ready(GATE)
    project(zacc, rows, inner, f, True)
    forward_ends(1)
    ends_start(s + 1, span, 0, 1)
    near_ready(GATE)
    project(zacc, rows, inner, fx, False)
    project(zacc, rows, inner, fy, False)

    def grad_part(owner):
        shard = pl.ds(pl.multiple_of(owner * share, share), share)
        gg[:, shard] = dot(bg[...], out_w[shard], across)

    own_ready(OUT)
    grad_part(f)
    serve_near(OUT)
    serve_far(GATE)
    far_ready(GATE)
    project(zacc, rows, inner, fd, False)
    near_ready(OUT)
    grad_part(fx)
    grad_part(fy)
    serve_far(OUT)
    far_ready(OUT)
    grad_part(fd)

    fulls = ((in_w, in_full), (out_w, out_full), (xp, xp_full), (dt, dt_full), (small, small_full))
    kept = [pltpu.make_async_copy(a, b, keep.at[n]) for n, (a, b) in enumerate(fulls)]
    for one in kept:
        one.start()

    def gate_step(t, carry):
        cols = columns(t)
        for c in range(seqs):
            tok = slice(c * ctx, (c + 1) * ctx)
            low = zacc[tok, cols].astype(BF16)
            gate[tok, cols] = low
            value = low.astype(F32)
            value = gg[tok, cols] * (value * jax.nn.sigmoid(value))
            for i in range(groups):
                dy[c * groups + i, :, cols] = value[i * GROUP : (i + 1) * GROUP]
        return carry

    lax.fori_loop(0, inner // tile, gate_step, 0)
    for c in range(seqs):
        backward_ends(c)
        ends_start(0, s, 1, c)

    def sums_wait(o, carry):
        j = lax.rem(s + o, span)
        pltpu.make_async_remote_copy(
            src_ref=sums, dst_ref=sums_in.at[j], send_sem=sums_send.at[j],
            recv_sem=sums_recv.at[j], device_id={"seq": j}, device_id_type=MESH,
        ).wait_recv()
        return carry

    lax.fori_loop(1, span, sums_wait, 0)

    def ends_wait(j, c):
        pltpu.make_async_remote_copy(
            src_ref=ends.at[0, c], dst_ref=ends_in.at[j, c], send_sem=relay_send.at[j, c],
            recv_sem=relay_recv.at[j, c], device_id={"seq": j}, device_id_type=MESH,
        ).wait_recv()

    start[...] = jnp.zeros(start.shape, F32)
    final[...] = jnp.zeros(final.shape, F32)

    def join(ref, j, c):
        ends_wait(j, c)

        def one(t, carry):
            cols = columns(t, CHUNK)
            rates = -jnp.exp(small[at_state:at_bias, cols]) * LOG2E
            decay = jnp.exp2(sums_in[j, c : c + 1, cols] * rates)
            ref[c, :, cols] = decay * ref[c, :, cols] + ends_in[j, c, :, cols].astype(F32)
            return carry

        lax.fori_loop(0, inner // CHUNK, one, 0)

    def join_start(j, carry):
        for c in range(seqs):
            join(start, j, c)
        return carry

    def join_final(o, carry):
        for c in range(seqs):
            join(final, span - 1 - o, c)
        return carry

    lax.fori_loop(0, s, join_start, 0)
    lax.fori_loop(0, span - 1 - s, join_final, 0)

    for one in started:
        one.wait_send()

    @pl.when(s < span - 1)
    def _():
        for c in range(seqs):
            edges(c).wait_send()

    def sent(o, carry):
        j = lax.rem(s + o, span)
        sums_copy(j).wait_send()
        for c in range(seqs):
            ends_copy(j, 0, c).wait_send()
        return carry

    lax.fori_loop(1, span, sent, 0)
    for one in kept:
        one.wait()


def front(x, og, lengths, taps, logs, cbias, dbias, skip, gain, in_own, out_own, xp_own, dt_own, seqs):
    rows, width = x.shape
    share, inner = taps.shape[1], 4 * taps.shape[1]
    state, rank, used = logs.shape[0], dt_own.shape[0], xp_own.shape[1]
    ctx = rows // seqs
    span = lax.axis_size("seq")
    vmem, dma = pltpu.VMEM, pltpu.SemaphoreType.DMA
    whole, anywhere = pl.BlockSpec(memory_space=vmem), pl.BlockSpec(memory_space=pl.ANY)
    shape = jax.ShapeDtypeStruct
    return pl.pallas_call(
        functools.partial(front_kernel, span),
        in_specs=[whole, whole, pl.BlockSpec(memory_space=pltpu.SMEM)]
        + [whole] * 6
        + [anywhere] * 4,
        out_specs=[whole] * 18 + [anywhere] * 5,
        out_shape=[
            shape((rows, width), BF16),
            shape((rows, width), BF16),
            shape((rows, LANES), F32),
            shape((seqs, ctx + GROUP, inner), BF16),
            shape((rows, inner), F32),
            shape((rows, inner), BF16),
            shape((rows, inner), BF16),
            shape((rows, inner), F32),
            shape((rows // GROUP, GROUP, inner), F32),
            shape((seqs, ctx, state, LANES), F32),
            shape((seqs, ctx, state, LANES), F32),
            shape((rows, GROUP * state), BF16),
            shape((rows, GROUP * state), BF16),
            shape((rows, inner), F32),
            shape((rows // GROUP, GROUP, inner), F32),
            shape((rows, rank), BF16),
            shape((seqs, state, inner), F32),
            shape((seqs, state, inner), F32),
            shape((width, 2 * inner), BF16),
            shape((inner, width), BF16),
            shape((inner, used), BF16),
            shape((rank, inner), BF16),
            shape((32, inner), F32),
        ],
        scratch_shapes=[
            vmem((width, 2 * inner), BF16),
            vmem((inner, width), BF16),
            vmem((inner, used), BF16),
            vmem((rank, inner), BF16),
            vmem((32, inner), F32),
            vmem((32, share), F32),
            vmem((seqs, GROUP, width), BF16),
            vmem((rows + seqs * GROUP, inner), F32),
            vmem((rows, inner), F32),
            vmem((rows + seqs * GROUP, width), BF16),
            vmem((rows // GROUP, GROUP, inner), F32),
            vmem((rows, used), F32),
            vmem((2, seqs, state, inner), BF16),
            vmem((8, inner), F32),
            vmem((span, seqs, state, inner), BF16),
            vmem((span, 8, inner), F32),
            dma((6, 12)),
            dma((6, 12)),
            dma((2, seqs)),
            dma((span, seqs)),
            dma((span, seqs)),
            dma((span,)),
            dma((span,)),
            dma((6, 4)),
            dma((5,)),
        ],
        compiler_params=pltpu.CompilerParams(
            collective_id=0, has_side_effects=True, vmem_limit_bytes=63 << 20
        ),
        name="front",
    )(x, og, lengths, taps, logs, cbias, dbias, skip, gain, in_own, out_own, xp_own, dt_own)


def back_kernel(
    span, state, rank,
    gated, zg, ug, rl, u, conv, lead, step_low, cacc, bacc, normed, x, og, bg, mask,
    in_w, out_w, xp, dt, small, racc, sums,
    hidden_out, input_grad, out_sum, in_sum, rest_sum,
    pg, mixed, cg, ng, rest, g, ra, rx, ry, zlo, zhi, tot, send, recv, halo, local,
):
    d, s, f = (lax.axis_index(a) for a in ("dp", "seq", "fsdp"))
    fx, fy, fd = f ^ 1, f ^ 2, f ^ 3
    chunks = tot.shape[0]
    rows, width = x.shape
    inner = gated.shape[1]
    seqs = cg.shape[0]
    ctx = rows // seqs
    parts = inner // CHUNK
    out_chunks = 2 * width // CHUNK
    in_chunks = 2 * parts
    last = out_chunks + in_chunks
    slots = g.shape[0]
    q = HR // 2
    root = (span - 1) // 2
    tox, toy, sib = {"fsdp": fx}, {"fsdp": fy}, {"dp": 1 - d}
    up, down = {"seq": jnp.minimum(s + 1, span - 1)}, {"seq": jnp.maximum(s - 1, 0)}
    contract = (((0,), (0,)), ((), ()))
    across = (((1,), (1,)), ((), ()))
    dot = lambda a, b, dims=(((1,), (0,)), ((), ())): lax.dot_general(
        a, b, dims, preferred_element_type=F32
    )

    cg[:, ctx:] = jnp.zeros((seqs, cg.shape[1] - ctx, inner), F32)
    barrier = pltpu.get_barrier_semaphore()
    for who in (tox, toy, sib):
        pl.semaphore_signal(barrier, inc=1, device_id=who, device_id_type=MESH)

    @pl.when(s > 0)
    def _():
        pl.semaphore_signal(barrier, inc=1, device_id=down, device_id_type=MESH)

    @pl.when(s < span - 1)
    def _():
        pl.semaphore_signal(barrier, inc=1, device_id=up, device_id_type=MESH)

    ends = (s == 0) | (s == span - 1)
    pl.semaphore_wait(barrier, jnp.where(ends, 4, 5) if span > 1 else 3)

    def copy(kind, c, src, dst, who):
        return pltpu.make_async_remote_copy(
            src_ref=src, dst_ref=dst, send_sem=send.at[kind, c], recv_sem=recv.at[kind, c],
            device_id=who, device_id_type=MESH,
        )

    lo, hi = slice(0, q), slice(q, HR)
    A = lambda c: copy(0, c, g.at[lax.rem(c, slots), :, 1 - d], ra.at[c], sib)
    X0 = lambda c: copy(1, c, ra.at[c, fd, lo], rx.at[c, 0], tox)
    X1 = lambda c: copy(2, c, ra.at[c, fx, lo], rx.at[c, 1], tox)
    X2 = lambda c: copy(3, c, ra.at[c, fx, hi], rx.at[c, 2], tox)
    Y0 = lambda c: copy(4, c, ra.at[c, fd, hi], ry.at[c, 0], toy)
    Y2 = lambda c: copy(5, c, ra.at[c, fy, hi], ry.at[c, 2], toy)
    Y1 = lambda c: copy(6, c, ra.at[c, fy, lo], ry.at[c, 1], toy)
    ZU = lambda c: copy(7, c, ra.at[c, f], zlo.at[c], up)
    ZD = lambda c: copy(8, c, ra.at[c, f], zhi.at[c], down)
    TU = lambda c: copy(9, c, tot.at[c, d], tot.at[c, d], up)
    TD = lambda c: copy(10, c, tot.at[c, d], tot.at[c, d], down)
    D = lambda c: copy(11, c, tot.at[c, d], tot.at[c, d], sib)
    below, above = s < root, s > root
    spot = jnp.where(below, s, jnp.where(above, span - 1 - s, 0))
    far = jnp.abs(s - root)
    most = max(root, span - 1 - root)

    def stage(c, run):
        @pl.when((c >= 0) & (c < chunks))
        def _():
            run(c)

    def produce(c):
        slot = lax.rem(c, slots)

        @pl.when(c >= slots)
        def _():
            A(c - slots).wait_send()

        @pl.when(c < out_chunks)
        def _():
            r = c // (width // CHUNK)
            col = lax.rem(c, width // CHUNK) * CHUNK
            right = bg[:, pl.ds(pl.multiple_of(col, CHUNK), CHUNK)]
            for j in range(4):
                for h in range(2):
                    at = j * (inner // 4) + h * (inner // 8) + r * HR
                    left = gated[:, pl.ds(pl.multiple_of(at, HR), HR)]
                    g[slot, j, h] = dot(left, right, contract).astype(BF16)

        @pl.when((c >= out_chunks) & (c < last))
        def _():
            right = mixed[c - out_chunks]
            for j in range(4):
                t = dot(normed[:, j * 2 * HR : (j + 1) * 2 * HR], right, contract).astype(BF16)
                g[slot, j, 0] = t[:HR]
                g[slot, j, 1] = t[HR:]

        @pl.when(c == last)
        def _():
            for j in range(4):
                for h in range(2):
                    cols = slice(j * CHUNK, (j + 1) * CHUNK)
                    g[slot, j, h] = rest[h * HR : (h + 1) * HR, cols].astype(BF16)

        A(c).start()

    def first_sum(c):
        A(c).wait_recv()
        for j in range(4):
            own = g[lax.rem(c, slots), j, d]
            ra[c, j] = (ra[c, j].astype(F32) + own.astype(F32)).astype(BF16)
        X0(c).start()
        Y0(c).start()
        X1(c).start()
        Y2(c).start()

    def second_sum(c):
        X0(c).wait_recv()
        ra[c, fy, lo] = (ra[c, fy, lo].astype(F32) + rx[c, 0].astype(F32)).astype(BF16)
        Y1(c).start()
        Y0(c).wait_recv()
        ra[c, fx, hi] = (ra[c, fx, hi].astype(F32) + ry[c, 0].astype(F32)).astype(BF16)
        X2(c).start()

    def third_sum(c):
        X1(c).wait_recv()
        Y2(c).wait_recv()
        X2(c).wait_recv()
        Y1(c).wait_recv()
        for k, part in enumerate((lo, hi)):
            total = ra[c, f, part].astype(F32) + rx[c, 1 + k].astype(F32) + ry[c, 1 + k].astype(F32)
            ra[c, f, part] = total.astype(BF16)

    def inward(c):
        @pl.when(below & (s > 0))
        def _():
            ZU(c).wait_recv()
            ra[c, f] = (ra[c, f].astype(F32) + zlo[c].astype(F32)).astype(BF16)

        @pl.when(above & (s < span - 1))
        def _():
            ZD(c).wait_recv()
            ra[c, f] = (ra[c, f].astype(F32) + zhi[c].astype(F32)).astype(BF16)

        pl.when(below)(lambda: ZU(c).start())
        pl.when(above)(lambda: ZD(c).start())

    def at_root(c):
        total = ra[c, f].astype(F32)
        if root > 0:
            ZU(c).wait_recv()
            total = total + zlo[c].astype(F32)
        if span - 1 > root:
            ZD(c).wait_recv()
            total = total + zhi[c].astype(F32)
        tot[c, d] = total.astype(BF16)
        if root > 0:
            TD(c).start()
        if span - 1 > root:
            TU(c).start()
        D(c).start()

    def outward(c):
        @pl.when(above)
        def _():
            TU(c).wait_recv()
            pl.when(s < span - 1)(lambda: TU(c).start())

        @pl.when(below)
        def _():
            TD(c).wait_recv()
            pl.when(s > 0)(lambda: TD(c).start())

        D(c).start()

    tile = 2 * LANES

    def columns(t, size=tile):
        return pl.ds(pl.multiple_of(t * size, size), size)

    def proj_work():
        step_grad = dot(rl[...], dt[...], across)
        r = lax.broadcasted_iota(jnp.int32, (rows, GROUP * state), 0)
        k = lax.broadcasted_iota(jnp.int32, (rows, GROUP * state), 1)
        own = lax.rem(r, GROUP) == k // state
        pick = lambda v: jnp.where(own, v[...], 0.0).astype(BF16)
        at = lax.rem(lax.broadcasted_iota(jnp.int32, (GROUP * state, LANES), 0), state)
        col = lax.broadcasted_iota(jnp.int32, (GROUP * state, LANES), 1)
        fold = lambda first: (col == at + first).astype(F32).astype(BF16)
        grads = jnp.concatenate([step_grad, jnp.zeros((rows, LANES - rank), F32)], 1)
        grads = grads + dot(pick(bacc), fold(rank)) + dot(pick(cacc), fold(rank + state))
        pg[...] = grads.astype(BF16)
        rest[...] = jnp.zeros(rest.shape, F32)
        first = TAPS + state + 4
        used = rank + 2 * state

        def weights(t, carry):
            cols = columns(t)
            rest[first : first + rank, cols] = dot(step_low[...], rl[:, cols], contract)
            rest[first + rank : first + rank + used, cols] = dot(pg[...], u[:, cols], contract)[:used]
            logs = racc[0, :, cols]
            kept = sums[0, :, :, cols]
            for c in range(1, seqs):
                logs = logs + racc[c, :, cols]
                kept = kept + sums[c, :, :, cols]
            rest[TAPS : TAPS + state, cols] = -logs * jnp.exp(small[TAPS : TAPS + state, cols])
            at = TAPS + state
            rest[at + 1 : at + 2, cols] = jnp.sum(kept[1], 0, keepdims=True)
            rest[at + 2 : at + 3, cols] = jnp.sum(kept[0], 0, keepdims=True)
            return carry

        lax.fori_loop(0, inner // tile, weights, 0)

    def conv_work(first, count):
        def one(t, carry):
            cols = columns(t)
            shift = jnp.zeros((1, tile), F32)
            taps = [jnp.zeros((1, tile), F32) for _ in range(TAPS)]
            for c in range(seqs):
                tok = slice(c * ctx, (c + 1) * ctx)
                weight = xp[columns(t)]
                back = dot(pg[tok, : weight.shape[1]], weight, across)
                _, slope = silu_parts(conv[tok, cols])
                grad = (ug[tok, cols] + back) * slope
                cg[c, :ctx, cols] = grad
                before = lead[c, :, cols].astype(F32)
                shift = shift + jnp.sum(grad, 0, keepdims=True)
                for k in range(TAPS):
                    at = GROUP - TAPS + 1 + k
                    taps[k] = taps[k] + jnp.sum(grad * before[at : at + ctx], 0, keepdims=True)
            for k in range(TAPS):
                rest[k : k + 1, cols] = taps[k]
            rest[TAPS + state : TAPS + state + 1, cols] = shift
            return carry

        lax.fori_loop(first, first + count, one, 0)

    edge = cg.shape[1] - ctx
    H = lambda: pltpu.make_async_remote_copy(
        src_ref=cg.at[:, :edge], dst_ref=cg.at[:, ctx:], send_sem=halo.at[0],
        recv_sem=halo.at[1], device_id=down, device_id_type=MESH,
    )

    def halo_send():
        pl.when(s > 0)(lambda: H().start())

    def stream_work():
        pl.when(s < span - 1)(lambda: H().wait_recv())

        def one(t, carry):
            cols = columns(t)
            for c in range(seqs):
                total = 0.0
                for k in range(TAPS):
                    at = TAPS - 1 - k
                    total = total + small[k : k + 1, cols] * cg[c, at : at + ctx, cols]
                half = pl.ds(pl.multiple_of(lax.rem(t, 2) * tile, tile), tile)
                mixed[parts + t // 2, c * ctx : (c + 1) * ctx, half] = total.astype(BF16)
            return carry

        lax.fori_loop(0, inner // tile, one, 0)
        pl.when(s > 0)(lambda: H().wait_send())

    def hidden_work():
        def one(t, carry):
            cols = columns(t)
            branch = dot(gated[...], out_w[:, cols])
            keep = mask[...]
            keep = jnp.concatenate([keep] * (tile // LANES), 1)
            hidden_out[:, cols] = (x[:, cols].astype(F32) + keep * branch).astype(BF16)
            return carry

        lax.fori_loop(0, width // tile, one, 0)

    def norm_work(first, count):
        def one(k, carry):
            cols = columns(lax.rem(k + parts, 2 * parts), CHUNK)
            ng[...] += dot(mixed[k], in_w[:, cols], across)
            return carry

        if first == 0:
            ng[...] = jnp.zeros(ng.shape, F32)
        lax.fori_loop(first, first + count, one, 0)

    def input_work():
        share = width // 4
        at = TAPS + state + 3
        gain = jnp.concatenate(
            [small[at : at + 1, j * CHUNK : j * CHUNK + share] for j in range(4)], 1
        )

        def one(r, total):
            tok = pl.ds(pl.multiple_of(r * GROUP, GROUP), GROUP)
            xs = x[tok].astype(F32)
            inverse = lax.rsqrt(jnp.mean(xs * xs, -1, keepdims=True) + EPS)
            grad = ng[tok]
            scaled = grad * gain
            slope = jnp.mean(scaled * xs, -1, keepdims=True)
            out = inverse * scaled - xs * (inverse * inverse * inverse * slope)
            input_grad[tok] = (out + og[tok].astype(F32)).astype(BF16)
            return total + grad * (xs * inverse)

        total = lax.fori_loop(0, rows // GROUP, one, jnp.zeros((GROUP, width), F32))
        total = jnp.sum(total, 0, keepdims=True)
        for j in range(4):
            rest[at : at + 1, j * CHUNK : j * CHUNK + share] = total[:, j * share : (j + 1) * share]

    mixed[:parts] = zg[...]
    tiles = inner // tile
    work = {
        0: proj_work,
        1: lambda: conv_work(0, tiles // 2),
        2: lambda: conv_work(tiles // 2, tiles // 2),
        3: halo_send,
        4: hidden_work,
        5: stream_work,
        last - 4: lambda: norm_work(0, parts),
        last - 3: lambda: norm_work(parts, parts),
        last - 2: input_work,
    }
    base = 1 + 2 * SLACK + 1

    def step(i, carry):
        stage(i, produce)
        stage(i - 1, first_sum)
        stage(i - 1 - SLACK, second_sum)
        stage(i - 1 - 2 * SLACK, third_sum)
        pl.when(s != root)(lambda: stage(i - base - SLACK * spot, inward))
        pl.when(s == root)(lambda: stage(i - base - SLACK * most, at_root))
        pl.when(s != root)(lambda: stage(i - base - SLACK * most - SLACK * far, outward))
        for at, run in work.items():
            pl.when(i == at)(run)
        return carry

    lax.fori_loop(0, chunks + base + 2 * SLACK * most + 1, step, 0)

    def finish(c, carry):
        pl.when(c >= chunks - slots)(lambda: A(c).wait_send())
        for t in (X0, X1, X2, Y0, Y1, Y2):
            t(c).wait_send()
        pl.when(below)(lambda: ZU(c).wait_send())
        pl.when(above)(lambda: ZD(c).wait_send())
        if root > 0:
            pl.when((s <= root) & (s > 0))(lambda: TD(c).wait_send())
        if span - 1 > root:
            pl.when((s >= root) & (s < span - 1))(lambda: TU(c).wait_send())
        D(c).wait_send()
        D(c).wait_recv()
        return carry

    lax.fori_loop(0, chunks, finish, 0)
    copies = []
    for c in range(chunks):
        for h in range(2):
            if c < out_chunks:
                r, col = c // (width // CHUNK), c % (width // CHUNK)
                first = h * (inner // 8) + r * HR
                to = out_sum.at[first : first + HR, col * CHUNK : (col + 1) * CHUNK]
            elif c < last:
                col = (c - out_chunks + parts) % (2 * parts)
                to = in_sum.at[h * HR : (h + 1) * HR, col * CHUNK : (col + 1) * CHUNK]
            else:
                to = rest_sum.at[h * HR : (h + 1) * HR]
            copies.append(pltpu.make_async_copy(tot.at[c, h], to, local.at[c, h]))
    for one in copies:
        one.start()
    for one in copies:
        one.wait()


def back(*args):
    gated, zg, _, _, _, _, _, step_low, cacc, _, _, x = args[:12]
    in_w, out_w = args[15:17]
    rows, inner = gated.shape
    width = x.shape[1]
    state = cacc.shape[1] // GROUP
    rank = step_low.shape[1]
    seqs = args[20].shape[0]
    span = lax.axis_size("seq")
    out_chunks, in_chunks = 2 * width // CHUNK, 2 * inner // CHUNK
    n = out_chunks + in_chunks + 1
    vmem, dma = pltpu.VMEM, pltpu.SemaphoreType.DMA
    any_space = pl.BlockSpec(memory_space=pl.ANY)
    whole = pl.BlockSpec(memory_space=vmem)
    shape = jax.ShapeDtypeStruct
    return pl.pallas_call(
        functools.partial(back_kernel, span, state, rank),
        in_specs=[whole] * len(args),
        out_specs=[whole, whole, any_space, any_space, any_space],
        out_shape=[
            shape((rows, width), BF16),
            shape((rows, width), BF16),
            shape((inner // 4, width), BF16),
            shape((width // 4, 2 * inner), BF16),
            shape((2 * HR, CHUNK), BF16),
        ],
        scratch_shapes=[
            vmem((rows, LANES), BF16),
            vmem((in_chunks, rows, CHUNK), BF16),
            vmem((seqs, rows // seqs + 8, inner), F32),
            vmem((rows, width), F32),
            vmem((2 * HR, inner), F32),
            vmem((4, 4, 2, HR, CHUNK), BF16),
            vmem((n, 4, HR, CHUNK), BF16),
            vmem((n, 3, HR // 2, CHUNK), BF16),
            vmem((n, 3, HR // 2, CHUNK), BF16),
            vmem((n, HR, CHUNK), BF16),
            vmem((n, HR, CHUNK), BF16),
            vmem((n, 2, HR, CHUNK), BF16),
            dma((12, n)),
            dma((12, n)),
            dma((2,)),
            dma((n, 2)),
        ],
        compiler_params=pltpu.CompilerParams(
            collective_id=1, has_side_effects=True, vmem_limit_bytes=63 << 20
        ),
        name="back",
    )(*args)


def local_specs(seqs, ctx, inner, state, width):
    groups = ctx // GROUP
    tok = pl.BlockSpec((1, groups, GROUP, width), lambda c, j: (c, 0, 0, j))
    wide = pl.BlockSpec((1, ctx, state, LANES), lambda c, j: (c, 0, 0, 0))
    rate = pl.BlockSpec((state, width), lambda c, j: (0, j))
    end = pl.BlockSpec((1, state, width), lambda c, j: (c, 0, j))
    diag = pl.BlockSpec((1, groups, GROUP, GROUP * state), lambda c, j: (c, 0, 0, 0))
    return tok, wide, rate, end, diag


def sweep(delta, u, dy, gated_grad, gate_in, raw, b_wide, c_wide, bbd, cbd, small, start, final):
    seqs, groups, _, inner = delta.shape
    ctx = groups * GROUP
    state = b_wide.shape[2]
    width = CHUNK
    tok, wide, _, end, diag = local_specs(seqs, ctx, inner, state, width)
    ones = jnp.asarray(np.kron(np.eye(GROUP), np.ones((1, state))), BF16)
    token = lambda t: jax.ShapeDtypeStruct(delta.shape, t)
    diag_shape = jax.ShapeDtypeStruct((seqs, groups, GROUP, GROUP * state), F32)
    chunked = pl.BlockSpec((1, 1, groups, GROUP, width), lambda c, j: (j, c, 0, 0, 0))
    chunked_shape = jax.ShapeDtypeStruct((inner // width, seqs, groups, GROUP, width), BF16)
    vmem = pltpu.VMEM
    return pl.pallas_call(
        sweep_kernel,
        grid=(seqs, inner // width),
        in_specs=[tok] * 6
        + [wide, wide, pl.BlockSpec((small.shape[0], width), lambda c, j: (0, j)), end, end]
        + [diag, diag, pl.BlockSpec(ones.shape, lambda c, j: (0, 0))],
        out_specs=[tok, chunked, tok, tok, diag, diag, end]
        + [pl.BlockSpec((1, 2, 8, width), lambda c, j: (c, 0, 0, j))],
        out_shape=[token(BF16), chunked_shape, token(F32), token(BF16)]
        + [diag_shape] * 2
        + [jax.ShapeDtypeStruct((seqs, state, inner), F32)]
        + [jax.ShapeDtypeStruct((seqs, 2, 8, inner), F32)],
        scratch_shapes=[
            vmem((groups, GROUP, width), F32),
            vmem((groups, GROUP, width), F32),
            vmem((ctx + 1, state, width), F32),
            vmem((ctx, state, width), F32),
            vmem((GROUP, state, width), BF16),
            vmem((GROUP, state, width), BF16),
        ],
        compiler_params=pltpu.CompilerParams(vmem_limit_bytes=56 << 20),
        name="sweep",
    )(
        delta, u, dy, gated_grad, gate_in, raw, b_wide, c_wide, small, start, final,
        cbd.reshape(diag_shape.shape), bbd.reshape(diag_shape.shape), ones,
    )


def body(
    hidden_in, lengths, norm_gain, in_weight, conv_weight, conv_bias, xproj_weight,
    dt_weight, dt_bias, a_log, skip_gain, out_weight, out_grad,
):
    seqs, ctx, width = hidden_in.shape
    taps, share = conv_weight.shape
    state = a_log.shape[0]
    rank = dt_weight.shape[0]
    rows = ctx * seqs
    row = lambda v: v.reshape(1, -1)
    x, og = hidden_in.reshape(rows, width), out_grad.reshape(rows, width)
    (
        normed, branch_grad, mask, lead, conv_out, u, gate_in, raw, delta, b_wide, c_wide, bbd, cbd,
        gated_grad, y_grad, step_low, start, final,
        in_matrix, out_matrix, proj_matrix, step_matrix, small,
    ) = front(
        x, og, lengths, conv_weight, a_log, row(conv_bias), row(dt_bias), row(skip_gain),
        row(norm_gain), in_weight, out_weight, xproj_weight, dt_weight, seqs,
    )
    grouped = lambda v: v.reshape(seqs, ctx // GROUP, GROUP, v.shape[-1])
    gated, z_grad, u_grad, raw_low, c_acc, b_acc, rate_grad, sums = sweep(
        *map(grouped, (delta, u, y_grad, gated_grad, gate_in, raw)),
        b_wide, c_wide, bbd, cbd, small, start, final,
    )
    flat = lambda v: v.reshape(rows, -1)
    hidden_out, input_grad, out_sum, in_sum, rest = back(
        flat(gated), z_grad.reshape(-1, rows, CHUNK), flat(u_grad), flat(raw_low), u, conv_out,
        lead, step_low, flat(c_acc), flat(b_acc), normed, x, og, branch_grad, mask,
        in_matrix, out_matrix, proj_matrix, step_matrix, small, rate_grad, sums,
    )
    rest = rest.astype(F32)
    shards = lax.axis_size("fsdp")
    at = taps + state
    return (
        hidden_out.reshape(seqs, ctx, width), input_grad.reshape(seqs, ctx, width),
        rest[at + 3, : width // shards], in_sum.astype(F32), rest[:taps], rest[at],
        rest[at + 4 + rank : at + 4 + rank + proj_matrix.shape[1]].T, rest[at + 4 : at + 4 + rank],
        rest[at + 1], rest[taps:at], rest[at + 2], out_sum.astype(F32),
    )


def solution(mesh):
    tokens = P(("dp", "fsdp"), "seq", None)
    return jax.shard_map(
        body,
        mesh=mesh,
        in_specs=(
            tokens, P(("dp", "fsdp")), P("fsdp"), P("fsdp", None), P(None, "fsdp"), P("fsdp"),
            P("fsdp", None), P(None, "fsdp"), P("fsdp"), P(None, "fsdp"), P("fsdp"),
            P("fsdp", None), tokens,
        ),
        out_specs=(
            tokens, tokens, P("fsdp"), P("fsdp", None), P(None, "fsdp"), P("fsdp"),
            P("fsdp", None), P(None, "fsdp"), P("fsdp"), P(None, "fsdp"), P("fsdp"),
            P("fsdp", None),
        ),
        check_vma=False,
    )
```

```python
import functools
import math

import jax
import jax.numpy as jnp
import numpy as np
from jax import lax
from jax.experimental import pallas as pl
from jax.experimental.pallas import tpu as pltpu
from jax.sharding import PartitionSpec as P

EPS = 1e-05
LOG2E = math.log2(math.e)
LANES = 128
GROUP = 16
F32 = jnp.float32
BF16 = jnp.bfloat16
MESH = pl.DeviceIdType.MESH
HR = 128
CHUNK = 512
SLACK = 1
TAPS = 4


def silu_parts(v):
    s = jax.nn.sigmoid(v)
    return v * s, s * (1.0 + v * (1.0 - s))


def front_kernel(
    span,
    x, og, lengths, taps_own, log_own, cbias_own, dbias_own, skip_own, gain_own,
    in_own, out_own, xp_own, dt_own,
    hidden_out, step_low, final, bbd,
    held_all, normed_full, bg_full, lead_full, slope_full, u_full, sig_full, delta_full,
    cw_full, dy_full, gated_full, zg_full, in_full, xp_full, dt_full, small_full,
    in_w, out_w, xp, dt, small, small_own, hx, acc, zacc, normed, v, proj, ends, sums,
    ends_in, sums_in, bg, mask, lead, slope, u, sig, delta, bw, cw, cbd, gg, dy, y, gated, zg,
    start, held,
    send, recv, halo, relay_send, relay_recv, sums_send, sums_recv, local, keep, held_sem,
):
    d, s, f = (lax.axis_index(a) for a in ("dp", "seq", "fsdp"))
    fx, fy, fd = f ^ 1, f ^ 2, f ^ 3
    tox, toy, sib = {"fsdp": fx}, {"fsdp": fy}, {"dp": 1 - d}
    rows, width = x.shape
    inner = u.shape[1]
    seqs = bw.shape[0]
    ctx = rows // seqs
    state, rank = log_own.shape[0], dt_own.shape[0]
    groups = ctx // GROUP
    share = inner // 4
    at_state, at_bias = TAPS, TAPS + state
    across = (((1,), (1,)), ((), ()))
    dot = lambda a, b, dims=(((1,), (0,)), ((), ())): lax.dot_general(
        a, b, dims, preferred_element_type=F32
    )

    for c in range(seqs):
        hx[c] = jnp.zeros((GROUP, width), BF16)
    barrier = pltpu.get_barrier_semaphore()
    for who in (tox, toy, sib):
        pl.semaphore_signal(barrier, inc=1, device_id=who, device_id_type=MESH)

    def greet(o, carry):
        who = {"seq": lax.rem(s + o, span)}
        pl.semaphore_signal(barrier, inc=1, device_id=who, device_id_type=MESH)
        return carry

    lax.fori_loop(1, span, greet, 0)
    small_own[...] = jnp.zeros(small_own.shape, F32)
    small_own[:TAPS] = taps_own[...]
    small_own[at_state:at_bias] = log_own[...]
    small_own[at_bias : at_bias + 1] = cbias_own[...]
    small_own[at_bias + 1 : at_bias + 2] = dbias_own[...]
    small_own[at_bias + 2 : at_bias + 3] = skip_own[...]
    small_own[at_bias + 3 : at_bias + 4, : width // 4] = gain_own[...]
    pl.semaphore_wait(barrier, 2 + span)

    SMALL, STREAM, PROJ, STEP, GATE, OUT = range(6)
    plan = (
        (small_own, small, 1, None),
        (in_own, in_w, 0, (0, inner)),
        (xp_own, xp, 0, None),
        (dt_own, dt, 1, None),
        (in_own, in_w, 0, (inner, 2 * inner)),
        (out_own, out_w, 0, None),
    )

    def window(p, owner, half, q):
        src, dst, dim, cols = plan[p]
        high, wide = src.shape
        part = high // 4
        at = (half * 2 + q) * part
        lo, hi = cols or (0, wide)
        if dim == 0:
            return dst.at[pl.ds(pl.multiple_of(owner * high + at, part), part), lo:hi]
        col = pl.ds(pl.multiple_of(owner * wide, wide), wide)
        return dst.at[pl.ds(pl.multiple_of(at, part), part), col]

    def own(p, half, q):
        src, _, _, cols = plan[p]
        high, wide = src.shape
        part = high // 4
        lo, hi = cols or (0, wide)
        return src.at[pl.ds(pl.multiple_of((half * 2 + q) * part, part), part), lo:hi]

    def copy(src, dst, p, kind, who):
        return pltpu.make_async_remote_copy(
            src_ref=src, dst_ref=dst, send_sem=send.at[p, kind], recv_sem=recv.at[p, kind],
            device_id=who, device_id_type=MESH,
        )

    started = []

    def go(one):
        one.start()
        started.append(one)

    def start_own(p):
        for q in (0, 1):
            go(copy(own(p, d, q), window(p, f, d, q), p, q, tox))
            go(copy(own(p, d, 1 - q), window(p, f, d, 1 - q), p, 3 - q, toy))

    def place_own(p):
        for half in (0, 1):
            for q in (0, 1):
                pltpu.make_async_copy(
                    own(p, half, q), window(p, f, half, q), local.at[p, half * 2 + q]
                ).start()

    def own_ready(p):
        for half in (0, 1):
            for q in (0, 1):
                pltpu.make_async_copy(
                    own(p, half, q), window(p, f, half, q), local.at[p, half * 2 + q]
                ).wait()

    def arrived(p, kind, owner, half, q):
        w = window(p, owner, half, q)
        copy(w, w, p, kind, sib).wait_recv()
        return w

    near = ((0, fx, 0), (3, fy, 1), (1, fx, 1), (2, fy, 0))
    diagonal = ((4, fd, 0), (5, fd, 1))

    def serve_near(p):
        for kind, owner, q in near:
            w = arrived(p, kind, owner, d, q)
            if kind == 0:
                go(copy(w, w, p, 4, toy))
            if kind == 3:
                go(copy(w, w, p, 5, tox))
            go(copy(w, w, p, 6 + kind, sib))

    def serve_far(p):
        for kind, owner, q in diagonal:
            w = arrived(p, kind, owner, d, q)
            go(copy(w, w, p, 6 + kind, sib))

    def near_ready(p):
        for kind, owner, q in near:
            arrived(p, 6 + kind, owner, 1 - d, q)

    def far_ready(p):
        for kind, owner, q in diagonal:
            arrived(p, 6 + kind, owner, 1 - d, q)

    for p in (SMALL, STREAM, PROJ, STEP):
        start_own(p)
    for p in range(6):
        place_own(p)
    def edges(c):
        return pltpu.make_async_remote_copy(
            src_ref=x.at[(c + 1) * ctx - GROUP : (c + 1) * ctx], dst_ref=hx.at[c],
            send_sem=halo.at[0, c], recv_sem=halo.at[1, c],
            device_id={"seq": jnp.minimum(s + 1, span - 1)}, device_id_type=MESH,
        )

    @pl.when(s < span - 1)
    def _():
        for c in range(seqs):
            edges(c).start()

    for c in range(seqs):
        t = s * ctx + lax.broadcasted_iota(jnp.int32, (ctx, LANES), 0)
        mask[c * ctx : (c + 1) * ctx] = (t < lengths[c]).astype(F32)

    def mask_step(r, carry):
        tok = pl.ds(pl.multiple_of(r * GROUP, GROUP), GROUP)
        held = jnp.concatenate([mask[tok]] * (width // LANES), 1)
        bg[tok] = (og[tok].astype(F32) * held).astype(BF16)
        return carry

    lax.fori_loop(0, rows // GROUP, mask_step, 0)

    serve_near(SMALL)
    serve_far(SMALL)
    near_ready(SMALL)
    far_ready(SMALL)
    own_ready(SMALL)

    @pl.when(s > 0)
    def _():
        for c in range(seqs):
            edges(c).wait_recv()

    gain_at = at_bias + 3
    gain = jnp.concatenate(
        [small[gain_at : gain_at + 1, j * share : j * share + width // 4] for j in range(4)], 1
    )

    def normalised(v):
        v = v.astype(F32)
        inverse = lax.rsqrt(jnp.mean(v * v, -1, keepdims=True) + EPS)
        return (v * inverse * gain).astype(BF16)

    def norm_step(r, carry):
        tok = pl.ds(pl.multiple_of(r * GROUP, GROUP), GROUP)
        normed[tok] = normalised(x[tok])
        return carry

    lax.fori_loop(0, rows // GROUP, norm_step, 0)
    for c in range(seqs):
        normed[rows + c * GROUP : rows + (c + 1) * GROUP] = normalised(hx[c])

    def project(total, high, first, owner, fresh):
        shard = pl.ds(pl.multiple_of(owner * (width // 4), width // 4), width // 4)
        left = normed[:high, shard]

        def one(t, carry):
            cols = pl.ds(pl.multiple_of(t * CHUNK, CHUNK), CHUNK)
            right = in_w[shard, pl.ds(pl.multiple_of(first + t * CHUNK, CHUNK), CHUNK)]
            part = dot(left, right)
            total[:, cols] = part if fresh else total[:, cols] + part
            return carry

        lax.fori_loop(0, inner // CHUNK, one, 0)

    tall = rows + seqs * GROUP
    own_ready(STREAM)
    project(acc, tall, 0, f, True)
    serve_near(STREAM)
    start_own(GATE)
    start_own(OUT)
    near_ready(STREAM)
    project(acc, tall, 0, fx, False)
    project(acc, tall, 0, fy, False)
    serve_far(STREAM)
    for p in (PROJ, STEP):
        serve_near(p)
        serve_far(p)
    far_ready(STREAM)
    project(acc, tall, 0, fd, False)

    tile = 2 * LANES

    def columns(t, size=tile):
        return pl.ds(pl.multiple_of(t * size, size), size)

    def conv_step(t, carry):
        cols = columns(t)
        for c in range(seqs):
            before = acc[rows + c * GROUP : rows + (c + 1) * GROUP, cols].astype(BF16)
            stream = acc[c * ctx : (c + 1) * ctx, cols].astype(BF16)
            lead[c, :GROUP, cols] = before
            lead[c, GROUP:, cols] = stream
            held = jnp.concatenate([before, stream], 0).astype(F32)
            total = small[at_bias : at_bias + 1, cols]
            for k in range(TAPS):
                at = GROUP - TAPS + 1 + k
                total = total + small[k : k + 1, cols] * held[at : at + ctx]
            value, grad = silu_parts(total)
            slope[c * ctx : (c + 1) * ctx, cols] = grad.astype(BF16)
            u[c * ctx : (c + 1) * ctx, cols] = value.astype(BF16)
        return carry

    lax.fori_loop(0, inner // tile, conv_step, 0)
    for p in (PROJ, STEP):
        near_ready(p)
        far_ready(p)
        own_ready(p)
    proj[...] = dot(u[...], xp[...])
    step_low[...] = proj[:, :rank].astype(BF16)

    def wide_step(i, carry):
        tok = pl.ds(pl.multiple_of(i * GROUP, GROUP), GROUP)
        held = proj[tok]
        for ref, first in ((bw, rank), (cw, rank + state)):
            value = held[:, first : first + state]
            c, at = i // groups, lax.rem(i, groups)
            ref[c, pl.ds(pl.multiple_of(at * GROUP, GROUP), GROUP)] = jnp.broadcast_to(
                value[:, :, None], (GROUP, state, LANES)
            )
        return carry

    lax.fori_loop(0, rows // GROUP, wide_step, 0)
    r = lax.broadcasted_iota(jnp.int32, (rows, GROUP * state), 0)
    k = lax.broadcasted_iota(jnp.int32, (rows, GROUP * state), 1)
    mine = lax.rem(r, GROUP) == k // state
    at = lax.broadcasted_iota(jnp.int32, (proj.shape[1], GROUP * state), 0)
    col = lax.rem(lax.broadcasted_iota(jnp.int32, (proj.shape[1], GROUP * state), 1), state)
    for ref, first in ((bbd, rank), (cbd, rank + state)):
        spread = (at == col + first).astype(F32).astype(BF16)
        ref[...] = jnp.where(mine, dot(proj[...].astype(BF16), spread), 0.0).astype(BF16)

    def delta_step(t, carry):
        cols = columns(t)
        for c in range(seqs):
            tok = slice(c * ctx, (c + 1) * ctx)
            value = dot(step_low[tok], dt[:, cols]) + small[at_bias + 1 : at_bias + 2, cols]
            sig[tok, cols] = jax.nn.sigmoid(value).astype(BF16)
            value = jnp.maximum(value, 0.0) + jnp.log1p(jnp.exp(-jnp.abs(value)))
            for i in range(groups):
                delta[c * groups + i, :, cols] = value[i * GROUP : (i + 1) * GROUP]
            sums[c : c + 1, cols] = jnp.sum(value, 0, keepdims=True)
            value = value * u[tok, cols].astype(F32)
            for i in range(groups):
                v[c * groups + i, :, cols] = value[i * GROUP : (i + 1) * GROUP]
        return carry

    sums[...] = jnp.zeros(sums.shape, F32)
    lax.fori_loop(0, inner // tile, delta_step, 0)

    def sums_copy(j):
        return pltpu.make_async_remote_copy(
            src_ref=sums, dst_ref=sums_in.at[s], send_sem=sums_send.at[j],
            recv_sem=sums_recv.at[s], device_id={"seq": j}, device_id_type=MESH,
        )

    def sums_start(o, carry):
        sums_copy(lax.rem(s + o, span)).start()
        return carry

    lax.fori_loop(1, span, sums_start, 0)

    def ends_copy(j, way, c):
        return pltpu.make_async_remote_copy(
            src_ref=ends.at[way, c], dst_ref=ends_in.at[s, c], send_sem=relay_send.at[j, c],
            recv_sem=relay_recv.at[s, c], device_id={"seq": j}, device_id_type=MESH,
        )

    def ends_start(first, count, way, c):
        def one(j, carry):
            ends_copy(j, way, c).start()
            return carry

        lax.fori_loop(first, count, one, 0)

    def forward_ends(c):
        for j in range(0, inner, CHUNK):
            cuts = [slice(j + i, j + i + LANES) for i in range(0, CHUNK, LANES)]
            rates = [-jnp.exp(small[at_state:at_bias, cut]) * LOG2E for cut in cuts]

            def one(i, h):
                h = list(h)
                for k in range(GROUP):
                    b = bw[c, i * GROUP + k]
                    for n, cut in enumerate(cuts):
                        step = delta[c * groups + i, k : k + 1, cut]
                        factor = jnp.exp2(jnp.broadcast_to(step, (state, LANES)) * rates[n])
                        row = jnp.broadcast_to(v[c * groups + i, k : k + 1, cut], (state, LANES))
                        h[n] = factor * h[n] + row * b
                return tuple(h)

            zero = tuple(jnp.zeros((state, LANES), F32) for _ in cuts)
            h = lax.fori_loop(0, groups, one, zero)
            for n, cut in enumerate(cuts):
                ends[0, c, :, cut] = h[n].astype(BF16)

    def backward_ends(c):
        for j in range(0, inner, CHUNK):
            cuts = [slice(j + i, j + i + LANES) for i in range(0, CHUNK, LANES)]
            rates = [-jnp.exp(small[at_state:at_bias, cut]) * LOG2E for cut in cuts]

            def one(i, carry):
                run, p = (list(value) for value in carry)
                for k in range(GROUP):
                    read = cw[c, i * GROUP + k]
                    for n, cut in enumerate(cuts):
                        step = delta[c * groups + i, k : k + 1, cut]
                        factor = jnp.exp2(jnp.broadcast_to(step, (state, LANES)) * rates[n])
                        row = dy[c * groups + i, k : k + 1, cut]
                        run[n] = run[n] * factor
                        p[n] = p[n] + run[n] * (read * jnp.broadcast_to(row, (state, LANES)))
                return tuple(run), tuple(p)

            one_s = tuple(jnp.ones((state, LANES), F32) for _ in cuts)
            zero = tuple(jnp.zeros((state, LANES), F32) for _ in cuts)
            _, p = lax.fori_loop(0, groups, one, (one_s, zero))
            for n, cut in enumerate(cuts):
                ends[1, c, :, cut] = p[n].astype(BF16)

    def stash(*pairs):
        for at, (src, dst) in pairs:
            one = pltpu.make_async_copy(src, dst, keep.at[at])
            one.start()
            kept.append(one)

    kept = []
    stash(
        (0, (normed.at[:rows], normed_full)), (1, (bg, bg_full)), (2, (lead, lead_full)),
        (3, (slope, slope_full)), (4, (u, u_full)), (5, (sig, sig_full)), (6, (delta, delta_full)),
        (7, (cw, cw_full)), (8, (xp, xp_full)), (9, (dt, dt_full)), (10, (small, small_full)),
    )

    def ends_wait(j, c):
        pltpu.make_async_remote_copy(
            src_ref=ends.at[0, c], dst_ref=ends_in.at[j, c], send_sem=relay_send.at[j, c],
            recv_sem=relay_recv.at[j, c], device_id={"seq": j}, device_id_type=MESH,
        ).wait_recv()

    def join(ref, j, c):
        ends_wait(j, c)

        def one(t, carry):
            cols = columns(t, CHUNK)
            rates = -jnp.exp(small[at_state:at_bias, cols]) * LOG2E
            decay = jnp.exp2(sums_in[j, c : c + 1, cols] * rates)
            ref[c, :, cols] = decay * ref[c, :, cols] + ends_in[j, c, :, cols].astype(F32)
            return carry

        lax.fori_loop(0, inner // CHUNK, one, 0)

    def join_start(j, carry):
        for c in range(seqs):
            join(start, j, c)
        return carry

    def join_final(o, carry):
        for c in range(seqs):
            join(final, span - 1 - o, c)
        return carry

    def sums_wait(o, carry):
        j = lax.rem(s + o, span)
        pltpu.make_async_remote_copy(
            src_ref=sums, dst_ref=sums_in.at[j], send_sem=sums_send.at[j],
            recv_sem=sums_recv.at[j], device_id={"seq": j}, device_id_type=MESH,
        ).wait_recv()
        return carry

    parts = inner // CHUNK
    blocks = seqs * parts

    def held_copy(b):
        slot = lax.rem(b, 2)
        return pltpu.make_async_copy(held.at[slot], held_all.at[b], held_sem.at[slot])

    def sweep_block(b, carry):
        c, slot = b // parts, lax.rem(b, 2)
        first = lax.rem(b, parts) * CHUNK
        cuts = [pl.ds(pl.multiple_of(first + n, LANES), LANES) for n in range(0, CHUNK, LANES)]
        tiles = [slice(n, n + LANES) for n in range(0, CHUNK, LANES)]
        all_cols = pl.ds(pl.multiple_of(first, CHUNK), CHUNK)
        rates = [-jnp.exp(small[at_state:at_bias, cut]) * LOG2E for cut in cuts]
        skip = small[at_bias + 2 : at_bias + 3, all_cols]

        @pl.when(b >= 2)
        def _():
            held_copy(b - 2).wait()

        h = tuple(start[c, :, cut] for cut in cuts)
        for n, cut in enumerate(tiles):
            held[slot, 0, :, cut] = h[n].astype(BF16)

        def one(i, h):
            h = list(h)
            g = c * groups + i
            for k in range(GROUP):
                b_in = bw[c, i * GROUP + k]
                for n, cut in enumerate(cuts):
                    step = jnp.broadcast_to(delta[g, k : k + 1, cut], (state, LANES))
                    row = jnp.broadcast_to(v[g, k : k + 1, cut], (state, LANES))
                    h[n] = jnp.exp2(step * rates[n]) * h[n] + row * b_in
                    held[slot, i * GROUP + k + 1, :, tiles[n]] = h[n].astype(BF16)
            states = held[slot, pl.ds(i * GROUP + 1, GROUP)].reshape(GROUP * state, CHUNK)
            tok = pl.ds(pl.multiple_of(g * GROUP, GROUP), GROUP)
            y[g, :, all_cols] = dot(cbd[tok], states) + skip * u[tok, all_cols].astype(F32)
            return tuple(h)

        lax.fori_loop(0, groups, one, h)
        held_copy(b).start()
        return carry

    def grad_part(owner):
        shard = pl.ds(pl.multiple_of(owner * share, share), share)
        gg[:, shard] = dot(bg[...], out_w[shard], across)

    forward_ends(0)
    ends_start(s + 1, span, 0, 0)
    serve_near(GATE)
    own_ready(GATE)
    forward_ends(1)
    ends_start(s + 1, span, 0, 1)
    near_ready(GATE)
    for owner, fresh in ((f, True), (fx, False), (fy, False)):
        project(zacc, rows, inner, owner, fresh)
    lax.fori_loop(1, span, sums_wait, 0)
    start[...] = jnp.zeros(start.shape, F32)
    lax.fori_loop(0, s, join_start, 0)
    lax.fori_loop(0, 2, sweep_block, 0)
    serve_far(GATE)
    lax.fori_loop(2, 4, sweep_block, 0)
    serve_near(OUT)
    far_ready(GATE)
    project(zacc, rows, inner, fd, False)
    lax.fori_loop(4, blocks - 1, sweep_block, 0)
    serve_far(OUT)
    stash((11, (in_w, in_full)))
    lax.fori_loop(blocks - 1, blocks, sweep_block, 0)
    own_ready(OUT)
    near_ready(OUT)
    for owner in (f, fx, fy):
        grad_part(owner)
    far_ready(OUT)
    grad_part(fd)

    def gate_step(t, carry):
        cols = columns(t)
        for c in range(seqs):
            tok = slice(c * ctx, (c + 1) * ctx)
            value, grad = silu_parts(zacc[tok, cols].astype(BF16).astype(F32))
            back = gg[tok, cols]
            pieces = [y[c * groups + i, :, cols] for i in range(groups)]
            scanned = jnp.concatenate(pieces, 0)
            gated[tok, cols] = (scanned * value).astype(BF16)
            half = pl.ds(pl.multiple_of(lax.rem(t, 2) * tile, tile), tile)
            zg[t // 2, tok, half] = (back * scanned * grad).astype(BF16)
            value = back * value
            for i in range(groups):
                dy[c * groups + i, :, cols] = value[i * GROUP : (i + 1) * GROUP]
        return carry

    lax.fori_loop(0, inner // tile, gate_step, 0)
    stash((12, (dy, dy_full)), (13, (gated, gated_full)), (14, (zg, zg_full)))
    for c in range(seqs):
        backward_ends(c)
        ends_start(0, s, 1, c)

    def hidden_step(t, carry):
        cols = columns(t)
        keep_rows = jnp.concatenate([mask[...]] * (tile // LANES), 1)
        branch = dot(gated[...], out_w[:, cols])
        hidden_out[:, cols] = (x[:, cols].astype(F32) + keep_rows * branch).astype(BF16)
        return carry

    lax.fori_loop(0, width // tile, hidden_step, 0)
    final[...] = jnp.zeros(final.shape, F32)
    lax.fori_loop(0, span - 1 - s, join_final, 0)

    for one in started:
        one.wait_send()

    @pl.when(s < span - 1)
    def _():
        for c in range(seqs):
            edges(c).wait_send()

    def sent(o, carry):
        j = lax.rem(s + o, span)
        sums_copy(j).wait_send()
        for c in range(seqs):
            ends_copy(j, 0, c).wait_send()
        return carry

    lax.fori_loop(1, span, sent, 0)
    for one in kept:
        one.wait()
    for b in range(max(blocks - 2, 0), blocks):
        held_copy(b).wait()


def front(x, og, lengths, taps, logs, cbias, dbias, skip, gain, in_own, out_own, xp_own, dt_own, seqs):
    rows, width = x.shape
    share, inner = taps.shape[1], 4 * taps.shape[1]
    state, rank, used = logs.shape[0], dt_own.shape[0], xp_own.shape[1]
    ctx = rows // seqs
    span = lax.axis_size("seq")
    parts = inner // CHUNK
    vmem, dma = pltpu.VMEM, pltpu.SemaphoreType.DMA
    whole, anywhere = pl.BlockSpec(memory_space=vmem), pl.BlockSpec(memory_space=pl.ANY)
    shape = jax.ShapeDtypeStruct
    grouped = (rows // GROUP, GROUP, inner)
    kept = [
        ((rows, width), BF16),
        ((rows, width), BF16),
        ((seqs, ctx + GROUP, inner), BF16),
        ((rows, inner), BF16),
        ((rows, inner), BF16),
        ((rows, inner), BF16),
        (grouped, F32),
        ((seqs, ctx, state, LANES), F32),
        (grouped, F32),
        ((rows, inner), BF16),
        ((parts, rows, CHUNK), BF16),
        ((width, 2 * inner), BF16),
        ((inner, used), BF16),
        ((rank, inner), BF16),
        ((32, inner), F32),
    ]
    held = (ctx + 1, state, CHUNK)
    return pl.pallas_call(
        functools.partial(front_kernel, span),
        in_specs=[whole, whole, pl.BlockSpec(memory_space=pltpu.SMEM)]
        + [whole] * 6
        + [anywhere] * 4,
        out_specs=[whole] * 4 + [anywhere] * (1 + len(kept)),
        out_shape=[
            shape((rows, width), BF16),
            shape((rows, rank), BF16),
            shape((seqs, state, inner), F32),
            shape((rows, GROUP * state), BF16),
            shape((seqs * parts,) + held, BF16),
        ]
        + [shape(*k) for k in kept],
        scratch_shapes=[
            vmem((width, 2 * inner), BF16),
            vmem((inner, width), BF16),
            vmem((inner, used), BF16),
            vmem((rank, inner), BF16),
            vmem((32, inner), F32),
            vmem((32, share), F32),
            vmem((seqs, GROUP, width), BF16),
            vmem((rows + seqs * GROUP, inner), F32),
            vmem((rows, inner), F32),
            vmem((rows + seqs * GROUP, width), BF16),
            vmem(grouped, F32),
            vmem((rows, used), F32),
            vmem((2, seqs, state, inner), BF16),
            vmem((8, inner), F32),
            vmem((span, seqs, state, inner), BF16),
            vmem((span, 8, inner), F32),
            vmem((rows, width), BF16),
            vmem((rows, LANES), F32),
            vmem((seqs, ctx + GROUP, inner), BF16),
            vmem((rows, inner), BF16),
            vmem((rows, inner), BF16),
            vmem((rows, inner), BF16),
            vmem(grouped, F32),
            vmem((seqs, ctx, state, LANES), F32),
            vmem((seqs, ctx, state, LANES), F32),
            vmem((rows, GROUP * state), BF16),
            vmem((rows, inner), F32),
            vmem(grouped, F32),
            vmem(grouped, F32),
            vmem((rows, inner), BF16),
            vmem((parts, rows, CHUNK), BF16),
            vmem((seqs, state, inner), F32),
            vmem((2,) + held, BF16),
            dma((6, 12)),
            dma((6, 12)),
            dma((2, seqs)),
            dma((span, seqs)),
            dma((span, seqs)),
            dma((span,)),
            dma((span,)),
            dma((6, 4)),
            dma((len(kept),)),
            dma((2,)),
        ],
        compiler_params=pltpu.CompilerParams(
            collective_id=0, has_side_effects=True, vmem_limit_bytes=63 << 20
        ),
        name="front",
    )(x, og, lengths, taps, logs, cbias, dbias, skip, gain, in_own, out_own, xp_own, dt_own)


def back_kernel(
    span, state, rank,
    gated, bg, step_low, final, bbd, ones, small, x, og,
    held_all, normed_full, lead_full, slope_full, u_full, sig_full, delta_full,
    cw_full, dy_full, zg_full, in_full, xp_full, dt_full,
    input_grad, out_sum, in_sum, rest_sum,
    normed, lead, slope, u, sig, delta, cw, dy, mixed, xp, dt, in_w, held, gs, ws, rl, cacc,
    bacc, logs, sums,
    pg, cg, ng, rest, g, ra, rx, ry, zlo, zhi, tot,
    send, recv, halo, local, load, held_sem, in_sem,
):
    d, s, f = (lax.axis_index(a) for a in ("dp", "seq", "fsdp"))
    fx, fy, fd = f ^ 1, f ^ 2, f ^ 3
    chunks = tot.shape[0]
    rows, width = x.shape
    inner = gated.shape[1]
    seqs = cg.shape[0]
    ctx = rows // seqs
    parts = inner // CHUNK
    out_chunks = 2 * width // CHUNK
    in_chunks = 2 * parts
    last = out_chunks + in_chunks
    slots = g.shape[0]
    q = HR // 2
    root = (span - 1) // 2
    tox, toy, sib = {"fsdp": fx}, {"fsdp": fy}, {"dp": 1 - d}
    up, down = {"seq": jnp.minimum(s + 1, span - 1)}, {"seq": jnp.maximum(s - 1, 0)}
    contract = (((0,), (0,)), ((), ()))
    across = (((1,), (1,)), ((), ()))
    dot = lambda a, b, dims=(((1,), (0,)), ((), ())): lax.dot_general(
        a, b, dims, preferred_element_type=F32
    )

    loads = (
        (mixed.at[:parts], zg_full), (normed, normed_full), (delta, delta_full), (dy, dy_full),
        (u, u_full), (cw, cw_full), (sig, sig_full), (slope, slope_full),
        (lead, lead_full), (xp, xp_full), (dt, dt_full),
    )
    loads = [pltpu.make_async_copy(src, dst, load.at[n]) for n, (dst, src) in enumerate(loads)]

    def held_copy(b):
        slot = lax.rem(b, 2)
        return pltpu.make_async_copy(held_all.at[b], held.at[slot], held_sem.at[slot])

    def in_copy(k):
        slot = lax.rem(k, 2)
        first = pl.multiple_of(lax.rem(k + parts, 2 * parts) * CHUNK, CHUNK)
        return pltpu.make_async_copy(in_full.at[:, pl.ds(first, CHUNK)], in_w.at[slot], in_sem.at[slot])

    held_copy(0).start()
    for one in loads[2:6]:
        one.start()
    held_copy(1).start()
    for one in loads[:2] + loads[6:]:
        one.start()
    cg[:, ctx:] = jnp.zeros((seqs, cg.shape[1] - ctx, inner), F32)
    barrier = pltpu.get_barrier_semaphore()
    for who in (tox, toy, sib):
        pl.semaphore_signal(barrier, inc=1, device_id=who, device_id_type=MESH)

    @pl.when(s > 0)
    def _():
        pl.semaphore_signal(barrier, inc=1, device_id=down, device_id_type=MESH)

    @pl.when(s < span - 1)
    def _():
        pl.semaphore_signal(barrier, inc=1, device_id=up, device_id_type=MESH)

    ends = (s == 0) | (s == span - 1)
    pl.semaphore_wait(barrier, jnp.where(ends, 4, 5) if span > 1 else 3)

    def copy(kind, c, src, dst, who):
        return pltpu.make_async_remote_copy(
            src_ref=src, dst_ref=dst, send_sem=send.at[kind, c], recv_sem=recv.at[kind, c],
            device_id=who, device_id_type=MESH,
        )

    lo, hi = slice(0, q), slice(q, HR)
    A = lambda c: copy(0, c, g.at[lax.rem(c, slots), :, 1 - d], ra.at[c], sib)
    X0 = lambda c: copy(1, c, ra.at[c, fd, lo], rx.at[c, 0], tox)
    X1 = lambda c: copy(2, c, ra.at[c, fx, lo], rx.at[c, 1], tox)
    X2 = lambda c: copy(3, c, ra.at[c, fx, hi], rx.at[c, 2], tox)
    Y0 = lambda c: copy(4, c, ra.at[c, fd, hi], ry.at[c, 0], toy)
    Y2 = lambda c: copy(5, c, ra.at[c, fy, hi], ry.at[c, 2], toy)
    Y1 = lambda c: copy(6, c, ra.at[c, fy, lo], ry.at[c, 1], toy)
    ZU = lambda c: copy(7, c, ra.at[c, f], zlo.at[c], up)
    ZD = lambda c: copy(8, c, ra.at[c, f], zhi.at[c], down)
    TU = lambda c: copy(9, c, tot.at[c, d], tot.at[c, d], up)
    TD = lambda c: copy(10, c, tot.at[c, d], tot.at[c, d], down)
    D = lambda c: copy(11, c, tot.at[c, d], tot.at[c, d], sib)
    below, above = s < root, s > root
    spot = jnp.where(below, s, jnp.where(above, span - 1 - s, 0))
    far = jnp.abs(s - root)
    most = max(root, span - 1 - root)

    def stage(c, run):
        @pl.when((c >= 0) & (c < chunks))
        def _():
            run(c)

    def produce(c):
        slot = lax.rem(c, slots)

        @pl.when(c >= slots)
        def _():
            A(c - slots).wait_send()

        @pl.when(c < out_chunks)
        def _():
            r = c // (width // CHUNK)
            col = lax.rem(c, width // CHUNK) * CHUNK
            right = bg[:, pl.ds(pl.multiple_of(col, CHUNK), CHUNK)]
            for j in range(4):
                for h in range(2):
                    at = j * (inner // 4) + h * (inner // 8) + r * HR
                    left = gated[:, pl.ds(pl.multiple_of(at, HR), HR)]
                    g[slot, j, h] = dot(left, right, contract).astype(BF16)

        @pl.when((c >= out_chunks) & (c < last))
        def _():
            right = mixed[c - out_chunks]
            for j in range(4):
                t = dot(normed[:, j * 2 * HR : (j + 1) * 2 * HR], right, contract).astype(BF16)
                g[slot, j, 0] = t[:HR]
                g[slot, j, 1] = t[HR:]

        @pl.when(c == last)
        def _():
            for j in range(4):
                for h in range(2):
                    cols = slice(j * CHUNK, (j + 1) * CHUNK)
                    g[slot, j, h] = rest[h * HR : (h + 1) * HR, cols].astype(BF16)

        A(c).start()

    def first_sum(c):
        A(c).wait_recv()
        for j in range(4):
            own = g[lax.rem(c, slots), j, d]
            ra[c, j] = (ra[c, j].astype(F32) + own.astype(F32)).astype(BF16)
        X0(c).start()
        Y0(c).start()
        X1(c).start()
        Y2(c).start()

    def second_sum(c):
        X0(c).wait_recv()
        ra[c, fy, lo] = (ra[c, fy, lo].astype(F32) + rx[c, 0].astype(F32)).astype(BF16)
        Y1(c).start()
        Y0(c).wait_recv()
        ra[c, fx, hi] = (ra[c, fx, hi].astype(F32) + ry[c, 0].astype(F32)).astype(BF16)
        X2(c).start()

    def third_sum(c):
        X1(c).wait_recv()
        Y2(c).wait_recv()
        X2(c).wait_recv()
        Y1(c).wait_recv()
        for k, part in enumerate((lo, hi)):
            total = ra[c, f, part].astype(F32) + rx[c, 1 + k].astype(F32) + ry[c, 1 + k].astype(F32)
            ra[c, f, part] = total.astype(BF16)

    def inward(c):
        @pl.when(below & (s > 0))
        def _():
            ZU(c).wait_recv()
            ra[c, f] = (ra[c, f].astype(F32) + zlo[c].astype(F32)).astype(BF16)

        @pl.when(above & (s < span - 1))
        def _():
            ZD(c).wait_recv()
            ra[c, f] = (ra[c, f].astype(F32) + zhi[c].astype(F32)).astype(BF16)

        pl.when(below)(lambda: ZU(c).start())
        pl.when(above)(lambda: ZD(c).start())

    def at_root(c):
        total = ra[c, f].astype(F32)
        if root > 0:
            ZU(c).wait_recv()
            total = total + zlo[c].astype(F32)
        if span - 1 > root:
            ZD(c).wait_recv()
            total = total + zhi[c].astype(F32)
        tot[c, d] = total.astype(BF16)
        if root > 0:
            TD(c).start()
        if span - 1 > root:
            TU(c).start()
        D(c).start()

    def outward(c):
        @pl.when(above)
        def _():
            TU(c).wait_recv()
            pl.when(s < span - 1)(lambda: TU(c).start())

        @pl.when(below)
        def _():
            TD(c).wait_recv()
            pl.when(s > 0)(lambda: TD(c).start())

        D(c).start()

    tile = 2 * LANES

    def columns(t, size=tile):
        return pl.ds(pl.multiple_of(t * size, size), size)

    def back_block(b):
        c, slot = b // parts, lax.rem(b, 2)
        groups = ctx // GROUP
        first = lax.rem(b, parts) * CHUNK
        cuts = [pl.ds(pl.multiple_of(first + n, LANES), LANES) for n in range(0, CHUNK, LANES)]
        tiles = [slice(n, n + LANES) for n in range(0, CHUNK, LANES)]
        cols = pl.ds(pl.multiple_of(first, CHUNK), CHUNK)
        rates = [-jnp.exp(small[TAPS : TAPS + state, cut]) * LOG2E for cut in cuts]
        skip = small[TAPS + state + 2 : TAPS + state + 3, cols]
        held_copy(b).wait()

        def one(turn, carry):
            i = groups - 1 - turn
            at = c * groups + i
            tok = pl.ds(pl.multiple_of(at * GROUP, GROUP), GROUP)
            p, total, kept = (list(value) for value in carry)
            for k in reversed(range(GROUP)):
                t = i * GROUP + k
                read = cw[c, t]
                for n, cut in enumerate(cuts):
                    row = lambda ref: jnp.broadcast_to(ref[at, k : k + 1, cut], (state, LANES))
                    step = row(delta)
                    grad = read * row(dy) + p[n]
                    p[n] = jnp.exp2(step * rates[n]) * grad
                    w = p[n] * held[slot, t, :, tiles[n]].astype(F32)
                    total[n] = total[n] + w * step
                    gs[k, :, tiles[n]] = grad.astype(BF16)
                    ws[k, :, tiles[n]] = (w * rates[n]).astype(BF16)
            grads = gs[...].reshape(GROUP * state, CHUNK)
            states = held[slot, pl.ds(i * GROUP + 1, GROUP)].reshape(GROUP * state, CHUNK)
            drive_grad = dot(bbd[tok], grads)
            delta_part = dot(ones[...], ws[...].reshape(GROUP * state, CHUNK))
            value, out, gain = u[tok, cols].astype(F32), dy[at, :, cols], delta[at, :, cols]
            bacc[tok] += dot((gain * value).astype(BF16), grads, across)
            cacc[tok] += dot(out.astype(BF16), states, across)
            raw_grad = drive_grad * value + delta_part * (1.0 / LOG2E)
            raw_grad = raw_grad * sig[tok, cols].astype(F32)
            rl[tok, cols] = raw_grad.astype(BF16)
            dy[at, :, cols] = out * skip + drive_grad * gain
            kept[0] = kept[0] + (out * value)[:8] + (out * value)[8:]
            kept[1] = kept[1] + raw_grad[:8] + raw_grad[8:]
            return tuple(p), tuple(total), tuple(kept)

        zero = tuple(jnp.zeros((state, LANES), F32) for _ in cuts)
        none = jnp.zeros((8, CHUNK), F32)
        begin = tuple(final[c, :, cut] for cut in cuts)
        _, total, kept = lax.fori_loop(0, groups, one, (begin, zero, (none, none)))
        for n, cut in enumerate(cuts):
            logs[:, cut] += total[n]
        sums[0, :, cols] += kept[0]
        sums[1, :, cols] += kept[1]

        @pl.when(b + 2 < blocks)
        def _():
            held_copy(b + 2).start()

    def proj_work():
        step_grad = dot(rl[...], dt[...], across)
        r = lax.broadcasted_iota(jnp.int32, (rows, GROUP * state), 0)
        k = lax.broadcasted_iota(jnp.int32, (rows, GROUP * state), 1)
        own = lax.rem(r, GROUP) == k // state
        pick = lambda v: jnp.where(own, v[...], 0.0).astype(BF16)
        at = lax.rem(lax.broadcasted_iota(jnp.int32, (GROUP * state, LANES), 0), state)
        col = lax.broadcasted_iota(jnp.int32, (GROUP * state, LANES), 1)
        fold = lambda first: (col == at + first).astype(F32).astype(BF16)
        grads = jnp.concatenate([step_grad, jnp.zeros((rows, LANES - rank), F32)], 1)
        grads = grads + dot(pick(bacc), fold(rank)) + dot(pick(cacc), fold(rank + state))
        pg[...] = grads.astype(BF16)

    def weight_work():
        first = TAPS + state + 4
        used = rank + 2 * state

        def weights(t, carry):
            cols = columns(t)
            rest[first : first + rank, cols] = dot(step_low[...], rl[:, cols], contract)
            rest[first + rank : first + rank + used, cols] = dot(pg[...], u[:, cols], contract)[:used]
            kept = -logs[:, cols] * jnp.exp(small[TAPS : TAPS + state, cols])
            rest[TAPS : TAPS + state, cols] = kept
            at = TAPS + state
            rest[at + 1 : at + 2, cols] = jnp.sum(sums[1, :, cols], 0, keepdims=True)
            rest[at + 2 : at + 3, cols] = jnp.sum(sums[0, :, cols], 0, keepdims=True)
            return carry

        lax.fori_loop(0, inner // tile, weights, 0)

    def conv_work(first, count):
        def one(t, carry):
            cols = columns(t)
            shift = jnp.zeros((1, tile), F32)
            taps = [jnp.zeros((1, tile), F32) for _ in range(TAPS)]
            for c in range(seqs):
                tok = slice(c * ctx, (c + 1) * ctx)
                weight = xp[columns(t)]
                back = dot(pg[tok, : weight.shape[1]], weight, across)
                own = range(c * ctx // GROUP, (c + 1) * ctx // GROUP)
                grad = jnp.concatenate([dy[at, :, cols] for at in own], 0) + back
                grad = grad * slope[tok, cols].astype(F32)
                cg[c, :ctx, cols] = grad
                before = lead[c, :, cols].astype(F32)
                shift = shift + jnp.sum(grad, 0, keepdims=True)
                for k in range(TAPS):
                    at = GROUP - TAPS + 1 + k
                    taps[k] = taps[k] + jnp.sum(grad * before[at : at + ctx], 0, keepdims=True)
            for k in range(TAPS):
                rest[k : k + 1, cols] = taps[k]
            rest[TAPS + state : TAPS + state + 1, cols] = shift
            return carry

        lax.fori_loop(first, first + count, one, 0)

    edge = cg.shape[1] - ctx
    H = lambda: pltpu.make_async_remote_copy(
        src_ref=cg.at[:, :edge], dst_ref=cg.at[:, ctx:], send_sem=halo.at[0],
        recv_sem=halo.at[1], device_id=down, device_id_type=MESH,
    )

    def halo_send():
        pl.when(s > 0)(lambda: H().start())

    def stream_work():
        pl.when(s < span - 1)(lambda: H().wait_recv())

        def one(t, carry):
            cols = columns(t)
            for c in range(seqs):
                total = 0.0
                for k in range(TAPS):
                    at = TAPS - 1 - k
                    total = total + small[k : k + 1, cols] * cg[c, at : at + ctx, cols]
                half = pl.ds(pl.multiple_of(lax.rem(t, 2) * tile, tile), tile)
                mixed[parts + t // 2, c * ctx : (c + 1) * ctx, half] = total.astype(BF16)
            return carry

        lax.fori_loop(0, inner // tile, one, 0)
        pl.when(s > 0)(lambda: H().wait_send())

    def norm_work(first, count):
        def one(k, carry):
            in_copy(k).wait()
            ng[...] += dot(mixed[k], in_w[lax.rem(k, 2)], across)

            @pl.when(k + 2 < 2 * parts)
            def _():
                in_copy(k + 2).start()

            return carry

        if first == 0:
            ng[...] = jnp.zeros(ng.shape, F32)
        lax.fori_loop(first, first + count, one, 0)

    def input_work():
        share = width // 4
        at = TAPS + state + 3
        gain = jnp.concatenate(
            [small[at : at + 1, j * CHUNK : j * CHUNK + share] for j in range(4)], 1
        )

        def one(r, total):
            tok = pl.ds(pl.multiple_of(r * GROUP, GROUP), GROUP)
            xs = x[tok].astype(F32)
            inverse = lax.rsqrt(jnp.mean(xs * xs, -1, keepdims=True) + EPS)
            grad = ng[tok]
            scaled = grad * gain
            slope = jnp.mean(scaled * xs, -1, keepdims=True)
            out = inverse * scaled - xs * (inverse * inverse * inverse * slope)
            input_grad[tok] = (out + og[tok].astype(F32)).astype(BF16)
            return total + grad * (xs * inverse)

        total = lax.fori_loop(0, rows // GROUP, one, jnp.zeros((GROUP, width), F32))
        total = jnp.sum(total, 0, keepdims=True)
        for j in range(4):
            rest[at : at + 1, j * CHUNK : j * CHUNK + share] = total[:, j * share : (j + 1) * share]

    blocks = seqs * parts
    tiles = inner // tile
    pause = 3
    held_back = out_chunks + parts
    base = 1 + 2 * SLACK + 1

    def prepare():
        for ref in (cacc, bacc, logs, sums, rest):
            ref[...] = jnp.zeros(ref.shape, F32)
        for one in loads[2:]:
            one.wait()

    def blocks_work(i):
        pl.when(i == 0)(prepare)
        pl.when(i < blocks)(lambda: back_block(i))

    def late_work(i):
        at = held_back

        @pl.when(i == at)
        def _():
            proj_work()
            conv_work(0, tiles)
            halo_send()
            in_copy(0).start()
            in_copy(1).start()

        pl.when(i == at + 1)(weight_work)
        pl.when(i == at + 2)(stream_work)
        pl.when(i == at + 4)(lambda: norm_work(0, parts))
        pl.when(i == at + 5)(lambda: norm_work(parts, parts))
        pl.when(i == at + 6)(input_work)

    def step(i, carry):
        def at(offset):
            k = i - offset
            return jnp.where(k < held_back, k, jnp.where(k < held_back + pause, -1, k - pause))

        @pl.when(i == out_chunks)
        def _():
            for one in loads[:2]:
                one.wait()

        stage(at(0), produce)
        stage(at(1), first_sum)
        stage(at(1 + SLACK), second_sum)
        stage(at(1 + 2 * SLACK), third_sum)
        pl.when(s != root)(lambda: stage(at(base + SLACK * spot), inward))
        pl.when(s == root)(lambda: stage(at(base + SLACK * most), at_root))
        pl.when(s != root)(lambda: stage(at(base + SLACK * most + SLACK * far), outward))
        blocks_work(i)
        late_work(i)
        return carry

    lax.fori_loop(0, chunks + pause + base + 2 * SLACK * most + 1, step, 0)

    def finish(c, carry):
        pl.when(c >= chunks - slots)(lambda: A(c).wait_send())
        for t in (X0, X1, X2, Y0, Y1, Y2):
            t(c).wait_send()
        pl.when(below)(lambda: ZU(c).wait_send())
        pl.when(above)(lambda: ZD(c).wait_send())
        if root > 0:
            pl.when((s <= root) & (s > 0))(lambda: TD(c).wait_send())
        if span - 1 > root:
            pl.when((s >= root) & (s < span - 1))(lambda: TU(c).wait_send())
        D(c).wait_send()
        D(c).wait_recv()
        return carry

    lax.fori_loop(0, chunks, finish, 0)
    copies = []
    for c in range(chunks):
        for h in range(2):
            if c < out_chunks:
                r, col = c // (width // CHUNK), c % (width // CHUNK)
                first = h * (inner // 8) + r * HR
                to = out_sum.at[first : first + HR, col * CHUNK : (col + 1) * CHUNK]
            elif c < last:
                col = (c - out_chunks + parts) % (2 * parts)
                to = in_sum.at[h * HR : (h + 1) * HR, col * CHUNK : (col + 1) * CHUNK]
            else:
                to = rest_sum.at[h * HR : (h + 1) * HR]
            copies.append(pltpu.make_async_copy(tot.at[c, h], to, local.at[c, h]))
    for one in copies:
        one.start()
    for one in copies:
        one.wait()


def back(gated, bg, step_low, final, bbd, small, x, og, far):
    rows, inner = gated.shape
    width = x.shape[1]
    seqs, state = final.shape[:2]
    ctx, rank, parts = rows // seqs, step_low.shape[1], inner // CHUNK
    span = lax.axis_size("seq")
    out_chunks, in_chunks = 2 * width // CHUNK, 2 * parts
    n = out_chunks + in_chunks + 1
    ones = jnp.asarray(np.kron(np.eye(GROUP), np.ones((1, state))), BF16)
    vmem, dma = pltpu.VMEM, pltpu.SemaphoreType.DMA
    anywhere = pl.BlockSpec(memory_space=pl.ANY)
    whole = pl.BlockSpec(memory_space=vmem)
    shape = jax.ShapeDtypeStruct
    like = lambda v: vmem(v.shape, v.dtype)
    (held, normed, lead, slope, u, sig, delta, cw, dy, zg, in_full, xp, dt) = far
    return pl.pallas_call(
        functools.partial(back_kernel, span, state, rank),
        in_specs=[whole] * 9 + [anywhere] * len(far),
        out_specs=[whole, anywhere, anywhere, anywhere],
        out_shape=[
            shape((rows, width), BF16),
            shape((inner // 4, width), BF16),
            shape((width // 4, 2 * inner), BF16),
            shape((2 * HR, CHUNK), BF16),
        ],
        scratch_shapes=[
            *map(like, (normed, lead, slope, u, sig, delta, cw, dy)),
            vmem((in_chunks, rows, CHUNK), BF16),
            like(xp),
            like(dt),
            vmem((2, width, CHUNK), BF16),
            vmem((2,) + held.shape[1:], BF16),
            vmem((GROUP, state, CHUNK), BF16),
            vmem((GROUP, state, CHUNK), BF16),
            vmem((rows, inner), BF16),
            vmem((rows, GROUP * state), F32),
            vmem((rows, GROUP * state), F32),
            vmem((state, inner), F32),
            vmem((2, 8, inner), F32),
            vmem((rows, LANES), BF16),
            vmem((seqs, ctx + 8, inner), F32),
            vmem((rows, width), F32),
            vmem((2 * HR, inner), F32),
            vmem((4, 4, 2, HR, CHUNK), BF16),
            vmem((n, 4, HR, CHUNK), BF16),
            vmem((n, 3, HR // 2, CHUNK), BF16),
            vmem((n, 3, HR // 2, CHUNK), BF16),
            vmem((n, HR, CHUNK), BF16),
            vmem((n, HR, CHUNK), BF16),
            vmem((n, 2, HR, CHUNK), BF16),
            dma((12, n)),
            dma((12, n)),
            dma((2,)),
            dma((n, 2)),
            dma((11,)),
            dma((2,)),
            dma((2,)),
        ],
        compiler_params=pltpu.CompilerParams(
            collective_id=1, has_side_effects=True, vmem_limit_bytes=63 << 20
        ),
        name="back",
    )(gated, bg, step_low, final, bbd, ones, small, x, og, *far)


def body(
    hidden_in, lengths, norm_gain, in_weight, conv_weight, conv_bias, xproj_weight,
    dt_weight, dt_bias, a_log, skip_gain, out_weight, out_grad,
):
    seqs, ctx, width = hidden_in.shape
    taps, share = conv_weight.shape
    state = a_log.shape[0]
    rank = dt_weight.shape[0]
    rows = ctx * seqs
    row = lambda v: v.reshape(1, -1)
    x, og = hidden_in.reshape(rows, width), out_grad.reshape(rows, width)
    (
        hidden_out, step_low, final, bbd, held, normed, branch_grad, lead, slope, u, sig, delta,
        c_wide, y_grad, gated, z_grad, in_matrix, proj_matrix, step_matrix, small,
    ) = front(
        x, og, lengths, conv_weight, a_log, row(conv_bias), row(dt_bias), row(skip_gain),
        row(norm_gain), in_weight, out_weight, xproj_weight, dt_weight, seqs,
    )
    far = (
        held, normed, lead, slope, u, sig, delta, c_wide, y_grad, z_grad, in_matrix,
        proj_matrix, step_matrix,
    )
    input_grad, out_sum, in_sum, rest = back(
        gated, branch_grad, step_low, final, bbd, small, x, og, far
    )
    rest = rest.astype(F32)
    shards = lax.axis_size("fsdp")
    at = taps + state
    return (
        hidden_out.reshape(seqs, ctx, width), input_grad.reshape(seqs, ctx, width),
        rest[at + 3, : width // shards], in_sum.astype(F32), rest[:taps], rest[at],
        rest[at + 4 + rank : at + 4 + rank + proj_matrix.shape[1]].T, rest[at + 4 : at + 4 + rank],
        rest[at + 1], rest[taps:at], rest[at + 2], out_sum.astype(F32),
    )


def solution(mesh):
    tokens = P(("dp", "fsdp"), "seq", None)
    return jax.shard_map(
        body,
        mesh=mesh,
        in_specs=(
            tokens, P(("dp", "fsdp")), P("fsdp"), P("fsdp", None), P(None, "fsdp"), P("fsdp"),
            P("fsdp", None), P(None, "fsdp"), P("fsdp"), P(None, "fsdp"), P("fsdp"),
            P("fsdp", None), tokens,
        ),
        out_specs=(
            tokens, tokens, P("fsdp"), P("fsdp", None), P(None, "fsdp"), P("fsdp"),
            P("fsdp", None), P(None, "fsdp"), P("fsdp"), P(None, "fsdp"), P("fsdp"),
            P("fsdp", None),
        ),
        check_vma=False,
    )
```

```python
import functools
import math

import jax
import jax.numpy as jnp
import numpy as np
from jax import lax
from jax.experimental import pallas as pl
from jax.experimental.pallas import tpu as pltpu
from jax.sharding import PartitionSpec as P

EPS = 1e-05
LOG2E = math.log2(math.e)
LANES = 128
GROUP = 16
F32 = jnp.float32
BF16 = jnp.bfloat16
MESH = pl.DeviceIdType.MESH
HR = 128
CHUNK = 512
SLACK = 1
TAPS = 4


def silu_parts(v):
    s = jax.nn.sigmoid(v)
    return v * s, s * (1.0 + v * (1.0 - s))


def rows_sum(stack, value, rising):
    row = lax.broadcasted_iota(jnp.int32, value.shape, 0)
    level = 0
    while stack and stack[-1][0] == level:
        _, other = stack.pop()
        first, second = (other, value) if rising else (value, other)
        low = (row & (1 << level)) == 0
        turned = pltpu.roll(jnp.where(low, second, first), 1 << level, 0)
        value = jnp.where(low, first, second) + turned
        level += 1
    stack.append((level, value))


def front_kernel(
    span,
    x, og, lengths, taps_own, log_own, cbias_own, dbias_own, skip_own, gain_own,
    in_own, out_own, xp_own, dt_own,
    hidden_out, step_low, final,
    held_all, normed_full, bg_full, lead_full, slope_full, u_full, sig_full, delta_full, bw_full,
    cw_full, dy_full, gated_full, zg_full, in_full, xp_full, dt_full, small_full,
    in_w, out_w, xp, dt, small, small_own, hx, acc, zacc, normed, v, proj, ends, sums,
    ends_in, sums_in, bg, mask, lead, slope, u, sig, delta, bw, cw, gg, dy, y, gated, zg,
    start, held,
    send, recv, halo, relay_send, relay_recv, sums_send, sums_recv, local, keep, held_sem,
):
    d, s, f = (lax.axis_index(a) for a in ("dp", "seq", "fsdp"))
    fx, fy, fd = f ^ 1, f ^ 2, f ^ 3
    tox, toy, sib = {"fsdp": fx}, {"fsdp": fy}, {"dp": 1 - d}
    rows, width = x.shape
    inner = u.shape[1]
    seqs = bw.shape[0]
    ctx = rows // seqs
    state, rank = log_own.shape[0], dt_own.shape[0]
    groups = ctx // GROUP
    share = inner // 4
    at_state, at_bias = TAPS, TAPS + state
    across = (((1,), (1,)), ((), ()))
    dot = lambda a, b, dims=(((1,), (0,)), ((), ())): lax.dot_general(
        a, b, dims, preferred_element_type=F32
    )

    for c in range(seqs):
        hx[c] = jnp.zeros((GROUP, width), BF16)
    barrier = pltpu.get_barrier_semaphore()
    for who in (tox, toy, sib):
        pl.semaphore_signal(barrier, inc=1, device_id=who, device_id_type=MESH)

    def greet(o, carry):
        who = {"seq": lax.rem(s + o, span)}
        pl.semaphore_signal(barrier, inc=1, device_id=who, device_id_type=MESH)
        return carry

    lax.fori_loop(1, span, greet, 0)
    small_own[...] = jnp.zeros(small_own.shape, F32)
    small_own[:TAPS] = taps_own[...]
    small_own[at_state:at_bias] = log_own[...]
    small_own[at_bias : at_bias + 1] = cbias_own[...]
    small_own[at_bias + 1 : at_bias + 2] = dbias_own[...]
    small_own[at_bias + 2 : at_bias + 3] = skip_own[...]
    small_own[at_bias + 3 : at_bias + 4, : width // 4] = gain_own[...]
    pl.semaphore_wait(barrier, 2 + span)

    SMALL, STREAM, PROJ, STEP, GATE, OUT = range(6)
    plan = (
        (small_own, small, 1, None),
        (in_own, in_w, 0, (0, inner)),
        (xp_own, xp, 0, None),
        (dt_own, dt, 1, None),
        (in_own, in_w, 0, (inner, 2 * inner)),
        (out_own, out_w, 0, None),
    )

    def window(p, owner, half, q):
        src, dst, dim, cols = plan[p]
        high, wide = src.shape
        part = high // 4
        at = (half * 2 + q) * part
        lo, hi = cols or (0, wide)
        if dim == 0:
            return dst.at[pl.ds(pl.multiple_of(owner * high + at, part), part), lo:hi]
        col = pl.ds(pl.multiple_of(owner * wide, wide), wide)
        return dst.at[pl.ds(pl.multiple_of(at, part), part), col]

    def own(p, half, q):
        src, _, _, cols = plan[p]
        high, wide = src.shape
        part = high // 4
        lo, hi = cols or (0, wide)
        return src.at[pl.ds(pl.multiple_of((half * 2 + q) * part, part), part), lo:hi]

    def copy(src, dst, p, kind, who):
        return pltpu.make_async_remote_copy(
            src_ref=src, dst_ref=dst, send_sem=send.at[p, kind], recv_sem=recv.at[p, kind],
            device_id=who, device_id_type=MESH,
        )

    started = []

    def go(one):
        one.start()
        started.append(one)

    def start_own(p):
        for q in (0, 1):
            go(copy(own(p, d, q), window(p, f, d, q), p, q, tox))
            go(copy(own(p, d, 1 - q), window(p, f, d, 1 - q), p, 3 - q, toy))

    def place_own(p):
        for half in (0, 1):
            for q in (0, 1):
                pltpu.make_async_copy(
                    own(p, half, q), window(p, f, half, q), local.at[p, half * 2 + q]
                ).start()

    def own_ready(p):
        for half in (0, 1):
            for q in (0, 1):
                pltpu.make_async_copy(
                    own(p, half, q), window(p, f, half, q), local.at[p, half * 2 + q]
                ).wait()

    def arrived(p, kind, owner, half, q):
        w = window(p, owner, half, q)
        copy(w, w, p, kind, sib).wait_recv()
        return w

    near = ((0, fx, 0), (3, fy, 1), (1, fx, 1), (2, fy, 0))
    diagonal = ((4, fd, 0), (5, fd, 1))

    def serve_near(p):
        for kind, owner, q in near:
            w = arrived(p, kind, owner, d, q)
            if kind == 0:
                go(copy(w, w, p, 4, toy))
            if kind == 3:
                go(copy(w, w, p, 5, tox))
            go(copy(w, w, p, 6 + kind, sib))

    def serve_far(p):
        for kind, owner, q in diagonal:
            w = arrived(p, kind, owner, d, q)
            go(copy(w, w, p, 6 + kind, sib))

    def near_ready(p):
        for kind, owner, q in near:
            arrived(p, 6 + kind, owner, 1 - d, q)

    def far_ready(p):
        for kind, owner, q in diagonal:
            arrived(p, 6 + kind, owner, 1 - d, q)

    for p in (SMALL, STREAM, PROJ, STEP):
        start_own(p)
    for p in range(6):
        place_own(p)
    def edges(c):
        return pltpu.make_async_remote_copy(
            src_ref=x.at[(c + 1) * ctx - GROUP : (c + 1) * ctx], dst_ref=hx.at[c],
            send_sem=halo.at[0, c], recv_sem=halo.at[1, c],
            device_id={"seq": jnp.minimum(s + 1, span - 1)}, device_id_type=MESH,
        )

    @pl.when(s < span - 1)
    def _():
        for c in range(seqs):
            edges(c).start()

    for c in range(seqs):
        t = s * ctx + lax.broadcasted_iota(jnp.int32, (ctx, LANES), 0)
        mask[c * ctx : (c + 1) * ctx] = (t < lengths[c]).astype(F32)

    def mask_step(r, carry):
        tok = pl.ds(pl.multiple_of(r * GROUP, GROUP), GROUP)
        held = jnp.concatenate([mask[tok]] * (width // LANES), 1)
        bg[tok] = (og[tok].astype(F32) * held).astype(BF16)
        return carry

    lax.fori_loop(0, rows // GROUP, mask_step, 0)

    serve_near(SMALL)
    serve_far(SMALL)
    near_ready(SMALL)
    far_ready(SMALL)
    own_ready(SMALL)

    @pl.when(s > 0)
    def _():
        for c in range(seqs):
            edges(c).wait_recv()

    gain_at = at_bias + 3
    gain = jnp.concatenate(
        [small[gain_at : gain_at + 1, j * share : j * share + width // 4] for j in range(4)], 1
    )

    def normalised(v):
        v = v.astype(F32)
        inverse = lax.rsqrt(jnp.mean(v * v, -1, keepdims=True) + EPS)
        return (v * inverse * gain).astype(BF16)

    def norm_step(r, carry):
        tok = pl.ds(pl.multiple_of(r * GROUP, GROUP), GROUP)
        normed[tok] = normalised(x[tok])
        return carry

    lax.fori_loop(0, rows // GROUP, norm_step, 0)
    for c in range(seqs):
        normed[rows + c * GROUP : rows + (c + 1) * GROUP] = normalised(hx[c])

    def project(total, high, first, owner, fresh):
        shard = pl.ds(pl.multiple_of(owner * (width // 4), width // 4), width // 4)
        left = normed[:high, shard]

        def one(t, carry):
            cols = pl.ds(pl.multiple_of(t * CHUNK, CHUNK), CHUNK)
            right = in_w[shard, pl.ds(pl.multiple_of(first + t * CHUNK, CHUNK), CHUNK)]
            part = dot(left, right)
            total[:, cols] = part if fresh else total[:, cols] + part
            return carry

        lax.fori_loop(0, inner // CHUNK, one, 0)

    tall = rows + seqs * GROUP
    own_ready(STREAM)
    project(acc, tall, 0, f, True)
    serve_near(STREAM)
    start_own(GATE)
    start_own(OUT)
    near_ready(STREAM)
    project(acc, tall, 0, fx, False)
    project(acc, tall, 0, fy, False)
    serve_far(STREAM)
    for p in (PROJ, STEP):
        serve_near(p)
        serve_far(p)
    far_ready(STREAM)
    project(acc, tall, 0, fd, False)

    tile = 2 * LANES

    def columns(t, size=tile):
        return pl.ds(pl.multiple_of(t * size, size), size)

    def conv_step(t, carry):
        cols = columns(t)
        for c in range(seqs):
            before = acc[rows + c * GROUP : rows + (c + 1) * GROUP, cols].astype(BF16)
            stream = acc[c * ctx : (c + 1) * ctx, cols].astype(BF16)
            lead[c, :GROUP, cols] = before
            lead[c, GROUP:, cols] = stream
            held = jnp.concatenate([before, stream], 0).astype(F32)
            total = small[at_bias : at_bias + 1, cols]
            for k in range(TAPS):
                at = GROUP - TAPS + 1 + k
                total = total + small[k : k + 1, cols] * held[at : at + ctx]
            value, grad = silu_parts(total)
            slope[c * ctx : (c + 1) * ctx, cols] = grad.astype(BF16)
            u[c * ctx : (c + 1) * ctx, cols] = value.astype(BF16)
        return carry

    lax.fori_loop(0, inner // tile, conv_step, 0)
    for p in (PROJ, STEP):
        near_ready(p)
        far_ready(p)
        own_ready(p)
    proj[...] = dot(u[...], xp[...])
    step_low[...] = proj[:, :rank].astype(BF16)

    def wide_step(i, carry):
        tok = pl.ds(pl.multiple_of(i * GROUP, GROUP), GROUP)
        held = proj[tok]
        for ref, first in ((bw, rank), (cw, rank + state)):
            value = held[:, first : first + state]
            c, at = i // groups, lax.rem(i, groups)
            ref[c, pl.ds(pl.multiple_of(at * GROUP, GROUP), GROUP)] = jnp.broadcast_to(
                value[:, :, None], (GROUP, state, LANES)
            )
        return carry

    lax.fori_loop(0, rows // GROUP, wide_step, 0)
    def delta_step(t, carry):
        cols = columns(t)
        for c in range(seqs):
            tok = slice(c * ctx, (c + 1) * ctx)
            value = dot(step_low[tok], dt[:, cols]) + small[at_bias + 1 : at_bias + 2, cols]
            sig[tok, cols] = jax.nn.sigmoid(value).astype(BF16)
            value = jnp.maximum(value, 0.0) + jnp.log1p(jnp.exp(-jnp.abs(value)))
            for i in range(groups):
                delta[c * groups + i, :, cols] = value[i * GROUP : (i + 1) * GROUP]
            sums[c : c + 1, cols] = jnp.sum(value, 0, keepdims=True)
            value = value * u[tok, cols].astype(F32)
            for i in range(groups):
                v[c * groups + i, :, cols] = value[i * GROUP : (i + 1) * GROUP]
        return carry

    sums[...] = jnp.zeros(sums.shape, F32)
    lax.fori_loop(0, inner // tile, delta_step, 0)

    def sums_copy(j):
        return pltpu.make_async_remote_copy(
            src_ref=sums, dst_ref=sums_in.at[s], send_sem=sums_send.at[j],
            recv_sem=sums_recv.at[s], device_id={"seq": j}, device_id_type=MESH,
        )

    def sums_start(o, carry):
        sums_copy(lax.rem(s + o, span)).start()
        return carry

    lax.fori_loop(1, span, sums_start, 0)

    def ends_copy(j, way, c):
        return pltpu.make_async_remote_copy(
            src_ref=ends.at[way, c], dst_ref=ends_in.at[s, c], send_sem=relay_send.at[j, c],
            recv_sem=relay_recv.at[s, c], device_id={"seq": j}, device_id_type=MESH,
        )

    def ends_start(first, count, way, c):
        def one(j, carry):
            ends_copy(j, way, c).start()
            return carry

        lax.fori_loop(first, count, one, 0)

    def forward_ends(c):
        for j in range(0, inner, CHUNK):
            cuts = [slice(j + i, j + i + LANES) for i in range(0, CHUNK, LANES)]
            rates = [-jnp.exp(small[at_state:at_bias, cut]) * LOG2E for cut in cuts]

            def one(i, h):
                h = list(h)
                for k in range(GROUP):
                    b = bw[c, i * GROUP + k]
                    for n, cut in enumerate(cuts):
                        step = delta[c * groups + i, k : k + 1, cut]
                        factor = jnp.exp2(jnp.broadcast_to(step, (state, LANES)) * rates[n])
                        row = jnp.broadcast_to(v[c * groups + i, k : k + 1, cut], (state, LANES))
                        h[n] = factor * h[n] + row * b
                return tuple(h)

            zero = tuple(jnp.zeros((state, LANES), F32) for _ in cuts)
            h = lax.fori_loop(0, groups, one, zero)
            for n, cut in enumerate(cuts):
                ends[0, c, :, cut] = h[n].astype(BF16)

    def backward_ends(c):
        for j in range(0, inner, CHUNK):
            cuts = [slice(j + i, j + i + LANES) for i in range(0, CHUNK, LANES)]
            rates = [-jnp.exp(small[at_state:at_bias, cut]) * LOG2E for cut in cuts]

            def one(i, carry):
                run, p = (list(value) for value in carry)
                for k in range(GROUP):
                    read = cw[c, i * GROUP + k]
                    for n, cut in enumerate(cuts):
                        step = delta[c * groups + i, k : k + 1, cut]
                        factor = jnp.exp2(jnp.broadcast_to(step, (state, LANES)) * rates[n])
                        row = dy[c * groups + i, k : k + 1, cut]
                        run[n] = run[n] * factor
                        p[n] = p[n] + run[n] * (read * jnp.broadcast_to(row, (state, LANES)))
                return tuple(run), tuple(p)

            one_s = tuple(jnp.ones((state, LANES), F32) for _ in cuts)
            zero = tuple(jnp.zeros((state, LANES), F32) for _ in cuts)
            _, p = lax.fori_loop(0, groups, one, (one_s, zero))
            for n, cut in enumerate(cuts):
                ends[1, c, :, cut] = p[n].astype(BF16)

    def stash(*pairs):
        for at, (src, dst) in pairs:
            one = pltpu.make_async_copy(src, dst, keep.at[at])
            one.start()
            kept.append(one)

    kept = []
    stash(
        (0, (normed.at[:rows], normed_full)), (1, (bg, bg_full)), (2, (lead, lead_full)),
        (3, (slope, slope_full)), (4, (u, u_full)), (5, (sig, sig_full)), (6, (delta, delta_full)),
        (7, (cw, cw_full)), (8, (xp, xp_full)), (9, (dt, dt_full)), (10, (small, small_full)),
        (15, (bw, bw_full)),
    )

    def ends_wait(j, c):
        pltpu.make_async_remote_copy(
            src_ref=ends.at[0, c], dst_ref=ends_in.at[j, c], send_sem=relay_send.at[j, c],
            recv_sem=relay_recv.at[j, c], device_id={"seq": j}, device_id_type=MESH,
        ).wait_recv()

    def join(ref, j, c):
        ends_wait(j, c)

        def one(t, carry):
            cols = columns(t, CHUNK)
            rates = -jnp.exp(small[at_state:at_bias, cols]) * LOG2E
            decay = jnp.exp2(sums_in[j, c : c + 1, cols] * rates)
            ref[c, :, cols] = decay * ref[c, :, cols] + ends_in[j, c, :, cols].astype(F32)
            return carry

        lax.fori_loop(0, inner // CHUNK, one, 0)

    def join_start(j, carry):
        for c in range(seqs):
            join(start, j, c)
        return carry

    def join_final(o, carry):
        for c in range(seqs):
            join(final, span - 1 - o, c)
        return carry

    def sums_wait(o, carry):
        j = lax.rem(s + o, span)
        pltpu.make_async_remote_copy(
            src_ref=sums, dst_ref=sums_in.at[j], send_sem=sums_send.at[j],
            recv_sem=sums_recv.at[j], device_id={"seq": j}, device_id_type=MESH,
        ).wait_recv()
        return carry

    parts = inner // CHUNK
    blocks = seqs * parts

    def held_copy(b):
        slot = lax.rem(b, 2)
        return pltpu.make_async_copy(held.at[slot], held_all.at[b], held_sem.at[slot])

    def sweep_block(b, carry):
        c, slot = b // parts, lax.rem(b, 2)
        first = lax.rem(b, parts) * CHUNK
        cuts = [pl.ds(pl.multiple_of(first + n, LANES), LANES) for n in range(0, CHUNK, LANES)]
        tiles = [slice(n, n + LANES) for n in range(0, CHUNK, LANES)]
        all_cols = pl.ds(pl.multiple_of(first, CHUNK), CHUNK)
        rates = [-jnp.exp(small[at_state:at_bias, cut]) * LOG2E for cut in cuts]
        skip = small[at_bias + 2 : at_bias + 3, all_cols]

        @pl.when(b >= 2)
        def _():
            held_copy(b - 2).wait()

        h = tuple(start[c, :, cut] for cut in cuts)
        for n, cut in enumerate(tiles):
            held[slot, 0, :, cut] = h[n].astype(BF16)

        def one(i, h):
            h = list(h)
            g = c * groups + i
            for first_row in range(0, GROUP, 8):
                stacks = [[] for _ in cuts]
                for k in range(first_row, first_row + 8):
                    b_in, read = bw[c, i * GROUP + k], cw[c, i * GROUP + k]
                    for n, cut in enumerate(cuts):
                        step = jnp.broadcast_to(delta[g, k : k + 1, cut], (state, LANES))
                        row = jnp.broadcast_to(v[g, k : k + 1, cut], (state, LANES))
                        h[n] = jnp.exp2(step * rates[n]) * h[n] + row * b_in
                        held[slot, i * GROUP + k + 1, :, tiles[n]] = h[n].astype(BF16)
                        part = h[n] * read
                        rows_sum(stacks[n], part[:8] + part[8:], True)
                for n, cut in enumerate(cuts):
                    y[g, first_row : first_row + 8, cut] = stacks[n][0][1]
            tok = pl.ds(pl.multiple_of(g * GROUP, GROUP), GROUP)
            y[g, :, all_cols] += skip * u[tok, all_cols].astype(F32)
            return tuple(h)

        lax.fori_loop(0, groups, one, h)
        held_copy(b).start()
        return carry

    def grad_part(owner):
        shard = pl.ds(pl.multiple_of(owner * share, share), share)
        gg[:, shard] = dot(bg[...], out_w[shard], across)

    forward_ends(0)
    ends_start(s + 1, span, 0, 0)
    serve_near(GATE)
    own_ready(GATE)
    forward_ends(1)
    ends_start(s + 1, span, 0, 1)
    near_ready(GATE)
    for owner, fresh in ((f, True), (fx, False), (fy, False)):
        project(zacc, rows, inner, owner, fresh)
    lax.fori_loop(1, span, sums_wait, 0)
    start[...] = jnp.zeros(start.shape, F32)
    lax.fori_loop(0, s, join_start, 0)
    lax.fori_loop(0, 2, sweep_block, 0)
    serve_far(GATE)
    lax.fori_loop(2, 4, sweep_block, 0)
    serve_near(OUT)
    far_ready(GATE)
    project(zacc, rows, inner, fd, False)
    lax.fori_loop(4, blocks - 1, sweep_block, 0)
    serve_far(OUT)
    stash((11, (in_w, in_full)))
    lax.fori_loop(blocks - 1, blocks, sweep_block, 0)
    own_ready(OUT)
    near_ready(OUT)
    for owner in (f, fx, fy):
        grad_part(owner)
    far_ready(OUT)
    grad_part(fd)

    def gate_step(t, carry):
        cols = columns(t)
        for c in range(seqs):
            tok = slice(c * ctx, (c + 1) * ctx)
            value, grad = silu_parts(zacc[tok, cols].astype(BF16).astype(F32))
            back = gg[tok, cols]
            pieces = [y[c * groups + i, :, cols] for i in range(groups)]
            scanned = jnp.concatenate(pieces, 0)
            gated[tok, cols] = (scanned * value).astype(BF16)
            half = pl.ds(pl.multiple_of(lax.rem(t, 2) * tile, tile), tile)
            zg[t // 2, tok, half] = (back * scanned * grad).astype(BF16)
            value = back * value
            for i in range(groups):
                dy[c * groups + i, :, cols] = value[i * GROUP : (i + 1) * GROUP]
        return carry

    lax.fori_loop(0, inner // tile, gate_step, 0)
    stash((12, (dy, dy_full)), (13, (gated, gated_full)), (14, (zg, zg_full)))
    for c in range(seqs):
        backward_ends(c)
        ends_start(0, s, 1, c)

    def hidden_step(t, carry):
        cols = columns(t)
        keep_rows = jnp.concatenate([mask[...]] * (tile // LANES), 1)
        branch = dot(gated[...], out_w[:, cols])
        hidden_out[:, cols] = (x[:, cols].astype(F32) + keep_rows * branch).astype(BF16)
        return carry

    lax.fori_loop(0, width // tile, hidden_step, 0)
    final[...] = jnp.zeros(final.shape, F32)
    lax.fori_loop(0, span - 1 - s, join_final, 0)

    for one in started:
        one.wait_send()

    @pl.when(s < span - 1)
    def _():
        for c in range(seqs):
            edges(c).wait_send()

    def sent(o, carry):
        j = lax.rem(s + o, span)
        sums_copy(j).wait_send()
        for c in range(seqs):
            ends_copy(j, 0, c).wait_send()
        return carry

    lax.fori_loop(1, span, sent, 0)
    for one in kept:
        one.wait()
    for b in range(max(blocks - 2, 0), blocks):
        held_copy(b).wait()


def front(x, og, lengths, taps, logs, cbias, dbias, skip, gain, in_own, out_own, xp_own, dt_own, seqs):
    rows, width = x.shape
    share, inner = taps.shape[1], 4 * taps.shape[1]
    state, rank, used = logs.shape[0], dt_own.shape[0], xp_own.shape[1]
    ctx = rows // seqs
    span = lax.axis_size("seq")
    parts = inner // CHUNK
    vmem, dma = pltpu.VMEM, pltpu.SemaphoreType.DMA
    whole, anywhere = pl.BlockSpec(memory_space=vmem), pl.BlockSpec(memory_space=pl.ANY)
    shape = jax.ShapeDtypeStruct
    grouped = (rows // GROUP, GROUP, inner)
    kept = [
        ((rows, width), BF16),
        ((rows, width), BF16),
        ((seqs, ctx + GROUP, inner), BF16),
        ((rows, inner), BF16),
        ((rows, inner), BF16),
        ((rows, inner), BF16),
        (grouped, F32),
        ((seqs, ctx, state, LANES), F32),
        ((seqs, ctx, state, LANES), F32),
        (grouped, F32),
        ((rows, inner), BF16),
        ((parts, rows, CHUNK), BF16),
        ((width, 2 * inner), BF16),
        ((inner, used), BF16),
        ((rank, inner), BF16),
        ((32, inner), F32),
    ]
    held = (ctx + 1, state, CHUNK)
    return pl.pallas_call(
        functools.partial(front_kernel, span),
        in_specs=[whole, whole, pl.BlockSpec(memory_space=pltpu.SMEM)]
        + [whole] * 6
        + [anywhere] * 4,
        out_specs=[whole] * 3 + [anywhere] * (1 + len(kept)),
        out_shape=[
            shape((rows, width), BF16),
            shape((rows, rank), BF16),
            shape((seqs, state, inner), F32),
            shape((seqs * parts,) + held, BF16),
        ]
        + [shape(*k) for k in kept],
        scratch_shapes=[
            vmem((width, 2 * inner), BF16),
            vmem((inner, width), BF16),
            vmem((inner, used), BF16),
            vmem((rank, inner), BF16),
            vmem((32, inner), F32),
            vmem((32, share), F32),
            vmem((seqs, GROUP, width), BF16),
            vmem((rows + seqs * GROUP, inner), F32),
            vmem((rows, inner), F32),
            vmem((rows + seqs * GROUP, width), BF16),
            vmem(grouped, F32),
            vmem((rows, used), F32),
            vmem((2, seqs, state, inner), BF16),
            vmem((8, inner), F32),
            vmem((span, seqs, state, inner), BF16),
            vmem((span, 8, inner), F32),
            vmem((rows, width), BF16),
            vmem((rows, LANES), F32),
            vmem((seqs, ctx + GROUP, inner), BF16),
            vmem((rows, inner), BF16),
            vmem((rows, inner), BF16),
            vmem((rows, inner), BF16),
            vmem(grouped, F32),
            vmem((seqs, ctx, state, LANES), F32),
            vmem((seqs, ctx, state, LANES), F32),
            vmem((rows, inner), F32),
            vmem(grouped, F32),
            vmem(grouped, F32),
            vmem((rows, inner), BF16),
            vmem((parts, rows, CHUNK), BF16),
            vmem((seqs, state, inner), F32),
            vmem((2,) + held, BF16),
            dma((6, 12)),
            dma((6, 12)),
            dma((2, seqs)),
            dma((span, seqs)),
            dma((span, seqs)),
            dma((span,)),
            dma((span,)),
            dma((6, 4)),
            dma((len(kept),)),
            dma((2,)),
        ],
        compiler_params=pltpu.CompilerParams(
            collective_id=0, has_side_effects=True, vmem_limit_bytes=63 << 20
        ),
        name="front",
    )(x, og, lengths, taps, logs, cbias, dbias, skip, gain, in_own, out_own, xp_own, dt_own)


def back_kernel(
    span, state, rank,
    gated, bg, step_low, final, small, x, og,
    held_all, normed_full, lead_full, slope_full, u_full, sig_full, delta_full, bw_full,
    cw_full, dy_full, zg_full, in_full, xp_full, dt_full,
    input_grad, out_sum, in_sum, rest_sum,
    normed, lead, slope, u, sig, delta, bw, cw, dy, mixed, xp, dt, in_w, held, v, rl, cacc,
    bacc, logs, sums,
    pg, pg_full, cg, ng, rest, g, ra, rx, ry, zlo, zhi, tot,
    send, recv, halo, local, load, held_sem, in_sem,
):
    d, s, f = (lax.axis_index(a) for a in ("dp", "seq", "fsdp"))
    fx, fy, fd = f ^ 1, f ^ 2, f ^ 3
    chunks = tot.shape[0]
    rows, width = x.shape
    inner = gated.shape[1]
    seqs = cg.shape[0]
    ctx = rows // seqs
    parts = inner // CHUNK
    out_chunks = 2 * width // CHUNK
    in_chunks = 2 * parts
    last = out_chunks + in_chunks
    slots = g.shape[0]
    q = HR // 2
    root = (span - 1) // 2
    tox, toy, sib = {"fsdp": fx}, {"fsdp": fy}, {"dp": 1 - d}
    up, down = {"seq": jnp.minimum(s + 1, span - 1)}, {"seq": jnp.maximum(s - 1, 0)}
    contract = (((0,), (0,)), ((), ()))
    across = (((1,), (1,)), ((), ()))
    dot = lambda a, b, dims=(((1,), (0,)), ((), ())): lax.dot_general(
        a, b, dims, preferred_element_type=F32
    )

    loads = (
        (mixed.at[:parts], zg_full), (normed, normed_full), (delta, delta_full), (dy, dy_full),
        (u, u_full), (cw, cw_full), (bw, bw_full), (sig, sig_full), (slope, slope_full),
        (lead, lead_full), (xp, xp_full), (dt, dt_full),
    )
    loads = [pltpu.make_async_copy(src, dst, load.at[n]) for n, (dst, src) in enumerate(loads)]

    def held_copy(b):
        slot = lax.rem(b, 2)
        return pltpu.make_async_copy(held_all.at[b], held.at[slot], held_sem.at[slot])

    def in_copy(k):
        slot = lax.rem(k, 2)
        first = pl.multiple_of(lax.rem(k + parts, 2 * parts) * CHUNK, CHUNK)
        return pltpu.make_async_copy(in_full.at[:, pl.ds(first, CHUNK)], in_w.at[slot], in_sem.at[slot])

    held_copy(0).start()
    for one in loads[2:7]:
        one.start()
    held_copy(1).start()
    for one in loads[:2] + loads[7:]:
        one.start()
    cg[:, ctx:] = jnp.zeros((seqs, cg.shape[1] - ctx, inner), F32)
    barrier = pltpu.get_barrier_semaphore()
    for who in (tox, toy, sib):
        pl.semaphore_signal(barrier, inc=1, device_id=who, device_id_type=MESH)

    @pl.when(s > 0)
    def _():
        pl.semaphore_signal(barrier, inc=1, device_id=down, device_id_type=MESH)

    @pl.when(s < span - 1)
    def _():
        pl.semaphore_signal(barrier, inc=1, device_id=up, device_id_type=MESH)

    ends = (s == 0) | (s == span - 1)
    pl.semaphore_wait(barrier, jnp.where(ends, 4, 5) if span > 1 else 3)

    def copy(kind, c, src, dst, who):
        return pltpu.make_async_remote_copy(
            src_ref=src, dst_ref=dst, send_sem=send.at[kind, c], recv_sem=recv.at[kind, c],
            device_id=who, device_id_type=MESH,
        )

    lo, hi = slice(0, q), slice(q, HR)
    A = lambda c: copy(0, c, g.at[lax.rem(c, slots), :, 1 - d], ra.at[c], sib)
    X0 = lambda c: copy(1, c, ra.at[c, fd, lo], rx.at[c, 0], tox)
    X1 = lambda c: copy(2, c, ra.at[c, fx, lo], rx.at[c, 1], tox)
    X2 = lambda c: copy(3, c, ra.at[c, fx, hi], rx.at[c, 2], tox)
    Y0 = lambda c: copy(4, c, ra.at[c, fd, hi], ry.at[c, 0], toy)
    Y2 = lambda c: copy(5, c, ra.at[c, fy, hi], ry.at[c, 2], toy)
    Y1 = lambda c: copy(6, c, ra.at[c, fy, lo], ry.at[c, 1], toy)
    ZU = lambda c: copy(7, c, ra.at[c, f], zlo.at[c], up)
    ZD = lambda c: copy(8, c, ra.at[c, f], zhi.at[c], down)
    TU = lambda c: copy(9, c, tot.at[c, d], tot.at[c, d], up)
    TD = lambda c: copy(10, c, tot.at[c, d], tot.at[c, d], down)
    D = lambda c: copy(11, c, tot.at[c, d], tot.at[c, d], sib)
    below, above = s < root, s > root
    spot = jnp.where(below, s, jnp.where(above, span - 1 - s, 0))
    far = jnp.abs(s - root)
    most = max(root, span - 1 - root)

    def stage(c, run):
        @pl.when((c >= 0) & (c < chunks))
        def _():
            run(c)

    def produce(c):
        slot = lax.rem(c, slots)

        @pl.when(c >= slots)
        def _():
            A(c - slots).wait_send()

        @pl.when(c < out_chunks)
        def _():
            r = c // (width // CHUNK)
            col = lax.rem(c, width // CHUNK) * CHUNK
            right = bg[:, pl.ds(pl.multiple_of(col, CHUNK), CHUNK)]
            for j in range(4):
                for h in range(2):
                    at = j * (inner // 4) + h * (inner // 8) + r * HR
                    left = gated[:, pl.ds(pl.multiple_of(at, HR), HR)]
                    g[slot, j, h] = dot(left, right, contract).astype(BF16)

        @pl.when((c >= out_chunks) & (c < last))
        def _():
            right = mixed[c - out_chunks]
            for j in range(4):
                t = dot(normed[:, j * 2 * HR : (j + 1) * 2 * HR], right, contract).astype(BF16)
                g[slot, j, 0] = t[:HR]
                g[slot, j, 1] = t[HR:]

        @pl.when(c == last)
        def _():
            for j in range(4):
                for h in range(2):
                    cols = slice(j * CHUNK, (j + 1) * CHUNK)
                    g[slot, j, h] = rest[h * HR : (h + 1) * HR, cols].astype(BF16)

        A(c).start()

    def first_sum(c):
        A(c).wait_recv()
        for j in range(4):
            own = g[lax.rem(c, slots), j, d]
            ra[c, j] = (ra[c, j].astype(F32) + own.astype(F32)).astype(BF16)
        X0(c).start()
        Y0(c).start()
        X1(c).start()
        Y2(c).start()

    def second_sum(c):
        X0(c).wait_recv()
        ra[c, fy, lo] = (ra[c, fy, lo].astype(F32) + rx[c, 0].astype(F32)).astype(BF16)
        Y1(c).start()
        Y0(c).wait_recv()
        ra[c, fx, hi] = (ra[c, fx, hi].astype(F32) + ry[c, 0].astype(F32)).astype(BF16)
        X2(c).start()

    def third_sum(c):
        X1(c).wait_recv()
        Y2(c).wait_recv()
        X2(c).wait_recv()
        Y1(c).wait_recv()
        for k, part in enumerate((lo, hi)):
            total = ra[c, f, part].astype(F32) + rx[c, 1 + k].astype(F32) + ry[c, 1 + k].astype(F32)
            ra[c, f, part] = total.astype(BF16)

    def inward(c):
        @pl.when(below & (s > 0))
        def _():
            ZU(c).wait_recv()
            ra[c, f] = (ra[c, f].astype(F32) + zlo[c].astype(F32)).astype(BF16)

        @pl.when(above & (s < span - 1))
        def _():
            ZD(c).wait_recv()
            ra[c, f] = (ra[c, f].astype(F32) + zhi[c].astype(F32)).astype(BF16)

        pl.when(below)(lambda: ZU(c).start())
        pl.when(above)(lambda: ZD(c).start())

    def at_root(c):
        total = ra[c, f].astype(F32)
        if root > 0:
            ZU(c).wait_recv()
            total = total + zlo[c].astype(F32)
        if span - 1 > root:
            ZD(c).wait_recv()
            total = total + zhi[c].astype(F32)
        tot[c, d] = total.astype(BF16)
        if root > 0:
            TD(c).start()
        if span - 1 > root:
            TU(c).start()
        D(c).start()

    def outward(c):
        @pl.when(above)
        def _():
            TU(c).wait_recv()
            pl.when(s < span - 1)(lambda: TU(c).start())

        @pl.when(below)
        def _():
            TD(c).wait_recv()
            pl.when(s > 0)(lambda: TD(c).start())

        D(c).start()

    tile = 2 * LANES

    def columns(t, size=tile):
        return pl.ds(pl.multiple_of(t * size, size), size)

    def back_block(b):
        c, slot = b // parts, lax.rem(b, 2)
        groups = ctx // GROUP
        first = lax.rem(b, parts) * CHUNK
        cuts = [pl.ds(pl.multiple_of(first + n, LANES), LANES) for n in range(0, CHUNK, LANES)]
        tiles = [slice(n, n + LANES) for n in range(0, CHUNK, LANES)]
        cols = pl.ds(pl.multiple_of(first, CHUNK), CHUNK)
        rates = [-jnp.exp(small[TAPS : TAPS + state, cut]) * LOG2E for cut in cuts]
        skip = small[TAPS + state + 2 : TAPS + state + 3, cols]
        held_copy(b).wait()

        def one(turn, carry):
            i = groups - 1 - turn
            at = c * groups + i
            tok = pl.ds(pl.multiple_of(at * GROUP, GROUP), GROUP)
            p, total, kept = (list(value) for value in carry)
            value, out, gain = u[tok, cols].astype(F32), dy[at, :, cols], delta[at, :, cols]
            v[...] = gain * value
            drive_parts, delta_parts = [[], []], [[], []]
            for pair in range(0, len(cuts), 2):
                which = range(pair, pair + 2)
                after = {n: held[slot, (i + 1) * GROUP, :, tiles[n]].astype(F32) for n in which}
                for half in (1, 0):
                    drives, deltas = ({n: [] for n in which} for _ in range(2))
                    for k in reversed(range(half * 8, half * 8 + 8)):
                        t = i * GROUP + k
                        b_in, read = bw[c, t], cw[c, t]
                        b_part = c_part = 0.0
                        for n in which:
                            row = lambda tile: jnp.broadcast_to(tile, (state, LANES))
                            step, back = row(delta[at, k : k + 1, cuts[n]]), row(dy[at, k : k + 1, cuts[n]])
                            grad = read * back + p[n]
                            p[n] = jnp.exp2(step * rates[n]) * grad
                            before = held[slot, t, :, tiles[n]].astype(F32)
                            w = p[n] * before
                            total[n] = total[n] + w * step
                            part = w * rates[n]
                            rows_sum(deltas[n], part[:8] + part[8:], False)
                            part = grad * b_in
                            rows_sum(drives[n], part[:8] + part[8:], False)
                            b_part = b_part + grad * row(v[k : k + 1, tiles[n]])
                            c_part = c_part + after[n] * back
                            after[n] = before
                        bacc[c * ctx + t] += b_part
                        cacc[c * ctx + t] += c_part
                    drive_parts[half] += [drives[n][0][1] for n in which]
                    delta_parts[half] += [deltas[n][0][1] for n in which]
            joined = lambda halves: jnp.concatenate([jnp.concatenate(h, 1) for h in halves], 0)
            drive_grad, delta_part = joined(drive_parts), joined(delta_parts)
            raw_grad = drive_grad * value + delta_part * (1.0 / LOG2E)
            raw_grad = raw_grad * sig[tok, cols].astype(F32)
            rl[tok, cols] = raw_grad.astype(BF16)
            dy[at, :, cols] = out * skip + drive_grad * gain
            kept[0] = kept[0] + (out * value)[:8] + (out * value)[8:]
            kept[1] = kept[1] + raw_grad[:8] + raw_grad[8:]
            return tuple(p), tuple(total), tuple(kept)

        zero = tuple(jnp.zeros((state, LANES), F32) for _ in cuts)
        none = jnp.zeros((8, CHUNK), F32)
        begin = tuple(final[c, :, cut] for cut in cuts)
        _, total, kept = lax.fori_loop(0, groups, one, (begin, zero, (none, none)))
        for n, cut in enumerate(cuts):
            logs[:, cut] += total[n]
        sums[0, :, cols] += kept[0]
        sums[1, :, cols] += kept[1]

        @pl.when(b + 2 < blocks)
        def _():
            held_copy(b + 2).start()

    def proj_work():
        step_grad = dot(rl[...], dt[...], across)
        col = lax.broadcasted_iota(jnp.int32, (state, LANES), 1)
        n = lax.broadcasted_iota(jnp.int32, (state, LANES), 0)
        ones = jnp.ones((LANES, LANES), BF16)

        def one(r, carry):
            tok = pl.ds(pl.multiple_of(r * GROUP, GROUP), GROUP)
            total = pg_full[tok]
            for ref, first in ((bacc, rank), (cacc, rank + state)):
                value = dot(ref[tok].reshape(GROUP * state, LANES).astype(BF16), ones)
                keep = jnp.where(col == n + first, value.reshape(GROUP, state, LANES), 0.0)
                total = total + jnp.sum(keep, 1)
            pg[tok] = total.astype(BF16)
            return carry

        pg_full[...] = jnp.concatenate([step_grad, jnp.zeros((rows, LANES - rank), F32)], 1)
        lax.fori_loop(0, rows // GROUP, one, 0)

    def weight_work():
        first = TAPS + state + 4
        used = rank + 2 * state

        def weights(t, carry):
            cols = columns(t)
            rest[first : first + rank, cols] = dot(step_low[...], rl[:, cols], contract)
            rest[first + rank : first + rank + used, cols] = dot(pg[...], u[:, cols], contract)[:used]
            kept = -logs[:, cols] * jnp.exp(small[TAPS : TAPS + state, cols])
            rest[TAPS : TAPS + state, cols] = kept
            at = TAPS + state
            rest[at + 1 : at + 2, cols] = jnp.sum(sums[1, :, cols], 0, keepdims=True)
            rest[at + 2 : at + 3, cols] = jnp.sum(sums[0, :, cols], 0, keepdims=True)
            return carry

        lax.fori_loop(0, inner // tile, weights, 0)

    def conv_work(first, count):
        def one(t, carry):
            cols = columns(t)
            shift = jnp.zeros((1, tile), F32)
            taps = [jnp.zeros((1, tile), F32) for _ in range(TAPS)]
            for c in range(seqs):
                tok = slice(c * ctx, (c + 1) * ctx)
                weight = xp[columns(t)]
                back = dot(pg[tok], weight, across)
                own = range(c * ctx // GROUP, (c + 1) * ctx // GROUP)
                grad = jnp.concatenate([dy[at, :, cols] for at in own], 0) + back
                grad = grad * slope[tok, cols].astype(F32)
                cg[c, :ctx, cols] = grad
                before = lead[c, :, cols].astype(F32)
                shift = shift + jnp.sum(grad, 0, keepdims=True)
                for k in range(TAPS):
                    at = GROUP - TAPS + 1 + k
                    taps[k] = taps[k] + jnp.sum(grad * before[at : at + ctx], 0, keepdims=True)
            for k in range(TAPS):
                rest[k : k + 1, cols] = taps[k]
            rest[TAPS + state : TAPS + state + 1, cols] = shift
            return carry

        lax.fori_loop(first, first + count, one, 0)

    edge = cg.shape[1] - ctx
    H = lambda: pltpu.make_async_remote_copy(
        src_ref=cg.at[:, :edge], dst_ref=cg.at[:, ctx:], send_sem=halo.at[0],
        recv_sem=halo.at[1], device_id=down, device_id_type=MESH,
    )

    def halo_send():
        pl.when(s > 0)(lambda: H().start())

    def stream_work():
        pl.when(s < span - 1)(lambda: H().wait_recv())

        def one(t, carry):
            cols = columns(t)
            for c in range(seqs):
                total = 0.0
                for k in range(TAPS):
                    at = TAPS - 1 - k
                    total = total + small[k : k + 1, cols] * cg[c, at : at + ctx, cols]
                half = pl.ds(pl.multiple_of(lax.rem(t, 2) * tile, tile), tile)
                mixed[parts + t // 2, c * ctx : (c + 1) * ctx, half] = total.astype(BF16)
            return carry

        lax.fori_loop(0, inner // tile, one, 0)
        pl.when(s > 0)(lambda: H().wait_send())

    def norm_work(first, count):
        def one(k, carry):
            in_copy(k).wait()
            ng[...] += dot(mixed[k], in_w[lax.rem(k, 2)], across)

            @pl.when(k + 2 < 2 * parts)
            def _():
                in_copy(k + 2).start()

            return carry

        if first == 0:
            ng[...] = jnp.zeros(ng.shape, F32)
        lax.fori_loop(first, first + count, one, 0)

    def input_work():
        share = width // 4
        at = TAPS + state + 3
        gain = jnp.concatenate(
            [small[at : at + 1, j * CHUNK : j * CHUNK + share] for j in range(4)], 1
        )

        def one(r, total):
            tok = pl.ds(pl.multiple_of(r * GROUP, GROUP), GROUP)
            xs = x[tok].astype(F32)
            inverse = lax.rsqrt(jnp.mean(xs * xs, -1, keepdims=True) + EPS)
            grad = ng[tok]
            scaled = grad * gain
            slope = jnp.mean(scaled * xs, -1, keepdims=True)
            out = inverse * scaled - xs * (inverse * inverse * inverse * slope)
            input_grad[tok] = (out + og[tok].astype(F32)).astype(BF16)
            return total + grad * (xs * inverse)

        total = lax.fori_loop(0, rows // GROUP, one, jnp.zeros((GROUP, width), F32))
        total = jnp.sum(total, 0, keepdims=True)
        for j in range(4):
            rest[at : at + 1, j * CHUNK : j * CHUNK + share] = total[:, j * share : (j + 1) * share]

    blocks = seqs * parts
    tiles = inner // tile
    pause = 3
    held_back = out_chunks + parts
    base = 1 + 2 * SLACK + 1

    def prepare():
        for ref in (cacc, bacc, logs, sums, rest):
            ref[...] = jnp.zeros(ref.shape, F32)
        for one in loads[2:]:
            one.wait()

    def blocks_work(i):
        pl.when(i == 0)(prepare)
        pl.when(i < blocks)(lambda: back_block(i))

    def late_work(i):
        at = held_back

        @pl.when(i == at)
        def _():
            proj_work()
            conv_work(0, tiles)
            halo_send()
            in_copy(0).start()
            in_copy(1).start()

        pl.when(i == at + 1)(weight_work)
        pl.when(i == at + 2)(stream_work)
        pl.when(i == at + 4)(lambda: norm_work(0, parts))
        pl.when(i == at + 5)(lambda: norm_work(parts, parts))
        pl.when(i == at + 6)(input_work)

    def step(i, carry):
        def at(offset):
            k = i - offset
            return jnp.where(k < held_back, k, jnp.where(k < held_back + pause, -1, k - pause))

        @pl.when(i == out_chunks)
        def _():
            for one in loads[:2]:
                one.wait()

        stage(at(0), produce)
        stage(at(1), first_sum)
        stage(at(1 + SLACK), second_sum)
        stage(at(1 + 2 * SLACK), third_sum)
        pl.when(s != root)(lambda: stage(at(base + SLACK * spot), inward))
        pl.when(s == root)(lambda: stage(at(base + SLACK * most), at_root))
        pl.when(s != root)(lambda: stage(at(base + SLACK * most + SLACK * far), outward))
        blocks_work(i)
        late_work(i)
        return carry

    lax.fori_loop(0, chunks + pause + base + 2 * SLACK * most + 1, step, 0)

    def finish(c, carry):
        pl.when(c >= chunks - slots)(lambda: A(c).wait_send())
        for t in (X0, X1, X2, Y0, Y1, Y2):
            t(c).wait_send()
        pl.when(below)(lambda: ZU(c).wait_send())
        pl.when(above)(lambda: ZD(c).wait_send())
        if root > 0:
            pl.when((s <= root) & (s > 0))(lambda: TD(c).wait_send())
        if span - 1 > root:
            pl.when((s >= root) & (s < span - 1))(lambda: TU(c).wait_send())
        D(c).wait_send()
        D(c).wait_recv()
        return carry

    lax.fori_loop(0, chunks, finish, 0)
    copies = []
    for c in range(chunks):
        for h in range(2):
            if c < out_chunks:
                r, col = c // (width // CHUNK), c % (width // CHUNK)
                first = h * (inner // 8) + r * HR
                to = out_sum.at[first : first + HR, col * CHUNK : (col + 1) * CHUNK]
            elif c < last:
                col = (c - out_chunks + parts) % (2 * parts)
                to = in_sum.at[h * HR : (h + 1) * HR, col * CHUNK : (col + 1) * CHUNK]
            else:
                to = rest_sum.at[h * HR : (h + 1) * HR]
            copies.append(pltpu.make_async_copy(tot.at[c, h], to, local.at[c, h]))
    for one in copies:
        one.start()
    for one in copies:
        one.wait()


def back(gated, bg, step_low, final, small, x, og, far):
    rows, inner = gated.shape
    width = x.shape[1]
    seqs, state = final.shape[:2]
    ctx, rank, parts = rows // seqs, step_low.shape[1], inner // CHUNK
    span = lax.axis_size("seq")
    out_chunks, in_chunks = 2 * width // CHUNK, 2 * parts
    n = out_chunks + in_chunks + 1
    vmem, dma = pltpu.VMEM, pltpu.SemaphoreType.DMA
    anywhere = pl.BlockSpec(memory_space=pl.ANY)
    whole = pl.BlockSpec(memory_space=vmem)
    shape = jax.ShapeDtypeStruct
    like = lambda v: vmem(v.shape, v.dtype)
    (held, normed, lead, slope, u, sig, delta, bw, cw, dy, zg, in_full, xp, dt) = far
    return pl.pallas_call(
        functools.partial(back_kernel, span, state, rank),
        in_specs=[whole] * 7 + [anywhere] * len(far),
        out_specs=[whole, anywhere, anywhere, anywhere],
        out_shape=[
            shape((rows, width), BF16),
            shape((inner // 4, width), BF16),
            shape((width // 4, 2 * inner), BF16),
            shape((2 * HR, CHUNK), BF16),
        ],
        scratch_shapes=[
            *map(like, (normed, lead, slope, u, sig, delta, bw, cw, dy)),
            vmem((in_chunks, rows, CHUNK), BF16),
            like(xp),
            like(dt),
            vmem((2, width, CHUNK), BF16),
            vmem((2,) + held.shape[1:], BF16),
            vmem((GROUP, CHUNK), F32),
            vmem((rows, inner), BF16),
            vmem((rows, state, LANES), F32),
            vmem((rows, state, LANES), F32),
            vmem((state, inner), F32),
            vmem((2, 8, inner), F32),
            vmem((rows, LANES), BF16),
            vmem((rows, LANES), F32),
            vmem((seqs, ctx + 8, inner), F32),
            vmem((rows, width), F32),
            vmem((2 * HR, inner), F32),
            vmem((4, 4, 2, HR, CHUNK), BF16),
            vmem((n, 4, HR, CHUNK), BF16),
            vmem((n, 3, HR // 2, CHUNK), BF16),
            vmem((n, 3, HR // 2, CHUNK), BF16),
            vmem((n, HR, CHUNK), BF16),
            vmem((n, HR, CHUNK), BF16),
            vmem((n, 2, HR, CHUNK), BF16),
            dma((12, n)),
            dma((12, n)),
            dma((2,)),
            dma((n, 2)),
            dma((12,)),
            dma((2,)),
            dma((2,)),
        ],
        compiler_params=pltpu.CompilerParams(
            collective_id=1, has_side_effects=True, vmem_limit_bytes=63 << 20
        ),
        name="back",
    )(gated, bg, step_low, final, small, x, og, *far)


def finish_kernel(state, rank, used, in_sum, out_sum, rest, gain, in_w, taps, cbias, xp, dt, dbias, logs, skip, out_w):
    in_w[...] = in_sum[...].astype(F32)
    out_w[...] = out_sum[...].astype(F32)
    at = TAPS + state
    row = lambda first, count=1: rest[...].astype(F32)[first : first + count]
    taps[...] = row(0, TAPS)
    logs[...] = row(TAPS, state)
    cbias[...] = row(at)
    dbias[...] = row(at + 1)
    skip[...] = row(at + 2)
    gain[...] = row(at + 3)[:, : gain.shape[1]]
    dt[...] = row(at + 4, rank)
    xp[...] = row(at + 4 + rank, used).T


def finish(in_sum, out_sum, rest, state, rank, used):
    steps = 4
    share = rest.shape[1]
    tall = lambda v: pl.BlockSpec((v.shape[0] // steps, v.shape[1]), lambda i: (i, 0))
    fixed = lambda *v: pl.BlockSpec(v, lambda i: (0, 0))
    small = [(1, in_sum.shape[0]), (TAPS, share), (1, share), (share, used), (rank, share)]
    small += [(1, share), (state, share), (1, share)]
    shape = lambda v: jax.ShapeDtypeStruct(v, F32)
    return pl.pallas_call(
        functools.partial(finish_kernel, state, rank, used),
        grid=(steps,),
        in_specs=[tall(in_sum), tall(out_sum), fixed(*rest.shape)],
        out_specs=[fixed(*small[0]), tall(in_sum)] + [fixed(*v) for v in small[1:]] + [tall(out_sum)],
        out_shape=[shape(small[0]), shape(in_sum.shape)]
        + [shape(v) for v in small[1:]]
        + [shape(out_sum.shape)],
        compiler_params=pltpu.CompilerParams(vmem_limit_bytes=32 << 20),
        name="finish",
    )(in_sum, out_sum, rest)


def body(
    hidden_in, lengths, norm_gain, in_weight, conv_weight, conv_bias, xproj_weight,
    dt_weight, dt_bias, a_log, skip_gain, out_weight, out_grad,
):
    seqs, ctx, width = hidden_in.shape
    taps, share = conv_weight.shape
    state = a_log.shape[0]
    rank = dt_weight.shape[0]
    rows = ctx * seqs
    row = lambda v: v.reshape(1, -1)
    x, og = hidden_in.reshape(rows, width), out_grad.reshape(rows, width)
    used = xproj_weight.shape[1]
    xp_own = jnp.pad(xproj_weight, ((0, 0), (0, LANES - used)))
    (
        hidden_out, step_low, final, held, normed, branch_grad, lead, slope, u, sig, delta,
        b_wide, c_wide, y_grad, gated, z_grad, in_matrix, proj_matrix, step_matrix, small,
    ) = front(
        x, og, lengths, conv_weight, a_log, row(conv_bias), row(dt_bias), row(skip_gain),
        row(norm_gain), in_weight, out_weight, xp_own, dt_weight, seqs,
    )
    far = (
        held, normed, lead, slope, u, sig, delta, b_wide, c_wide, y_grad, z_grad, in_matrix,
        proj_matrix, step_matrix,
    )
    input_grad, out_sum, in_sum, rest = back(
        gated, branch_grad, step_low, final, small, x, og, far
    )
    gain, in_w, taps_grad, cbias, proj_w, step_w, dbias, logs, skip, out_w = finish(
        in_sum, out_sum, rest, state, rank, used
    )
    flat = lambda v: v.reshape(-1)
    return (
        hidden_out.reshape(seqs, ctx, width), input_grad.reshape(seqs, ctx, width), flat(gain), in_w,
        taps_grad, flat(cbias), proj_w, step_w, flat(dbias), logs, flat(skip), out_w,
    )


def solution(mesh):
    tokens = P(("dp", "fsdp"), "seq", None)
    return jax.shard_map(
        body,
        mesh=mesh,
        in_specs=(
            tokens, P(("dp", "fsdp")), P("fsdp"), P("fsdp", None), P(None, "fsdp"), P("fsdp"),
            P("fsdp", None), P(None, "fsdp"), P("fsdp"), P(None, "fsdp"), P("fsdp"),
            P("fsdp", None), tokens,
        ),
        out_specs=(
            tokens, tokens, P("fsdp"), P("fsdp", None), P(None, "fsdp"), P("fsdp"),
            P("fsdp", None), P(None, "fsdp"), P("fsdp"), P(None, "fsdp"), P("fsdp"),
            P("fsdp", None),
        ),
        check_vma=False,
    )
```

```python
import functools
import math

import jax
import jax.numpy as jnp
import numpy as np
from jax import lax
from jax.experimental import pallas as pl
from jax.experimental.pallas import tpu as pltpu
from jax.sharding import PartitionSpec as P

EPS = 1e-05
LOG2E = math.log2(math.e)
LANES = 128
GROUP = 16
F32 = jnp.float32
BF16 = jnp.bfloat16
MESH = pl.DeviceIdType.MESH
HR = 128
CHUNK = 512
SLACK = 1
TAPS = 4
HELD = 3


def silu_parts(v):
    s = jax.nn.sigmoid(v)
    return v * s, s * (1.0 + v * (1.0 - s))


def rows_sum(stack, value, rising):
    row = lax.broadcasted_iota(jnp.int32, value.shape, 0)
    level = 0
    while stack and stack[-1][0] == level:
        _, other = stack.pop()
        first, second = (other, value) if rising else (value, other)
        low = (row & (1 << level)) == 0
        turned = pltpu.roll(jnp.where(low, second, first), 1 << level, 0)
        value = jnp.where(low, first, second) + turned
        level += 1
    stack.append((level, value))


def front_kernel(
    span,
    x, og, lengths, taps_own, log_own, cbias_own, dbias_own, skip_own, gain_own,
    in_own, out_own, xp_own, dt_own,
    hidden_out, step_low, final,
    held_all, normed_full, bg_full, lead_full, slope_full, u_full, sig_full, delta_full, bw_full,
    cw_full, dy_full, gated_full, zg_full, in_full, xp_full, dt_full, small_full,
    in_w, out_w, xp, dt, small, small_own, hx, acc, zacc, normed, v, proj, ends, sums,
    ends_in, sums_in, bg, mask, lead, slope, u, sig, delta, bw, cw, gg, dy, y, gated, zg,
    start, held,
    send, recv, halo, relay_send, relay_recv, sums_send, sums_recv, local, keep, held_sem,
):
    d, s, f = (lax.axis_index(a) for a in ("dp", "seq", "fsdp"))
    fx, fy, fd = f ^ 1, f ^ 2, f ^ 3
    tox, toy, tod, sib = {"fsdp": fx}, {"fsdp": fy}, {"fsdp": fd}, {"dp": 1 - d}
    rows, width = x.shape
    inner = u.shape[1]
    seqs = bw.shape[0]
    ctx = rows // seqs
    state, rank = log_own.shape[0], dt_own.shape[0]
    groups = ctx // GROUP
    share = inner // 4
    at_state, at_bias = TAPS, TAPS + state
    across = (((1,), (1,)), ((), ()))
    dot = lambda a, b, dims=(((1,), (0,)), ((), ())): lax.dot_general(
        a, b, dims, preferred_element_type=F32
    )

    for c in range(seqs):
        hx[c] = jnp.zeros((GROUP, width), BF16)
    barrier = pltpu.get_barrier_semaphore()
    for who in (tox, toy, tod, sib):
        pl.semaphore_signal(barrier, inc=1, device_id=who, device_id_type=MESH)

    def greet(o, carry):
        who = {"seq": lax.rem(s + o, span)}
        pl.semaphore_signal(barrier, inc=1, device_id=who, device_id_type=MESH)
        return carry

    lax.fori_loop(1, span, greet, 0)
    small_own[...] = jnp.zeros(small_own.shape, F32)
    small_own[:TAPS] = taps_own[...]
    small_own[at_state:at_bias] = log_own[...]
    small_own[at_bias : at_bias + 1] = cbias_own[...]
    small_own[at_bias + 1 : at_bias + 2] = dbias_own[...]
    small_own[at_bias + 2 : at_bias + 3] = skip_own[...]
    small_own[at_bias + 3 : at_bias + 4, : width // 4] = gain_own[...]
    pl.semaphore_wait(barrier, 3 + span)

    SMALL, STREAM, PROJ, STEP, GATE, OUT = range(6)
    plan = (
        (small_own, small, 1, None),
        (in_own, in_w, 0, (0, inner)),
        (xp_own, xp, 0, None),
        (dt_own, dt, 1, None),
        (in_own, in_w, 0, (inner, 2 * inner)),
        (out_own, out_w, 0, None),
    )

    def window(p, owner, half, q):
        src, dst, dim, cols = plan[p]
        high, wide = src.shape
        part = high // 4
        at = (half * 2 + q) * part
        lo, hi = cols or (0, wide)
        if dim == 0:
            return dst.at[pl.ds(pl.multiple_of(owner * high + at, part), part), lo:hi]
        col = pl.ds(pl.multiple_of(owner * wide, wide), wide)
        return dst.at[pl.ds(pl.multiple_of(at, part), part), col]

    def own(p, half, q):
        src, _, _, cols = plan[p]
        high, wide = src.shape
        part = high // 4
        lo, hi = cols or (0, wide)
        return src.at[pl.ds(pl.multiple_of((half * 2 + q) * part, part), part), lo:hi]

    def copy(src, dst, p, kind, who):
        return pltpu.make_async_remote_copy(
            src_ref=src, dst_ref=dst, send_sem=send.at[p, kind], recv_sem=recv.at[p, kind],
            device_id=who, device_id_type=MESH,
        )

    started = []

    def go(one):
        one.start()
        started.append(one)

    def start_own(p, routed=False):
        for q in (0, 1):
            go(copy(own(p, d, q), window(p, f, d, q), p, q, tox))
            go(copy(own(p, d, 1 - q), window(p, f, d, 1 - q), p, 3 - q, toy))
        if routed:
            for q in (0, 1):
                go(copy(own(p, d, q), window(p, f, d, q), p, 4 + q, tod))

    def small_copy(at, owner, part, who):
        rows_of = slice(*((at_bias - at_bias % 8, at_bias + 4), (0, at_bias - at_bias % 8))[part])
        cols = pl.ds(pl.multiple_of(owner * share, share), share)
        return pltpu.make_async_remote_copy(
            src_ref=small_own.at[rows_of], dst_ref=small.at[rows_of, cols],
            send_sem=send.at[SMALL, 3 * part + at], recv_sem=recv.at[SMALL, 3 * part + at],
            device_id=who, device_id_type=MESH,
        )

    def small_start(part):
        for at, who in enumerate((tox, toy, tod)):
            go(small_copy(at, f, part, who))

    def small_ready(part):
        for at, owner in enumerate((fx, fy, fd)):
            small_copy(at, owner, part, sib).wait_recv()

    def place_own(p):
        for half in (0, 1):
            for q in (0, 1):
                pltpu.make_async_copy(
                    own(p, half, q), window(p, f, half, q), local.at[p, half * 2 + q]
                ).start()

    def own_ready(p):
        for half in (0, 1):
            for q in (0, 1):
                pltpu.make_async_copy(
                    own(p, half, q), window(p, f, half, q), local.at[p, half * 2 + q]
                ).wait()

    def arrived(p, kind, owner, half, q):
        w = window(p, owner, half, q)
        copy(w, w, p, kind, sib).wait_recv()
        return w

    near = ((0, fx, 0), (3, fy, 1), (1, fx, 1), (2, fy, 0))
    diagonal = ((4, fd, 0), (5, fd, 1))

    def serve_near(p, routed=False):
        for kind, owner, q in near:
            w = arrived(p, kind, owner, d, q)
            if kind == 0 and not routed:
                go(copy(w, w, p, 4, toy))
            if kind == 3 and not routed:
                go(copy(w, w, p, 5, tox))
            go(copy(w, w, p, 6 + kind, sib))

    def serve_far(p):
        for kind, owner, q in diagonal:
            w = arrived(p, kind, owner, d, q)
            go(copy(w, w, p, 6 + kind, sib))

    def near_ready(p):
        for kind, owner, q in near:
            arrived(p, 6 + kind, owner, 1 - d, q)

    def far_ready(p):
        for kind, owner, q in diagonal:
            arrived(p, 6 + kind, owner, 1 - d, q)

    small_start(0)
    start_own(STREAM)
    for p in (STREAM, PROJ, STEP, GATE, OUT):
        place_own(p)
    pltpu.make_async_copy(
        small_own, small.at[:, pl.ds(pl.multiple_of(f * share, share), share)], local.at[SMALL, 0]
    ).start()
    def edges(c):
        return pltpu.make_async_remote_copy(
            src_ref=x.at[(c + 1) * ctx - GROUP : (c + 1) * ctx], dst_ref=hx.at[c],
            send_sem=halo.at[0, c], recv_sem=halo.at[1, c],
            device_id={"seq": jnp.minimum(s + 1, span - 1)}, device_id_type=MESH,
        )

    @pl.when(s < span - 1)
    def _():
        for c in range(seqs):
            edges(c).start()

    for c in range(seqs):
        t = s * ctx + lax.broadcasted_iota(jnp.int32, (ctx, LANES), 0)
        mask[c * ctx : (c + 1) * ctx] = (t < lengths[c]).astype(F32)

    def mask_step(r, carry):
        tok = pl.ds(pl.multiple_of(r * GROUP, GROUP), GROUP)
        held = jnp.concatenate([mask[tok]] * (width // LANES), 1)
        bg[tok] = (og[tok].astype(F32) * held).astype(BF16)
        return carry

    lax.fori_loop(0, rows // GROUP, mask_step, 0)

    pltpu.make_async_copy(
        small_own, small.at[:, pl.ds(pl.multiple_of(f * share, share), share)], local.at[SMALL, 0]
    ).wait()
    small_ready(0)

    @pl.when(s > 0)
    def _():
        for c in range(seqs):
            edges(c).wait_recv()

    gain_at = at_bias + 3
    gain = jnp.concatenate(
        [small[gain_at : gain_at + 1, j * share : j * share + width // 4] for j in range(4)], 1
    )

    def normalised(v):
        v = v.astype(F32)
        inverse = lax.rsqrt(jnp.mean(v * v, -1, keepdims=True) + EPS)
        return (v * inverse * gain).astype(BF16)

    def norm_step(r, carry):
        tok = pl.ds(pl.multiple_of(r * GROUP, GROUP), GROUP)
        normed[tok] = normalised(x[tok])
        return carry

    lax.fori_loop(0, rows // GROUP, norm_step, 0)
    for c in range(seqs):
        normed[rows + c * GROUP : rows + (c + 1) * GROUP] = normalised(hx[c])

    def project(total, high, first, owner, fresh):
        shard = pl.ds(pl.multiple_of(owner * (width // 4), width // 4), width // 4)
        left = normed[:high, shard]

        def one(t, carry):
            cols = pl.ds(pl.multiple_of(t * CHUNK, CHUNK), CHUNK)
            right = in_w[shard, pl.ds(pl.multiple_of(first + t * CHUNK, CHUNK), CHUNK)]
            part = dot(left, right)
            total[:, cols] = part if fresh else total[:, cols] + part
            return carry

        lax.fori_loop(0, inner // CHUNK, one, 0)

    tall = rows + seqs * GROUP
    own_ready(STREAM)
    project(acc, tall, 0, f, True)
    serve_near(STREAM)
    small_start(1)
    start_own(PROJ, True)
    start_own(STEP, True)
    start_own(GATE)
    near_ready(STREAM)
    project(acc, tall, 0, fx, False)
    project(acc, tall, 0, fy, False)
    serve_far(STREAM)
    far_ready(STREAM)
    project(acc, tall, 0, fd, False)
    small_ready(1)

    tile = 2 * LANES

    def columns(t, size=tile):
        return pl.ds(pl.multiple_of(t * size, size), size)

    def conv_step(t, carry):
        cols = columns(t)
        for c in range(seqs):
            before = acc[rows + c * GROUP : rows + (c + 1) * GROUP, cols].astype(BF16)
            stream = acc[c * ctx : (c + 1) * ctx, cols].astype(BF16)
            lead[c, :GROUP, cols] = before
            lead[c, GROUP:, cols] = stream
            held = jnp.concatenate([before, stream], 0).astype(F32)
            total = small[at_bias : at_bias + 1, cols]
            for k in range(TAPS):
                at = GROUP - TAPS + 1 + k
                total = total + small[k : k + 1, cols] * held[at : at + ctx]
            value, grad = silu_parts(total)
            slope[c * ctx : (c + 1) * ctx, cols] = grad.astype(BF16)
            u[c * ctx : (c + 1) * ctx, cols] = value.astype(BF16)
        return carry

    lax.fori_loop(0, inner // tile, conv_step, 0)
    for p in (PROJ, STEP):
        serve_near(p, True)
        serve_far(p)
    for p in (PROJ, STEP):
        near_ready(p)
        far_ready(p)
        own_ready(p)
    proj[...] = dot(u[...], xp[...])
    step_low[...] = proj[:, :rank].astype(BF16)

    def wide_step(i, carry):
        tok = pl.ds(pl.multiple_of(i * GROUP, GROUP), GROUP)
        held = proj[tok]
        for ref, first in ((bw, rank), (cw, rank + state)):
            value = held[:, first : first + state]
            c, at = i // groups, lax.rem(i, groups)
            ref[c, pl.ds(pl.multiple_of(at * GROUP, GROUP), GROUP)] = jnp.broadcast_to(
                value[:, :, None], (GROUP, state, LANES)
            )
        return carry

    lax.fori_loop(0, rows // GROUP, wide_step, 0)
    def delta_step(t, carry):
        cols = columns(t)
        for c in range(seqs):
            tok = slice(c * ctx, (c + 1) * ctx)
            value = dot(step_low[tok], dt[:, cols]) + small[at_bias + 1 : at_bias + 2, cols]
            sig[tok, cols] = jax.nn.sigmoid(value).astype(BF16)
            value = jnp.maximum(value, 0.0) + jnp.log1p(jnp.exp(-jnp.abs(value)))
            for i in range(groups):
                delta[c * groups + i, :, cols] = value[i * GROUP : (i + 1) * GROUP]
            sums[c : c + 1, cols] = jnp.sum(value, 0, keepdims=True)
            value = value * u[tok, cols].astype(F32)
            for i in range(groups):
                v[c * groups + i, :, cols] = value[i * GROUP : (i + 1) * GROUP]
        return carry

    sums[...] = jnp.zeros(sums.shape, F32)
    lax.fori_loop(0, inner // tile, delta_step, 0)

    def sums_copy(j):
        return pltpu.make_async_remote_copy(
            src_ref=sums, dst_ref=sums_in.at[s], send_sem=sums_send.at[j],
            recv_sem=sums_recv.at[s], device_id={"seq": j}, device_id_type=MESH,
        )

    def sums_start(o, carry):
        sums_copy(lax.rem(s + o, span)).start()
        return carry

    lax.fori_loop(1, span, sums_start, 0)

    def ends_copy(j, way, c):
        return pltpu.make_async_remote_copy(
            src_ref=ends.at[way, c], dst_ref=ends_in.at[s, c], send_sem=relay_send.at[j, c],
            recv_sem=relay_recv.at[s, c], device_id={"seq": j}, device_id_type=MESH,
        )

    def ends_start(first, count, way, c):
        def one(j, carry):
            ends_copy(j, way, c).start()
            return carry

        lax.fori_loop(first, count, one, 0)

    def forward_ends(c):
        for j in range(0, inner, CHUNK):
            cuts = [slice(j + i, j + i + LANES) for i in range(0, CHUNK, LANES)]
            rates = [-jnp.exp(small[at_state:at_bias, cut]) * LOG2E for cut in cuts]

            def one(i, h):
                h = list(h)
                for k in range(GROUP):
                    b = bw[c, i * GROUP + k]
                    for n, cut in enumerate(cuts):
                        step = delta[c * groups + i, k : k + 1, cut]
                        factor = jnp.exp2(jnp.broadcast_to(step, (state, LANES)) * rates[n])
                        row = jnp.broadcast_to(v[c * groups + i, k : k + 1, cut], (state, LANES))
                        h[n] = factor * h[n] + row * b
                return tuple(h)

            zero = tuple(jnp.zeros((state, LANES), F32) for _ in cuts)
            h = lax.fori_loop(0, groups, one, zero)
            for n, cut in enumerate(cuts):
                ends[0, c, :, cut] = h[n].astype(BF16)

    def backward_ends(c):
        for j in range(0, inner, CHUNK):
            cuts = [slice(j + i, j + i + LANES) for i in range(0, CHUNK, LANES)]
            rates = [-jnp.exp(small[at_state:at_bias, cut]) * LOG2E for cut in cuts]

            def one(i, carry):
                run, p = (list(value) for value in carry)
                for k in range(GROUP):
                    read = cw[c, i * GROUP + k]
                    for n, cut in enumerate(cuts):
                        step = delta[c * groups + i, k : k + 1, cut]
                        factor = jnp.exp2(jnp.broadcast_to(step, (state, LANES)) * rates[n])
                        row = dy[c * groups + i, k : k + 1, cut]
                        run[n] = run[n] * factor
                        p[n] = p[n] + run[n] * (read * jnp.broadcast_to(row, (state, LANES)))
                return tuple(run), tuple(p)

            one_s = tuple(jnp.ones((state, LANES), F32) for _ in cuts)
            zero = tuple(jnp.zeros((state, LANES), F32) for _ in cuts)
            _, p = lax.fori_loop(0, groups, one, (one_s, zero))
            for n, cut in enumerate(cuts):
                ends[1, c, :, cut] = p[n].astype(BF16)

    def stash(*pairs):
        for at, (src, dst) in pairs:
            one = pltpu.make_async_copy(src, dst, keep.at[at])
            one.start()
            kept.append(one)

    kept = []
    stash(
        (0, (normed.at[:rows], normed_full)), (1, (bg, bg_full)), (2, (lead, lead_full)),
        (3, (slope, slope_full)), (4, (u, u_full)), (5, (sig, sig_full)), (6, (delta, delta_full)),
        (7, (cw, cw_full)), (8, (xp, xp_full)), (9, (dt, dt_full)), (10, (small, small_full)),
        (15, (bw, bw_full)),
    )

    def ends_wait(j, c):
        pltpu.make_async_remote_copy(
            src_ref=ends.at[0, c], dst_ref=ends_in.at[j, c], send_sem=relay_send.at[j, c],
            recv_sem=relay_recv.at[j, c], device_id={"seq": j}, device_id_type=MESH,
        ).wait_recv()

    def join(ref, j, c):
        ends_wait(j, c)

        def one(t, carry):
            cols = columns(t, CHUNK)
            rates = -jnp.exp(small[at_state:at_bias, cols]) * LOG2E
            decay = jnp.exp2(sums_in[j, c : c + 1, cols] * rates)
            ref[c, :, cols] = decay * ref[c, :, cols] + ends_in[j, c, :, cols].astype(F32)
            return carry

        lax.fori_loop(0, inner // CHUNK, one, 0)

    def join_start(c):
        def one(j, carry):
            join(start, j, c)
            return carry

        lax.fori_loop(0, s, one, 0)

    def join_final(o, carry):
        for c in range(seqs):
            join(final, span - 1 - o, c)
        return carry

    def sums_wait(o, carry):
        j = lax.rem(s + o, span)
        pltpu.make_async_remote_copy(
            src_ref=sums, dst_ref=sums_in.at[j], send_sem=sums_send.at[j],
            recv_sem=sums_recv.at[j], device_id={"seq": j}, device_id_type=MESH,
        ).wait_recv()
        return carry

    parts = inner // CHUNK
    blocks = seqs * parts

    def held_copy(b):
        slot = lax.rem(b, HELD)
        return pltpu.make_async_copy(held.at[slot], held_all.at[b], held_sem.at[slot])

    def sweep_block(b, carry):
        c, slot = b // parts, lax.rem(b, HELD)
        first = lax.rem(b, parts) * CHUNK
        cuts = [pl.ds(pl.multiple_of(first + n, LANES), LANES) for n in range(0, CHUNK, LANES)]
        tiles = [slice(n, n + LANES) for n in range(0, CHUNK, LANES)]
        all_cols = pl.ds(pl.multiple_of(first, CHUNK), CHUNK)
        rates = [-jnp.exp(small[at_state:at_bias, cut]) * LOG2E for cut in cuts]
        skip = small[at_bias + 2 : at_bias + 3, all_cols]

        @pl.when(b >= HELD)
        def _():
            held_copy(b - HELD).wait()

        h = tuple(start[c, :, cut] for cut in cuts)
        for n, cut in enumerate(tiles):
            held[slot, 0, :, cut] = h[n].astype(BF16)

        def one(i, h):
            h = list(h)
            g = c * groups + i
            for first_row in range(0, GROUP, 8):
                stacks = [[] for _ in cuts]
                for k in range(first_row, first_row + 8):
                    b_in, read = bw[c, i * GROUP + k], cw[c, i * GROUP + k]
                    for n, cut in enumerate(cuts):
                        step = jnp.broadcast_to(delta[g, k : k + 1, cut], (state, LANES))
                        row = jnp.broadcast_to(v[g, k : k + 1, cut], (state, LANES))
                        h[n] = jnp.exp2(step * rates[n]) * h[n] + row * b_in
                        held[slot, i * GROUP + k + 1, :, tiles[n]] = h[n].astype(BF16)
                        part = h[n] * read
                        rows_sum(stacks[n], part[:8] + part[8:], True)
                for n, cut in enumerate(cuts):
                    y[g, first_row : first_row + 8, cut] = stacks[n][0][1]
            tok = pl.ds(pl.multiple_of(g * GROUP, GROUP), GROUP)
            y[g, :, all_cols] += skip * u[tok, all_cols].astype(F32)
            return tuple(h)

        lax.fori_loop(0, groups, one, h)
        held_copy(b).start()
        return carry

    def grad_part(owner):
        shard = pl.ds(pl.multiple_of(owner * share, share), share)
        gg[:, shard] = dot(bg[...], out_w[shard], across)

    forward_ends(0)
    ends_start(s + 1, span, 0, 0)
    serve_near(GATE)
    start_own(OUT)
    own_ready(GATE)
    forward_ends(1)
    ends_start(s + 1, span, 0, 1)
    lax.fori_loop(1, span, sums_wait, 0)
    start[...] = jnp.zeros(start.shape, F32)
    join_start(0)
    serve_far(GATE)
    lax.fori_loop(0, parts // 2, sweep_block, 0)
    near_ready(GATE)
    far_ready(GATE)
    stash((11, (in_w, in_full)))

    def gate_project(t, carry):
        cols = columns(t, CHUNK)
        right = in_w[:, pl.ds(pl.multiple_of(inner + t * CHUNK, CHUNK), CHUNK)]
        zacc[:, cols] = dot(normed[:rows], right)
        return carry

    lax.fori_loop(0, parts, gate_project, 0)
    serve_near(OUT)
    lax.fori_loop(parts // 2, parts, sweep_block, 0)
    serve_far(OUT)
    own_ready(OUT)
    near_ready(OUT)
    for owner in (f, fx, fy):
        grad_part(owner)
    far_ready(OUT)
    grad_part(fd)

    def gate_step(t, carry):
        cols = columns(t)
        for c in range(seqs):
            tok = slice(c * ctx, (c + 1) * ctx)
            value, grad = silu_parts(zacc[tok, cols].astype(BF16).astype(F32))
            pieces = [y[c * groups + i, :, cols] for i in range(groups)]
            scanned = jnp.concatenate(pieces, 0)
            gated[tok, cols] = (scanned * value).astype(BF16)
            half = pl.ds(pl.multiple_of(lax.rem(t, 2) * tile, tile), tile)
            zg[t // 2, tok, half] = (gg[tok, cols] * scanned * grad).astype(BF16)
        return carry

    def back_step(t, carry):
        cols = columns(t)
        for c in range(seqs):
            tok = slice(c * ctx, (c + 1) * ctx)
            value = zacc[tok, cols].astype(BF16).astype(F32)
            value = gg[tok, cols] * (value * jax.nn.sigmoid(value))
            for i in range(groups):
                dy[c * groups + i, :, cols] = value[i * GROUP : (i + 1) * GROUP]
        return carry

    lax.fori_loop(0, inner // tile, back_step, 0)
    stash((12, (dy, dy_full)))
    for c in range(seqs):
        backward_ends(c)
        ends_start(0, s, 1, c)
    for c in range(1, seqs):
        join_start(c)
    lax.fori_loop(parts, blocks, sweep_block, 0)
    lax.fori_loop(0, inner // tile, gate_step, 0)
    stash((13, (gated, gated_full)), (14, (zg, zg_full)))

    def hidden_step(t, carry):
        cols = columns(t)
        keep_rows = jnp.concatenate([mask[...]] * (tile // LANES), 1)
        branch = dot(gated[...], out_w[:, cols])
        hidden_out[:, cols] = (x[:, cols].astype(F32) + keep_rows * branch).astype(BF16)
        return carry

    lax.fori_loop(0, width // tile, hidden_step, 0)
    final[...] = jnp.zeros(final.shape, F32)
    lax.fori_loop(0, span - 1 - s, join_final, 0)

    for one in started:
        one.wait_send()

    @pl.when(s < span - 1)
    def _():
        for c in range(seqs):
            edges(c).wait_send()

    def sent(o, carry):
        j = lax.rem(s + o, span)
        sums_copy(j).wait_send()
        for c in range(seqs):
            ends_copy(j, 0, c).wait_send()
        return carry

    lax.fori_loop(1, span, sent, 0)
    for one in kept:
        one.wait()
    for b in range(max(blocks - HELD, 0), blocks):
        held_copy(b).wait()


def front(x, og, lengths, taps, logs, cbias, dbias, skip, gain, in_own, out_own, xp_own, dt_own, seqs):
    rows, width = x.shape
    share, inner = taps.shape[1], 4 * taps.shape[1]
    state, rank, used = logs.shape[0], dt_own.shape[0], xp_own.shape[1]
    ctx = rows // seqs
    span = lax.axis_size("seq")
    parts = inner // CHUNK
    vmem, dma = pltpu.VMEM, pltpu.SemaphoreType.DMA
    whole, anywhere = pl.BlockSpec(memory_space=vmem), pl.BlockSpec(memory_space=pl.ANY)
    shape = jax.ShapeDtypeStruct
    grouped = (rows // GROUP, GROUP, inner)
    kept = [
        ((rows, width), BF16),
        ((rows, width), BF16),
        ((seqs, ctx + GROUP, inner), BF16),
        ((rows, inner), BF16),
        ((rows, inner), BF16),
        ((rows, inner), BF16),
        (grouped, F32),
        ((seqs, ctx, state, LANES), F32),
        ((seqs, ctx, state, LANES), F32),
        (grouped, F32),
        ((rows, inner), BF16),
        ((parts, rows, CHUNK), BF16),
        ((width, 2 * inner), BF16),
        ((inner, used), BF16),
        ((rank, inner), BF16),
        ((32, inner), F32),
    ]
    held = (ctx + 1, state, CHUNK)
    return pl.pallas_call(
        functools.partial(front_kernel, span),
        in_specs=[whole, whole, pl.BlockSpec(memory_space=pltpu.SMEM)]
        + [whole] * 6
        + [anywhere] * 4,
        out_specs=[whole] * 3 + [anywhere] * (1 + len(kept)),
        out_shape=[
            shape((rows, width), BF16),
            shape((rows, rank), BF16),
            shape((seqs, state, inner), F32),
            shape((seqs * parts,) + held, BF16),
        ]
        + [shape(*k) for k in kept],
        scratch_shapes=[
            vmem((width, 2 * inner), BF16),
            vmem((inner, width), BF16),
            vmem((inner, used), BF16),
            vmem((rank, inner), BF16),
            vmem((32, inner), F32),
            vmem((32, share), F32),
            vmem((seqs, GROUP, width), BF16),
            vmem((rows + seqs * GROUP, inner), F32),
            vmem((rows, inner), F32),
            vmem((rows + seqs * GROUP, width), BF16),
            vmem(grouped, F32),
            vmem((rows, used), F32),
            vmem((2, seqs, state, inner), BF16),
            vmem((8, inner), F32),
            vmem((span, seqs, state, inner), BF16),
            vmem((span, 8, inner), F32),
            vmem((rows, width), BF16),
            vmem((rows, LANES), F32),
            vmem((seqs, ctx + GROUP, inner), BF16),
            vmem((rows, inner), BF16),
            vmem((rows, inner), BF16),
            vmem((rows, inner), BF16),
            vmem(grouped, F32),
            vmem((seqs, ctx, state, LANES), F32),
            vmem((seqs, ctx, state, LANES), F32),
            vmem((rows, inner), F32),
            vmem(grouped, F32),
            vmem(grouped, F32),
            vmem((rows, inner), BF16),
            vmem((parts, rows, CHUNK), BF16),
            vmem((seqs, state, inner), F32),
            vmem((HELD,) + held, BF16),
            dma((6, 12)),
            dma((6, 12)),
            dma((2, seqs)),
            dma((span, seqs)),
            dma((span, seqs)),
            dma((span,)),
            dma((span,)),
            dma((6, 4)),
            dma((len(kept),)),
            dma((HELD,)),
        ],
        compiler_params=pltpu.CompilerParams(
            collective_id=0, has_side_effects=True, vmem_limit_bytes=63 << 20
        ),
        name="front",
    )(x, og, lengths, taps, logs, cbias, dbias, skip, gain, in_own, out_own, xp_own, dt_own)


def back_kernel(
    span, state, rank,
    gated, bg, step_low, final, small, x, og,
    held_all, normed_full, lead_full, slope_full, u_full, sig_full, delta_full, bw_full,
    cw_full, dy_full, zg_full, in_full, xp_full, dt_full,
    input_grad, out_sum, in_sum, rest_sum,
    normed, lead, slope, u, sig, delta, bw, cw, dy, mixed, xp, dt, in_w, held, v, rl, cacc,
    bacc, logs, sums,
    pg, pg_full, cg, ng, rest, g, ra, rx, ry, zlo, zhi, tot,
    send, recv, halo, local, load, held_sem, in_sem,
):
    d, s, f = (lax.axis_index(a) for a in ("dp", "seq", "fsdp"))
    fx, fy, fd = f ^ 1, f ^ 2, f ^ 3
    chunks = tot.shape[0]
    rows, width = x.shape
    inner = gated.shape[1]
    seqs = cg.shape[0]
    ctx = rows // seqs
    parts = inner // CHUNK
    out_chunks = 2 * width // CHUNK
    in_chunks = 2 * parts
    last = out_chunks + in_chunks
    slots = g.shape[0]
    q = HR // 2
    root = (span - 1) // 2
    tox, toy, sib = {"fsdp": fx}, {"fsdp": fy}, {"dp": 1 - d}
    up, down = {"seq": jnp.minimum(s + 1, span - 1)}, {"seq": jnp.maximum(s - 1, 0)}
    contract = (((0,), (0,)), ((), ()))
    across = (((1,), (1,)), ((), ()))
    dot = lambda a, b, dims=(((1,), (0,)), ((), ())): lax.dot_general(
        a, b, dims, preferred_element_type=F32
    )

    loads = (
        (mixed.at[:parts], zg_full), (normed, normed_full), (delta, delta_full), (dy, dy_full),
        (u, u_full), (cw, cw_full), (bw, bw_full), (sig, sig_full), (slope, slope_full),
        (lead, lead_full), (xp, xp_full), (dt, dt_full),
    )
    loads = [pltpu.make_async_copy(src, dst, load.at[n]) for n, (dst, src) in enumerate(loads)]

    def held_copy(b):
        slot = lax.rem(b, 2)
        return pltpu.make_async_copy(held_all.at[b], held.at[slot], held_sem.at[slot])

    def in_copy(k):
        slot = lax.rem(k, 2)
        first = pl.multiple_of(lax.rem(k + parts, 2 * parts) * CHUNK, CHUNK)
        return pltpu.make_async_copy(in_full.at[:, pl.ds(first, CHUNK)], in_w.at[slot], in_sem.at[slot])

    held_copy(0).start()
    for one in loads[2:7]:
        one.start()
    held_copy(1).start()
    for one in loads[:2] + loads[7:]:
        one.start()
    cg[:, ctx:] = jnp.zeros((seqs, cg.shape[1] - ctx, inner), F32)
    barrier = pltpu.get_barrier_semaphore()
    for who in (tox, toy, sib):
        pl.semaphore_signal(barrier, inc=1, device_id=who, device_id_type=MESH)

    @pl.when(s > 0)
    def _():
        pl.semaphore_signal(barrier, inc=1, device_id=down, device_id_type=MESH)

    @pl.when(s < span - 1)
    def _():
        pl.semaphore_signal(barrier, inc=1, device_id=up, device_id_type=MESH)

    ends = (s == 0) | (s == span - 1)
    pl.semaphore_wait(barrier, jnp.where(ends, 4, 5) if span > 1 else 3)

    def copy(kind, c, src, dst, who):
        return pltpu.make_async_remote_copy(
            src_ref=src, dst_ref=dst, send_sem=send.at[kind, c], recv_sem=recv.at[kind, c],
            device_id=who, device_id_type=MESH,
        )

    lo, hi = slice(0, q), slice(q, HR)
    A = lambda c: copy(0, c, g.at[lax.rem(c, slots), :, 1 - d], ra.at[c], sib)
    X0 = lambda c: copy(1, c, ra.at[c, fd, lo], rx.at[c, 0], tox)
    X1 = lambda c: copy(2, c, ra.at[c, fx, lo], rx.at[c, 1], tox)
    X2 = lambda c: copy(3, c, ra.at[c, fx, hi], rx.at[c, 2], tox)
    Y0 = lambda c: copy(4, c, ra.at[c, fd, hi], ry.at[c, 0], toy)
    Y2 = lambda c: copy(5, c, ra.at[c, fy, hi], ry.at[c, 2], toy)
    Y1 = lambda c: copy(6, c, ra.at[c, fy, lo], ry.at[c, 1], toy)
    ZU = lambda c: copy(7, c, ra.at[c, f], zlo.at[c], up)
    ZD = lambda c: copy(8, c, ra.at[c, f], zhi.at[c], down)
    TU = lambda c: copy(9, c, tot.at[c, d], tot.at[c, d], up)
    TD = lambda c: copy(10, c, tot.at[c, d], tot.at[c, d], down)
    D = lambda c: copy(11, c, tot.at[c, d], tot.at[c, d], sib)
    below, above = s < root, s > root
    spot = jnp.where(below, s, jnp.where(above, span - 1 - s, 0))
    far = jnp.abs(s - root)
    most = max(root, span - 1 - root)

    def stage(c, run):
        @pl.when((c >= 0) & (c < chunks))
        def _():
            run(c)

    def produce(c):
        slot = lax.rem(c, slots)

        @pl.when(c >= slots)
        def _():
            A(c - slots).wait_send()

        @pl.when(c < out_chunks)
        def _():
            r = c // (width // CHUNK)
            col = lax.rem(c, width // CHUNK) * CHUNK
            right = bg[:, pl.ds(pl.multiple_of(col, CHUNK), CHUNK)]
            for j in range(4):
                for h in range(2):
                    at = j * (inner // 4) + h * (inner // 8) + r * HR
                    left = gated[:, pl.ds(pl.multiple_of(at, HR), HR)]
                    g[slot, j, h] = dot(left, right, contract).astype(BF16)

        @pl.when((c >= out_chunks) & (c < last))
        def _():
            right = mixed[c - out_chunks]
            for j in range(4):
                t = dot(normed[:, j * 2 * HR : (j + 1) * 2 * HR], right, contract).astype(BF16)
                g[slot, j, 0] = t[:HR]
                g[slot, j, 1] = t[HR:]

        @pl.when(c == last)
        def _():
            for j in range(4):
                for h in range(2):
                    cols = slice(j * CHUNK, (j + 1) * CHUNK)
                    g[slot, j, h] = rest[h * HR : (h + 1) * HR, cols].astype(BF16)

        A(c).start()

    def first_sum(c):
        A(c).wait_recv()
        for j in range(4):
            own = g[lax.rem(c, slots), j, d]
            ra[c, j] = (ra[c, j].astype(F32) + own.astype(F32)).astype(BF16)
        X0(c).start()
        Y0(c).start()
        X1(c).start()
        Y2(c).start()

    def second_sum(c):
        X0(c).wait_recv()
        ra[c, fy, lo] = (ra[c, fy, lo].astype(F32) + rx[c, 0].astype(F32)).astype(BF16)
        Y1(c).start()
        Y0(c).wait_recv()
        ra[c, fx, hi] = (ra[c, fx, hi].astype(F32) + ry[c, 0].astype(F32)).astype(BF16)
        X2(c).start()

    def third_sum(c):
        X1(c).wait_recv()
        Y2(c).wait_recv()
        X2(c).wait_recv()
        Y1(c).wait_recv()
        for k, part in enumerate((lo, hi)):
            total = ra[c, f, part].astype(F32) + rx[c, 1 + k].astype(F32) + ry[c, 1 + k].astype(F32)
            ra[c, f, part] = total.astype(BF16)

    def inward(c):
        @pl.when(below & (s > 0))
        def _():
            ZU(c).wait_recv()
            ra[c, f] = (ra[c, f].astype(F32) + zlo[c].astype(F32)).astype(BF16)

        @pl.when(above & (s < span - 1))
        def _():
            ZD(c).wait_recv()
            ra[c, f] = (ra[c, f].astype(F32) + zhi[c].astype(F32)).astype(BF16)

        pl.when(below)(lambda: ZU(c).start())
        pl.when(above)(lambda: ZD(c).start())

    def at_root(c):
        total = ra[c, f].astype(F32)
        if root > 0:
            ZU(c).wait_recv()
            total = total + zlo[c].astype(F32)
        if span - 1 > root:
            ZD(c).wait_recv()
            total = total + zhi[c].astype(F32)
        tot[c, d] = total.astype(BF16)
        if root > 0:
            TD(c).start()
        if span - 1 > root:
            TU(c).start()
        D(c).start()

    def outward(c):
        @pl.when(above)
        def _():
            TU(c).wait_recv()
            pl.when(s < span - 1)(lambda: TU(c).start())

        @pl.when(below)
        def _():
            TD(c).wait_recv()
            pl.when(s > 0)(lambda: TD(c).start())

        D(c).start()

    tile = 2 * LANES

    def columns(t, size=tile):
        return pl.ds(pl.multiple_of(t * size, size), size)

    def back_block(b):
        c, slot = b // parts, lax.rem(b, 2)
        groups = ctx // GROUP
        first = lax.rem(b, parts) * CHUNK
        cuts = [pl.ds(pl.multiple_of(first + n, LANES), LANES) for n in range(0, CHUNK, LANES)]
        tiles = [slice(n, n + LANES) for n in range(0, CHUNK, LANES)]
        cols = pl.ds(pl.multiple_of(first, CHUNK), CHUNK)
        rates = [-jnp.exp(small[TAPS : TAPS + state, cut]) * LOG2E for cut in cuts]
        skip = small[TAPS + state + 2 : TAPS + state + 3, cols]
        held_copy(b).wait()

        def one(turn, carry):
            i = groups - 1 - turn
            at = c * groups + i
            tok = pl.ds(pl.multiple_of(at * GROUP, GROUP), GROUP)
            p, total, kept = (list(value) for value in carry)
            value, out, gain = u[tok, cols].astype(F32), dy[at, :, cols], delta[at, :, cols]
            v[...] = gain * value
            drive_parts, delta_parts = [[], []], [[], []]
            for pair in range(0, len(cuts), 2):
                which = range(pair, pair + 2)
                after = {n: held[slot, (i + 1) * GROUP, :, tiles[n]].astype(F32) for n in which}
                for half in (1, 0):
                    drives, deltas = ({n: [] for n in which} for _ in range(2))
                    for k in reversed(range(half * 8, half * 8 + 8)):
                        t = i * GROUP + k
                        b_in, read = bw[c, t], cw[c, t]
                        b_part = c_part = 0.0
                        for n in which:
                            row = lambda tile: jnp.broadcast_to(tile, (state, LANES))
                            step, back = row(delta[at, k : k + 1, cuts[n]]), row(dy[at, k : k + 1, cuts[n]])
                            grad = read * back + p[n]
                            p[n] = jnp.exp2(step * rates[n]) * grad
                            before = held[slot, t, :, tiles[n]].astype(F32)
                            w = p[n] * before
                            total[n] = total[n] + w * step
                            part = w * rates[n]
                            rows_sum(deltas[n], part[:8] + part[8:], False)
                            part = grad * b_in
                            rows_sum(drives[n], part[:8] + part[8:], False)
                            b_part = b_part + grad * row(v[k : k + 1, tiles[n]])
                            c_part = c_part + after[n] * back
                            after[n] = before
                        bacc[c * ctx + t] += b_part
                        cacc[c * ctx + t] += c_part
                    drive_parts[half] += [drives[n][0][1] for n in which]
                    delta_parts[half] += [deltas[n][0][1] for n in which]
            joined = lambda halves: jnp.concatenate([jnp.concatenate(h, 1) for h in halves], 0)
            drive_grad, delta_part = joined(drive_parts), joined(delta_parts)
            raw_grad = drive_grad * value + delta_part * (1.0 / LOG2E)
            raw_grad = raw_grad * sig[tok, cols].astype(F32)
            rl[tok, cols] = raw_grad.astype(BF16)
            dy[at, :, cols] = out * skip + drive_grad * gain
            kept[0] = kept[0] + (out * value)[:8] + (out * value)[8:]
            kept[1] = kept[1] + raw_grad[:8] + raw_grad[8:]
            return tuple(p), tuple(total), tuple(kept)

        zero = tuple(jnp.zeros((state, LANES), F32) for _ in cuts)
        none = jnp.zeros((8, CHUNK), F32)
        begin = tuple(final[c, :, cut] for cut in cuts)
        _, total, kept = lax.fori_loop(0, groups, one, (begin, zero, (none, none)))
        for n, cut in enumerate(cuts):
            logs[:, cut] += total[n]
        sums[0, :, cols] += kept[0]
        sums[1, :, cols] += kept[1]

        @pl.when(b + 2 < blocks)
        def _():
            held_copy(b + 2).start()

    def proj_work():
        step_grad = dot(rl[...], dt[...], across)
        col = lax.broadcasted_iota(jnp.int32, (state, LANES), 1)
        n = lax.broadcasted_iota(jnp.int32, (state, LANES), 0)
        ones = jnp.ones((LANES, LANES), BF16)

        def one(r, carry):
            tok = pl.ds(pl.multiple_of(r * GROUP, GROUP), GROUP)
            total = pg_full[tok]
            for ref, first in ((bacc, rank), (cacc, rank + state)):
                value = dot(ref[tok].reshape(GROUP * state, LANES).astype(BF16), ones)
                keep = jnp.where(col == n + first, value.reshape(GROUP, state, LANES), 0.0)
                total = total + jnp.sum(keep, 1)
            pg[tok] = total.astype(BF16)
            return carry

        pg_full[...] = jnp.concatenate([step_grad, jnp.zeros((rows, LANES - rank), F32)], 1)
        lax.fori_loop(0, rows // GROUP, one, 0)

    def weight_work():
        first = TAPS + state + 4
        used = rank + 2 * state

        def weights(t, carry):
            cols = columns(t)
            rest[first : first + rank, cols] = dot(step_low[...], rl[:, cols], contract)
            rest[first + rank : first + rank + used, cols] = dot(pg[...], u[:, cols], contract)[:used]
            kept = -logs[:, cols] * jnp.exp(small[TAPS : TAPS + state, cols])
            rest[TAPS : TAPS + state, cols] = kept
            at = TAPS + state
            rest[at + 1 : at + 2, cols] = jnp.sum(sums[1, :, cols], 0, keepdims=True)
            rest[at + 2 : at + 3, cols] = jnp.sum(sums[0, :, cols], 0, keepdims=True)
            return carry

        lax.fori_loop(0, inner // tile, weights, 0)

    def conv_work(first, count):
        def one(t, carry):
            cols = columns(t)
            shift = jnp.zeros((1, tile), F32)
            taps = [jnp.zeros((1, tile), F32) for _ in range(TAPS)]
            for c in range(seqs):
                tok = slice(c * ctx, (c + 1) * ctx)
                weight = xp[columns(t)]
                back = dot(pg[tok], weight, across)
                own = range(c * ctx // GROUP, (c + 1) * ctx // GROUP)
                grad = jnp.concatenate([dy[at, :, cols] for at in own], 0) + back
                grad = grad * slope[tok, cols].astype(F32)
                cg[c, :ctx, cols] = grad
                before = lead[c, :, cols].astype(F32)
                shift = shift + jnp.sum(grad, 0, keepdims=True)
                for k in range(TAPS):
                    at = GROUP - TAPS + 1 + k
                    taps[k] = taps[k] + jnp.sum(grad * before[at : at + ctx], 0, keepdims=True)
            for k in range(TAPS):
                rest[k : k + 1, cols] = taps[k]
            rest[TAPS + state : TAPS + state + 1, cols] = shift
            return carry

        lax.fori_loop(first, first + count, one, 0)

    edge = cg.shape[1] - ctx
    H = lambda: pltpu.make_async_remote_copy(
        src_ref=cg.at[:, :edge], dst_ref=cg.at[:, ctx:], send_sem=halo.at[0],
        recv_sem=halo.at[1], device_id=down, device_id_type=MESH,
    )

    def halo_send():
        pl.when(s > 0)(lambda: H().start())

    def stream_work():
        pl.when(s < span - 1)(lambda: H().wait_recv())

        def one(t, carry):
            cols = columns(t)
            for c in range(seqs):
                total = 0.0
                for k in range(TAPS):
                    at = TAPS - 1 - k
                    total = total + small[k : k + 1, cols] * cg[c, at : at + ctx, cols]
                half = pl.ds(pl.multiple_of(lax.rem(t, 2) * tile, tile), tile)
                mixed[parts + t // 2, c * ctx : (c + 1) * ctx, half] = total.astype(BF16)
            return carry

        lax.fori_loop(0, inner // tile, one, 0)
        pl.when(s > 0)(lambda: H().wait_send())

    def norm_work(first, count):
        def one(k, carry):
            in_copy(k).wait()
            ng[...] += dot(mixed[k], in_w[lax.rem(k, 2)], across)

            @pl.when(k + 2 < 2 * parts)
            def _():
                in_copy(k + 2).start()

            return carry

        if first == 0:
            ng[...] = jnp.zeros(ng.shape, F32)
        lax.fori_loop(first, first + count, one, 0)

    def input_work():
        share = width // 4
        at = TAPS + state + 3
        gain = jnp.concatenate(
            [small[at : at + 1, j * CHUNK : j * CHUNK + share] for j in range(4)], 1
        )

        def one(r, total):
            tok = pl.ds(pl.multiple_of(r * GROUP, GROUP), GROUP)
            xs = x[tok].astype(F32)
            inverse = lax.rsqrt(jnp.mean(xs * xs, -1, keepdims=True) + EPS)
            grad = ng[tok]
            scaled = grad * gain
            slope = jnp.mean(scaled * xs, -1, keepdims=True)
            out = inverse * scaled - xs * (inverse * inverse * inverse * slope)
            input_grad[tok] = (out + og[tok].astype(F32)).astype(BF16)
            return total + grad * (xs * inverse)

        total = lax.fori_loop(0, rows // GROUP, one, jnp.zeros((GROUP, width), F32))
        total = jnp.sum(total, 0, keepdims=True)
        for j in range(4):
            rest[at : at + 1, j * CHUNK : j * CHUNK + share] = total[:, j * share : (j + 1) * share]

    blocks = seqs * parts
    tiles = inner // tile
    pause = 3
    held_back = out_chunks + parts
    base = 1 + 2 * SLACK + 1

    def prepare():
        for ref in (cacc, bacc, logs, sums, rest):
            ref[...] = jnp.zeros(ref.shape, F32)
        for one in loads[2:]:
            one.wait()

    def blocks_work(i):
        pl.when(i == 0)(prepare)
        pl.when(i < blocks)(lambda: back_block(i))

    def late_work(i):
        at = held_back

        @pl.when(i == at)
        def _():
            proj_work()
            conv_work(0, tiles)
            halo_send()
            in_copy(0).start()
            in_copy(1).start()

        pl.when(i == at + 1)(weight_work)
        pl.when(i == at + 2)(stream_work)
        pl.when(i == at + 4)(lambda: norm_work(0, parts))
        pl.when(i == at + 5)(lambda: norm_work(parts, parts))
        pl.when(i == at + 6)(input_work)

    def step(i, carry):
        def at(offset):
            k = i - offset
            return jnp.where(k < held_back, k, jnp.where(k < held_back + pause, -1, k - pause))

        @pl.when(i == out_chunks)
        def _():
            for one in loads[:2]:
                one.wait()

        stage(at(0), produce)
        stage(at(1), first_sum)
        stage(at(1 + SLACK), second_sum)
        stage(at(1 + 2 * SLACK), third_sum)
        pl.when(s != root)(lambda: stage(at(base + SLACK * spot), inward))
        pl.when(s == root)(lambda: stage(at(base + SLACK * most), at_root))
        pl.when(s != root)(lambda: stage(at(base + SLACK * most + SLACK * far), outward))
        blocks_work(i)
        late_work(i)
        return carry

    lax.fori_loop(0, chunks + pause + base + 2 * SLACK * most + 1, step, 0)

    def finish(c, carry):
        pl.when(c >= chunks - slots)(lambda: A(c).wait_send())
        for t in (X0, X1, X2, Y0, Y1, Y2):
            t(c).wait_send()
        pl.when(below)(lambda: ZU(c).wait_send())
        pl.when(above)(lambda: ZD(c).wait_send())
        if root > 0:
            pl.when((s <= root) & (s > 0))(lambda: TD(c).wait_send())
        if span - 1 > root:
            pl.when((s >= root) & (s < span - 1))(lambda: TU(c).wait_send())
        D(c).wait_send()
        D(c).wait_recv()
        return carry

    lax.fori_loop(0, chunks, finish, 0)
    copies = []
    for c in range(chunks):
        for h in range(2):
            if c < out_chunks:
                r, col = c // (width // CHUNK), c % (width // CHUNK)
                first = h * (inner // 8) + r * HR
                to = out_sum.at[first : first + HR, col * CHUNK : (col + 1) * CHUNK]
            elif c < last:
                col = (c - out_chunks + parts) % (2 * parts)
                to = in_sum.at[h * HR : (h + 1) * HR, col * CHUNK : (col + 1) * CHUNK]
            else:
                to = rest_sum.at[h * HR : (h + 1) * HR]
            copies.append(pltpu.make_async_copy(tot.at[c, h], to, local.at[c, h]))
    for one in copies:
        one.start()
    for one in copies:
        one.wait()


def back(gated, bg, step_low, final, small, x, og, far):
    rows, inner = gated.shape
    width = x.shape[1]
    seqs, state = final.shape[:2]
    ctx, rank, parts = rows // seqs, step_low.shape[1], inner // CHUNK
    span = lax.axis_size("seq")
    out_chunks, in_chunks = 2 * width // CHUNK, 2 * parts
    n = out_chunks + in_chunks + 1
    vmem, dma = pltpu.VMEM, pltpu.SemaphoreType.DMA
    anywhere = pl.BlockSpec(memory_space=pl.ANY)
    whole = pl.BlockSpec(memory_space=vmem)
    shape = jax.ShapeDtypeStruct
    like = lambda v: vmem(v.shape, v.dtype)
    (held, normed, lead, slope, u, sig, delta, bw, cw, dy, zg, in_full, xp, dt) = far
    return pl.pallas_call(
        functools.partial(back_kernel, span, state, rank),
        in_specs=[whole] * 7 + [anywhere] * len(far),
        out_specs=[whole, anywhere, anywhere, anywhere],
        out_shape=[
            shape((rows, width), BF16),
            shape((inner // 4, width), BF16),
            shape((width // 4, 2 * inner), BF16),
            shape((2 * HR, CHUNK), BF16),
        ],
        scratch_shapes=[
            *map(like, (normed, lead, slope, u, sig, delta, bw, cw, dy)),
            vmem((in_chunks, rows, CHUNK), BF16),
            like(xp),
            like(dt),
            vmem((2, width, CHUNK), BF16),
            vmem((2,) + held.shape[1:], BF16),
            vmem((GROUP, CHUNK), F32),
            vmem((rows, inner), BF16),
            vmem((rows, state, LANES), F32),
            vmem((rows, state, LANES), F32),
            vmem((state, inner), F32),
            vmem((2, 8, inner), F32),
            vmem((rows, LANES), BF16),
            vmem((rows, LANES), F32),
            vmem((seqs, ctx + 8, inner), F32),
            vmem((rows, width), F32),
            vmem((2 * HR, inner), F32),
            vmem((4, 4, 2, HR, CHUNK), BF16),
            vmem((n, 4, HR, CHUNK), BF16),
            vmem((n, 3, HR // 2, CHUNK), BF16),
            vmem((n, 3, HR // 2, CHUNK), BF16),
            vmem((n, HR, CHUNK), BF16),
            vmem((n, HR, CHUNK), BF16),
            vmem((n, 2, HR, CHUNK), BF16),
            dma((12, n)),
            dma((12, n)),
            dma((2,)),
            dma((n, 2)),
            dma((12,)),
            dma((2,)),
            dma((2,)),
        ],
        compiler_params=pltpu.CompilerParams(
            collective_id=1, has_side_effects=True, vmem_limit_bytes=63 << 20
        ),
        name="back",
    )(gated, bg, step_low, final, small, x, og, *far)


def finish_kernel(state, rank, used, in_sum, out_sum, rest, gain, in_w, taps, cbias, xp, dt, dbias, logs, skip, out_w):
    in_w[...] = in_sum[...].astype(F32)
    out_w[...] = out_sum[...].astype(F32)
    at = TAPS + state
    row = lambda first, count=1: rest[...].astype(F32)[first : first + count]
    taps[...] = row(0, TAPS)
    logs[...] = row(TAPS, state)
    cbias[...] = row(at)
    dbias[...] = row(at + 1)
    skip[...] = row(at + 2)
    gain[...] = row(at + 3)[:, : gain.shape[1]]
    dt[...] = row(at + 4, rank)
    xp[...] = row(at + 4 + rank, used).T


def finish(in_sum, out_sum, rest, state, rank, used):
    steps = 4
    share = rest.shape[1]
    tall = lambda v: pl.BlockSpec((v.shape[0] // steps, v.shape[1]), lambda i: (i, 0))
    fixed = lambda *v: pl.BlockSpec(v, lambda i: (0, 0))
    small = [(1, in_sum.shape[0]), (TAPS, share), (1, share), (share, used), (rank, share)]
    small += [(1, share), (state, share), (1, share)]
    shape = lambda v: jax.ShapeDtypeStruct(v, F32)
    return pl.pallas_call(
        functools.partial(finish_kernel, state, rank, used),
        grid=(steps,),
        in_specs=[tall(in_sum), tall(out_sum), fixed(*rest.shape)],
        out_specs=[fixed(*small[0]), tall(in_sum)] + [fixed(*v) for v in small[1:]] + [tall(out_sum)],
        out_shape=[shape(small[0]), shape(in_sum.shape)]
        + [shape(v) for v in small[1:]]
        + [shape(out_sum.shape)],
        compiler_params=pltpu.CompilerParams(vmem_limit_bytes=32 << 20),
        name="finish",
    )(in_sum, out_sum, rest)


def body(
    hidden_in, lengths, norm_gain, in_weight, conv_weight, conv_bias, xproj_weight,
    dt_weight, dt_bias, a_log, skip_gain, out_weight, out_grad,
):
    seqs, ctx, width = hidden_in.shape
    taps, share = conv_weight.shape
    state = a_log.shape[0]
    rank = dt_weight.shape[0]
    rows = ctx * seqs
    row = lambda v: v.reshape(1, -1)
    x, og = hidden_in.reshape(rows, width), out_grad.reshape(rows, width)
    used = xproj_weight.shape[1]
    xp_own = jnp.pad(xproj_weight, ((0, 0), (0, LANES - used)))
    (
        hidden_out, step_low, final, held, normed, branch_grad, lead, slope, u, sig, delta,
        b_wide, c_wide, y_grad, gated, z_grad, in_matrix, proj_matrix, step_matrix, small,
    ) = front(
        x, og, lengths, conv_weight, a_log, row(conv_bias), row(dt_bias), row(skip_gain),
        row(norm_gain), in_weight, out_weight, xp_own, dt_weight, seqs,
    )
    far = (
        held, normed, lead, slope, u, sig, delta, b_wide, c_wide, y_grad, z_grad, in_matrix,
        proj_matrix, step_matrix,
    )
    input_grad, out_sum, in_sum, rest = back(
        gated, branch_grad, step_low, final, small, x, og, far
    )
    gain, in_w, taps_grad, cbias, proj_w, step_w, dbias, logs, skip, out_w = finish(
        in_sum, out_sum, rest, state, rank, used
    )
    flat = lambda v: v.reshape(-1)
    return (
        hidden_out.reshape(seqs, ctx, width), input_grad.reshape(seqs, ctx, width), flat(gain), in_w,
        taps_grad, flat(cbias), proj_w, step_w, flat(dbias), logs, flat(skip), out_w,
    )


def solution(mesh):
    tokens = P(("dp", "fsdp"), "seq", None)
    return jax.shard_map(
        body,
        mesh=mesh,
        in_specs=(
            tokens, P(("dp", "fsdp")), P("fsdp"), P("fsdp", None), P(None, "fsdp"), P("fsdp"),
            P("fsdp", None), P(None, "fsdp"), P("fsdp"), P(None, "fsdp"), P("fsdp"),
            P("fsdp", None), tokens,
        ),
        out_specs=(
            tokens, tokens, P("fsdp"), P("fsdp", None), P(None, "fsdp"), P("fsdp"),
            P("fsdp", None), P(None, "fsdp"), P("fsdp"), P(None, "fsdp"), P("fsdp"),
            P("fsdp", None),
        ),
        check_vma=False,
    )
```

```python
import functools
import math

import jax
import jax.numpy as jnp
import numpy as np
from jax import lax
from jax.experimental import pallas as pl
from jax.experimental.pallas import tpu as pltpu
from jax.sharding import PartitionSpec as P

EPS = 1e-05
LOG2E = math.log2(math.e)
LANES = 128
GROUP = 16
F32 = jnp.float32
BF16 = jnp.bfloat16
MESH = pl.DeviceIdType.MESH
HR = 128
CHUNK = 512
SLACK = 2
TAPS = 4
HELD = 3


def silu_parts(v):
    s = jax.nn.sigmoid(v)
    return v * s, s * (1.0 + v * (1.0 - s))


def rows_sum(stack, value, rising):
    row = lax.broadcasted_iota(jnp.int32, value.shape, 0)
    level = 0
    while stack and stack[-1][0] == level:
        _, other = stack.pop()
        first, second = (other, value) if rising else (value, other)
        low = (row & (1 << level)) == 0
        turned = pltpu.roll(jnp.where(low, second, first), 1 << level, 0)
        value = jnp.where(low, first, second) + turned
        level += 1
    stack.append((level, value))


def front_kernel(
    span,
    x, og, lengths, taps_own, log_own, cbias_own, dbias_own, skip_own, gain_own,
    in_own, out_own, xp_own, dt_own,
    hidden_out, step_low, final,
    held_all, normed_full, bg_full, lead_full, slope_full, u_full, sig_full, delta_full, bw_full,
    cw_full, dy_full, gated_full, zg_full, in_full, xp_full, dt_full, small_full,
    in_w, out_w, xp, dt, small, small_own, hx, acc, zacc, normed, v, proj, ends, sums,
    ends_in, sums_in, bg, mask, lead, slope, u, sig, delta, bw, cw, gg, dy, y, gated, zg,
    start, held,
    send, recv, halo, relay_send, relay_recv, sums_send, sums_recv, local, keep, held_sem,
):
    d, s, f = (lax.axis_index(a) for a in ("dp", "seq", "fsdp"))
    fx, fy, fd = f ^ 1, f ^ 2, f ^ 3
    tox, toy, tod, sib = {"fsdp": fx}, {"fsdp": fy}, {"fsdp": fd}, {"dp": 1 - d}
    rows, width = x.shape
    inner = u.shape[1]
    seqs = bw.shape[0]
    ctx = rows // seqs
    state, rank = log_own.shape[0], dt_own.shape[0]
    groups = ctx // GROUP
    share = inner // 4
    at_bias = state + TAPS
    across = (((1,), (1,)), ((), ()))
    dot = lambda a, b, dims=(((1,), (0,)), ((), ())): lax.dot_general(
        a, b, dims, preferred_element_type=F32
    )

    for c in range(seqs):
        hx[c] = jnp.zeros((GROUP, width), BF16)
    barrier = pltpu.get_barrier_semaphore()
    for who in (tox, toy, tod, sib):
        pl.semaphore_signal(barrier, inc=1, device_id=who, device_id_type=MESH)

    def greet(o, carry):
        who = {"seq": lax.rem(s + o, span)}
        pl.semaphore_signal(barrier, inc=1, device_id=who, device_id_type=MESH)
        return carry

    lax.fori_loop(1, span, greet, 0)
    small_own[...] = jnp.zeros(small_own.shape, F32)
    small_own[:state] = log_own[...]
    small_own[state:at_bias] = taps_own[...]
    small_own[at_bias : at_bias + 1] = cbias_own[...]
    small_own[at_bias + 1 : at_bias + 2] = dbias_own[...]
    small_own[at_bias + 2 : at_bias + 3] = skip_own[...]
    small_own[at_bias + 3 : at_bias + 4, : width // 4] = gain_own[...]
    pl.semaphore_wait(barrier, 3 + span)

    SMALL, STREAM, PROJ, STEP, GATE, OUT = range(6)
    plan = (
        (small_own, small, 1, None),
        (in_own, in_w, 0, (0, inner)),
        (xp_own, xp, 0, None),
        (dt_own, dt, 1, None),
        (in_own, in_w, 0, (inner, 2 * inner)),
        (out_own, out_w, 0, None),
    )

    def window(p, owner, half, q):
        src, dst, dim, cols = plan[p]
        high, wide = src.shape
        part = high // 4
        at = (half * 2 + q) * part
        lo, hi = cols or (0, wide)
        if dim == 0:
            return dst.at[pl.ds(pl.multiple_of(owner * high + at, part), part), lo:hi]
        col = pl.ds(pl.multiple_of(owner * wide, wide), wide)
        return dst.at[pl.ds(pl.multiple_of(at, part), part), col]

    def own(p, half, q):
        src, _, _, cols = plan[p]
        high, wide = src.shape
        part = high // 4
        lo, hi = cols or (0, wide)
        return src.at[pl.ds(pl.multiple_of((half * 2 + q) * part, part), part), lo:hi]

    def copy(src, dst, p, kind, who):
        return pltpu.make_async_remote_copy(
            src_ref=src, dst_ref=dst, send_sem=send.at[p, kind], recv_sem=recv.at[p, kind],
            device_id=who, device_id_type=MESH,
        )

    started = []

    def go(one):
        one.start()
        started.append(one)

    def start_own(p, routed=False):
        for q in (0, 1):
            go(copy(own(p, d, q), window(p, f, d, q), p, q, tox))
            go(copy(own(p, d, 1 - q), window(p, f, d, 1 - q), p, 3 - q, toy))
        if routed:
            for q in (0, 1):
                go(copy(own(p, d, q), window(p, f, d, q), p, 4 + q, tod))

    def small_copy(at, owner, part, who):
        rows_of = slice(*((state, at_bias + 4), (0, state))[part])
        cols = pl.ds(pl.multiple_of(owner * share, share), share)
        return pltpu.make_async_remote_copy(
            src_ref=small_own.at[rows_of], dst_ref=small.at[rows_of, cols],
            send_sem=send.at[SMALL, 3 * part + at], recv_sem=recv.at[SMALL, 3 * part + at],
            device_id=who, device_id_type=MESH,
        )

    def small_start(part):
        for at, who in enumerate((tox, toy, tod)):
            go(small_copy(at, f, part, who))

    def small_ready(part):
        for at, owner in enumerate((fx, fy, fd)):
            small_copy(at, owner, part, sib).wait_recv()

    def place_own(p):
        for half in (0, 1):
            for q in (0, 1):
                pltpu.make_async_copy(
                    own(p, half, q), window(p, f, half, q), local.at[p, half * 2 + q]
                ).start()

    def own_ready(p):
        for half in (0, 1):
            for q in (0, 1):
                pltpu.make_async_copy(
                    own(p, half, q), window(p, f, half, q), local.at[p, half * 2 + q]
                ).wait()

    def arrived(p, kind, owner, half, q):
        w = window(p, owner, half, q)
        copy(w, w, p, kind, sib).wait_recv()
        return w

    near = ((0, fx, 0), (3, fy, 1), (1, fx, 1), (2, fy, 0))
    diagonal = ((4, fd, 0), (5, fd, 1))

    def serve_near(p, routed=False):
        for kind, owner, q in near:
            w = arrived(p, kind, owner, d, q)
            if kind == 0 and not routed:
                go(copy(w, w, p, 4, toy))
            if kind == 3 and not routed:
                go(copy(w, w, p, 5, tox))
            go(copy(w, w, p, 6 + kind, sib))

    def serve_far(p):
        for kind, owner, q in diagonal:
            w = arrived(p, kind, owner, d, q)
            go(copy(w, w, p, 6 + kind, sib))

    def near_ready(p):
        for kind, owner, q in near:
            arrived(p, 6 + kind, owner, 1 - d, q)

    def far_ready(p):
        for kind, owner, q in diagonal:
            arrived(p, 6 + kind, owner, 1 - d, q)

    small_start(0)
    start_own(STREAM)
    for p in (STREAM, PROJ, STEP, GATE, OUT):
        place_own(p)
    pltpu.make_async_copy(
        small_own, small.at[:, pl.ds(pl.multiple_of(f * share, share), share)], local.at[SMALL, 0]
    ).start()
    def edges(c):
        return pltpu.make_async_remote_copy(
            src_ref=x.at[(c + 1) * ctx - GROUP : (c + 1) * ctx], dst_ref=hx.at[c],
            send_sem=halo.at[0, c], recv_sem=halo.at[1, c],
            device_id={"seq": jnp.minimum(s + 1, span - 1)}, device_id_type=MESH,
        )

    @pl.when(s < span - 1)
    def _():
        for c in range(seqs):
            edges(c).start()

    for c in range(seqs):
        t = s * ctx + lax.broadcasted_iota(jnp.int32, (ctx, LANES), 0)
        mask[c * ctx : (c + 1) * ctx] = (t < lengths[c]).astype(F32)

    def mask_step(r, carry):
        tok = pl.ds(pl.multiple_of(r * GROUP, GROUP), GROUP)
        held = jnp.concatenate([mask[tok]] * (width // LANES), 1)
        bg[tok] = (og[tok].astype(F32) * held).astype(BF16)
        return carry

    lax.fori_loop(0, rows // GROUP, mask_step, 0)

    pltpu.make_async_copy(
        small_own, small.at[:, pl.ds(pl.multiple_of(f * share, share), share)], local.at[SMALL, 0]
    ).wait()
    small_ready(0)

    @pl.when(s > 0)
    def _():
        for c in range(seqs):
            edges(c).wait_recv()

    gain_at = at_bias + 3
    gain = jnp.concatenate(
        [small[gain_at : gain_at + 1, j * share : j * share + width // 4] for j in range(4)], 1
    )

    def normalised(v):
        v = v.astype(F32)
        inverse = lax.rsqrt(jnp.mean(v * v, -1, keepdims=True) + EPS)
        return (v * inverse * gain).astype(BF16)

    def norm_step(r, carry):
        tok = pl.ds(pl.multiple_of(r * GROUP, GROUP), GROUP)
        normed[tok] = normalised(x[tok])
        return carry

    lax.fori_loop(0, rows // GROUP, norm_step, 0)
    for c in range(seqs):
        normed[rows + c * GROUP : rows + (c + 1) * GROUP] = normalised(hx[c])

    def project(total, high, first, owner, fresh):
        shard = pl.ds(pl.multiple_of(owner * (width // 4), width // 4), width // 4)
        left = normed[:high, shard]

        def one(t, carry):
            cols = pl.ds(pl.multiple_of(t * CHUNK, CHUNK), CHUNK)
            right = in_w[shard, pl.ds(pl.multiple_of(first + t * CHUNK, CHUNK), CHUNK)]
            part = dot(left, right)
            total[:, cols] = part if fresh else total[:, cols] + part
            return carry

        lax.fori_loop(0, inner // CHUNK, one, 0)

    tall = rows + seqs * GROUP
    own_ready(STREAM)
    project(acc, tall, 0, f, True)
    serve_near(STREAM)
    small_start(1)
    start_own(PROJ, True)
    start_own(STEP, True)
    start_own(GATE)
    near_ready(STREAM)
    project(acc, tall, 0, fx, False)
    project(acc, tall, 0, fy, False)
    serve_far(STREAM)
    far_ready(STREAM)
    project(acc, tall, 0, fd, False)
    small_ready(1)

    tile = 2 * LANES

    def columns(t, size=tile):
        return pl.ds(pl.multiple_of(t * size, size), size)

    def conv_step(t, carry):
        cols = columns(t)
        for c in range(seqs):
            before = acc[rows + c * GROUP : rows + (c + 1) * GROUP, cols].astype(BF16)
            stream = acc[c * ctx : (c + 1) * ctx, cols].astype(BF16)
            lead[c, :GROUP, cols] = before
            lead[c, GROUP:, cols] = stream
            held = jnp.concatenate([before, stream], 0).astype(F32)
            total = small[at_bias : at_bias + 1, cols]
            for k in range(TAPS):
                at = GROUP - TAPS + 1 + k
                total = total + small[state + k : state + k + 1, cols] * held[at : at + ctx]
            value, grad = silu_parts(total)
            slope[c * ctx : (c + 1) * ctx, cols] = grad.astype(BF16)
            u[c * ctx : (c + 1) * ctx, cols] = value.astype(BF16)
        return carry

    lax.fori_loop(0, inner // tile, conv_step, 0)
    for p in (PROJ, STEP):
        serve_near(p, True)
        serve_far(p)
    for p in (PROJ, STEP):
        near_ready(p)
        far_ready(p)
        own_ready(p)
    proj[...] = dot(u[...], xp[...])
    step_low[...] = proj[:, :rank].astype(BF16)

    def wide_step(i, carry):
        tok = pl.ds(pl.multiple_of(i * GROUP, GROUP), GROUP)
        held = proj[tok]
        for ref, first in ((bw, rank), (cw, rank + state)):
            value = held[:, first : first + state]
            c, at = i // groups, lax.rem(i, groups)
            ref[c, pl.ds(pl.multiple_of(at * GROUP, GROUP), GROUP)] = jnp.broadcast_to(
                value[:, :, None], (GROUP, state, LANES)
            )
        return carry

    lax.fori_loop(0, rows // GROUP, wide_step, 0)
    def delta_step(t, carry):
        cols = columns(t)
        for c in range(seqs):
            tok = slice(c * ctx, (c + 1) * ctx)
            value = dot(step_low[tok], dt[:, cols]) + small[at_bias + 1 : at_bias + 2, cols]
            sig[tok, cols] = jax.nn.sigmoid(value).astype(BF16)
            value = jnp.maximum(value, 0.0) + jnp.log1p(jnp.exp(-jnp.abs(value)))
            for i in range(groups):
                delta[c * groups + i, :, cols] = value[i * GROUP : (i + 1) * GROUP]
            sums[c : c + 1, cols] = jnp.sum(value, 0, keepdims=True)
            value = value * u[tok, cols].astype(F32)
            for i in range(groups):
                v[c * groups + i, :, cols] = value[i * GROUP : (i + 1) * GROUP]
        return carry

    sums[...] = jnp.zeros(sums.shape, F32)
    lax.fori_loop(0, inner // tile, delta_step, 0)

    def sums_copy(j):
        return pltpu.make_async_remote_copy(
            src_ref=sums, dst_ref=sums_in.at[s], send_sem=sums_send.at[j],
            recv_sem=sums_recv.at[s], device_id={"seq": j}, device_id_type=MESH,
        )

    def sums_start(o, carry):
        sums_copy(lax.rem(s + o, span)).start()
        return carry

    lax.fori_loop(1, span, sums_start, 0)

    def ends_copy(j, way, c):
        return pltpu.make_async_remote_copy(
            src_ref=ends.at[way, c], dst_ref=ends_in.at[s, c], send_sem=relay_send.at[j, c],
            recv_sem=relay_recv.at[s, c], device_id={"seq": j}, device_id_type=MESH,
        )

    def ends_start(first, count, way, c):
        def one(j, carry):
            ends_copy(j, way, c).start()
            return carry

        lax.fori_loop(first, count, one, 0)

    def forward_ends(c):
        for j in range(0, inner, CHUNK):
            cuts = [slice(j + i, j + i + LANES) for i in range(0, CHUNK, LANES)]
            rates = [-jnp.exp(small[:state, cut]) * LOG2E for cut in cuts]

            def one(i, h):
                h = list(h)
                for k in range(GROUP):
                    b = bw[c, i * GROUP + k]
                    for n, cut in enumerate(cuts):
                        step = delta[c * groups + i, k : k + 1, cut]
                        factor = jnp.exp2(jnp.broadcast_to(step, (state, LANES)) * rates[n])
                        row = jnp.broadcast_to(v[c * groups + i, k : k + 1, cut], (state, LANES))
                        h[n] = factor * h[n] + row * b
                return tuple(h)

            zero = tuple(jnp.zeros((state, LANES), F32) for _ in cuts)
            h = lax.fori_loop(0, groups, one, zero)
            for n, cut in enumerate(cuts):
                ends[0, c, :, cut] = h[n].astype(BF16)

    def backward_ends(c):
        for j in range(0, inner, CHUNK):
            cuts = [slice(j + i, j + i + LANES) for i in range(0, CHUNK, LANES)]
            rates = [-jnp.exp(small[:state, cut]) * LOG2E for cut in cuts]

            def one(i, carry):
                run, p = (list(value) for value in carry)
                for k in range(GROUP):
                    read = cw[c, i * GROUP + k]
                    for n, cut in enumerate(cuts):
                        step = delta[c * groups + i, k : k + 1, cut]
                        factor = jnp.exp2(jnp.broadcast_to(step, (state, LANES)) * rates[n])
                        row = dy[c * groups + i, k : k + 1, cut]
                        run[n] = run[n] * factor
                        p[n] = p[n] + run[n] * (read * jnp.broadcast_to(row, (state, LANES)))
                return tuple(run), tuple(p)

            one_s = tuple(jnp.ones((state, LANES), F32) for _ in cuts)
            zero = tuple(jnp.zeros((state, LANES), F32) for _ in cuts)
            _, p = lax.fori_loop(0, groups, one, (one_s, zero))
            for n, cut in enumerate(cuts):
                ends[1, c, :, cut] = p[n].astype(BF16)

    def stash(*pairs):
        for at, (src, dst) in pairs:
            one = pltpu.make_async_copy(src, dst, keep.at[at])
            one.start()
            kept.append(one)

    kept = []
    stash(
        (0, (normed.at[:rows], normed_full)), (1, (bg, bg_full)), (2, (lead, lead_full)),
        (3, (slope, slope_full)), (4, (u, u_full)), (5, (sig, sig_full)), (6, (delta, delta_full)),
        (7, (cw, cw_full)), (8, (xp, xp_full)), (9, (dt, dt_full)), (10, (small, small_full)),
        (15, (bw, bw_full)),
    )

    def ends_wait(j, c):
        pltpu.make_async_remote_copy(
            src_ref=ends.at[0, c], dst_ref=ends_in.at[j, c], send_sem=relay_send.at[j, c],
            recv_sem=relay_recv.at[j, c], device_id={"seq": j}, device_id_type=MESH,
        ).wait_recv()

    def join(ref, j, c):
        ends_wait(j, c)

        def one(t, carry):
            cols = columns(t, CHUNK)
            rates = -jnp.exp(small[:state, cols]) * LOG2E
            decay = jnp.exp2(sums_in[j, c : c + 1, cols] * rates)
            ref[c, :, cols] = decay * ref[c, :, cols] + ends_in[j, c, :, cols].astype(F32)
            return carry

        lax.fori_loop(0, inner // CHUNK, one, 0)

    def join_start(c):
        def one(j, carry):
            join(start, j, c)
            return carry

        lax.fori_loop(0, s, one, 0)

    def join_final(o, carry):
        for c in range(seqs):
            join(final, span - 1 - o, c)
        return carry

    def sums_wait(o, carry):
        j = lax.rem(s + o, span)
        pltpu.make_async_remote_copy(
            src_ref=sums, dst_ref=sums_in.at[j], send_sem=sums_send.at[j],
            recv_sem=sums_recv.at[j], device_id={"seq": j}, device_id_type=MESH,
        ).wait_recv()
        return carry

    parts = inner // CHUNK
    blocks = seqs * parts

    def held_copy(b):
        slot = lax.rem(b, HELD)
        return pltpu.make_async_copy(held.at[slot], held_all.at[b], held_sem.at[slot])

    def sweep_block(b, carry):
        c, slot = b // parts, lax.rem(b, HELD)
        first = lax.rem(b, parts) * CHUNK
        cuts = [pl.ds(pl.multiple_of(first + n, LANES), LANES) for n in range(0, CHUNK, LANES)]
        tiles = [slice(n, n + LANES) for n in range(0, CHUNK, LANES)]
        all_cols = pl.ds(pl.multiple_of(first, CHUNK), CHUNK)
        rates = [-jnp.exp(small[:state, cut]) * LOG2E for cut in cuts]
        skip = small[at_bias + 2 : at_bias + 3, all_cols]

        @pl.when(b >= HELD)
        def _():
            held_copy(b - HELD).wait()

        h = tuple(start[c, :, cut] for cut in cuts)
        for n, cut in enumerate(tiles):
            held[slot, 0, :, cut] = h[n].astype(BF16)

        def one(i, h):
            h = list(h)
            g = c * groups + i
            for first_row in range(0, GROUP, 8):
                stacks = [[] for _ in cuts]
                for k in range(first_row, first_row + 8):
                    b_in, read = bw[c, i * GROUP + k], cw[c, i * GROUP + k]
                    for n, cut in enumerate(cuts):
                        step = jnp.broadcast_to(delta[g, k : k + 1, cut], (state, LANES))
                        row = jnp.broadcast_to(v[g, k : k + 1, cut], (state, LANES))
                        h[n] = jnp.exp2(step * rates[n]) * h[n] + row * b_in
                        held[slot, i * GROUP + k + 1, :, tiles[n]] = h[n].astype(BF16)
                        part = h[n] * read
                        rows_sum(stacks[n], part[:8] + part[8:], True)
                for n, cut in enumerate(cuts):
                    y[g, first_row : first_row + 8, cut] = stacks[n][0][1]
            tok = pl.ds(pl.multiple_of(g * GROUP, GROUP), GROUP)
            y[g, :, all_cols] += skip * u[tok, all_cols].astype(F32)
            return tuple(h)

        lax.fori_loop(0, groups, one, h)
        held_copy(b).start()
        return carry

    def grad_part(owner):
        shard = pl.ds(pl.multiple_of(owner * share, share), share)
        gg[:, shard] = dot(bg[...], out_w[shard], across)

    forward_ends(0)
    ends_start(s + 1, span, 0, 0)
    serve_near(GATE)
    start_own(OUT)
    own_ready(GATE)
    forward_ends(1)
    ends_start(s + 1, span, 0, 1)
    lax.fori_loop(1, span, sums_wait, 0)
    start[...] = jnp.zeros(start.shape, F32)
    join_start(0)
    serve_far(GATE)
    lax.fori_loop(0, parts // 2, sweep_block, 0)
    near_ready(GATE)
    far_ready(GATE)
    stash((11, (in_w, in_full)))

    def gate_project(t, carry):
        cols = columns(t, CHUNK)
        right = in_w[:, pl.ds(pl.multiple_of(inner + t * CHUNK, CHUNK), CHUNK)]
        zacc[:, cols] = dot(normed[:rows], right)
        return carry

    lax.fori_loop(0, parts, gate_project, 0)
    serve_near(OUT)
    lax.fori_loop(parts // 2, parts, sweep_block, 0)
    serve_far(OUT)
    own_ready(OUT)
    near_ready(OUT)
    for owner in (f, fx, fy):
        grad_part(owner)
    far_ready(OUT)
    grad_part(fd)

    def gate_step(t, carry):
        cols = columns(t)
        for c in range(seqs):
            tok = slice(c * ctx, (c + 1) * ctx)
            value, grad = silu_parts(zacc[tok, cols].astype(BF16).astype(F32))
            pieces = [y[c * groups + i, :, cols] for i in range(groups)]
            scanned = jnp.concatenate(pieces, 0)
            gated[tok, cols] = (scanned * value).astype(BF16)
            half = pl.ds(pl.multiple_of(lax.rem(t, 2) * tile, tile), tile)
            zg[t // 2, tok, half] = (gg[tok, cols] * scanned * grad).astype(BF16)
        return carry

    def back_step(t, carry):
        cols = columns(t)
        for c in range(seqs):
            tok = slice(c * ctx, (c + 1) * ctx)
            value = zacc[tok, cols].astype(BF16).astype(F32)
            value = gg[tok, cols] * (value * jax.nn.sigmoid(value))
            for i in range(groups):
                dy[c * groups + i, :, cols] = value[i * GROUP : (i + 1) * GROUP]
        return carry

    lax.fori_loop(0, inner // tile, back_step, 0)
    stash((12, (dy, dy_full)))
    for c in range(seqs):
        backward_ends(c)
        ends_start(0, s, 1, c)
    for c in range(1, seqs):
        join_start(c)
    lax.fori_loop(parts, blocks, sweep_block, 0)
    lax.fori_loop(0, inner // tile, gate_step, 0)
    stash((13, (gated, gated_full)), (14, (zg, zg_full)))

    def hidden_step(t, carry):
        cols = columns(t)
        keep_rows = jnp.concatenate([mask[...]] * (tile // LANES), 1)
        branch = dot(gated[...], out_w[:, cols])
        hidden_out[:, cols] = (x[:, cols].astype(F32) + keep_rows * branch).astype(BF16)
        return carry

    lax.fori_loop(0, width // tile, hidden_step, 0)
    final[...] = jnp.zeros(final.shape, F32)
    lax.fori_loop(0, span - 1 - s, join_final, 0)

    for one in started:
        one.wait_send()

    @pl.when(s < span - 1)
    def _():
        for c in range(seqs):
            edges(c).wait_send()

    def sent(o, carry):
        j = lax.rem(s + o, span)
        sums_copy(j).wait_send()
        for c in range(seqs):
            ends_copy(j, 0, c).wait_send()
        return carry

    lax.fori_loop(1, span, sent, 0)
    for one in kept:
        one.wait()
    for b in range(max(blocks - HELD, 0), blocks):
        held_copy(b).wait()


def front(x, og, lengths, taps, logs, cbias, dbias, skip, gain, in_own, out_own, xp_own, dt_own, seqs):
    rows, width = x.shape
    share, inner = taps.shape[1], 4 * taps.shape[1]
    state, rank, used = logs.shape[0], dt_own.shape[0], xp_own.shape[1]
    ctx = rows // seqs
    span = lax.axis_size("seq")
    parts = inner // CHUNK
    vmem, dma = pltpu.VMEM, pltpu.SemaphoreType.DMA
    whole, anywhere = pl.BlockSpec(memory_space=vmem), pl.BlockSpec(memory_space=pl.ANY)
    shape = jax.ShapeDtypeStruct
    grouped = (rows // GROUP, GROUP, inner)
    kept = [
        ((rows, width), BF16),
        ((rows, width), BF16),
        ((seqs, ctx + GROUP, inner), BF16),
        ((rows, inner), BF16),
        ((rows, inner), BF16),
        ((rows, inner), BF16),
        (grouped, F32),
        ((seqs, ctx, state, LANES), F32),
        ((seqs, ctx, state, LANES), F32),
        (grouped, F32),
        ((rows, inner), BF16),
        ((parts, rows, CHUNK), BF16),
        ((width, 2 * inner), BF16),
        ((inner, used), BF16),
        ((rank, inner), BF16),
        ((32, inner), F32),
    ]
    held = (ctx + 1, state, CHUNK)
    return pl.pallas_call(
        functools.partial(front_kernel, span),
        in_specs=[whole, whole, pl.BlockSpec(memory_space=pltpu.SMEM)]
        + [whole] * 6
        + [anywhere] * 4,
        out_specs=[whole] * 3 + [anywhere] * (1 + len(kept)),
        out_shape=[
            shape((rows, width), BF16),
            shape((rows, rank), BF16),
            shape((seqs, state, inner), F32),
            shape((seqs * parts,) + held, BF16),
        ]
        + [shape(*k) for k in kept],
        scratch_shapes=[
            vmem((width, 2 * inner), BF16),
            vmem((inner, width), BF16),
            vmem((inner, used), BF16),
            vmem((rank, inner), BF16),
            vmem((32, inner), F32),
            vmem((32, share), F32),
            vmem((seqs, GROUP, width), BF16),
            vmem((rows + seqs * GROUP, inner), F32),
            vmem((rows, inner), F32),
            vmem((rows + seqs * GROUP, width), BF16),
            vmem(grouped, F32),
            vmem((rows, used), F32),
            vmem((2, seqs, state, inner), BF16),
            vmem((8, inner), F32),
            vmem((span, seqs, state, inner), BF16),
            vmem((span, 8, inner), F32),
            vmem((rows, width), BF16),
            vmem((rows, LANES), F32),
            vmem((seqs, ctx + GROUP, inner), BF16),
            vmem((rows, inner), BF16),
            vmem((rows, inner), BF16),
            vmem((rows, inner), BF16),
            vmem(grouped, F32),
            vmem((seqs, ctx, state, LANES), F32),
            vmem((seqs, ctx, state, LANES), F32),
            vmem((rows, inner), F32),
            vmem(grouped, F32),
            vmem(grouped, F32),
            vmem((rows, inner), BF16),
            vmem((parts, rows, CHUNK), BF16),
            vmem((seqs, state, inner), F32),
            vmem((HELD,) + held, BF16),
            dma((6, 12)),
            dma((6, 12)),
            dma((2, seqs)),
            dma((span, seqs)),
            dma((span, seqs)),
            dma((span,)),
            dma((span,)),
            dma((6, 4)),
            dma((len(kept),)),
            dma((HELD,)),
        ],
        compiler_params=pltpu.CompilerParams(
            collective_id=0, has_side_effects=True, vmem_limit_bytes=63 << 20
        ),
        name="front",
    )(x, og, lengths, taps, logs, cbias, dbias, skip, gain, in_own, out_own, xp_own, dt_own)


def back_kernel(
    span, state, rank,
    gated, bg, step_low, final, small, x, og,
    held_all, normed_full, lead_full, slope_full, u_full, sig_full, delta_full, bw_full,
    cw_full, dy_full, zg_full, in_full, xp_full, dt_full,
    input_grad, out_sum, in_sum, rest_sum,
    normed, lead, slope, u, sig, delta, bw, cw, dy, mixed, xp, dt, in_w, held, v, rl, cacc,
    bacc, logs, sums,
    pg, pg_full, cg, ng, rest, g, ra, rx, ry, zlo, zhi, tot,
    send, recv, halo, local, load, held_sem, in_sem,
):
    d, s, f = (lax.axis_index(a) for a in ("dp", "seq", "fsdp"))
    fx, fy, fd = f ^ 1, f ^ 2, f ^ 3
    chunks = tot.shape[0]
    rows, width = x.shape
    inner = gated.shape[1]
    seqs = cg.shape[0]
    ctx = rows // seqs
    parts = inner // CHUNK
    out_chunks = 2 * width // CHUNK
    in_chunks = 2 * parts
    last = out_chunks + in_chunks
    slots = g.shape[0]
    q = HR // 2
    roots = ((span - 1) // 2, span // 2)
    most = span // 2
    tox, toy, sib = {"fsdp": fx}, {"fsdp": fy}, {"dp": 1 - d}
    up, down = {"seq": jnp.minimum(s + 1, span - 1)}, {"seq": jnp.maximum(s - 1, 0)}
    contract = (((0,), (0,)), ((), ()))
    across = (((1,), (1,)), ((), ()))
    dot = lambda a, b, dims=(((1,), (0,)), ((), ())): lax.dot_general(
        a, b, dims, preferred_element_type=F32
    )

    parts_of = lambda v, c: v.at[pl.ds(c * (v.shape[0] // seqs), v.shape[0] // seqs)]
    by_context = ((delta, delta_full), (dy, dy_full), (u, u_full), (cw, cw_full), (bw, bw_full), (sig, sig_full))
    pairs = [
        (parts_of(dst, c), parts_of(src, c)) for c in range(seqs) for dst, src in by_context
    ]
    first_loads = len(pairs)
    pairs += [
        (mixed.at[:parts], zg_full), (normed, normed_full), (slope, slope_full), (lead, lead_full),
        (xp, xp_full), (dt, dt_full),
    ]
    loads = [pltpu.make_async_copy(src, dst, load.at[n]) for n, (dst, src) in enumerate(pairs)]

    def held_copy(b):
        slot = lax.rem(b, 2)
        return pltpu.make_async_copy(held_all.at[b], held.at[slot], held_sem.at[slot])

    def in_copy(k):
        slot = lax.rem(k, 2)
        first = pl.multiple_of(lax.rem(k + parts, 2 * parts) * CHUNK, CHUNK)
        return pltpu.make_async_copy(in_full.at[:, pl.ds(first, CHUNK)], in_w.at[slot], in_sem.at[slot])

    held_copy(0).start()
    for one in loads[: len(by_context)]:
        one.start()
    held_copy(1).start()
    for one in loads[len(by_context) :]:
        one.start()
    cg[:, ctx:] = jnp.zeros((seqs, cg.shape[1] - ctx, inner), F32)
    barrier = pltpu.get_barrier_semaphore()
    for who in (tox, toy, sib):
        pl.semaphore_signal(barrier, inc=1, device_id=who, device_id_type=MESH)

    @pl.when(s > 0)
    def _():
        pl.semaphore_signal(barrier, inc=1, device_id=down, device_id_type=MESH)

    @pl.when(s < span - 1)
    def _():
        pl.semaphore_signal(barrier, inc=1, device_id=up, device_id_type=MESH)

    ends = (s == 0) | (s == span - 1)
    pl.semaphore_wait(barrier, jnp.where(ends, 4, 5) if span > 1 else 3)

    def copy(kind, c, src, dst, who):
        return pltpu.make_async_remote_copy(
            src_ref=src, dst_ref=dst, send_sem=send.at[kind, c], recv_sem=recv.at[kind, c],
            device_id=who, device_id_type=MESH,
        )

    lo, hi = slice(0, q), slice(q, HR)
    A = lambda c: copy(0, c, g.at[lax.rem(c, slots), :, 1 - d], ra.at[c], sib)
    X0 = lambda c: copy(1, c, ra.at[c, fd, lo], rx.at[c, 0], tox)
    X1 = lambda c: copy(2, c, ra.at[c, fx, lo], rx.at[c, 1], tox)
    X2 = lambda c: copy(3, c, ra.at[c, fx, hi], rx.at[c, 2], tox)
    Y0 = lambda c: copy(4, c, ra.at[c, fd, hi], ry.at[c, 0], toy)
    Y2 = lambda c: copy(5, c, ra.at[c, fy, hi], ry.at[c, 2], toy)
    Y1 = lambda c: copy(6, c, ra.at[c, fy, lo], ry.at[c, 1], toy)
    part = (lo, hi)
    ZU = lambda c, h: copy(7 + h, c, ra.at[c, f, part[h]], zlo.at[c, part[h]], up)
    ZD = lambda c, h: copy(9 + h, c, ra.at[c, f, part[h]], zhi.at[c, part[h]], down)
    TU = lambda c, h: copy(11 + h, c, tot.at[c, d, part[h]], tot.at[c, d, part[h]], up)
    TD = lambda c, h: copy(13 + h, c, tot.at[c, d, part[h]], tot.at[c, d, part[h]], down)
    D = lambda c, h: copy(15 + h, c, tot.at[c, d, part[h]], tot.at[c, d, part[h]], sib)
    below, above = [s < r for r in roots], [s > r for r in roots]
    spot = [
        jnp.where(below[h], s, jnp.where(above[h], span - 1 - s, 0)) for h in range(2)
    ]
    far = [jnp.abs(s - r) for r in roots]

    def stage(c, run):
        @pl.when((c >= 0) & (c < chunks))
        def _():
            run(c)

    def produce(c):
        slot = lax.rem(c, slots)

        @pl.when(c >= slots)
        def _():
            A(c - slots).wait_send()

        @pl.when(c < out_chunks)
        def _():
            r = c // (width // CHUNK)
            col = lax.rem(c, width // CHUNK) * CHUNK
            right = bg[:, pl.ds(pl.multiple_of(col, CHUNK), CHUNK)]
            for j in range(4):
                for h in range(2):
                    at = j * (inner // 4) + h * (inner // 8) + r * HR
                    left = gated[:, pl.ds(pl.multiple_of(at, HR), HR)]
                    g[slot, j, h] = dot(left, right, contract).astype(BF16)

        @pl.when((c >= out_chunks) & (c < last))
        def _():
            right = mixed[c - out_chunks]
            for j in range(4):
                t = dot(normed[:, j * 2 * HR : (j + 1) * 2 * HR], right, contract).astype(BF16)
                g[slot, j, 0] = t[:HR]
                g[slot, j, 1] = t[HR:]

        @pl.when(c == last)
        def _():
            for j in range(4):
                for h in range(2):
                    cols = slice(j * CHUNK, (j + 1) * CHUNK)
                    g[slot, j, h] = rest[h * HR : (h + 1) * HR, cols].astype(BF16)

        A(c).start()

    def first_sum(c):
        A(c).wait_recv()
        for j in range(4):
            own = g[lax.rem(c, slots), j, d]
            ra[c, j] = ra[c, j] + own
        X0(c).start()
        Y0(c).start()
        X1(c).start()
        Y2(c).start()

    def second_sum(c):
        X0(c).wait_recv()
        ra[c, fy, lo] = ra[c, fy, lo] + rx[c, 0]
        Y1(c).start()
        Y0(c).wait_recv()
        ra[c, fx, hi] = ra[c, fx, hi] + ry[c, 0]
        X2(c).start()

    def third_sum(c):
        X1(c).wait_recv()
        Y2(c).wait_recv()
        X2(c).wait_recv()
        Y1(c).wait_recv()
        for k, piece in enumerate((lo, hi)):
            total = ra[c, f, piece].astype(F32) + rx[c, 1 + k].astype(F32) + ry[c, 1 + k].astype(F32)
            ra[c, f, piece] = total.astype(BF16)

    def inward(c, h):
        @pl.when(below[h] & (s > 0))
        def _():
            ZU(c, h).wait_recv()
            ra[c, f, part[h]] = ra[c, f, part[h]] + zlo[c, part[h]]

        @pl.when(above[h] & (s < span - 1))
        def _():
            ZD(c, h).wait_recv()
            ra[c, f, part[h]] = ra[c, f, part[h]] + zhi[c, part[h]]

        pl.when(below[h])(lambda: ZU(c, h).start())
        pl.when(above[h])(lambda: ZD(c, h).start())

    def at_root(c, h):
        total = ra[c, f, part[h]].astype(F32)
        if roots[h] > 0:
            ZU(c, h).wait_recv()
            total = total + zlo[c, part[h]].astype(F32)
        if span - 1 > roots[h]:
            ZD(c, h).wait_recv()
            total = total + zhi[c, part[h]].astype(F32)
        tot[c, d, part[h]] = total.astype(BF16)
        if roots[h] > 0:
            TD(c, h).start()
        if span - 1 > roots[h]:
            TU(c, h).start()
        D(c, h).start()

    def outward(c, h):
        @pl.when(above[h])
        def _():
            TU(c, h).wait_recv()
            pl.when(s < span - 1)(lambda: TU(c, h).start())

        @pl.when(below[h])
        def _():
            TD(c, h).wait_recv()
            pl.when(s > 0)(lambda: TD(c, h).start())

        D(c, h).start()

    tile = 2 * LANES

    def columns(t, size=tile):
        return pl.ds(pl.multiple_of(t * size, size), size)

    def back_block(b):
        c, slot = b // parts, lax.rem(b, 2)
        groups = ctx // GROUP
        first = lax.rem(b, parts) * CHUNK
        cuts = [pl.ds(pl.multiple_of(first + n, LANES), LANES) for n in range(0, CHUNK, LANES)]
        tiles = [slice(n, n + LANES) for n in range(0, CHUNK, LANES)]
        cols = pl.ds(pl.multiple_of(first, CHUNK), CHUNK)
        rates = [-jnp.exp(small[:state, cut]) * LOG2E for cut in cuts]
        skip = small[TAPS + state + 2 : TAPS + state + 3, cols]
        held_copy(b).wait()

        def one(turn, carry):
            i = groups - 1 - turn
            at = c * groups + i
            tok = pl.ds(pl.multiple_of(at * GROUP, GROUP), GROUP)
            p, total, kept = (list(value) for value in carry)
            value, out, gain = u[tok, cols].astype(F32), dy[at, :, cols], delta[at, :, cols]
            v[...] = gain * value
            drive_parts, delta_parts = [[], []], [[], []]
            for pair in range(0, len(cuts), 2):
                which = range(pair, pair + 2)
                after = {n: held[slot, (i + 1) * GROUP, :, tiles[n]].astype(F32) for n in which}
                for half in (1, 0):
                    drives, deltas = ({n: [] for n in which} for _ in range(2))
                    for k in reversed(range(half * 8, half * 8 + 8)):
                        t = i * GROUP + k
                        b_in, read = bw[c, t], cw[c, t]
                        b_parts, c_parts = [], []
                        for n in which:
                            row = lambda tile: jnp.broadcast_to(tile, (state, LANES))
                            step, back = row(delta[at, k : k + 1, cuts[n]]), row(dy[at, k : k + 1, cuts[n]])
                            grad = read * back + p[n]
                            p[n] = jnp.exp2(step * rates[n]) * grad
                            before = held[slot, t, :, tiles[n]].astype(F32)
                            w = p[n] * before
                            total[n] = total[n] + w * step
                            part = w * rates[n]
                            rows_sum(deltas[n], part[:8] + part[8:], False)
                            part = grad * b_in
                            rows_sum(drives[n], part[:8] + part[8:], False)
                            b_parts.append(grad * row(v[k : k + 1, tiles[n]]))
                            c_parts.append(after[n] * back)
                            after[n] = before
                        bacc[c * ctx + t] += b_parts[0] + b_parts[1]
                        cacc[c * ctx + t] += c_parts[0] + c_parts[1]
                    drive_parts[half] += [drives[n][0][1] for n in which]
                    delta_parts[half] += [deltas[n][0][1] for n in which]
            joined = lambda halves: jnp.concatenate([jnp.concatenate(h, 1) for h in halves], 0)
            drive_grad, delta_part = joined(drive_parts), joined(delta_parts)
            raw_grad = drive_grad * value + delta_part * (1.0 / LOG2E)
            raw_grad = raw_grad * sig[tok, cols].astype(F32)
            rl[tok, cols] = raw_grad.astype(BF16)
            dy[at, :, cols] = out * skip + drive_grad * gain
            kept[0] = kept[0] + (out * value)[:8] + (out * value)[8:]
            kept[1] = kept[1] + raw_grad[:8] + raw_grad[8:]
            return tuple(p), tuple(total), tuple(kept)

        zero = tuple(jnp.zeros((state, LANES), F32) for _ in cuts)
        none = jnp.zeros((8, CHUNK), F32)
        begin = tuple(final[c, :, cut] for cut in cuts)
        _, total, kept = lax.fori_loop(0, groups, one, (begin, zero, (none, none)))
        for n, cut in enumerate(cuts):
            logs[:, cut] += total[n]
        sums[0, :, cols] += kept[0]
        sums[1, :, cols] += kept[1]

        @pl.when(b + 2 < blocks)
        def _():
            held_copy(b + 2).start()

    def proj_work():
        step_grad = dot(rl[...], dt[...], across)
        col = lax.broadcasted_iota(jnp.int32, (state, LANES), 1)
        n = lax.broadcasted_iota(jnp.int32, (state, LANES), 0)
        ones = jnp.ones((LANES, LANES), BF16)

        def one(r, carry):
            tok = pl.ds(pl.multiple_of(r * GROUP, GROUP), GROUP)
            total = pg_full[tok]
            for ref, first in ((bacc, rank), (cacc, rank + state)):
                value = dot(ref[tok].reshape(GROUP * state, LANES).astype(BF16), ones)
                keep = jnp.where(col == n + first, value.reshape(GROUP, state, LANES), 0.0)
                total = total + jnp.sum(keep, 1)
            pg[tok] = total.astype(BF16)
            return carry

        pg_full[...] = jnp.concatenate([step_grad, jnp.zeros((rows, LANES - rank), F32)], 1)
        lax.fori_loop(0, rows // GROUP, one, 0)

    def weight_work():
        first = TAPS + state + 4
        used = rank + 2 * state

        def weights(t, carry):
            cols = columns(t)
            rest[first : first + rank, cols] = dot(step_low[...], rl[:, cols], contract)
            rest[first + rank : first + rank + used, cols] = dot(pg[...], u[:, cols], contract)[:used]
            kept = -logs[:, cols] * jnp.exp(small[:state, cols])
            rest[:state, cols] = kept
            at = TAPS + state
            rest[at + 1 : at + 2, cols] = jnp.sum(sums[1, :, cols], 0, keepdims=True)
            rest[at + 2 : at + 3, cols] = jnp.sum(sums[0, :, cols], 0, keepdims=True)
            return carry

        lax.fori_loop(0, inner // tile, weights, 0)

    def conv_work(first, count):
        def one(t, carry):
            cols = columns(t)
            shift = jnp.zeros((1, tile), F32)
            taps = [jnp.zeros((1, tile), F32) for _ in range(TAPS)]
            for c in range(seqs):
                tok = slice(c * ctx, (c + 1) * ctx)
                weight = xp[columns(t)]
                back = dot(pg[tok], weight, across)
                own = range(c * ctx // GROUP, (c + 1) * ctx // GROUP)
                grad = jnp.concatenate([dy[at, :, cols] for at in own], 0) + back
                grad = grad * slope[tok, cols].astype(F32)
                cg[c, :ctx, cols] = grad
                before = lead[c, :, cols].astype(F32)
                shift = shift + jnp.sum(grad, 0, keepdims=True)
                for k in range(TAPS):
                    at = GROUP - TAPS + 1 + k
                    taps[k] = taps[k] + jnp.sum(grad * before[at : at + ctx], 0, keepdims=True)
            for k in range(TAPS):
                rest[state + k : state + k + 1, cols] = taps[k]
            rest[TAPS + state : TAPS + state + 1, cols] = shift
            return carry

        lax.fori_loop(first, first + count, one, 0)

    edge = cg.shape[1] - ctx
    H = lambda: pltpu.make_async_remote_copy(
        src_ref=cg.at[:, :edge], dst_ref=cg.at[:, ctx:], send_sem=halo.at[0],
        recv_sem=halo.at[1], device_id=down, device_id_type=MESH,
    )

    def halo_send():
        pl.when(s > 0)(lambda: H().start())

    def stream_work():
        pl.when(s < span - 1)(lambda: H().wait_recv())

        def one(t, carry):
            cols = columns(t)
            for c in range(seqs):
                total = 0.0
                for k in range(TAPS):
                    at = TAPS - 1 - k
                    total = total + small[state + k : state + k + 1, cols] * cg[c, at : at + ctx, cols]
                half = pl.ds(pl.multiple_of(lax.rem(t, 2) * tile, tile), tile)
                mixed[parts + t // 2, c * ctx : (c + 1) * ctx, half] = total.astype(BF16)
            return carry

        lax.fori_loop(0, inner // tile, one, 0)
        pl.when(s > 0)(lambda: H().wait_send())

    def norm_work(first, count):
        def one(k, carry):
            in_copy(k).wait()
            ng[...] += dot(mixed[k], in_w[lax.rem(k, 2)], across)

            @pl.when(k + 2 < 2 * parts)
            def _():
                in_copy(k + 2).start()

            return carry

        if first == 0:
            ng[...] = jnp.zeros(ng.shape, F32)
        lax.fori_loop(first, first + count, one, 0)

    def input_work():
        share = width // 4
        at = TAPS + state + 3
        gain = jnp.concatenate(
            [small[at : at + 1, j * CHUNK : j * CHUNK + share] for j in range(4)], 1
        )

        def one(r, total):
            tok = pl.ds(pl.multiple_of(r * GROUP, GROUP), GROUP)
            xs = x[tok].astype(F32)
            inverse = lax.rsqrt(jnp.mean(xs * xs, -1, keepdims=True) + EPS)
            grad = ng[tok]
            scaled = grad * gain
            slope = jnp.mean(scaled * xs, -1, keepdims=True)
            out = inverse * scaled - xs * (inverse * inverse * inverse * slope)
            input_grad[tok] = (out + og[tok].astype(F32)).astype(BF16)
            return total + grad * (xs * inverse)

        total = lax.fori_loop(0, rows // GROUP, one, jnp.zeros((GROUP, width), F32))
        total = jnp.sum(total, 0, keepdims=True)
        for j in range(4):
            rest[at : at + 1, j * CHUNK : j * CHUNK + share] = total[:, j * share : (j + 1) * share]

    blocks = seqs * parts
    tiles = inner // tile
    pause = 3
    held_back = out_chunks + parts
    base = 1 + 2 * SLACK + 1

    def prepare():
        for ref in (cacc, bacc, logs, sums, rest):
            ref[...] = jnp.zeros(ref.shape, F32)

    def blocks_work(i):
        pl.when(i == 0)(prepare)
        for c in range(seqs):

            @pl.when(i == c * parts)
            def _():
                for one in loads[c * len(by_context) : (c + 1) * len(by_context)]:
                    one.wait()

        pl.when(i < blocks)(lambda: back_block(i))

    def late_work(i):
        at = held_back

        @pl.when(i == at)
        def _():
            proj_work()
            conv_work(0, tiles)
            halo_send()
            in_copy(0).start()
            in_copy(1).start()

        pl.when(i == at + 1)(weight_work)
        pl.when(i == at + 2)(stream_work)
        pl.when(i == at + 4)(lambda: norm_work(0, parts))
        pl.when(i == at + 5)(lambda: norm_work(parts, parts))
        pl.when(i == at + 6)(input_work)

    def step(i, carry):
        def at(offset):
            k = i - offset
            return jnp.where(k < held_back, k, jnp.where(k < held_back + pause, -1, k - pause))

        @pl.when(i == out_chunks)
        def _():
            for one in loads[first_loads:]:
                one.wait()

        for h in range(2):
            run = lambda f: lambda c: f(c, h)
            away = s != roots[h]
            pl.when(away)(lambda: stage(at(base + SLACK * (most + far[h])), run(outward)))
            pl.when(~away)(lambda: stage(at(base + SLACK * most), run(at_root)))
            pl.when(away)(lambda: stage(at(base + SLACK * spot[h]), run(inward)))
        stage(at(1 + 2 * SLACK), third_sum)
        stage(at(1 + SLACK), second_sum)
        stage(at(1), first_sum)
        stage(at(0), produce)
        blocks_work(i)
        late_work(i)
        return carry

    lax.fori_loop(0, chunks + pause + base + 2 * SLACK * most + 1, step, 0)

    def finish(c, carry):
        pl.when(c >= chunks - slots)(lambda: A(c).wait_send())
        for t in (X0, X1, X2, Y0, Y1, Y2):
            t(c).wait_send()
        for h, root in enumerate(roots):
            pl.when(below[h])(lambda: ZU(c, h).wait_send())
            pl.when(above[h])(lambda: ZD(c, h).wait_send())
            if root > 0:
                pl.when((s <= root) & (s > 0))(lambda: TD(c, h).wait_send())
            if span - 1 > root:
                pl.when((s >= root) & (s < span - 1))(lambda: TU(c, h).wait_send())
            D(c, h).wait_send()
            D(c, h).wait_recv()
        return carry

    lax.fori_loop(0, chunks, finish, 0)
    copies = []
    for c in range(chunks):
        for h in range(2):
            if c < out_chunks:
                r, col = c // (width // CHUNK), c % (width // CHUNK)
                first = h * (inner // 8) + r * HR
                to = out_sum.at[first : first + HR, col * CHUNK : (col + 1) * CHUNK]
            elif c < last:
                col = (c - out_chunks + parts) % (2 * parts)
                to = in_sum.at[h * HR : (h + 1) * HR, col * CHUNK : (col + 1) * CHUNK]
            else:
                to = rest_sum.at[h * HR : (h + 1) * HR]
            copies.append(pltpu.make_async_copy(tot.at[c, h], to, local.at[c, h]))
    for one in copies:
        one.start()
    for one in copies:
        one.wait()


def back(gated, bg, step_low, final, small, x, og, far):
    rows, inner = gated.shape
    width = x.shape[1]
    seqs, state = final.shape[:2]
    ctx, rank, parts = rows // seqs, step_low.shape[1], inner // CHUNK
    span = lax.axis_size("seq")
    out_chunks, in_chunks = 2 * width // CHUNK, 2 * parts
    n = out_chunks + in_chunks + 1
    vmem, dma = pltpu.VMEM, pltpu.SemaphoreType.DMA
    anywhere = pl.BlockSpec(memory_space=pl.ANY)
    whole = pl.BlockSpec(memory_space=vmem)
    shape = jax.ShapeDtypeStruct
    like = lambda v: vmem(v.shape, v.dtype)
    (held, normed, lead, slope, u, sig, delta, bw, cw, dy, zg, in_full, xp, dt) = far
    return pl.pallas_call(
        functools.partial(back_kernel, span, state, rank),
        in_specs=[whole] * 7 + [anywhere] * len(far),
        out_specs=[whole, anywhere, anywhere, anywhere],
        out_shape=[
            shape((rows, width), BF16),
            shape((inner // 4, width), BF16),
            shape((width // 4, 2 * inner), BF16),
            shape((2 * HR, CHUNK), BF16),
        ],
        scratch_shapes=[
            *map(like, (normed, lead, slope, u, sig, delta, bw, cw, dy)),
            vmem((in_chunks, rows, CHUNK), BF16),
            like(xp),
            like(dt),
            vmem((2, width, CHUNK), BF16),
            vmem((2,) + held.shape[1:], BF16),
            vmem((GROUP, CHUNK), F32),
            vmem((rows, inner), BF16),
            vmem((rows, state, LANES), F32),
            vmem((rows, state, LANES), F32),
            vmem((state, inner), F32),
            vmem((2, 8, inner), F32),
            vmem((rows, LANES), BF16),
            vmem((rows, LANES), F32),
            vmem((seqs, ctx + 8, inner), F32),
            vmem((rows, width), F32),
            vmem((2 * HR, inner), F32),
            vmem((4, 4, 2, HR, CHUNK), BF16),
            vmem((n, 4, HR, CHUNK), BF16),
            vmem((n, 3, HR // 2, CHUNK), BF16),
            vmem((n, 3, HR // 2, CHUNK), BF16),
            vmem((n, HR, CHUNK), BF16),
            vmem((n, HR, CHUNK), BF16),
            vmem((n, 2, HR, CHUNK), BF16),
            dma((17, n)),
            dma((17, n)),
            dma((2,)),
            dma((n, 2)),
            dma((12 + 6,)),
            dma((2,)),
            dma((2,)),
        ],
        compiler_params=pltpu.CompilerParams(
            collective_id=1, has_side_effects=True, vmem_limit_bytes=63 << 20
        ),
        name="back",
    )(gated, bg, step_low, final, small, x, og, *far)


def finish_kernel(state, rank, used, in_sum, out_sum, rest, gain, in_w, taps, cbias, xp, dt, dbias, logs, skip, out_w):
    in_w[...] = in_sum[...].astype(F32)
    out_w[...] = out_sum[...].astype(F32)
    at = TAPS + state
    row = lambda first, count=1: rest[...].astype(F32)[first : first + count]
    logs[...] = row(0, state)
    taps[...] = row(state, TAPS)
    cbias[...] = row(at)
    dbias[...] = row(at + 1)
    skip[...] = row(at + 2)
    gain[...] = row(at + 3)[:, : gain.shape[1]]
    dt[...] = row(at + 4, rank)
    xp[...] = row(at + 4 + rank, used).T


def finish(in_sum, out_sum, rest, state, rank, used):
    steps = 4
    share = rest.shape[1]
    tall = lambda v: pl.BlockSpec((v.shape[0] // steps, v.shape[1]), lambda i: (i, 0))
    fixed = lambda *v: pl.BlockSpec(v, lambda i: (0, 0))
    small = [(1, in_sum.shape[0]), (TAPS, share), (1, share), (share, used), (rank, share)]
    small += [(1, share), (state, share), (1, share)]
    shape = lambda v: jax.ShapeDtypeStruct(v, F32)
    return pl.pallas_call(
        functools.partial(finish_kernel, state, rank, used),
        grid=(steps,),
        in_specs=[tall(in_sum), tall(out_sum), fixed(*rest.shape)],
        out_specs=[fixed(*small[0]), tall(in_sum)] + [fixed(*v) for v in small[1:]] + [tall(out_sum)],
        out_shape=[shape(small[0]), shape(in_sum.shape)]
        + [shape(v) for v in small[1:]]
        + [shape(out_sum.shape)],
        compiler_params=pltpu.CompilerParams(vmem_limit_bytes=32 << 20),
        name="finish",
    )(in_sum, out_sum, rest)


def body(
    hidden_in, lengths, norm_gain, in_weight, conv_weight, conv_bias, xproj_weight,
    dt_weight, dt_bias, a_log, skip_gain, out_weight, out_grad,
):
    seqs, ctx, width = hidden_in.shape
    taps, share = conv_weight.shape
    state = a_log.shape[0]
    rank = dt_weight.shape[0]
    rows = ctx * seqs
    row = lambda v: v.reshape(1, -1)
    x, og = hidden_in.reshape(rows, width), out_grad.reshape(rows, width)
    used = xproj_weight.shape[1]
    xp_own = jnp.pad(xproj_weight, ((0, 0), (0, LANES - used)))
    (
        hidden_out, step_low, final, held, normed, branch_grad, lead, slope, u, sig, delta,
        b_wide, c_wide, y_grad, gated, z_grad, in_matrix, proj_matrix, step_matrix, small,
    ) = front(
        x, og, lengths, conv_weight, a_log, row(conv_bias), row(dt_bias), row(skip_gain),
        row(norm_gain), in_weight, out_weight, xp_own, dt_weight, seqs,
    )
    far = (
        held, normed, lead, slope, u, sig, delta, b_wide, c_wide, y_grad, z_grad, in_matrix,
        proj_matrix, step_matrix,
    )
    input_grad, out_sum, in_sum, rest = back(
        gated, branch_grad, step_low, final, small, x, og, far
    )
    gain, in_w, taps_grad, cbias, proj_w, step_w, dbias, logs, skip, out_w = finish(
        in_sum, out_sum, rest, state, rank, used
    )
    flat = lambda v: v.reshape(-1)
    return (
        hidden_out.reshape(seqs, ctx, width), input_grad.reshape(seqs, ctx, width), flat(gain), in_w,
        taps_grad, flat(cbias), proj_w, step_w, flat(dbias), logs, flat(skip), out_w,
    )


def solution(mesh):
    tokens = P(("dp", "fsdp"), "seq", None)
    return jax.shard_map(
        body,
        mesh=mesh,
        in_specs=(
            tokens, P(("dp", "fsdp")), P("fsdp"), P("fsdp", None), P(None, "fsdp"), P("fsdp"),
            P("fsdp", None), P(None, "fsdp"), P("fsdp"), P(None, "fsdp"), P("fsdp"),
            P("fsdp", None), tokens,
        ),
        out_specs=(
            tokens, tokens, P("fsdp"), P("fsdp", None), P(None, "fsdp"), P("fsdp"),
            P("fsdp", None), P(None, "fsdp"), P("fsdp"), P(None, "fsdp"), P("fsdp"),
            P("fsdp", None),
        ),
        check_vma=False,
    )
```

```python
import functools
import math

import jax
import jax.numpy as jnp
import numpy as np
from jax import lax
from jax.experimental import pallas as pl
from jax.experimental.pallas import tpu as pltpu
from jax.sharding import PartitionSpec as P

EPS = 1e-05
LOG2E = math.log2(math.e)
LANES = 128
GROUP = 16
F32 = jnp.float32
BF16 = jnp.bfloat16
MESH = pl.DeviceIdType.MESH
HR = 128
CHUNK = 512
SLACK = 2
TAPS = 4
HELD = 3


def silu_parts(v):
    s = jax.nn.sigmoid(v)
    return v * s, s * (1.0 + v * (1.0 - s))


def rows_sum(stack, value, rising):
    row = lax.broadcasted_iota(jnp.int32, value.shape, 0)
    level = 0
    while stack and stack[-1][0] == level:
        _, other = stack.pop()
        first, second = (other, value) if rising else (value, other)
        low = (row & (1 << level)) == 0
        turned = pltpu.roll(jnp.where(low, second, first), 1 << level, 0)
        value = jnp.where(low, first, second) + turned
        level += 1
    stack.append((level, value))


def front_kernel(
    span,
    x, og, lengths, taps_own, log_own, cbias_own, dbias_own, skip_own, gain_own,
    xp_tall, in_own, out_own, dt_own,
    hidden_out, step_low, final,
    held_all, normed_full, bg_full, lead_full, slope_full, u_full, sig_full, delta_full, bw_full,
    cw_full, dy_full, gated_full, zg_full, in_full, xp_full, dt_full, small_full,
    in_w, out_w, xp, dt, small, small_own, xp_own, hx, acc, zacc, normed, v, proj, ends, sums,
    ends_in, sums_in, bg, mask, lead, slope, u, sig, delta, bw, cw, gg, dy, y, gated, zg,
    start, held,
    send, recv, halo, relay_send, relay_recv, sums_send, sums_recv, local, keep, held_sem,
):
    d, s, f = (lax.axis_index(a) for a in ("dp", "seq", "fsdp"))
    fx, fy, fd = f ^ 1, f ^ 2, f ^ 3
    tox, toy, tod, sib = {"fsdp": fx}, {"fsdp": fy}, {"fsdp": fd}, {"dp": 1 - d}
    rows, width = x.shape
    inner = u.shape[1]
    seqs = bw.shape[0]
    ctx = rows // seqs
    state, rank = log_own.shape[0], dt_own.shape[0]
    groups = ctx // GROUP
    share = inner // 4
    at_bias = state + TAPS
    across = (((1,), (1,)), ((), ()))
    dot = lambda a, b, dims=(((1,), (0,)), ((), ())): lax.dot_general(
        a, b, dims, preferred_element_type=F32
    )

    for c in range(seqs):
        hx[c] = jnp.zeros((GROUP, width), BF16)
    barrier = pltpu.get_barrier_semaphore()
    for who in (tox, toy, tod, sib):
        pl.semaphore_signal(barrier, inc=1, device_id=who, device_id_type=MESH)

    def greet(o, carry):
        who = {"seq": lax.rem(s + o, span)}
        pl.semaphore_signal(barrier, inc=1, device_id=who, device_id_type=MESH)
        return carry

    lax.fori_loop(1, span, greet, 0)
    blank = jnp.zeros((LANES - xp_tall.shape[0], share), BF16)
    xp_own[...] = jnp.concatenate([xp_tall[...], blank], 0).T
    small_own[...] = jnp.zeros(small_own.shape, F32)
    small_own[:state] = log_own[...]
    small_own[state:at_bias] = taps_own[...]
    small_own[at_bias : at_bias + 1] = cbias_own[...]
    small_own[at_bias + 1 : at_bias + 2] = dbias_own[...]
    small_own[at_bias + 2 : at_bias + 3] = skip_own[...]
    small_own[at_bias + 3 : at_bias + 4, : width // 4] = gain_own[...]
    pl.semaphore_wait(barrier, 3 + span)

    SMALL, STREAM, PROJ, STEP, GATE, OUT = range(6)
    plan = (
        (small_own, small, 1, None),
        (in_own, in_w, 0, (0, inner)),
        (xp_own, xp, 0, None),
        (dt_own, dt, 1, None),
        (in_own, in_w, 0, (inner, 2 * inner)),
        (out_own, out_w, 0, None),
    )

    def window(p, owner, half, q):
        src, dst, dim, cols = plan[p]
        high, wide = src.shape
        part = high // 4
        at = (half * 2 + q) * part
        lo, hi = cols or (0, wide)
        if dim == 0:
            return dst.at[pl.ds(pl.multiple_of(owner * high + at, part), part), lo:hi]
        col = pl.ds(pl.multiple_of(owner * wide, wide), wide)
        return dst.at[pl.ds(pl.multiple_of(at, part), part), col]

    def own(p, half, q):
        src, _, _, cols = plan[p]
        high, wide = src.shape
        part = high // 4
        lo, hi = cols or (0, wide)
        return src.at[pl.ds(pl.multiple_of((half * 2 + q) * part, part), part), lo:hi]

    def copy(src, dst, p, kind, who):
        return pltpu.make_async_remote_copy(
            src_ref=src, dst_ref=dst, send_sem=send.at[p, kind], recv_sem=recv.at[p, kind],
            device_id=who, device_id_type=MESH,
        )

    started = []

    def go(one):
        one.start()
        started.append(one)

    def start_own(p, routed=False):
        for q in (0, 1):
            go(copy(own(p, d, q), window(p, f, d, q), p, q, tox))
            go(copy(own(p, d, 1 - q), window(p, f, d, 1 - q), p, 3 - q, toy))
        if routed:
            for q in (0, 1):
                go(copy(own(p, d, q), window(p, f, d, q), p, 4 + q, tod))

    def small_copy(at, owner, part, who):
        rows_of = slice(*((state, at_bias + 4), (0, state))[part])
        cols = pl.ds(pl.multiple_of(owner * share, share), share)
        return pltpu.make_async_remote_copy(
            src_ref=small_own.at[rows_of], dst_ref=small.at[rows_of, cols],
            send_sem=send.at[SMALL, 3 * part + at], recv_sem=recv.at[SMALL, 3 * part + at],
            device_id=who, device_id_type=MESH,
        )

    def small_start(part):
        for at, who in enumerate((tox, toy, tod)):
            go(small_copy(at, f, part, who))

    def small_ready(part):
        for at, owner in enumerate((fx, fy, fd)):
            small_copy(at, owner, part, sib).wait_recv()

    def place_own(p):
        for half in (0, 1):
            for q in (0, 1):
                pltpu.make_async_copy(
                    own(p, half, q), window(p, f, half, q), local.at[p, half * 2 + q]
                ).start()

    def own_ready(p):
        for half in (0, 1):
            for q in (0, 1):
                pltpu.make_async_copy(
                    own(p, half, q), window(p, f, half, q), local.at[p, half * 2 + q]
                ).wait()

    def arrived(p, kind, owner, half, q):
        w = window(p, owner, half, q)
        copy(w, w, p, kind, sib).wait_recv()
        return w

    near = ((0, fx, 0), (3, fy, 1), (1, fx, 1), (2, fy, 0))
    diagonal = ((4, fd, 0), (5, fd, 1))

    def serve_near(p, routed=False):
        for kind, owner, q in near:
            w = arrived(p, kind, owner, d, q)
            if kind == 0 and not routed:
                go(copy(w, w, p, 4, toy))
            if kind == 3 and not routed:
                go(copy(w, w, p, 5, tox))
            go(copy(w, w, p, 6 + kind, sib))

    def serve_far(p):
        for kind, owner, q in diagonal:
            w = arrived(p, kind, owner, d, q)
            go(copy(w, w, p, 6 + kind, sib))

    def near_ready(p):
        for kind, owner, q in near:
            arrived(p, 6 + kind, owner, 1 - d, q)

    def far_ready(p):
        for kind, owner, q in diagonal:
            arrived(p, 6 + kind, owner, 1 - d, q)

    odd = lax.rem(s, 2)
    across_seq = {"seq": s + 1 - 2 * odd}
    owners = (fx, fx, fy, fy, fd, fd, fx, fy, fd)
    thirds = (0, 1, 0, 1, 0, 1, 2, 2, 2)

    def third(ref, p, base, half, which):
        _, _, _, cols = plan[p]
        high = plan[p][0].shape[0]
        tall = high // 2
        wide = tall if cols is None else cols[1] - cols[0]
        side = wide * 5 // 16
        first = (odd * (wide - side), side, (1 - odd) * (wide - side))[which]
        size = (side, wide - 2 * side, side)[which]
        row = base + half * tall
        if cols is None:
            return ref.at[pl.ds(pl.multiple_of(row + first, GROUP), size)]
        col = pl.ds(pl.multiple_of(cols[0] + first, LANES), size)
        return ref.at[pl.ds(pl.multiple_of(row, tall), tall), col]

    def place(p, kind, half):
        high = plan[p][0].shape[0]
        return third(plan[p][1], p, owners[kind] * high, half, thirds[kind])

    def start_thirds(p):
        for kind, which, who in ((0, 0, tox), (3, 1, toy), (1, 1, tox), (2, 0, toy)):
            to = third(plan[p][1], p, f * plan[p][0].shape[0], d, which)
            go(copy(third(plan[p][0], p, 0, d, which), to, p, kind, who))

    def serve(p, kinds):
        onward = {0: ((4, toy), (6, across_seq)), 2: ((7, across_seq),), 3: ((5, tox),)}
        onward[4] = ((8, across_seq),)
        for kind in kinds:
            w = place(p, kind, d)
            copy(w, w, p, kind, sib).wait_recv()
            for to, who in onward.get(kind, ()):
                go(copy(w, w, p, to, who))
            go(copy(w, w, p, 9 + kind, sib))

    serve_first = lambda p: serve(p, (0, 3, 1, 2))
    serve_rest = lambda p: serve(p, (4, 5, 6, 7, 8))

    def ready(p):
        own_ready(p)
        for kind in range(9):
            w = place(p, kind, 1 - d)
            copy(w, w, p, 9 + kind, sib).wait_recv()

    small_start(0)
    start_thirds(STREAM)
    for p in (STREAM, PROJ, STEP, GATE, OUT):
        place_own(p)
    pltpu.make_async_copy(
        small_own, small.at[:, pl.ds(pl.multiple_of(f * share, share), share)], local.at[SMALL, 0]
    ).start()
    def edges(c):
        return pltpu.make_async_remote_copy(
            src_ref=x.at[(c + 1) * ctx - GROUP : (c + 1) * ctx], dst_ref=hx.at[c],
            send_sem=halo.at[0, c], recv_sem=halo.at[1, c],
            device_id={"seq": jnp.minimum(s + 1, span - 1)}, device_id_type=MESH,
        )

    @pl.when(s < span - 1)
    def _():
        for c in range(seqs):
            edges(c).start()

    for c in range(seqs):
        t = s * ctx + lax.broadcasted_iota(jnp.int32, (ctx, LANES), 0)
        mask[c * ctx : (c + 1) * ctx] = (t < lengths[c]).astype(F32)

    def mask_step(r, carry):
        tok = pl.ds(pl.multiple_of(r * GROUP, GROUP), GROUP)
        held = jnp.concatenate([mask[tok]] * (width // LANES), 1)
        bg[tok] = (og[tok].astype(F32) * held).astype(BF16)
        return carry

    lax.fori_loop(0, rows // GROUP, mask_step, 0)

    pltpu.make_async_copy(
        small_own, small.at[:, pl.ds(pl.multiple_of(f * share, share), share)], local.at[SMALL, 0]
    ).wait()
    small_ready(0)

    @pl.when(s > 0)
    def _():
        for c in range(seqs):
            edges(c).wait_recv()

    gain_at = at_bias + 3
    gain = jnp.concatenate(
        [small[gain_at : gain_at + 1, j * share : j * share + width // 4] for j in range(4)], 1
    )

    def normalised(v):
        v = v.astype(F32)
        inverse = lax.rsqrt(jnp.mean(v * v, -1, keepdims=True) + EPS)
        return (v * inverse * gain).astype(BF16)

    def norm_step(r, carry):
        tok = pl.ds(pl.multiple_of(r * GROUP, GROUP), GROUP)
        normed[tok] = normalised(x[tok])
        return carry

    lax.fori_loop(0, rows // GROUP, norm_step, 0)
    for c in range(seqs):
        normed[rows + c * GROUP : rows + (c + 1) * GROUP] = normalised(hx[c])

    def project(total, high, first):
        def one(t, carry):
            cols = pl.ds(pl.multiple_of(t * CHUNK, CHUNK), CHUNK)
            right = in_w[:, pl.ds(pl.multiple_of(first + t * CHUNK, CHUNK), CHUNK)]
            total[:, cols] = dot(normed[:high], right)
            return carry

        lax.fori_loop(0, inner // CHUNK, one, 0)

    tall = rows + seqs * GROUP
    serve_first(STREAM)
    small_start(1)
    start_own(PROJ, True)
    start_own(STEP, True)
    start_own(GATE)
    serve_rest(STREAM)
    ready(STREAM)
    project(acc, tall, 0)
    small_ready(1)

    tile = 2 * LANES

    def columns(t, size=tile):
        return pl.ds(pl.multiple_of(t * size, size), size)

    def conv_step(t, carry):
        cols = columns(t)
        for c in range(seqs):
            before = acc[rows + c * GROUP : rows + (c + 1) * GROUP, cols].astype(BF16)
            stream = acc[c * ctx : (c + 1) * ctx, cols].astype(BF16)
            lead[c, :GROUP, cols] = before
            lead[c, GROUP:, cols] = stream
            held = jnp.concatenate([before, stream], 0).astype(F32)
            total = small[at_bias : at_bias + 1, cols]
            for k in range(TAPS):
                at = GROUP - TAPS + 1 + k
                total = total + small[state + k : state + k + 1, cols] * held[at : at + ctx]
            value, grad = silu_parts(total)
            slope[c * ctx : (c + 1) * ctx, cols] = grad.astype(BF16)
            u[c * ctx : (c + 1) * ctx, cols] = value.astype(BF16)
        return carry

    lax.fori_loop(0, inner // tile, conv_step, 0)
    for p in (PROJ, STEP):
        serve_near(p, True)
        serve_far(p)
    for p in (PROJ, STEP):
        near_ready(p)
        far_ready(p)
        own_ready(p)
    proj[...] = dot(u[...], xp[...])
    step_low[...] = proj[:, :rank].astype(BF16)

    def wide_step(i, carry):
        tok = pl.ds(pl.multiple_of(i * GROUP, GROUP), GROUP)
        held = proj[tok]
        for ref, first in ((bw, rank), (cw, rank + state)):
            value = held[:, first : first + state]
            c, at = i // groups, lax.rem(i, groups)
            ref[c, pl.ds(pl.multiple_of(at * GROUP, GROUP), GROUP)] = jnp.broadcast_to(
                value[:, :, None], (GROUP, state, LANES)
            )
        return carry

    lax.fori_loop(0, rows // GROUP, wide_step, 0)
    def delta_step(t, carry):
        cols = columns(t)
        for c in range(seqs):
            tok = slice(c * ctx, (c + 1) * ctx)
            value = dot(step_low[tok], dt[:, cols]) + small[at_bias + 1 : at_bias + 2, cols]
            sig[tok, cols] = jax.nn.sigmoid(value).astype(BF16)
            value = jnp.maximum(value, 0.0) + jnp.log1p(jnp.exp(-jnp.abs(value)))
            for i in range(groups):
                delta[c * groups + i, :, cols] = value[i * GROUP : (i + 1) * GROUP]
            sums[c : c + 1, cols] = jnp.sum(value, 0, keepdims=True)
            value = value * u[tok, cols].astype(F32)
            for i in range(groups):
                v[c * groups + i, :, cols] = value[i * GROUP : (i + 1) * GROUP]
        return carry

    sums[...] = jnp.zeros(sums.shape, F32)
    lax.fori_loop(0, inner // tile, delta_step, 0)

    def sums_copy(j):
        return pltpu.make_async_remote_copy(
            src_ref=sums, dst_ref=sums_in.at[s], send_sem=sums_send.at[j],
            recv_sem=sums_recv.at[s], device_id={"seq": j}, device_id_type=MESH,
        )

    def sums_start(o, carry):
        sums_copy(lax.rem(s + o, span)).start()
        return carry

    lax.fori_loop(1, span, sums_start, 0)

    def ends_copy(j, way, c):
        return pltpu.make_async_remote_copy(
            src_ref=ends.at[way, c], dst_ref=ends_in.at[s, c], send_sem=relay_send.at[j, c],
            recv_sem=relay_recv.at[s, c], device_id={"seq": j}, device_id_type=MESH,
        )

    def ends_start(first, count, way, c):
        def one(j, carry):
            ends_copy(j, way, c).start()
            return carry

        lax.fori_loop(first, count, one, 0)

    def forward_ends(c):
        for j in range(0, inner, CHUNK):
            cuts = [slice(j + i, j + i + LANES) for i in range(0, CHUNK, LANES)]
            rates = [-jnp.exp(small[:state, cut]) * LOG2E for cut in cuts]

            def one(i, h):
                h = list(h)
                for k in range(GROUP):
                    b = bw[c, i * GROUP + k]
                    for n, cut in enumerate(cuts):
                        step = delta[c * groups + i, k : k + 1, cut]
                        factor = jnp.exp2(jnp.broadcast_to(step, (state, LANES)) * rates[n])
                        row = jnp.broadcast_to(v[c * groups + i, k : k + 1, cut], (state, LANES))
                        h[n] = factor * h[n] + row * b
                return tuple(h)

            zero = tuple(jnp.zeros((state, LANES), F32) for _ in cuts)
            h = lax.fori_loop(0, groups, one, zero)
            for n, cut in enumerate(cuts):
                ends[0, c, :, cut] = h[n].astype(BF16)

    def backward_ends(c):
        for j in range(0, inner, CHUNK):
            cuts = [slice(j + i, j + i + LANES) for i in range(0, CHUNK, LANES)]
            rates = [-jnp.exp(small[:state, cut]) * LOG2E for cut in cuts]

            def one(i, carry):
                run, p = (list(value) for value in carry)
                for k in range(GROUP):
                    read = cw[c, i * GROUP + k]
                    for n, cut in enumerate(cuts):
                        step = delta[c * groups + i, k : k + 1, cut]
                        factor = jnp.exp2(jnp.broadcast_to(step, (state, LANES)) * rates[n])
                        row = dy[c * groups + i, k : k + 1, cut]
                        run[n] = run[n] * factor
                        p[n] = p[n] + run[n] * (read * jnp.broadcast_to(row, (state, LANES)))
                return tuple(run), tuple(p)

            one_s = tuple(jnp.ones((state, LANES), F32) for _ in cuts)
            zero = tuple(jnp.zeros((state, LANES), F32) for _ in cuts)
            _, p = lax.fori_loop(0, groups, one, (one_s, zero))
            for n, cut in enumerate(cuts):
                ends[1, c, :, cut] = p[n].astype(BF16)

    def stash(*pairs):
        for at, (src, dst) in pairs:
            one = pltpu.make_async_copy(src, dst, keep.at[at])
            one.start()
            kept.append(one)

    kept = []
    stash(
        (0, (normed.at[:rows], normed_full)), (1, (bg, bg_full)), (2, (lead, lead_full)),
        (3, (slope, slope_full)), (4, (u, u_full)), (5, (sig, sig_full)), (6, (delta, delta_full)),
        (7, (cw, cw_full)), (8, (xp, xp_full)), (9, (dt, dt_full)), (10, (small, small_full)),
        (15, (bw, bw_full)),
    )

    def ends_wait(j, c):
        pltpu.make_async_remote_copy(
            src_ref=ends.at[0, c], dst_ref=ends_in.at[j, c], send_sem=relay_send.at[j, c],
            recv_sem=relay_recv.at[j, c], device_id={"seq": j}, device_id_type=MESH,
        ).wait_recv()

    def join(ref, j, c):
        ends_wait(j, c)

        def one(t, carry):
            cols = columns(t, CHUNK)
            rates = -jnp.exp(small[:state, cols]) * LOG2E
            decay = jnp.exp2(sums_in[j, c : c + 1, cols] * rates)
            ref[c, :, cols] = decay * ref[c, :, cols] + ends_in[j, c, :, cols].astype(F32)
            return carry

        lax.fori_loop(0, inner // CHUNK, one, 0)

    def join_start(c):
        def one(j, carry):
            join(start, j, c)
            return carry

        lax.fori_loop(0, s, one, 0)

    def join_final(o, carry):
        for c in range(seqs):
            join(final, span - 1 - o, c)
        return carry

    def sums_wait(o, carry):
        j = lax.rem(s + o, span)
        pltpu.make_async_remote_copy(
            src_ref=sums, dst_ref=sums_in.at[j], send_sem=sums_send.at[j],
            recv_sem=sums_recv.at[j], device_id={"seq": j}, device_id_type=MESH,
        ).wait_recv()
        return carry

    parts = inner // CHUNK
    blocks = seqs * parts

    def held_copy(b):
        slot = lax.rem(b, HELD)
        return pltpu.make_async_copy(held.at[slot], held_all.at[b], held_sem.at[slot])

    def sweep_block(b, carry):
        c, slot = b // parts, lax.rem(b, HELD)
        first = lax.rem(b, parts) * CHUNK
        cuts = [pl.ds(pl.multiple_of(first + n, LANES), LANES) for n in range(0, CHUNK, LANES)]
        tiles = [slice(n, n + LANES) for n in range(0, CHUNK, LANES)]
        all_cols = pl.ds(pl.multiple_of(first, CHUNK), CHUNK)
        rates = [-jnp.exp(small[:state, cut]) * LOG2E for cut in cuts]
        skip = small[at_bias + 2 : at_bias + 3, all_cols]

        @pl.when(b >= HELD)
        def _():
            held_copy(b - HELD).wait()

        h = tuple(start[c, :, cut] for cut in cuts)
        for n, cut in enumerate(tiles):
            held[slot, 0, :, cut] = h[n].astype(BF16)

        def one(i, h):
            h = list(h)
            g = c * groups + i
            for first_row in range(0, GROUP, 8):
                stacks = [[] for _ in cuts]
                for k in range(first_row, first_row + 8):
                    b_in, read = bw[c, i * GROUP + k], cw[c, i * GROUP + k]
                    for n, cut in enumerate(cuts):
                        step = jnp.broadcast_to(delta[g, k : k + 1, cut], (state, LANES))
                        row = jnp.broadcast_to(v[g, k : k + 1, cut], (state, LANES))
                        h[n] = jnp.exp2(step * rates[n]) * h[n] + row * b_in
                        held[slot, i * GROUP + k + 1, :, tiles[n]] = h[n].astype(BF16)
                        part = h[n] * read
                        rows_sum(stacks[n], part[:8] + part[8:], True)
                for n, cut in enumerate(cuts):
                    y[g, first_row : first_row + 8, cut] = stacks[n][0][1]
            tok = pl.ds(pl.multiple_of(g * GROUP, GROUP), GROUP)
            y[g, :, all_cols] += skip * u[tok, all_cols].astype(F32)
            return tuple(h)

        lax.fori_loop(0, groups, one, h)
        held_copy(b).start()
        return carry

    def grad_part(owner):
        shard = pl.ds(pl.multiple_of(owner * share, share), share)
        gg[:, shard] = dot(bg[...], out_w[shard], across)

    forward_ends(0)
    ends_start(s + 1, span, 0, 0)
    serve_near(GATE)
    start_own(OUT)
    own_ready(GATE)
    forward_ends(1)
    ends_start(s + 1, span, 0, 1)
    lax.fori_loop(1, span, sums_wait, 0)
    start[...] = jnp.zeros(start.shape, F32)
    join_start(0)
    serve_far(GATE)
    lax.fori_loop(0, parts // 2, sweep_block, 0)
    near_ready(GATE)
    far_ready(GATE)
    stash((11, (in_w, in_full)))

    project(zacc, rows, inner)
    serve_near(OUT)
    lax.fori_loop(parts // 2, parts, sweep_block, 0)
    serve_far(OUT)
    own_ready(OUT)
    near_ready(OUT)
    for owner in (f, fx, fy):
        grad_part(owner)
    far_ready(OUT)
    grad_part(fd)

    def gate_step(t, carry):
        cols = columns(t)
        for c in range(seqs):
            tok = slice(c * ctx, (c + 1) * ctx)
            value, grad = silu_parts(zacc[tok, cols].astype(BF16).astype(F32))
            pieces = [y[c * groups + i, :, cols] for i in range(groups)]
            scanned = jnp.concatenate(pieces, 0)
            gated[tok, cols] = (scanned * value).astype(BF16)
            half = pl.ds(pl.multiple_of(lax.rem(t, 2) * tile, tile), tile)
            zg[t // 2, tok, half] = (gg[tok, cols] * scanned * grad).astype(BF16)
        return carry

    def back_step(t, carry):
        cols = columns(t)
        for c in range(seqs):
            tok = slice(c * ctx, (c + 1) * ctx)
            value = zacc[tok, cols].astype(BF16).astype(F32)
            value = gg[tok, cols] * (value * jax.nn.sigmoid(value))
            for i in range(groups):
                dy[c * groups + i, :, cols] = value[i * GROUP : (i + 1) * GROUP]
        return carry

    lax.fori_loop(0, inner // tile, back_step, 0)
    stash((12, (dy, dy_full)))
    for c in range(seqs):
        backward_ends(c)
        ends_start(0, s, 1, c)
    for c in range(1, seqs):
        join_start(c)
    lax.fori_loop(parts, blocks, sweep_block, 0)
    lax.fori_loop(0, inner // tile, gate_step, 0)
    stash((13, (gated, gated_full)), (14, (zg, zg_full)))

    def hidden_step(t, carry):
        cols = columns(t)
        keep_rows = jnp.concatenate([mask[...]] * (tile // LANES), 1)
        branch = dot(gated[...], out_w[:, cols])
        hidden_out[:, cols] = (x[:, cols].astype(F32) + keep_rows * branch).astype(BF16)
        return carry

    lax.fori_loop(0, width // tile, hidden_step, 0)
    final[...] = jnp.zeros(final.shape, F32)
    lax.fori_loop(0, span - 1 - s, join_final, 0)

    for one in started:
        one.wait_send()

    @pl.when(s < span - 1)
    def _():
        for c in range(seqs):
            edges(c).wait_send()

    def sent(o, carry):
        j = lax.rem(s + o, span)
        sums_copy(j).wait_send()
        for c in range(seqs):
            ends_copy(j, 0, c).wait_send()
        return carry

    lax.fori_loop(1, span, sent, 0)
    for one in kept:
        one.wait()
    for b in range(max(blocks - HELD, 0), blocks):
        held_copy(b).wait()


def front(x, og, lengths, taps, logs, cbias, dbias, skip, gain, xp_tall, in_own, out_own, dt_own, seqs):
    rows, width = x.shape
    share, inner = taps.shape[1], 4 * taps.shape[1]
    state, rank, used = logs.shape[0], dt_own.shape[0], LANES
    ctx = rows // seqs
    span = lax.axis_size("seq")
    parts = inner // CHUNK
    vmem, dma = pltpu.VMEM, pltpu.SemaphoreType.DMA
    whole, anywhere = pl.BlockSpec(memory_space=vmem), pl.BlockSpec(memory_space=pl.ANY)
    shape = jax.ShapeDtypeStruct
    grouped = (rows // GROUP, GROUP, inner)
    kept = [
        ((rows, width), BF16),
        ((rows, width), BF16),
        ((seqs, ctx + GROUP, inner), BF16),
        ((rows, inner), BF16),
        ((rows, inner), BF16),
        ((rows, inner), BF16),
        (grouped, F32),
        ((seqs, ctx, state, LANES), F32),
        ((seqs, ctx, state, LANES), F32),
        (grouped, F32),
        ((rows, inner), BF16),
        ((parts, rows, CHUNK), BF16),
        ((width, 2 * inner), BF16),
        ((inner, used), BF16),
        ((rank, inner), BF16),
        ((32, inner), F32),
    ]
    held = (ctx + 1, state, CHUNK)
    return pl.pallas_call(
        functools.partial(front_kernel, span),
        in_specs=[whole, whole, pl.BlockSpec(memory_space=pltpu.SMEM)]
        + [whole] * 7
        + [anywhere] * 3,
        out_specs=[whole] * 3 + [anywhere] * (1 + len(kept)),
        out_shape=[
            shape((rows, width), BF16),
            shape((rows, rank), BF16),
            shape((seqs, state, inner), F32),
            shape((seqs * parts,) + held, BF16),
        ]
        + [shape(*k) for k in kept],
        scratch_shapes=[
            vmem((width, 2 * inner), BF16),
            vmem((inner, width), BF16),
            vmem((inner, used), BF16),
            vmem((rank, inner), BF16),
            vmem((32, inner), F32),
            vmem((32, share), F32),
            vmem((share, LANES), BF16),
            vmem((seqs, GROUP, width), BF16),
            vmem((rows + seqs * GROUP, inner), F32),
            vmem((rows, inner), F32),
            vmem((rows + seqs * GROUP, width), BF16),
            vmem(grouped, F32),
            vmem((rows, used), F32),
            vmem((2, seqs, state, inner), BF16),
            vmem((8, inner), F32),
            vmem((span, seqs, state, inner), BF16),
            vmem((span, 8, inner), F32),
            vmem((rows, width), BF16),
            vmem((rows, LANES), F32),
            vmem((seqs, ctx + GROUP, inner), BF16),
            vmem((rows, inner), BF16),
            vmem((rows, inner), BF16),
            vmem((rows, inner), BF16),
            vmem(grouped, F32),
            vmem((seqs, ctx, state, LANES), F32),
            vmem((seqs, ctx, state, LANES), F32),
            vmem((rows, inner), F32),
            vmem(grouped, F32),
            vmem(grouped, F32),
            vmem((rows, inner), BF16),
            vmem((parts, rows, CHUNK), BF16),
            vmem((seqs, state, inner), F32),
            vmem((HELD,) + held, BF16),
            dma((6, 18)),
            dma((6, 18)),
            dma((2, seqs)),
            dma((span, seqs)),
            dma((span, seqs)),
            dma((span,)),
            dma((span,)),
            dma((6, 4)),
            dma((len(kept),)),
            dma((HELD,)),
        ],
        compiler_params=pltpu.CompilerParams(
            collective_id=0, has_side_effects=True, vmem_limit_bytes=63 << 20
        ),
        name="front",
    )(x, og, lengths, taps, logs, cbias, dbias, skip, gain, xp_tall, in_own, out_own, dt_own)


def back_kernel(
    span, state, rank,
    gated, bg, step_low, final, small, x, og,
    held_all, normed_full, lead_full, slope_full, u_full, sig_full, delta_full, bw_full,
    cw_full, dy_full, zg_full, in_full, xp_full, dt_full,
    input_grad, out_sum, in_sum, rest_sum,
    normed, lead, slope, u, sig, delta, bw, cw, dy, mixed, xp, dt, in_w, held, v, rl, cacc,
    bacc, logs, sums,
    pg, pg_full, cg, ng, rest, g, ra, rx, ry, zlo, zhi, tot,
    send, recv, halo, local, load, held_sem, in_sem,
):
    d, s, f = (lax.axis_index(a) for a in ("dp", "seq", "fsdp"))
    fx, fy, fd = f ^ 1, f ^ 2, f ^ 3
    chunks = tot.shape[0]
    rows, width = x.shape
    inner = gated.shape[1]
    seqs = cg.shape[0]
    ctx = rows // seqs
    parts = inner // CHUNK
    out_chunks = 2 * width // CHUNK
    in_chunks = 2 * parts
    last = out_chunks + in_chunks
    slots = g.shape[0]
    q = HR // 2
    roots = ((span - 1) // 2, span // 2)
    most = span // 2
    tox, toy, sib = {"fsdp": fx}, {"fsdp": fy}, {"dp": 1 - d}
    up, down = {"seq": jnp.minimum(s + 1, span - 1)}, {"seq": jnp.maximum(s - 1, 0)}
    contract = (((0,), (0,)), ((), ()))
    across = (((1,), (1,)), ((), ()))
    dot = lambda a, b, dims=(((1,), (0,)), ((), ())): lax.dot_general(
        a, b, dims, preferred_element_type=F32
    )

    parts_of = lambda v, c: v.at[pl.ds(c * (v.shape[0] // seqs), v.shape[0] // seqs)]
    by_context = ((delta, delta_full), (dy, dy_full), (u, u_full), (cw, cw_full), (bw, bw_full), (sig, sig_full))
    pairs = [
        (parts_of(dst, c), parts_of(src, c)) for c in range(seqs) for dst, src in by_context
    ]
    first_loads = len(pairs)
    pairs += [
        (mixed.at[:parts], zg_full), (normed, normed_full), (slope, slope_full), (lead, lead_full),
        (xp, xp_full), (dt, dt_full),
    ]
    loads = [pltpu.make_async_copy(src, dst, load.at[n]) for n, (dst, src) in enumerate(pairs)]

    def held_copy(b):
        slot = lax.rem(b, 2)
        return pltpu.make_async_copy(held_all.at[b], held.at[slot], held_sem.at[slot])

    def in_copy(k):
        slot = lax.rem(k, 2)
        first = pl.multiple_of(lax.rem(k + parts, 2 * parts) * CHUNK, CHUNK)
        return pltpu.make_async_copy(in_full.at[:, pl.ds(first, CHUNK)], in_w.at[slot], in_sem.at[slot])

    held_copy(0).start()
    for one in loads[: len(by_context)]:
        one.start()
    held_copy(1).start()
    for one in loads[len(by_context) :]:
        one.start()
    cg[:, ctx:] = jnp.zeros((seqs, cg.shape[1] - ctx, inner), F32)
    barrier = pltpu.get_barrier_semaphore()
    for who in (tox, toy, sib):
        pl.semaphore_signal(barrier, inc=1, device_id=who, device_id_type=MESH)

    @pl.when(s > 0)
    def _():
        pl.semaphore_signal(barrier, inc=1, device_id=down, device_id_type=MESH)

    @pl.when(s < span - 1)
    def _():
        pl.semaphore_signal(barrier, inc=1, device_id=up, device_id_type=MESH)

    ends = (s == 0) | (s == span - 1)
    pl.semaphore_wait(barrier, jnp.where(ends, 4, 5) if span > 1 else 3)

    def copy(kind, c, src, dst, who):
        return pltpu.make_async_remote_copy(
            src_ref=src, dst_ref=dst, send_sem=send.at[kind, c], recv_sem=recv.at[kind, c],
            device_id=who, device_id_type=MESH,
        )

    lo, hi = slice(0, q), slice(q, HR)
    A = lambda c: copy(0, c, g.at[lax.rem(c, slots), :, 1 - d], ra.at[c], sib)
    X0 = lambda c: copy(1, c, ra.at[c, fd, lo], rx.at[c, 0], tox)
    X1 = lambda c: copy(2, c, ra.at[c, fx, lo], rx.at[c, 1], tox)
    X2 = lambda c: copy(3, c, ra.at[c, fx, hi], rx.at[c, 2], tox)
    Y0 = lambda c: copy(4, c, ra.at[c, fd, hi], ry.at[c, 0], toy)
    Y2 = lambda c: copy(5, c, ra.at[c, fy, hi], ry.at[c, 2], toy)
    Y1 = lambda c: copy(6, c, ra.at[c, fy, lo], ry.at[c, 1], toy)
    part = (lo, hi)
    ZU = lambda c, h: copy(7 + h, c, ra.at[c, f, part[h]], zlo.at[c, part[h]], up)
    ZD = lambda c, h: copy(9 + h, c, ra.at[c, f, part[h]], zhi.at[c, part[h]], down)
    TU = lambda c, h: copy(11 + h, c, tot.at[c, d, part[h]], tot.at[c, d, part[h]], up)
    TD = lambda c, h: copy(13 + h, c, tot.at[c, d, part[h]], tot.at[c, d, part[h]], down)
    D = lambda c, h: copy(15 + h, c, tot.at[c, d, part[h]], tot.at[c, d, part[h]], sib)
    below, above = [s < r for r in roots], [s > r for r in roots]
    spot = [
        jnp.where(below[h], s, jnp.where(above[h], span - 1 - s, 0)) for h in range(2)
    ]
    far = [jnp.abs(s - r) for r in roots]

    def stage(c, run):
        @pl.when((c >= 0) & (c < chunks))
        def _():
            run(c)

    def produce(c):
        slot = lax.rem(c, slots)

        @pl.when(c >= slots)
        def _():
            A(c - slots).wait_send()

        @pl.when(c < out_chunks)
        def _():
            r = c // (width // CHUNK)
            col = lax.rem(c, width // CHUNK) * CHUNK
            right = bg[:, pl.ds(pl.multiple_of(col, CHUNK), CHUNK)]
            for j in range(4):
                for h in range(2):
                    at = j * (inner // 4) + h * (inner // 8) + r * HR
                    left = gated[:, pl.ds(pl.multiple_of(at, HR), HR)]
                    g[slot, j, h] = dot(left, right, contract).astype(BF16)

        @pl.when((c >= out_chunks) & (c < last))
        def _():
            right = mixed[c - out_chunks]
            for j in range(4):
                t = dot(normed[:, j * 2 * HR : (j + 1) * 2 * HR], right, contract).astype(BF16)
                g[slot, j, 0] = t[:HR]
                g[slot, j, 1] = t[HR:]

        @pl.when(c == last)
        def _():
            for j in range(4):
                for h in range(2):
                    cols = slice(j * CHUNK, (j + 1) * CHUNK)
                    g[slot, j, h] = rest[h * HR : (h + 1) * HR, cols].astype(BF16)

        A(c).start()

    def first_sum(c):
        A(c).wait_recv()
        for j in range(4):
            own = g[lax.rem(c, slots), j, d]
            ra[c, j] = ra[c, j] + own
        X0(c).start()
        Y0(c).start()
        X1(c).start()
        Y2(c).start()

    def second_sum(c):
        X0(c).wait_recv()
        ra[c, fy, lo] = ra[c, fy, lo] + rx[c, 0]
        Y1(c).start()
        Y0(c).wait_recv()
        ra[c, fx, hi] = ra[c, fx, hi] + ry[c, 0]
        X2(c).start()

    def third_sum(c):
        X1(c).wait_recv()
        Y2(c).wait_recv()
        X2(c).wait_recv()
        Y1(c).wait_recv()
        for k, piece in enumerate((lo, hi)):
            total = ra[c, f, piece].astype(F32) + rx[c, 1 + k].astype(F32) + ry[c, 1 + k].astype(F32)
            ra[c, f, piece] = total.astype(BF16)

    def inward(c, h):
        @pl.when(below[h] & (s > 0))
        def _():
            ZU(c, h).wait_recv()
            ra[c, f, part[h]] = ra[c, f, part[h]] + zlo[c, part[h]]

        @pl.when(above[h] & (s < span - 1))
        def _():
            ZD(c, h).wait_recv()
            ra[c, f, part[h]] = ra[c, f, part[h]] + zhi[c, part[h]]

        pl.when(below[h])(lambda: ZU(c, h).start())
        pl.when(above[h])(lambda: ZD(c, h).start())

    def at_root(c, h):
        total = ra[c, f, part[h]].astype(F32)
        if roots[h] > 0:
            ZU(c, h).wait_recv()
            total = total + zlo[c, part[h]].astype(F32)
        if span - 1 > roots[h]:
            ZD(c, h).wait_recv()
            total = total + zhi[c, part[h]].astype(F32)
        tot[c, d, part[h]] = total.astype(BF16)
        if roots[h] > 0:
            TD(c, h).start()
        if span - 1 > roots[h]:
            TU(c, h).start()
        D(c, h).start()

    def outward(c, h):
        @pl.when(above[h])
        def _():
            TU(c, h).wait_recv()
            pl.when(s < span - 1)(lambda: TU(c, h).start())

        @pl.when(below[h])
        def _():
            TD(c, h).wait_recv()
            pl.when(s > 0)(lambda: TD(c, h).start())

        D(c, h).start()

    tile = 2 * LANES

    def columns(t, size=tile):
        return pl.ds(pl.multiple_of(t * size, size), size)

    def back_block(b):
        c, slot = b // parts, lax.rem(b, 2)
        groups = ctx // GROUP
        first = lax.rem(b, parts) * CHUNK
        cuts = [pl.ds(pl.multiple_of(first + n, LANES), LANES) for n in range(0, CHUNK, LANES)]
        tiles = [slice(n, n + LANES) for n in range(0, CHUNK, LANES)]
        cols = pl.ds(pl.multiple_of(first, CHUNK), CHUNK)
        rates = [-jnp.exp(small[:state, cut]) * LOG2E for cut in cuts]
        skip = small[TAPS + state + 2 : TAPS + state + 3, cols]
        held_copy(b).wait()

        def one(turn, carry):
            i = groups - 1 - turn
            at = c * groups + i
            tok = pl.ds(pl.multiple_of(at * GROUP, GROUP), GROUP)
            p, total, kept = (list(value) for value in carry)
            value, out, gain = u[tok, cols].astype(F32), dy[at, :, cols], delta[at, :, cols]
            v[...] = gain * value
            drive_parts, delta_parts = [[], []], [[], []]
            for pair in range(0, len(cuts), 2):
                which = range(pair, pair + 2)
                after = {n: held[slot, (i + 1) * GROUP, :, tiles[n]].astype(F32) for n in which}
                for half in (1, 0):
                    drives, deltas = ({n: [] for n in which} for _ in range(2))
                    for k in reversed(range(half * 8, half * 8 + 8)):
                        t = i * GROUP + k
                        b_in, read = bw[c, t], cw[c, t]
                        b_parts, c_parts = [], []
                        for n in which:
                            row = lambda tile: jnp.broadcast_to(tile, (state, LANES))
                            step, back = row(delta[at, k : k + 1, cuts[n]]), row(dy[at, k : k + 1, cuts[n]])
                            grad = read * back + p[n]
                            p[n] = jnp.exp2(step * rates[n]) * grad
                            before = held[slot, t, :, tiles[n]].astype(F32)
                            w = p[n] * before
                            total[n] = total[n] + w * step
                            part = w * rates[n]
                            rows_sum(deltas[n], part[:8] + part[8:], False)
                            part = grad * b_in
                            rows_sum(drives[n], part[:8] + part[8:], False)
                            b_parts.append(grad * row(v[k : k + 1, tiles[n]]))
                            c_parts.append(after[n] * back)
                            after[n] = before
                        bacc[c * ctx + t] += b_parts[0] + b_parts[1]
                        cacc[c * ctx + t] += c_parts[0] + c_parts[1]
                    drive_parts[half] += [drives[n][0][1] for n in which]
                    delta_parts[half] += [deltas[n][0][1] for n in which]
            joined = lambda halves: jnp.concatenate([jnp.concatenate(h, 1) for h in halves], 0)
            drive_grad, delta_part = joined(drive_parts), joined(delta_parts)
            raw_grad = drive_grad * value + delta_part * (1.0 / LOG2E)
            raw_grad = raw_grad * sig[tok, cols].astype(F32)
            rl[tok, cols] = raw_grad.astype(BF16)
            dy[at, :, cols] = out * skip + drive_grad * gain
            kept[0] = kept[0] + (out * value)[:8] + (out * value)[8:]
            kept[1] = kept[1] + raw_grad[:8] + raw_grad[8:]
            return tuple(p), tuple(total), tuple(kept)

        zero = tuple(jnp.zeros((state, LANES), F32) for _ in cuts)
        none = jnp.zeros((8, CHUNK), F32)
        begin = tuple(final[c, :, cut] for cut in cuts)
        _, total, kept = lax.fori_loop(0, groups, one, (begin, zero, (none, none)))
        for n, cut in enumerate(cuts):
            logs[:, cut] += total[n]
        sums[0, :, cols] += kept[0]
        sums[1, :, cols] += kept[1]

        @pl.when(b + 2 < blocks)
        def _():
            held_copy(b + 2).start()

    def proj_work():
        step_grad = dot(rl[...], dt[...], across)
        col = lax.broadcasted_iota(jnp.int32, (state, LANES), 1)
        n = lax.broadcasted_iota(jnp.int32, (state, LANES), 0)
        ones = jnp.ones((LANES, LANES), BF16)

        def one(r, carry):
            tok = pl.ds(pl.multiple_of(r * GROUP, GROUP), GROUP)
            total = pg_full[tok]
            for ref, first in ((bacc, rank), (cacc, rank + state)):
                value = dot(ref[tok].reshape(GROUP * state, LANES).astype(BF16), ones)
                keep = jnp.where(col == n + first, value.reshape(GROUP, state, LANES), 0.0)
                total = total + jnp.sum(keep, 1)
            pg[tok] = total.astype(BF16)
            return carry

        pg_full[...] = jnp.concatenate([step_grad, jnp.zeros((rows, LANES - rank), F32)], 1)
        lax.fori_loop(0, rows // GROUP, one, 0)

    def weight_work():
        first = TAPS + state + 4
        used = rank + 2 * state

        def weights(t, carry):
            cols = columns(t)
            rest[first : first + rank, cols] = dot(step_low[...], rl[:, cols], contract)
            rest[first + rank : first + rank + used, cols] = dot(pg[...], u[:, cols], contract)[:used]
            kept = -logs[:, cols] * jnp.exp(small[:state, cols])
            rest[:state, cols] = kept
            at = TAPS + state
            rest[at + 1 : at + 2, cols] = jnp.sum(sums[1, :, cols], 0, keepdims=True)
            rest[at + 2 : at + 3, cols] = jnp.sum(sums[0, :, cols], 0, keepdims=True)
            return carry

        lax.fori_loop(0, inner // tile, weights, 0)

    def conv_work(first, count):
        def one(t, carry):
            cols = columns(t)
            shift = jnp.zeros((1, tile), F32)
            taps = [jnp.zeros((1, tile), F32) for _ in range(TAPS)]
            for c in range(seqs):
                tok = slice(c * ctx, (c + 1) * ctx)
                weight = xp[columns(t)]
                back = dot(pg[tok], weight, across)
                own = range(c * ctx // GROUP, (c + 1) * ctx // GROUP)
                grad = jnp.concatenate([dy[at, :, cols] for at in own], 0) + back
                grad = grad * slope[tok, cols].astype(F32)
                cg[c, :ctx, cols] = grad
                before = lead[c, :, cols].astype(F32)
                shift = shift + jnp.sum(grad, 0, keepdims=True)
                for k in range(TAPS):
                    at = GROUP - TAPS + 1 + k
                    taps[k] = taps[k] + jnp.sum(grad * before[at : at + ctx], 0, keepdims=True)
            for k in range(TAPS):
                rest[state + k : state + k + 1, cols] = taps[k]
            rest[TAPS + state : TAPS + state + 1, cols] = shift
            return carry

        lax.fori_loop(first, first + count, one, 0)

    edge = cg.shape[1] - ctx
    H = lambda: pltpu.make_async_remote_copy(
        src_ref=cg.at[:, :edge], dst_ref=cg.at[:, ctx:], send_sem=halo.at[0],
        recv_sem=halo.at[1], device_id=down, device_id_type=MESH,
    )

    def halo_send():
        pl.when(s > 0)(lambda: H().start())

    def stream_work():
        pl.when(s < span - 1)(lambda: H().wait_recv())

        def one(t, carry):
            cols = columns(t)
            for c in range(seqs):
                total = 0.0
                for k in range(TAPS):
                    at = TAPS - 1 - k
                    total = total + small[state + k : state + k + 1, cols] * cg[c, at : at + ctx, cols]
                half = pl.ds(pl.multiple_of(lax.rem(t, 2) * tile, tile), tile)
                mixed[parts + t // 2, c * ctx : (c + 1) * ctx, half] = total.astype(BF16)
            return carry

        lax.fori_loop(0, inner // tile, one, 0)
        pl.when(s > 0)(lambda: H().wait_send())

    def norm_work(first, count):
        def one(k, carry):
            in_copy(k).wait()
            ng[...] += dot(mixed[k], in_w[lax.rem(k, 2)], across)

            @pl.when(k + 2 < 2 * parts)
            def _():
                in_copy(k + 2).start()

            return carry

        if first == 0:
            ng[...] = jnp.zeros(ng.shape, F32)
        lax.fori_loop(first, first + count, one, 0)

    def input_work():
        share = width // 4
        at = TAPS + state + 3
        gain = jnp.concatenate(
            [small[at : at + 1, j * CHUNK : j * CHUNK + share] for j in range(4)], 1
        )

        def one(r, total):
            tok = pl.ds(pl.multiple_of(r * GROUP, GROUP), GROUP)
            xs = x[tok].astype(F32)
            inverse = lax.rsqrt(jnp.mean(xs * xs, -1, keepdims=True) + EPS)
            grad = ng[tok]
            scaled = grad * gain
            slope = jnp.mean(scaled * xs, -1, keepdims=True)
            out = inverse * scaled - xs * (inverse * inverse * inverse * slope)
            input_grad[tok] = (out + og[tok].astype(F32)).astype(BF16)
            return total + grad * (xs * inverse)

        total = lax.fori_loop(0, rows // GROUP, one, jnp.zeros((GROUP, width), F32))
        total = jnp.sum(total, 0, keepdims=True)
        for j in range(4):
            rest[at : at + 1, j * CHUNK : j * CHUNK + share] = total[:, j * share : (j + 1) * share]

    blocks = seqs * parts
    tiles = inner // tile
    pause = 3
    held_back = out_chunks + parts
    base = 1 + 2 * SLACK + 1

    def prepare():
        for ref in (cacc, bacc, logs, sums, rest):
            ref[...] = jnp.zeros(ref.shape, F32)

    def blocks_work(i):
        pl.when(i == 0)(prepare)
        for c in range(seqs):

            @pl.when(i == c * parts)
            def _():
                for one in loads[c * len(by_context) : (c + 1) * len(by_context)]:
                    one.wait()

        pl.when(i < blocks)(lambda: back_block(i))

    def late_work(i):
        at = held_back

        @pl.when(i == at)
        def _():
            proj_work()
            conv_work(0, tiles)
            halo_send()
            in_copy(0).start()
            in_copy(1).start()

        pl.when(i == at + 1)(weight_work)
        pl.when(i == at + 2)(stream_work)
        pl.when(i == at + 4)(lambda: norm_work(0, parts))
        pl.when(i == at + 5)(lambda: norm_work(parts, parts))
        pl.when(i == at + 6)(input_work)

    def step(i, carry):
        def at(offset):
            k = i - offset
            return jnp.where(k < held_back, k, jnp.where(k < held_back + pause, -1, k - pause))

        @pl.when(i == out_chunks)
        def _():
            for one in loads[first_loads:]:
                one.wait()

        for h in range(2):
            run = lambda f: lambda c: f(c, h)
            away = s != roots[h]
            pl.when(away)(lambda: stage(at(base + SLACK * (most + far[h])), run(outward)))
            pl.when(~away)(lambda: stage(at(base + SLACK * most), run(at_root)))
            pl.when(away)(lambda: stage(at(base + SLACK * spot[h]), run(inward)))
        stage(at(1 + 2 * SLACK), third_sum)
        stage(at(1 + SLACK), second_sum)
        stage(at(1), first_sum)
        stage(at(0), produce)
        blocks_work(i)
        late_work(i)
        return carry

    lax.fori_loop(0, chunks + pause + base + 2 * SLACK * most + 1, step, 0)

    def finish(c, carry):
        pl.when(c >= chunks - slots)(lambda: A(c).wait_send())
        for t in (X0, X1, X2, Y0, Y1, Y2):
            t(c).wait_send()
        for h, root in enumerate(roots):
            pl.when(below[h])(lambda: ZU(c, h).wait_send())
            pl.when(above[h])(lambda: ZD(c, h).wait_send())
            if root > 0:
                pl.when((s <= root) & (s > 0))(lambda: TD(c, h).wait_send())
            if span - 1 > root:
                pl.when((s >= root) & (s < span - 1))(lambda: TU(c, h).wait_send())
            D(c, h).wait_send()
            D(c, h).wait_recv()
        return carry

    lax.fori_loop(0, chunks, finish, 0)
    copies = []
    for c in range(chunks):
        for h in range(2):
            if c < out_chunks:
                r, col = c // (width // CHUNK), c % (width // CHUNK)
                first = h * (inner // 8) + r * HR
                to = out_sum.at[first : first + HR, col * CHUNK : (col + 1) * CHUNK]
            elif c < last:
                col = (c - out_chunks + parts) % (2 * parts)
                to = in_sum.at[h * HR : (h + 1) * HR, col * CHUNK : (col + 1) * CHUNK]
            else:
                to = rest_sum.at[h * HR : (h + 1) * HR]
            copies.append(pltpu.make_async_copy(tot.at[c, h], to, local.at[c, h]))
    for one in copies:
        one.start()
    for one in copies:
        one.wait()


def back(gated, bg, step_low, final, small, x, og, far):
    rows, inner = gated.shape
    width = x.shape[1]
    seqs, state = final.shape[:2]
    ctx, rank, parts = rows // seqs, step_low.shape[1], inner // CHUNK
    span = lax.axis_size("seq")
    out_chunks, in_chunks = 2 * width // CHUNK, 2 * parts
    n = out_chunks + in_chunks + 1
    vmem, dma = pltpu.VMEM, pltpu.SemaphoreType.DMA
    anywhere = pl.BlockSpec(memory_space=pl.ANY)
    whole = pl.BlockSpec(memory_space=vmem)
    shape = jax.ShapeDtypeStruct
    like = lambda v: vmem(v.shape, v.dtype)
    (held, normed, lead, slope, u, sig, delta, bw, cw, dy, zg, in_full, xp, dt) = far
    return pl.pallas_call(
        functools.partial(back_kernel, span, state, rank),
        in_specs=[whole] * 7 + [anywhere] * len(far),
        out_specs=[whole, anywhere, anywhere, anywhere],
        out_shape=[
            shape((rows, width), BF16),
            shape((inner // 4, width), BF16),
            shape((width // 4, 2 * inner), BF16),
            shape((2 * HR, CHUNK), BF16),
        ],
        scratch_shapes=[
            *map(like, (normed, lead, slope, u, sig, delta, bw, cw, dy)),
            vmem((in_chunks, rows, CHUNK), BF16),
            like(xp),
            like(dt),
            vmem((2, width, CHUNK), BF16),
            vmem((2,) + held.shape[1:], BF16),
            vmem((GROUP, CHUNK), F32),
            vmem((rows, inner), BF16),
            vmem((rows, state, LANES), F32),
            vmem((rows, state, LANES), F32),
            vmem((state, inner), F32),
            vmem((2, 8, inner), F32),
            vmem((rows, LANES), BF16),
            vmem((rows, LANES), F32),
            vmem((seqs, ctx + 8, inner), F32),
            vmem((rows, width), F32),
            vmem((2 * HR, inner), F32),
            vmem((4, 4, 2, HR, CHUNK), BF16),
            vmem((n, 4, HR, CHUNK), BF16),
            vmem((n, 3, HR // 2, CHUNK), BF16),
            vmem((n, 3, HR // 2, CHUNK), BF16),
            vmem((n, HR, CHUNK), BF16),
            vmem((n, HR, CHUNK), BF16),
            vmem((n, 2, HR, CHUNK), BF16),
            dma((17, n)),
            dma((17, n)),
            dma((2,)),
            dma((n, 2)),
            dma((12 + 6,)),
            dma((2,)),
            dma((2,)),
        ],
        compiler_params=pltpu.CompilerParams(
            collective_id=1, has_side_effects=True, vmem_limit_bytes=63 << 20
        ),
        name="back",
    )(gated, bg, step_low, final, small, x, og, *far)


def finish_kernel(
    state, rank, used, in_sum, out_sum, rest, hidden, grad,
    gain, in_w, taps, cbias, xp, dt, dbias, logs, skip, out_w, hidden_out, grad_out,
):
    hidden_out[...] = hidden[...]
    grad_out[...] = grad[...]
    in_w[...] = in_sum[...].astype(F32)
    out_w[...] = out_sum[...].astype(F32)
    at = TAPS + state
    row = lambda first, count=1: rest[...].astype(F32)[first : first + count]
    logs[...] = row(0, state)
    taps[...] = row(state, TAPS)
    cbias[...] = row(at)
    dbias[...] = row(at + 1)
    skip[...] = row(at + 2)
    gain[...] = row(at + 3)[:, : gain.shape[1]]
    dt[...] = row(at + 4, rank)
    xp[...] = row(at + 4 + rank, used)


def finish(in_sum, out_sum, rest, hidden, grad, state, rank, used):
    steps = 2
    share = rest.shape[1]
    tall = lambda v: pl.BlockSpec((v.shape[0] // steps, v.shape[1]), lambda i: (i, 0))
    fixed = lambda *v: pl.BlockSpec(v, lambda i: (0, 0))
    small = [(1, in_sum.shape[0]), (TAPS, share), (1, share), (used, share), (rank, share)]
    small += [(1, share), (state, share), (1, share)]
    shape = lambda v: jax.ShapeDtypeStruct(v, F32)
    return pl.pallas_call(
        functools.partial(finish_kernel, state, rank, used),
        grid=(steps,),
        in_specs=[tall(in_sum), tall(out_sum), fixed(*rest.shape), tall(hidden), tall(grad)],
        out_specs=[fixed(*small[0]), tall(in_sum)]
        + [fixed(*v) for v in small[1:]]
        + [tall(out_sum), tall(hidden), tall(grad)],
        out_shape=[shape(small[0]), shape(in_sum.shape)]
        + [shape(v) for v in small[1:]]
        + [shape(out_sum.shape)]
        + [jax.ShapeDtypeStruct(v.shape, v.dtype) for v in (hidden, grad)],
        compiler_params=pltpu.CompilerParams(vmem_limit_bytes=63 << 20),
        name="finish",
    )(in_sum, out_sum, rest, hidden, grad)


def body(
    hidden_in, lengths, norm_gain, in_weight, conv_weight, conv_bias, xproj_weight,
    dt_weight, dt_bias, a_log, skip_gain, out_weight, out_grad,
):
    seqs, ctx, width = hidden_in.shape
    taps, share = conv_weight.shape
    state = a_log.shape[0]
    rank = dt_weight.shape[0]
    rows = ctx * seqs
    row = lambda v: v.reshape(1, -1)
    x, og = hidden_in.reshape(rows, width), out_grad.reshape(rows, width)
    used = xproj_weight.shape[1]
    (
        hidden_out, step_low, final, held, normed, branch_grad, lead, slope, u, sig, delta,
        b_wide, c_wide, y_grad, gated, z_grad, in_matrix, proj_matrix, step_matrix, small,
    ) = front(
        x, og, lengths, conv_weight, a_log, row(conv_bias), row(dt_bias), row(skip_gain),
        row(norm_gain), xproj_weight.T, in_weight, out_weight, dt_weight, seqs,
    )
    far = (
        held, normed, lead, slope, u, sig, delta, b_wide, c_wide, y_grad, z_grad, in_matrix,
        proj_matrix, step_matrix,
    )
    input_grad, out_sum, in_sum, rest = back(
        gated, branch_grad, step_low, final, small, x, og, far
    )
    (
        gain, in_w, taps_grad, cbias, proj_w, step_w, dbias, logs, skip, out_w, hidden_out, input_grad,
    ) = finish(in_sum, out_sum, rest, hidden_out, input_grad, state, rank, used)
    flat = lambda v: v.reshape(-1)
    return (
        hidden_out.reshape(seqs, ctx, width), input_grad.reshape(seqs, ctx, width), flat(gain), in_w,
        taps_grad, flat(cbias), proj_w.T, step_w, flat(dbias), logs, flat(skip), out_w,
    )


def solution(mesh):
    tokens = P(("dp", "fsdp"), "seq", None)
    return jax.shard_map(
        body,
        mesh=mesh,
        in_specs=(
            tokens, P(("dp", "fsdp")), P("fsdp"), P("fsdp", None), P(None, "fsdp"), P("fsdp"),
            P("fsdp", None), P(None, "fsdp"), P("fsdp"), P(None, "fsdp"), P("fsdp"),
            P("fsdp", None), tokens,
        ),
        out_specs=(
            tokens, tokens, P("fsdp"), P("fsdp", None), P(None, "fsdp"), P("fsdp"),
            P("fsdp", None), P(None, "fsdp"), P("fsdp"), P(None, "fsdp"), P("fsdp"),
            P("fsdp", None),
        ),
        check_vma=False,
    )
```

```python
import functools
import math

import jax
import jax.numpy as jnp
import numpy as np
from jax import lax
from jax.experimental import pallas as pl
from jax.experimental.pallas import tpu as pltpu
from jax.sharding import PartitionSpec as P

EPS = 1e-05
LOG2E = math.log2(math.e)
LANES = 128
GROUP = 16
F32 = jnp.float32
BF16 = jnp.bfloat16
MESH = pl.DeviceIdType.MESH
HR = 128
CHUNK = 512
SLACK = 2
TAPS = 4
HELD = 3


def silu_parts(v):
    s = jax.nn.sigmoid(v)
    return v * s, s * (1.0 + v * (1.0 - s))


def rows_sum(stack, value, rising):
    row = lax.broadcasted_iota(jnp.int32, value.shape, 0)
    level = 0
    while stack and stack[-1][0] == level:
        _, other = stack.pop()
        first, second = (other, value) if rising else (value, other)
        low = (row & (1 << level)) == 0
        turned = pltpu.roll(jnp.where(low, second, first), 1 << level, 0)
        value = jnp.where(low, first, second) + turned
        level += 1
    stack.append((level, value))


def front_kernel(
    span,
    x, og, lengths, taps_own, log_own, cbias_own, dbias_own, skip_own, gain_own,
    xp_tall, in_own, out_own, dt_own,
    hidden_out, step_low, final,
    held_all, normed_full, bg_full, lead_full, slope_full, u_full, sig_full, delta_full, bw_full,
    cw_full, dy_full, gated_full, zg_full, in_full, xp_full, dt_full, small_full,
    in_w, out_w, xp, dt, small, small_own, xp_own, hx, acc, zacc, normed, v, proj, ends, sums,
    ends_in, sums_in, bg, mask, lead, slope, u, sig, delta, bw, cw, gg, dy, y, gated, zg,
    start, held,
    send, recv, halo, relay_send, relay_recv, sums_send, sums_recv, local, keep, held_sem,
):
    d, s, f = (lax.axis_index(a) for a in ("dp", "seq", "fsdp"))
    fx, fy, fd = f ^ 1, f ^ 2, f ^ 3
    tox, toy, tod, sib = {"fsdp": fx}, {"fsdp": fy}, {"fsdp": fd}, {"dp": 1 - d}
    rows, width = x.shape
    inner = u.shape[1]
    seqs = bw.shape[0]
    ctx = rows // seqs
    state, rank = log_own.shape[0], dt_own.shape[0]
    groups = ctx // GROUP
    share = inner // 4
    at_bias = state + TAPS
    across = (((1,), (1,)), ((), ()))
    dot = lambda a, b, dims=(((1,), (0,)), ((), ())): lax.dot_general(
        a, b, dims, preferred_element_type=F32
    )

    for c in range(seqs):
        hx[c] = jnp.zeros((GROUP, width), BF16)
    barrier = pltpu.get_barrier_semaphore()
    for who in (tox, toy, tod, sib):
        pl.semaphore_signal(barrier, inc=1, device_id=who, device_id_type=MESH)

    def greet(o, carry):
        who = {"seq": lax.rem(s + o, span)}
        pl.semaphore_signal(barrier, inc=1, device_id=who, device_id_type=MESH)
        return carry

    lax.fori_loop(1, span, greet, 0)
    blank = jnp.zeros((LANES - xp_tall.shape[0], share), BF16)
    xp_own[...] = jnp.concatenate([xp_tall[...], blank], 0).T
    small_own[...] = jnp.zeros(small_own.shape, F32)
    small_own[:state] = log_own[...]
    small_own[state:at_bias] = taps_own[...]
    small_own[at_bias : at_bias + 1] = cbias_own[...]
    small_own[at_bias + 1 : at_bias + 2] = dbias_own[...]
    small_own[at_bias + 2 : at_bias + 3] = skip_own[...]
    small_own[at_bias + 3 : at_bias + 4, : width // 4] = gain_own[...]
    pl.semaphore_wait(barrier, 3 + span)

    SMALL, STREAM, PROJ, STEP, GATE, OUT = range(6)
    plan = (
        (small_own, small, 1, None),
        (in_own, in_w, 0, (0, inner)),
        (xp_own, xp, 0, None),
        (dt_own, dt, 1, None),
        (in_own, in_w, 0, (inner, 2 * inner)),
        (out_own, out_w, 0, None),
    )

    def window(p, owner, half, q):
        src, dst, dim, cols = plan[p]
        high, wide = src.shape
        part = high // 4
        at = (half * 2 + q) * part
        lo, hi = cols or (0, wide)
        if dim == 0:
            return dst.at[pl.ds(pl.multiple_of(owner * high + at, part), part), lo:hi]
        col = pl.ds(pl.multiple_of(owner * wide, wide), wide)
        return dst.at[pl.ds(pl.multiple_of(at, part), part), col]

    def own(p, half, q):
        src, _, _, cols = plan[p]
        high, wide = src.shape
        part = high // 4
        lo, hi = cols or (0, wide)
        return src.at[pl.ds(pl.multiple_of((half * 2 + q) * part, part), part), lo:hi]

    def copy(src, dst, p, kind, who):
        return pltpu.make_async_remote_copy(
            src_ref=src, dst_ref=dst, send_sem=send.at[p, kind], recv_sem=recv.at[p, kind],
            device_id=who, device_id_type=MESH,
        )

    started = []

    def go(one):
        one.start()
        started.append(one)

    def start_own(p, routed=False):
        for q in (0, 1):
            go(copy(own(p, d, q), window(p, f, d, q), p, q, tox))
            go(copy(own(p, d, 1 - q), window(p, f, d, 1 - q), p, 3 - q, toy))
        if routed:
            for q in (0, 1):
                go(copy(own(p, d, q), window(p, f, d, q), p, 4 + q, tod))

    def small_copy(at, owner, part, who):
        rows_of = slice(*((state, at_bias + 4), (0, state))[part])
        cols = pl.ds(pl.multiple_of(owner * share, share), share)
        return pltpu.make_async_remote_copy(
            src_ref=small_own.at[rows_of], dst_ref=small.at[rows_of, cols],
            send_sem=send.at[SMALL, 3 * part + at], recv_sem=recv.at[SMALL, 3 * part + at],
            device_id=who, device_id_type=MESH,
        )

    def small_start(part):
        for at, who in enumerate((tox, toy, tod)):
            go(small_copy(at, f, part, who))

    def small_ready(part):
        for at, owner in enumerate((fx, fy, fd)):
            small_copy(at, owner, part, sib).wait_recv()

    def place_own(p):
        for half in (0, 1):
            for q in (0, 1):
                pltpu.make_async_copy(
                    own(p, half, q), window(p, f, half, q), local.at[p, half * 2 + q]
                ).start()

    def own_ready(p):
        for half in (0, 1):
            for q in (0, 1):
                pltpu.make_async_copy(
                    own(p, half, q), window(p, f, half, q), local.at[p, half * 2 + q]
                ).wait()

    def arrived(p, kind, owner, half, q):
        w = window(p, owner, half, q)
        copy(w, w, p, kind, sib).wait_recv()
        return w

    near = ((0, fx, 0), (3, fy, 1), (1, fx, 1), (2, fy, 0))
    diagonal = ((4, fd, 0), (5, fd, 1))

    def serve_near(p, routed=False):
        for kind, owner, q in near:
            w = arrived(p, kind, owner, d, q)
            if kind == 0 and not routed:
                go(copy(w, w, p, 4, toy))
            if kind == 3 and not routed:
                go(copy(w, w, p, 5, tox))
            go(copy(w, w, p, 6 + kind, sib))

    def serve_far(p):
        for kind, owner, q in diagonal:
            w = arrived(p, kind, owner, d, q)
            go(copy(w, w, p, 6 + kind, sib))

    def near_ready(p):
        for kind, owner, q in near:
            arrived(p, 6 + kind, owner, 1 - d, q)

    def far_ready(p):
        for kind, owner, q in diagonal:
            arrived(p, 6 + kind, owner, 1 - d, q)

    odd = lax.rem(s, 2)
    across_seq = {"seq": s + 1 - 2 * odd}
    owners = (fx, fx, fy, fy, fd, fd, fx, fy, fd)
    thirds = (0, 1, 0, 1, 0, 1, 2, 2, 2)

    def third(ref, p, base, half, which):
        _, _, _, cols = plan[p]
        high = plan[p][0].shape[0]
        tall = high // 2
        wide = tall if cols is None else cols[1] - cols[0]
        side = wide * 5 // 16
        first = (odd * (wide - side), side, (1 - odd) * (wide - side))[which]
        size = (side, wide - 2 * side, side)[which]
        row = base + half * tall
        if cols is None:
            return ref.at[pl.ds(pl.multiple_of(row + first, GROUP), size)]
        col = pl.ds(pl.multiple_of(cols[0] + first, LANES), size)
        return ref.at[pl.ds(pl.multiple_of(row, tall), tall), col]

    def place(p, kind, half):
        high = plan[p][0].shape[0]
        return third(plan[p][1], p, owners[kind] * high, half, thirds[kind])

    def start_thirds(p):
        for kind, which, who in ((0, 0, tox), (3, 1, toy), (1, 1, tox), (2, 0, toy)):
            to = third(plan[p][1], p, f * plan[p][0].shape[0], d, which)
            go(copy(third(plan[p][0], p, 0, d, which), to, p, kind, who))

    def serve(p, kinds):
        onward = {0: ((4, toy), (6, across_seq)), 2: ((7, across_seq),), 3: ((5, tox),)}
        onward[4] = ((8, across_seq),)
        for kind in kinds:
            w = place(p, kind, d)
            copy(w, w, p, kind, sib).wait_recv()
            for to, who in onward.get(kind, ()):
                go(copy(w, w, p, to, who))
            go(copy(w, w, p, 9 + kind, sib))

    serve_first = lambda p: serve(p, (0, 3, 1, 2))
    serve_rest = lambda p: serve(p, (4, 5, 6, 7, 8))

    def ready(p):
        own_ready(p)
        for kind in range(9):
            w = place(p, kind, 1 - d)
            copy(w, w, p, 9 + kind, sib).wait_recv()

    small_start(0)
    start_thirds(STREAM)
    for p in (STREAM, PROJ, STEP, GATE, OUT):
        place_own(p)
    pltpu.make_async_copy(
        small_own, small.at[:, pl.ds(pl.multiple_of(f * share, share), share)], local.at[SMALL, 0]
    ).start()
    def edges(c):
        return pltpu.make_async_remote_copy(
            src_ref=x.at[(c + 1) * ctx - GROUP : (c + 1) * ctx], dst_ref=hx.at[c],
            send_sem=halo.at[0, c], recv_sem=halo.at[1, c],
            device_id={"seq": jnp.minimum(s + 1, span - 1)}, device_id_type=MESH,
        )

    @pl.when(s < span - 1)
    def _():
        for c in range(seqs):
            edges(c).start()

    for c in range(seqs):
        t = s * ctx + lax.broadcasted_iota(jnp.int32, (ctx, LANES), 0)
        mask[c * ctx : (c + 1) * ctx] = (t < lengths[c]).astype(F32)

    def mask_step(r, carry):
        tok = pl.ds(pl.multiple_of(r * GROUP, GROUP), GROUP)
        held = jnp.concatenate([mask[tok]] * (width // LANES), 1)
        bg[tok] = (og[tok].astype(F32) * held).astype(BF16)
        return carry

    lax.fori_loop(0, rows // GROUP, mask_step, 0)

    pltpu.make_async_copy(
        small_own, small.at[:, pl.ds(pl.multiple_of(f * share, share), share)], local.at[SMALL, 0]
    ).wait()
    small_ready(0)

    @pl.when(s > 0)
    def _():
        for c in range(seqs):
            edges(c).wait_recv()

    gain_at = at_bias + 3
    gain = jnp.concatenate(
        [small[gain_at : gain_at + 1, j * share : j * share + width // 4] for j in range(4)], 1
    )

    def normalised(v):
        v = v.astype(F32)
        inverse = lax.rsqrt(jnp.mean(v * v, -1, keepdims=True) + EPS)
        return (v * inverse * gain).astype(BF16)

    def norm_step(r, carry):
        tok = pl.ds(pl.multiple_of(r * GROUP, GROUP), GROUP)
        normed[tok] = normalised(x[tok])
        return carry

    lax.fori_loop(0, rows // GROUP, norm_step, 0)
    for c in range(seqs):
        normed[rows + c * GROUP : rows + (c + 1) * GROUP] = normalised(hx[c])

    def project(total, high, first):
        def one(t, carry):
            cols = pl.ds(pl.multiple_of(t * CHUNK, CHUNK), CHUNK)
            right = in_w[:, pl.ds(pl.multiple_of(first + t * CHUNK, CHUNK), CHUNK)]
            total[:, cols] = dot(normed[:high], right)
            return carry

        lax.fori_loop(0, inner // CHUNK, one, 0)

    tall = rows + seqs * GROUP
    serve_first(STREAM)
    small_start(1)
    start_own(PROJ, True)
    start_own(STEP, True)
    start_own(GATE)
    serve_rest(STREAM)
    ready(STREAM)
    project(acc, tall, 0)
    small_ready(1)

    tile = 2 * LANES

    def columns(t, size=tile):
        return pl.ds(pl.multiple_of(t * size, size), size)

    def conv_step(t, carry):
        cols = columns(t)
        for c in range(seqs):
            before = acc[rows + c * GROUP : rows + (c + 1) * GROUP, cols].astype(BF16)
            stream = acc[c * ctx : (c + 1) * ctx, cols].astype(BF16)
            lead[c, :GROUP, cols] = before
            lead[c, GROUP:, cols] = stream
            held = jnp.concatenate([before, stream], 0).astype(F32)
            total = small[at_bias : at_bias + 1, cols]
            for k in range(TAPS):
                at = GROUP - TAPS + 1 + k
                total = total + small[state + k : state + k + 1, cols] * held[at : at + ctx]
            value, grad = silu_parts(total)
            slope[c * ctx : (c + 1) * ctx, cols] = grad.astype(BF16)
            u[c * ctx : (c + 1) * ctx, cols] = value.astype(BF16)
        return carry

    lax.fori_loop(0, inner // tile, conv_step, 0)
    for p in (PROJ, STEP):
        serve_near(p, True)
        serve_far(p)
    for p in (PROJ, STEP):
        near_ready(p)
        far_ready(p)
        own_ready(p)
    proj[...] = dot(u[...], xp[...])
    step_low[...] = proj[:, :rank].astype(BF16)

    def wide_step(i, carry):
        tok = pl.ds(pl.multiple_of(i * GROUP, GROUP), GROUP)
        held = proj[tok]
        for ref, first in ((bw, rank), (cw, rank + state)):
            value = held[:, first : first + state]
            c, at = i // groups, lax.rem(i, groups)
            ref[c, pl.ds(pl.multiple_of(at * GROUP, GROUP), GROUP)] = jnp.broadcast_to(
                value[:, :, None], (GROUP, state, LANES)
            )
        return carry

    lax.fori_loop(0, rows // GROUP, wide_step, 0)
    def delta_step(t, carry):
        cols = columns(t)
        for c in range(seqs):
            tok = slice(c * ctx, (c + 1) * ctx)
            value = dot(step_low[tok], dt[:, cols]) + small[at_bias + 1 : at_bias + 2, cols]
            sig[tok, cols] = jax.nn.sigmoid(value).astype(BF16)
            value = jnp.maximum(value, 0.0) + jnp.log1p(jnp.exp(-jnp.abs(value)))
            for i in range(groups):
                delta[c * groups + i, :, cols] = value[i * GROUP : (i + 1) * GROUP]
            sums[c : c + 1, cols] = jnp.sum(value, 0, keepdims=True)
            value = value * u[tok, cols].astype(F32)
            for i in range(groups):
                v[c * groups + i, :, cols] = value[i * GROUP : (i + 1) * GROUP]
        return carry

    sums[...] = jnp.zeros(sums.shape, F32)
    lax.fori_loop(0, inner // tile, delta_step, 0)

    def sums_copy(j):
        return pltpu.make_async_remote_copy(
            src_ref=sums, dst_ref=sums_in.at[s], send_sem=sums_send.at[j],
            recv_sem=sums_recv.at[s], device_id={"seq": j}, device_id_type=MESH,
        )

    def sums_start(o, carry):
        sums_copy(lax.rem(s + o, span)).start()
        return carry

    lax.fori_loop(1, span, sums_start, 0)

    def ends_copy(j, way, c):
        return pltpu.make_async_remote_copy(
            src_ref=ends.at[way, c], dst_ref=ends_in.at[s, c], send_sem=relay_send.at[j, c],
            recv_sem=relay_recv.at[s, c], device_id={"seq": j}, device_id_type=MESH,
        )

    def ends_start(first, count, way, c):
        def one(j, carry):
            ends_copy(j, way, c).start()
            return carry

        lax.fori_loop(first, count, one, 0)

    def forward_ends(c):
        for j in range(0, inner, CHUNK):
            cuts = [slice(j + i, j + i + LANES) for i in range(0, CHUNK, LANES)]
            rates = [-jnp.exp(small[:state, cut]) * LOG2E for cut in cuts]

            def one(i, h):
                h = list(h)
                for k in range(GROUP):
                    b = bw[c, i * GROUP + k]
                    for n, cut in enumerate(cuts):
                        step = delta[c * groups + i, k : k + 1, cut]
                        factor = jnp.exp2(jnp.broadcast_to(step, (state, LANES)) * rates[n])
                        row = jnp.broadcast_to(v[c * groups + i, k : k + 1, cut], (state, LANES))
                        h[n] = factor * h[n] + row * b
                return tuple(h)

            zero = tuple(jnp.zeros((state, LANES), F32) for _ in cuts)
            h = lax.fori_loop(0, groups, one, zero)
            for n, cut in enumerate(cuts):
                ends[0, c, :, cut] = h[n].astype(BF16)

    def backward_ends(c):
        for j in range(0, inner, CHUNK):
            cuts = [slice(j + i, j + i + LANES) for i in range(0, CHUNK, LANES)]
            rates = [-jnp.exp(small[:state, cut]) * LOG2E for cut in cuts]

            def one(i, carry):
                run, p = (list(value) for value in carry)
                for k in range(GROUP):
                    read = cw[c, i * GROUP + k]
                    for n, cut in enumerate(cuts):
                        step = delta[c * groups + i, k : k + 1, cut]
                        factor = jnp.exp2(jnp.broadcast_to(step, (state, LANES)) * rates[n])
                        row = dy[c * groups + i, k : k + 1, cut]
                        run[n] = run[n] * factor
                        p[n] = p[n] + run[n] * (read * jnp.broadcast_to(row, (state, LANES)))
                return tuple(run), tuple(p)

            one_s = tuple(jnp.ones((state, LANES), F32) for _ in cuts)
            zero = tuple(jnp.zeros((state, LANES), F32) for _ in cuts)
            _, p = lax.fori_loop(0, groups, one, (one_s, zero))
            for n, cut in enumerate(cuts):
                ends[1, c, :, cut] = p[n].astype(BF16)

    def stash(*pairs):
        for at, (src, dst) in pairs:
            one = pltpu.make_async_copy(src, dst, keep.at[at])
            one.start()
            kept.append(one)

    kept = []
    stash(
        (0, (normed.at[:rows], normed_full)), (1, (bg, bg_full)), (2, (lead, lead_full)),
        (3, (slope, slope_full)), (4, (u, u_full)), (5, (sig, sig_full)), (6, (delta, delta_full)),
        (7, (cw, cw_full)), (8, (xp, xp_full)), (9, (dt, dt_full)), (10, (small, small_full)),
        (15, (bw, bw_full)),
    )

    def ends_wait(j, c):
        pltpu.make_async_remote_copy(
            src_ref=ends.at[0, c], dst_ref=ends_in.at[j, c], send_sem=relay_send.at[j, c],
            recv_sem=relay_recv.at[j, c], device_id={"seq": j}, device_id_type=MESH,
        ).wait_recv()

    def join(ref, j, c):
        ends_wait(j, c)

        def one(t, carry):
            cols = columns(t, CHUNK)
            rates = -jnp.exp(small[:state, cols]) * LOG2E
            decay = jnp.exp2(sums_in[j, c : c + 1, cols] * rates)
            ref[c, :, cols] = decay * ref[c, :, cols] + ends_in[j, c, :, cols].astype(F32)
            return carry

        lax.fori_loop(0, inner // CHUNK, one, 0)

    def join_start(c):
        def one(j, carry):
            join(start, j, c)
            return carry

        lax.fori_loop(0, s, one, 0)

    def join_final(o, carry):
        for c in range(seqs):
            join(final, span - 1 - o, c)
        return carry

    def sums_wait(o, carry):
        j = lax.rem(s + o, span)
        pltpu.make_async_remote_copy(
            src_ref=sums, dst_ref=sums_in.at[j], send_sem=sums_send.at[j],
            recv_sem=sums_recv.at[j], device_id={"seq": j}, device_id_type=MESH,
        ).wait_recv()
        return carry

    parts = inner // CHUNK
    blocks = seqs * parts

    def held_copy(b):
        slot = lax.rem(b, HELD)
        return pltpu.make_async_copy(held.at[slot], held_all.at[b], held_sem.at[slot])

    def sweep_block(b, carry):
        c, slot = b // parts, lax.rem(b, HELD)
        first = lax.rem(b, parts) * CHUNK
        cuts = [pl.ds(pl.multiple_of(first + n, LANES), LANES) for n in range(0, CHUNK, LANES)]
        tiles = [slice(n, n + LANES) for n in range(0, CHUNK, LANES)]
        all_cols = pl.ds(pl.multiple_of(first, CHUNK), CHUNK)
        rates = [-jnp.exp(small[:state, cut]) * LOG2E for cut in cuts]
        skip = small[at_bias + 2 : at_bias + 3, all_cols]

        @pl.when(b >= HELD)
        def _():
            held_copy(b - HELD).wait()

        h = tuple(start[c, :, cut] for cut in cuts)
        for n, cut in enumerate(tiles):
            held[slot, 0, :, cut] = h[n].astype(BF16)

        def one(i, h):
            h = list(h)
            g = c * groups + i
            for first_row in range(0, GROUP, 8):
                stacks = [[] for _ in cuts]
                for k in range(first_row, first_row + 8):
                    b_in, read = bw[c, i * GROUP + k], cw[c, i * GROUP + k]
                    for n, cut in enumerate(cuts):
                        step = jnp.broadcast_to(delta[g, k : k + 1, cut], (state, LANES))
                        row = jnp.broadcast_to(v[g, k : k + 1, cut], (state, LANES))
                        h[n] = jnp.exp2(step * rates[n]) * h[n] + row * b_in
                        held[slot, i * GROUP + k + 1, :, tiles[n]] = h[n].astype(BF16)
                        part = h[n] * read
                        rows_sum(stacks[n], part[:8] + part[8:], True)
                for n, cut in enumerate(cuts):
                    y[g, first_row : first_row + 8, cut] = stacks[n][0][1]
            tok = pl.ds(pl.multiple_of(g * GROUP, GROUP), GROUP)
            y[g, :, all_cols] += skip * u[tok, all_cols].astype(F32)
            return tuple(h)

        lax.fori_loop(0, groups, one, h)
        held_copy(b).start()
        return carry

    def grad_part(owner):
        shard = pl.ds(pl.multiple_of(owner * share, share), share)
        gg[:, shard] = dot(bg[...], out_w[shard], across)

    forward_ends(0)
    ends_start(s + 1, span, 0, 0)
    serve_near(GATE)
    start_own(OUT)
    own_ready(GATE)
    forward_ends(1)
    ends_start(s + 1, span, 0, 1)
    lax.fori_loop(1, span, sums_wait, 0)
    start[...] = jnp.zeros(start.shape, F32)
    join_start(0)
    serve_far(GATE)
    lax.fori_loop(0, parts // 2, sweep_block, 0)
    near_ready(GATE)
    far_ready(GATE)
    stash((11, (in_w, in_full)))

    project(zacc, rows, inner)
    serve_near(OUT)
    lax.fori_loop(parts // 2, parts, sweep_block, 0)
    serve_far(OUT)
    own_ready(OUT)
    near_ready(OUT)
    for owner in (f, fx, fy):
        grad_part(owner)
    far_ready(OUT)
    grad_part(fd)

    def gate_step(t, carry):
        cols = columns(t)
        for c in range(seqs):
            tok = slice(c * ctx, (c + 1) * ctx)
            value, grad = silu_parts(zacc[tok, cols].astype(BF16).astype(F32))
            pieces = [y[c * groups + i, :, cols] for i in range(groups)]
            scanned = jnp.concatenate(pieces, 0)
            gated[tok, cols] = (scanned * value).astype(BF16)
            half = pl.ds(pl.multiple_of(lax.rem(t, 2) * tile, tile), tile)
            zg[t // 2, tok, half] = (gg[tok, cols] * scanned * grad).astype(BF16)
        return carry

    def back_step(t, carry):
        cols = columns(t)
        for c in range(seqs):
            tok = slice(c * ctx, (c + 1) * ctx)
            value = zacc[tok, cols].astype(BF16).astype(F32)
            value = gg[tok, cols] * (value * jax.nn.sigmoid(value))
            for i in range(groups):
                dy[c * groups + i, :, cols] = value[i * GROUP : (i + 1) * GROUP]
        return carry

    lax.fori_loop(0, inner // tile, back_step, 0)
    stash((12, (dy, dy_full)))
    for c in range(seqs):
        backward_ends(c)
        ends_start(0, s, 1, c)
    for c in range(1, seqs):
        join_start(c)
    lax.fori_loop(parts, blocks, sweep_block, 0)
    lax.fori_loop(0, inner // tile, gate_step, 0)
    stash((13, (gated, gated_full)), (14, (zg, zg_full)))

    def hidden_step(t, carry):
        cols = columns(t)
        keep_rows = jnp.concatenate([mask[...]] * (tile // LANES), 1)
        branch = dot(gated[...], out_w[:, cols])
        hidden_out[:, cols] = (x[:, cols].astype(F32) + keep_rows * branch).astype(BF16)
        return carry

    lax.fori_loop(0, width // tile, hidden_step, 0)
    final[...] = jnp.zeros(final.shape, F32)
    lax.fori_loop(0, span - 1 - s, join_final, 0)

    for one in started:
        one.wait_send()

    @pl.when(s < span - 1)
    def _():
        for c in range(seqs):
            edges(c).wait_send()

    def sent(o, carry):
        j = lax.rem(s + o, span)
        sums_copy(j).wait_send()
        for c in range(seqs):
            ends_copy(j, 0, c).wait_send()
        return carry

    lax.fori_loop(1, span, sent, 0)
    for one in kept:
        one.wait()
    for b in range(max(blocks - HELD, 0), blocks):
        held_copy(b).wait()


def front(x, og, lengths, taps, logs, cbias, dbias, skip, gain, xp_tall, in_own, out_own, dt_own, seqs):
    rows, width = x.shape
    share, inner = taps.shape[1], 4 * taps.shape[1]
    state, rank, used = logs.shape[0], dt_own.shape[0], LANES
    ctx = rows // seqs
    span = lax.axis_size("seq")
    parts = inner // CHUNK
    vmem, dma = pltpu.VMEM, pltpu.SemaphoreType.DMA
    whole, anywhere = pl.BlockSpec(memory_space=vmem), pl.BlockSpec(memory_space=pl.ANY)
    shape = jax.ShapeDtypeStruct
    grouped = (rows // GROUP, GROUP, inner)
    kept = [
        ((rows, width), BF16),
        ((rows, width), BF16),
        ((seqs, ctx + GROUP, inner), BF16),
        ((rows, inner), BF16),
        ((rows, inner), BF16),
        ((rows, inner), BF16),
        (grouped, F32),
        ((seqs, ctx, state, LANES), F32),
        ((seqs, ctx, state, LANES), F32),
        (grouped, F32),
        ((rows, inner), BF16),
        ((parts, rows, CHUNK), BF16),
        ((width, 2 * inner), BF16),
        ((inner, used), BF16),
        ((rank, inner), BF16),
        ((32, inner), F32),
    ]
    held = (ctx + 1, state, CHUNK)
    return pl.pallas_call(
        functools.partial(front_kernel, span),
        in_specs=[whole, whole, pl.BlockSpec(memory_space=pltpu.SMEM)]
        + [whole] * 7
        + [anywhere] * 3,
        out_specs=[whole] * 3 + [anywhere] * (1 + len(kept)),
        out_shape=[
            shape((rows, width), BF16),
            shape((rows, rank), BF16),
            shape((seqs, state, inner), F32),
            shape((seqs * parts,) + held, BF16),
        ]
        + [shape(*k) for k in kept],
        scratch_shapes=[
            vmem((width, 2 * inner), BF16),
            vmem((inner, width), BF16),
            vmem((inner, used), BF16),
            vmem((rank, inner), BF16),
            vmem((32, inner), F32),
            vmem((32, share), F32),
            vmem((share, LANES), BF16),
            vmem((seqs, GROUP, width), BF16),
            vmem((rows + seqs * GROUP, inner), F32),
            vmem((rows, inner), F32),
            vmem((rows + seqs * GROUP, width), BF16),
            vmem(grouped, F32),
            vmem((rows, used), F32),
            vmem((2, seqs, state, inner), BF16),
            vmem((8, inner), F32),
            vmem((span, seqs, state, inner), BF16),
            vmem((span, 8, inner), F32),
            vmem((rows, width), BF16),
            vmem((rows, LANES), F32),
            vmem((seqs, ctx + GROUP, inner), BF16),
            vmem((rows, inner), BF16),
            vmem((rows, inner), BF16),
            vmem((rows, inner), BF16),
            vmem(grouped, F32),
            vmem((seqs, ctx, state, LANES), F32),
            vmem((seqs, ctx, state, LANES), F32),
            vmem((rows, inner), F32),
            vmem(grouped, F32),
            vmem(grouped, F32),
            vmem((rows, inner), BF16),
            vmem((parts, rows, CHUNK), BF16),
            vmem((seqs, state, inner), F32),
            vmem((HELD,) + held, BF16),
            dma((6, 18)),
            dma((6, 18)),
            dma((2, seqs)),
            dma((span, seqs)),
            dma((span, seqs)),
            dma((span,)),
            dma((span,)),
            dma((6, 4)),
            dma((len(kept),)),
            dma((HELD,)),
        ],
        compiler_params=pltpu.CompilerParams(
            collective_id=0, has_side_effects=True, vmem_limit_bytes=63 << 20
        ),
        name="front",
    )(x, og, lengths, taps, logs, cbias, dbias, skip, gain, xp_tall, in_own, out_own, dt_own)


def back_kernel(
    span, state, rank,
    gated, bg, step_low, final, small, x_full, og_full,
    held_all, normed_full, lead_full, slope_full, u_full, sig_full, delta_full, bw_full,
    cw_full, dy_full, zg_full, in_full, xp_full, dt_full,
    input_grad, out_sum, in_sum, rest_sum,
    normed, lead, slope, u, sig, delta, bw, cw, dy, mixed, xp, dt, in_w, held, v, rl, cacc,
    bacc, logs, sums, x, og,
    pg, pg_full, cg, ng, rest, g, ra, rx, ry, zlo, zhi, tot,
    send, recv, halo, local, load, held_sem, in_sem,
):
    d, s, f = (lax.axis_index(a) for a in ("dp", "seq", "fsdp"))
    fx, fy, fd = f ^ 1, f ^ 2, f ^ 3
    chunks = tot.shape[0]
    rows, width = x.shape
    inner = gated.shape[1]
    seqs = cg.shape[0]
    ctx = rows // seqs
    parts = inner // CHUNK
    out_chunks = 2 * width // CHUNK
    in_chunks = 2 * parts
    last = out_chunks + in_chunks
    slots = g.shape[0]
    q = HR // 2
    roots = ((span - 1) // 2, span // 2)
    most = span // 2
    tox, toy, sib = {"fsdp": fx}, {"fsdp": fy}, {"dp": 1 - d}
    up, down = {"seq": jnp.minimum(s + 1, span - 1)}, {"seq": jnp.maximum(s - 1, 0)}
    contract = (((0,), (0,)), ((), ()))
    across = (((1,), (1,)), ((), ()))
    dot = lambda a, b, dims=(((1,), (0,)), ((), ())): lax.dot_general(
        a, b, dims, preferred_element_type=F32
    )

    parts_of = lambda v, c: v.at[pl.ds(c * (v.shape[0] // seqs), v.shape[0] // seqs)]
    by_context = ((delta, delta_full), (dy, dy_full), (u, u_full), (cw, cw_full), (bw, bw_full), (sig, sig_full))
    pairs = [
        (parts_of(dst, c), parts_of(src, c)) for c in range(seqs) for dst, src in by_context
    ]
    first_loads = len(pairs)
    pairs += [
        (mixed.at[:parts], zg_full), (normed, normed_full), (slope, slope_full), (lead, lead_full),
        (xp, xp_full), (dt, dt_full), (x, x_full), (og, og_full),
    ]
    loads = [pltpu.make_async_copy(src, dst, load.at[n]) for n, (dst, src) in enumerate(pairs)]

    def held_copy(b):
        slot = lax.rem(b, 2)
        return pltpu.make_async_copy(held_all.at[b], held.at[slot], held_sem.at[slot])

    def in_copy(k):
        slot = lax.rem(k, 2)
        first = pl.multiple_of(lax.rem(k + parts, 2 * parts) * CHUNK, CHUNK)
        return pltpu.make_async_copy(in_full.at[:, pl.ds(first, CHUNK)], in_w.at[slot], in_sem.at[slot])

    held_copy(0).start()
    for one in loads[: len(by_context)]:
        one.start()
    held_copy(1).start()
    for one in loads[len(by_context) :]:
        one.start()
    cg[:, ctx:] = jnp.zeros((seqs, cg.shape[1] - ctx, inner), F32)
    barrier = pltpu.get_barrier_semaphore()
    for who in (tox, toy, sib):
        pl.semaphore_signal(barrier, inc=1, device_id=who, device_id_type=MESH)

    @pl.when(s > 0)
    def _():
        pl.semaphore_signal(barrier, inc=1, device_id=down, device_id_type=MESH)

    @pl.when(s < span - 1)
    def _():
        pl.semaphore_signal(barrier, inc=1, device_id=up, device_id_type=MESH)

    ends = (s == 0) | (s == span - 1)
    pl.semaphore_wait(barrier, jnp.where(ends, 4, 5) if span > 1 else 3)

    def copy(kind, c, src, dst, who):
        return pltpu.make_async_remote_copy(
            src_ref=src, dst_ref=dst, send_sem=send.at[kind, c], recv_sem=recv.at[kind, c],
            device_id=who, device_id_type=MESH,
        )

    lo, hi = slice(0, q), slice(q, HR)
    A = lambda c: copy(0, c, g.at[lax.rem(c, slots), :, 1 - d], ra.at[c], sib)
    X0 = lambda c: copy(1, c, ra.at[c, fd, lo], rx.at[c, 0], tox)
    X1 = lambda c: copy(2, c, ra.at[c, fx, lo], rx.at[c, 1], tox)
    X2 = lambda c: copy(3, c, ra.at[c, fx, hi], rx.at[c, 2], tox)
    Y0 = lambda c: copy(4, c, ra.at[c, fd, hi], ry.at[c, 0], toy)
    Y2 = lambda c: copy(5, c, ra.at[c, fy, hi], ry.at[c, 2], toy)
    Y1 = lambda c: copy(6, c, ra.at[c, fy, lo], ry.at[c, 1], toy)
    part = (lo, hi)
    ZU = lambda c, h: copy(7 + h, c, ra.at[c, f, part[h]], zlo.at[c, part[h]], up)
    ZD = lambda c, h: copy(9 + h, c, ra.at[c, f, part[h]], zhi.at[c, part[h]], down)
    TU = lambda c, h: copy(11 + h, c, tot.at[c, d, part[h]], tot.at[c, d, part[h]], up)
    TD = lambda c, h: copy(13 + h, c, tot.at[c, d, part[h]], tot.at[c, d, part[h]], down)
    D = lambda c, h: copy(15 + h, c, tot.at[c, d, part[h]], tot.at[c, d, part[h]], sib)
    below, above = [s < r for r in roots], [s > r for r in roots]
    spot = [
        jnp.where(below[h], s, jnp.where(above[h], span - 1 - s, 0)) for h in range(2)
    ]
    far = [jnp.abs(s - r) for r in roots]

    def stage(c, run):
        @pl.when((c >= 0) & (c < chunks))
        def _():
            run(c)

    def produce(c):
        slot = lax.rem(c, slots)

        @pl.when(c >= slots)
        def _():
            A(c - slots).wait_send()

        @pl.when(c < out_chunks)
        def _():
            r = c // (width // CHUNK)
            col = lax.rem(c, width // CHUNK) * CHUNK
            right = bg[:, pl.ds(pl.multiple_of(col, CHUNK), CHUNK)]
            for j in range(4):
                for h in range(2):
                    at = j * (inner // 4) + h * (inner // 8) + r * HR
                    left = gated[:, pl.ds(pl.multiple_of(at, HR), HR)]
                    g[slot, j, h] = dot(left, right, contract).astype(BF16)

        @pl.when((c >= out_chunks) & (c < last))
        def _():
            right = mixed[c - out_chunks]
            for j in range(4):
                t = dot(normed[:, j * 2 * HR : (j + 1) * 2 * HR], right, contract).astype(BF16)
                g[slot, j, 0] = t[:HR]
                g[slot, j, 1] = t[HR:]

        @pl.when(c == last)
        def _():
            for j in range(4):
                for h in range(2):
                    cols = slice(j * CHUNK, (j + 1) * CHUNK)
                    g[slot, j, h] = rest[h * HR : (h + 1) * HR, cols].astype(BF16)

        A(c).start()

    def first_sum(c):
        A(c).wait_recv()
        for j in range(4):
            own = g[lax.rem(c, slots), j, d]
            ra[c, j] = ra[c, j] + own
        X0(c).start()
        Y0(c).start()
        X1(c).start()
        Y2(c).start()

    def second_sum(c):
        X0(c).wait_recv()
        ra[c, fy, lo] = ra[c, fy, lo] + rx[c, 0]
        Y1(c).start()
        Y0(c).wait_recv()
        ra[c, fx, hi] = ra[c, fx, hi] + ry[c, 0]
        X2(c).start()

    def third_sum(c):
        X1(c).wait_recv()
        Y2(c).wait_recv()
        X2(c).wait_recv()
        Y1(c).wait_recv()
        for k, piece in enumerate((lo, hi)):
            total = ra[c, f, piece].astype(F32) + rx[c, 1 + k].astype(F32) + ry[c, 1 + k].astype(F32)
            ra[c, f, piece] = total.astype(BF16)

    def inward(c, h):
        @pl.when(below[h] & (s > 0))
        def _():
            ZU(c, h).wait_recv()
            ra[c, f, part[h]] = ra[c, f, part[h]] + zlo[c, part[h]]

        @pl.when(above[h] & (s < span - 1))
        def _():
            ZD(c, h).wait_recv()
            ra[c, f, part[h]] = ra[c, f, part[h]] + zhi[c, part[h]]

        pl.when(below[h])(lambda: ZU(c, h).start())
        pl.when(above[h])(lambda: ZD(c, h).start())

    def at_root(c, h):
        total = ra[c, f, part[h]].astype(F32)
        if roots[h] > 0:
            ZU(c, h).wait_recv()
            total = total + zlo[c, part[h]].astype(F32)
        if span - 1 > roots[h]:
            ZD(c, h).wait_recv()
            total = total + zhi[c, part[h]].astype(F32)
        tot[c, d, part[h]] = total.astype(BF16)
        if roots[h] > 0:
            TD(c, h).start()
        if span - 1 > roots[h]:
            TU(c, h).start()
        D(c, h).start()

    def outward(c, h):
        @pl.when(above[h])
        def _():
            TU(c, h).wait_recv()
            pl.when(s < span - 1)(lambda: TU(c, h).start())

        @pl.when(below[h])
        def _():
            TD(c, h).wait_recv()
            pl.when(s > 0)(lambda: TD(c, h).start())

        D(c, h).start()

    tile = 2 * LANES

    def columns(t, size=tile):
        return pl.ds(pl.multiple_of(t * size, size), size)

    def back_block(b):
        c, slot = b // parts, lax.rem(b, 2)
        groups = ctx // GROUP
        first = lax.rem(b, parts) * CHUNK
        cuts = [pl.ds(pl.multiple_of(first + n, LANES), LANES) for n in range(0, CHUNK, LANES)]
        tiles = [slice(n, n + LANES) for n in range(0, CHUNK, LANES)]
        cols = pl.ds(pl.multiple_of(first, CHUNK), CHUNK)
        rates = [-jnp.exp(small[:state, cut]) * LOG2E for cut in cuts]
        skip = small[TAPS + state + 2 : TAPS + state + 3, cols]
        held_copy(b).wait()

        def one(turn, carry):
            i = groups - 1 - turn
            at = c * groups + i
            tok = pl.ds(pl.multiple_of(at * GROUP, GROUP), GROUP)
            p, total, kept = (list(value) for value in carry)
            value, out, gain = u[tok, cols].astype(F32), dy[at, :, cols], delta[at, :, cols]
            v[...] = gain * value
            drive_parts, delta_parts = [[], []], [[], []]
            for pair in range(0, len(cuts), 2):
                which = range(pair, pair + 2)
                after = {n: held[slot, (i + 1) * GROUP, :, tiles[n]].astype(F32) for n in which}
                for half in (1, 0):
                    drives, deltas = ({n: [] for n in which} for _ in range(2))
                    for k in reversed(range(half * 8, half * 8 + 8)):
                        t = i * GROUP + k
                        b_in, read = bw[c, t], cw[c, t]
                        b_parts, c_parts = [], []
                        for n in which:
                            row = lambda tile: jnp.broadcast_to(tile, (state, LANES))
                            step, back = row(delta[at, k : k + 1, cuts[n]]), row(dy[at, k : k + 1, cuts[n]])
                            grad = read * back + p[n]
                            p[n] = jnp.exp2(step * rates[n]) * grad
                            before = held[slot, t, :, tiles[n]].astype(F32)
                            w = p[n] * before
                            total[n] = total[n] + w * step
                            part = w * rates[n]
                            rows_sum(deltas[n], part[:8] + part[8:], False)
                            part = grad * b_in
                            rows_sum(drives[n], part[:8] + part[8:], False)
                            b_parts.append(grad * row(v[k : k + 1, tiles[n]]))
                            c_parts.append(after[n] * back)
                            after[n] = before
                        bacc[c * ctx + t] += b_parts[0] + b_parts[1]
                        cacc[c * ctx + t] += c_parts[0] + c_parts[1]
                    drive_parts[half] += [drives[n][0][1] for n in which]
                    delta_parts[half] += [deltas[n][0][1] for n in which]
            joined = lambda halves: jnp.concatenate([jnp.concatenate(h, 1) for h in halves], 0)
            drive_grad, delta_part = joined(drive_parts), joined(delta_parts)
            raw_grad = drive_grad * value + delta_part * (1.0 / LOG2E)
            raw_grad = raw_grad * sig[tok, cols].astype(F32)
            rl[tok, cols] = raw_grad.astype(BF16)
            dy[at, :, cols] = out * skip + drive_grad * gain
            kept[0] = kept[0] + (out * value)[:8] + (out * value)[8:]
            kept[1] = kept[1] + raw_grad[:8] + raw_grad[8:]
            return tuple(p), tuple(total), tuple(kept)

        zero = tuple(jnp.zeros((state, LANES), F32) for _ in cuts)
        none = jnp.zeros((8, CHUNK), F32)
        begin = tuple(final[c, :, cut] for cut in cuts)
        _, total, kept = lax.fori_loop(0, groups, one, (begin, zero, (none, none)))
        for n, cut in enumerate(cuts):
            logs[:, cut] += total[n]
        sums[0, :, cols] += kept[0]
        sums[1, :, cols] += kept[1]

        @pl.when(b + 2 < blocks)
        def _():
            held_copy(b + 2).start()

    def proj_work():
        step_grad = dot(rl[...], dt[...], across)
        col = lax.broadcasted_iota(jnp.int32, (state, LANES), 1)
        n = lax.broadcasted_iota(jnp.int32, (state, LANES), 0)
        ones = jnp.ones((LANES, LANES), BF16)

        def one(r, carry):
            tok = pl.ds(pl.multiple_of(r * GROUP, GROUP), GROUP)
            total = pg_full[tok]
            for ref, first in ((bacc, rank), (cacc, rank + state)):
                value = dot(ref[tok].reshape(GROUP * state, LANES).astype(BF16), ones)
                keep = jnp.where(col == n + first, value.reshape(GROUP, state, LANES), 0.0)
                total = total + jnp.sum(keep, 1)
            pg[tok] = total.astype(BF16)
            return carry

        pg_full[...] = jnp.concatenate([step_grad, jnp.zeros((rows, LANES - rank), F32)], 1)
        lax.fori_loop(0, rows // GROUP, one, 0)

    def weight_work():
        first = TAPS + state + 4
        used = rank + 2 * state

        def weights(t, carry):
            cols = columns(t)
            rest[first : first + rank, cols] = dot(step_low[...], rl[:, cols], contract)
            rest[first + rank : first + rank + used, cols] = dot(pg[...], u[:, cols], contract)[:used]
            kept = -logs[:, cols] * jnp.exp(small[:state, cols])
            rest[:state, cols] = kept
            at = TAPS + state
            rest[at + 1 : at + 2, cols] = jnp.sum(sums[1, :, cols], 0, keepdims=True)
            rest[at + 2 : at + 3, cols] = jnp.sum(sums[0, :, cols], 0, keepdims=True)
            return carry

        lax.fori_loop(0, inner // tile, weights, 0)

    def conv_work(first, count):
        def one(t, carry):
            cols = columns(t)
            shift = jnp.zeros((1, tile), F32)
            taps = [jnp.zeros((1, tile), F32) for _ in range(TAPS)]
            for c in range(seqs):
                tok = slice(c * ctx, (c + 1) * ctx)
                weight = xp[columns(t)]
                back = dot(pg[tok], weight, across)
                own = range(c * ctx // GROUP, (c + 1) * ctx // GROUP)
                grad = jnp.concatenate([dy[at, :, cols] for at in own], 0) + back
                grad = grad * slope[tok, cols].astype(F32)
                cg[c, :ctx, cols] = grad
                before = lead[c, :, cols].astype(F32)
                shift = shift + jnp.sum(grad, 0, keepdims=True)
                for k in range(TAPS):
                    at = GROUP - TAPS + 1 + k
                    taps[k] = taps[k] + jnp.sum(grad * before[at : at + ctx], 0, keepdims=True)
            for k in range(TAPS):
                rest[state + k : state + k + 1, cols] = taps[k]
            rest[TAPS + state : TAPS + state + 1, cols] = shift
            return carry

        lax.fori_loop(first, first + count, one, 0)

    edge = cg.shape[1] - ctx
    H = lambda: pltpu.make_async_remote_copy(
        src_ref=cg.at[:, :edge], dst_ref=cg.at[:, ctx:], send_sem=halo.at[0],
        recv_sem=halo.at[1], device_id=down, device_id_type=MESH,
    )

    def halo_send():
        pl.when(s > 0)(lambda: H().start())

    def stream_work():
        pl.when(s < span - 1)(lambda: H().wait_recv())

        def one(t, carry):
            cols = columns(t)
            for c in range(seqs):
                total = 0.0
                for k in range(TAPS):
                    at = TAPS - 1 - k
                    total = total + small[state + k : state + k + 1, cols] * cg[c, at : at + ctx, cols]
                half = pl.ds(pl.multiple_of(lax.rem(t, 2) * tile, tile), tile)
                mixed[parts + t // 2, c * ctx : (c + 1) * ctx, half] = total.astype(BF16)
            return carry

        lax.fori_loop(0, inner // tile, one, 0)
        pl.when(s > 0)(lambda: H().wait_send())

    def norm_work(first, count):
        def one(k, carry):
            in_copy(k).wait()
            ng[...] += dot(mixed[k], in_w[lax.rem(k, 2)], across)

            @pl.when(k + 2 < 2 * parts)
            def _():
                in_copy(k + 2).start()

            return carry

        if first == 0:
            ng[...] = jnp.zeros(ng.shape, F32)
        lax.fori_loop(first, first + count, one, 0)

    def input_work():
        share = width // 4
        at = TAPS + state + 3
        gain = jnp.concatenate(
            [small[at : at + 1, j * CHUNK : j * CHUNK + share] for j in range(4)], 1
        )

        def one(r, total):
            tok = pl.ds(pl.multiple_of(r * GROUP, GROUP), GROUP)
            xs = x[tok].astype(F32)
            inverse = lax.rsqrt(jnp.mean(xs * xs, -1, keepdims=True) + EPS)
            grad = ng[tok]
            scaled = grad * gain
            slope = jnp.mean(scaled * xs, -1, keepdims=True)
            out = inverse * scaled - xs * (inverse * inverse * inverse * slope)
            input_grad[tok] = (out + og[tok].astype(F32)).astype(BF16)
            return total + grad * (xs * inverse)

        total = lax.fori_loop(0, rows // GROUP, one, jnp.zeros((GROUP, width), F32))
        total = jnp.sum(total, 0, keepdims=True)
        for j in range(4):
            rest[at : at + 1, j * CHUNK : j * CHUNK + share] = total[:, j * share : (j + 1) * share]

    blocks = seqs * parts
    tiles = inner // tile
    pause = 3
    held_back = out_chunks + parts
    base = 1 + 2 * SLACK + 1

    def prepare():
        for ref in (cacc, bacc, logs, sums, rest):
            ref[...] = jnp.zeros(ref.shape, F32)

    def blocks_work(i):
        pl.when(i == 0)(prepare)
        for c in range(seqs):

            @pl.when(i == c * parts)
            def _():
                for one in loads[c * len(by_context) : (c + 1) * len(by_context)]:
                    one.wait()

        pl.when(i < blocks)(lambda: back_block(i))

    def late_work(i):
        at = held_back

        @pl.when(i == at)
        def _():
            proj_work()
            conv_work(0, tiles)
            halo_send()
            in_copy(0).start()
            in_copy(1).start()

        pl.when(i == at + 1)(weight_work)
        pl.when(i == at + 2)(stream_work)
        pl.when(i == at + 4)(lambda: norm_work(0, parts))
        pl.when(i == at + 5)(lambda: norm_work(parts, parts))
        pl.when(i == at + 6)(input_work)

    def step(i, carry):
        def at(offset):
            k = i - offset
            return jnp.where(k < held_back, k, jnp.where(k < held_back + pause, -1, k - pause))

        @pl.when(i == out_chunks)
        def _():
            for one in loads[first_loads:]:
                one.wait()

        for h in range(2):
            run = lambda f: lambda c: f(c, h)
            away = s != roots[h]
            pl.when(away)(lambda: stage(at(base + SLACK * (most + far[h])), run(outward)))
            pl.when(~away)(lambda: stage(at(base + SLACK * most), run(at_root)))
            pl.when(away)(lambda: stage(at(base + SLACK * spot[h]), run(inward)))
        stage(at(1 + 2 * SLACK), third_sum)
        stage(at(1 + SLACK), second_sum)
        stage(at(1), first_sum)
        stage(at(0), produce)
        blocks_work(i)
        late_work(i)
        return carry

    lax.fori_loop(0, chunks + pause + base + 2 * SLACK * most + 1, step, 0)

    def finish(c, carry):
        pl.when(c >= chunks - slots)(lambda: A(c).wait_send())
        for t in (X0, X1, X2, Y0, Y1, Y2):
            t(c).wait_send()
        for h, root in enumerate(roots):
            pl.when(below[h])(lambda: ZU(c, h).wait_send())
            pl.when(above[h])(lambda: ZD(c, h).wait_send())
            if root > 0:
                pl.when((s <= root) & (s > 0))(lambda: TD(c, h).wait_send())
            if span - 1 > root:
                pl.when((s >= root) & (s < span - 1))(lambda: TU(c, h).wait_send())
            D(c, h).wait_send()
            D(c, h).wait_recv()
        return carry

    lax.fori_loop(0, chunks, finish, 0)
    copies = []
    for c in range(chunks):
        for h in range(2):
            if c < out_chunks:
                r, col = c // (width // CHUNK), c % (width // CHUNK)
                first = h * (inner // 8) + r * HR
                to = out_sum.at[first : first + HR, col * CHUNK : (col + 1) * CHUNK]
            elif c < last:
                col = (c - out_chunks + parts) % (2 * parts)
                to = in_sum.at[h * HR : (h + 1) * HR, col * CHUNK : (col + 1) * CHUNK]
            else:
                to = rest_sum.at[h * HR : (h + 1) * HR]
            copies.append(pltpu.make_async_copy(tot.at[c, h], to, local.at[c, h]))
    for one in copies:
        one.start()
    for one in copies:
        one.wait()


def back(gated, bg, step_low, final, small, x, og, far):
    rows, inner = gated.shape
    width = x.shape[1]
    seqs, state = final.shape[:2]
    ctx, rank, parts = rows // seqs, step_low.shape[1], inner // CHUNK
    span = lax.axis_size("seq")
    out_chunks, in_chunks = 2 * width // CHUNK, 2 * parts
    n = out_chunks + in_chunks + 1
    vmem, dma = pltpu.VMEM, pltpu.SemaphoreType.DMA
    anywhere = pl.BlockSpec(memory_space=pl.ANY)
    whole = pl.BlockSpec(memory_space=vmem)
    shape = jax.ShapeDtypeStruct
    like = lambda v: vmem(v.shape, v.dtype)
    (held, normed, lead, slope, u, sig, delta, bw, cw, dy, zg, in_full, xp, dt) = far
    return pl.pallas_call(
        functools.partial(back_kernel, span, state, rank),
        in_specs=[whole] * 5 + [anywhere] * (2 + len(far)),
        out_specs=[whole, anywhere, anywhere, anywhere],
        out_shape=[
            shape((rows, width), BF16),
            shape((inner // 4, width), BF16),
            shape((width // 4, 2 * inner), BF16),
            shape((2 * HR, CHUNK), BF16),
        ],
        scratch_shapes=[
            *map(like, (normed, lead, slope, u, sig, delta, bw, cw, dy)),
            vmem((in_chunks, rows, CHUNK), BF16),
            like(xp),
            like(dt),
            vmem((2, width, CHUNK), BF16),
            vmem((2,) + held.shape[1:], BF16),
            vmem((GROUP, CHUNK), F32),
            vmem((rows, inner), BF16),
            vmem((rows, state, LANES), F32),
            vmem((rows, state, LANES), F32),
            vmem((state, inner), F32),
            vmem((2, 8, inner), F32),
            like(x),
            like(og),
            vmem((rows, LANES), BF16),
            vmem((rows, LANES), F32),
            vmem((seqs, ctx + 8, inner), F32),
            vmem((rows, width), F32),
            vmem((2 * HR, inner), F32),
            vmem((4, 4, 2, HR, CHUNK), BF16),
            vmem((n, 4, HR, CHUNK), BF16),
            vmem((n, 3, HR // 2, CHUNK), BF16),
            vmem((n, 3, HR // 2, CHUNK), BF16),
            vmem((n, HR, CHUNK), BF16),
            vmem((n, HR, CHUNK), BF16),
            vmem((n, 2, HR, CHUNK), BF16),
            dma((17, n)),
            dma((17, n)),
            dma((2,)),
            dma((n, 2)),
            dma((12 + 8,)),
            dma((2,)),
            dma((2,)),
        ],
        compiler_params=pltpu.CompilerParams(
            collective_id=1, has_side_effects=True, vmem_limit_bytes=63 << 20
        ),
        name="back",
    )(gated, bg, step_low, final, small, x, og, *far)


def finish_kernel(
    state, rank, used, in_sum, out_sum, rest, hidden, grad,
    gain, in_w, taps, cbias, xp, dt, dbias, logs, skip, out_w, hidden_out, grad_out,
):
    hidden_out[...] = hidden[...]
    grad_out[...] = grad[...]
    in_w[...] = in_sum[...].astype(F32)
    out_w[...] = out_sum[...].astype(F32)
    at = TAPS + state
    row = lambda first, count=1: rest[...].astype(F32)[first : first + count]
    logs[...] = row(0, state)
    taps[...] = row(state, TAPS)
    cbias[...] = row(at)
    dbias[...] = row(at + 1)
    skip[...] = row(at + 2)
    gain[...] = row(at + 3)[:, : gain.shape[1]]
    dt[...] = row(at + 4, rank)
    xp[...] = row(at + 4 + rank, used)


def finish(in_sum, out_sum, rest, hidden, grad, state, rank, used):
    steps = 2
    share = rest.shape[1]
    tall = lambda v: pl.BlockSpec((v.shape[0] // steps, v.shape[1]), lambda i: (i, 0))
    fixed = lambda *v: pl.BlockSpec(v, lambda i: (0, 0))
    small = [(1, in_sum.shape[0]), (TAPS, share), (1, share), (used, share), (rank, share)]
    small += [(1, share), (state, share), (1, share)]
    shape = lambda v: jax.ShapeDtypeStruct(v, F32)
    return pl.pallas_call(
        functools.partial(finish_kernel, state, rank, used),
        grid=(steps,),
        in_specs=[tall(in_sum), tall(out_sum), fixed(*rest.shape), tall(hidden), tall(grad)],
        out_specs=[fixed(*small[0]), tall(in_sum)]
        + [fixed(*v) for v in small[1:]]
        + [tall(out_sum), tall(hidden), tall(grad)],
        out_shape=[shape(small[0]), shape(in_sum.shape)]
        + [shape(v) for v in small[1:]]
        + [shape(out_sum.shape)]
        + [jax.ShapeDtypeStruct(v.shape, v.dtype) for v in (hidden, grad)],
        compiler_params=pltpu.CompilerParams(vmem_limit_bytes=63 << 20),
        name="finish",
    )(in_sum, out_sum, rest, hidden, grad)


def body(
    hidden_in, lengths, norm_gain, in_weight, conv_weight, conv_bias, xproj_weight,
    dt_weight, dt_bias, a_log, skip_gain, out_weight, out_grad,
):
    seqs, ctx, width = hidden_in.shape
    taps, share = conv_weight.shape
    state = a_log.shape[0]
    rank = dt_weight.shape[0]
    rows = ctx * seqs
    row = lambda v: v.reshape(1, -1)
    x, og = hidden_in.reshape(rows, width), out_grad.reshape(rows, width)
    used = xproj_weight.shape[1]
    (
        hidden_out, step_low, final, held, normed, branch_grad, lead, slope, u, sig, delta,
        b_wide, c_wide, y_grad, gated, z_grad, in_matrix, proj_matrix, step_matrix, small,
    ) = front(
        x, og, lengths, conv_weight, a_log, row(conv_bias), row(dt_bias), row(skip_gain),
        row(norm_gain), xproj_weight.T, in_weight, out_weight, dt_weight, seqs,
    )
    far = (
        held, normed, lead, slope, u, sig, delta, b_wide, c_wide, y_grad, z_grad, in_matrix,
        proj_matrix, step_matrix,
    )
    input_grad, out_sum, in_sum, rest = back(
        gated, branch_grad, step_low, final, small, x, og, far
    )
    (
        gain, in_w, taps_grad, cbias, proj_w, step_w, dbias, logs, skip, out_w, hidden_out, input_grad,
    ) = finish(in_sum, out_sum, rest, hidden_out, input_grad, state, rank, used)
    flat = lambda v: v.reshape(-1)
    return (
        hidden_out.reshape(seqs, ctx, width), input_grad.reshape(seqs, ctx, width), flat(gain), in_w,
        taps_grad, flat(cbias), proj_w.T, step_w, flat(dbias), logs, flat(skip), out_w,
    )


def solution(mesh):
    tokens = P(("dp", "fsdp"), "seq", None)
    return jax.shard_map(
        body,
        mesh=mesh,
        in_specs=(
            tokens, P(("dp", "fsdp")), P("fsdp"), P("fsdp", None), P(None, "fsdp"), P("fsdp"),
            P("fsdp", None), P(None, "fsdp"), P("fsdp"), P(None, "fsdp"), P("fsdp"),
            P("fsdp", None), tokens,
        ),
        out_specs=(
            tokens, tokens, P("fsdp"), P("fsdp", None), P(None, "fsdp"), P("fsdp"),
            P("fsdp", None), P(None, "fsdp"), P("fsdp"), P(None, "fsdp"), P("fsdp"),
            P("fsdp", None),
        ),
        check_vma=False,
    )
```
